32 devices in a mesh: grp: 16 (over z, x, core), slab: 2 (over y).
Axes of the slice: x: 2, y: 2, z: 4, core: 2. Of those that a mesh axis runs over, the one named last changes fastest.
Arguments:
- fwd_fields: float32 [16, 6, 16, 128, 128], P('grp', None, 'slab'), may hold values from -6 to 6
- adj_fields: float32 [16, 6, 16, 128, 128], P('grp', None, 'slab'), may hold values from -6 to 6
- density: float32 [16, 128, 128], P('slab', 'grp'), may hold values from 0 to 1
- block_ids: int32 [16], replicated, may hold values from 0 to 15, each once
- material_idx: int32 [16], replicated, may hold values from 0 to 3
- material_eps: float32 [4], replicated, may hold values from 1 to 12
- source_pos: int32 [16, 3], P('grp'), may hold values from 0 to 127, as said below
- wave_idx: int32 [16], P('grp'), may hold values from 0 to 3
Outputs:
- final_fields: float32 [16, 6, 16, 128, 128], P('grp', None, 'slab')
- grad_density: float32 [16, 128, 128], P('slab', 'grp')
The draws below stay inside these ranges and needn't reach their ends.
Inputs may be any that keep to these rules, and one draw needn't show every extreme that they name: `block_ids`: a permutation of the 16 blocks. `source_pos`: cells inside the window: z below 16, x below 128, y below 128; some group's z is 0, some group's x is 127 and some group's y is 127.
All inputs are finite; a program needn't handle non-finite values.
Results may differ from the reference program's by a relative error of at most 0.0003.
Values sent between devices are 32-bit elements; how exact they have to be, the bound alone decides.
No kernel may reach another device: no remote copies, remote signals or barrier semaphores. Data moves between devices by JAX's collectives and lax.ppermute only.
A program may use at most 64 MiB of HBM per device.

```python
import math
import jax
import jax.numpy as jnp
from jax import lax

X = 128
Y = 128
STEPS = 4
NWAVE = 4
NMAT = 4
GROUPS = 16
NBLK = 16
BX = 8
NZ = 16


def draw_source_pos(key, part):
    key_z, key_x, key_y, key_pick = jax.random.split(key, 4)
    depth_pos = jax.random.randint(key_z, (GROUPS,), 0, NZ)
    row_pos = jax.random.randint(key_x, (GROUPS,), 0, X)
    col_pos = jax.random.randint(key_y, (GROUPS,), 0, Y)
    picks = jax.random.randint(key_pick, (3,), 0, GROUPS)
    group_ids = jnp.arange(GROUPS, dtype=jnp.int32)
    depth_pos = jnp.where(group_ids == picks[0], 0, depth_pos)
    row_pos = jnp.where(group_ids == picks[1], X - 1, row_pos)
    col_pos = jnp.where(group_ids == picks[2], Y - 1, col_pos)
    return jnp.stack([depth_pos, row_pos, col_pos], axis=1).astype(jnp.int32)


def with_ends(drawn, own_key, least, high):
    longest = drawn.shape.index(max(drawn.shape))
    spots = []
    for shift in (0, 1):
        where = [jax.random.randint(jax.random.fold_in(own_key, axis), (), 0, length) for axis, length in enumerate(drawn.shape)]
        where[longest] = (where[longest] + shift) % drawn.shape[longest]
        spots.append(tuple(where))
    return drawn.at[spots[0]].set(least).at[spots[1]].set(high)


def block_levels(rng, dims, pieces, smallest, top_value):
    loudness = 1.0
    for dim, shards_of in pieces:
        draws = jax.random.uniform(jax.random.fold_in(jax.random.fold_in(rng, 6), dim), (shards_of,), jnp.float32, smallest / len(pieces), top_value / len(pieces))
        loudness = loudness * jnp.repeat(jnp.exp(draws), dims[dim] // shards_of).reshape((-1,) + (1,) * (len(dims) - 1 - dim))
    return loudness


def bell_draw(key, extent, deviation, reach, cuts=(), kind=jnp.bfloat16):
    drawn = jax.random.normal(key, extent, jnp.float32) * deviation
    if len(cuts) > 0:
        drawn = block_levels(key, extent, cuts, -0.22, 0.18) * drawn
    return jnp.clip(drawn, min=-reach, max=reach).astype(kind)


def setup_inputs(seed: int = 0) -> dict:
    splits = jax.random.split(jax.random.key(seed), 9)
    fwd_fields = bell_draw(splits[0], (GROUPS, 6, NZ, X, Y), 1.0, 6.0, ((0, 16), (2, 2)), jnp.float32)
    adj_fields = bell_draw(splits[1], (GROUPS, 6, NZ, X, Y), 1.0, 6.0, ((0, 16), (2, 2)), jnp.float32)
    density = jnp.clip(1.0 * jax.random.uniform(splits[2], (NZ, X, Y), jnp.float32) ** block_levels(splits[2], (NZ, X, Y), ((0, 2), (1, 16)), -0.2, 0.2), 0.0, 1.0)
    block_ids = jax.random.permutation(splits[3], NBLK).astype(jnp.int32)
    material_idx = with_ends(jax.random.randint(splits[4], (NBLK,), 0, NMAT), jax.random.fold_in(splits[4], 1), 0, NMAT - 1).astype(jnp.int32)
    material_eps = jnp.clip(jnp.exp(jax.random.uniform(splits[5], (NMAT,), jnp.float32, math.log(1.0), math.log(12.0))), 1.0, 12.0)
    source_pos = draw_source_pos(jax.random.fold_in(splits[8], 71), 0)
    wave_idx = with_ends(jax.random.randint(splits[7], (GROUPS,), 0, NWAVE), jax.random.fold_in(splits[7], 1), 0, NWAVE - 1).astype(jnp.int32)
    return dict(fwd_fields=fwd_fields, adj_fields=adj_fields, density=density, block_ids=block_ids, material_idx=material_idx, material_eps=material_eps, source_pos=source_pos, wave_idx=wave_idx)


COURANT = 0.5
AMPLITUDE = 4.0

def fwd_diff(field, axis):
    pads = [(0, 0)] * field.ndim
    pads[axis] = (0, 1)
    padded = jnp.pad(field, pads)
    return lax.slice_in_dim(padded, 1, field.shape[axis] + 1, axis=axis) - field

def bwd_diff(field, axis):
    pads = [(0, 0)] * field.ndim
    pads[axis] = (1, 0)
    padded = jnp.pad(field, pads)
    return field - lax.slice_in_dim(padded, 0, field.shape[axis], axis=axis)

def filter_xy(values):
    padded = jnp.pad(values, ((0, 0), (1, 1), (1, 1)))
    rows = padded[:, :-2] + 2.0 * padded[:, 1:-1] + padded[:, 2:]
    return (rows[:, :, :-2] + 2.0 * rows[:, :, 1:-1] + rows[:, :, 2:]) / 16.0

def source_profile(zcoord, xcoord, ycoord, position, width_x, width_y):
    in_plane = (zcoord == position[0]).astype(jnp.float32)
    offset_x = (xcoord - position[1]).astype(jnp.float32) / (width_x / 4.0)
    offset_y = (ycoord - position[2]).astype(jnp.float32) / (width_y / 4.0)
    return in_plane * jnp.exp(-0.5 * (offset_x * offset_x + offset_y * offset_y))

def advance(comps, coef, drive):
    ex, ey, ez, hx, hy, hz = comps
    hx = hx - COURANT * (fwd_diff(ez, 2) - fwd_diff(ey, 0))
    hy = hy - COURANT * (fwd_diff(ex, 0) - fwd_diff(ez, 1))
    hz = hz - COURANT * (fwd_diff(ey, 1) - fwd_diff(ex, 2))
    ex = ex + coef * (bwd_diff(hz, 2) - bwd_diff(hy, 0))
    ey = ey + coef * (bwd_diff(hx, 0) - bwd_diff(hz, 1))
    ez = ez + coef * (bwd_diff(hy, 1) - bwd_diff(hx, 2)) + drive
    return (ex, ey, ez, hx, hy, hz)

def reference(fwd_fields, adj_fields, density, block_ids, material_idx, material_eps, source_pos, wave_idx):
    blocks = density.reshape(NZ, NBLK, BX, Y)
    placed = jnp.zeros_like(blocks).at[:, block_ids].set(blocks).reshape(NZ, X, Y)
    smooth = filter_xy(placed)
    base_rows = jnp.repeat(material_eps[material_idx], BX)
    eps = base_rows[None, :, None] + 3.0 * smooth
    coef = 0.5 / eps
    zcoord = lax.broadcasted_iota(jnp.int32, (NZ, X, Y), 0)
    xcoord = lax.broadcasted_iota(jnp.int32, (NZ, X, Y), 1)
    ycoord = lax.broadcasted_iota(jnp.int32, (NZ, X, Y), 2)

    def one_group(total, inputs):
        fwd, adj, pos, wave = inputs
        profile = source_profile(zcoord, xcoord, ycoord, pos, X, Y)
        omega = 2.0 * math.pi / (6.0 + 2.0 * wave.astype(jnp.float32))
        fcomp = tuple((fwd[c] for c in range(6)))
        acomp = tuple((adj[c] for c in range(6)))
        for step in range(STEPS):
            drive = AMPLITUDE * jnp.sin(omega * (step + 1.0)) * profile
            fcomp = advance(fcomp, coef, drive)
            acomp = advance(acomp, coef, 0.0)
            total = total + (fcomp[0] * acomp[0] + fcomp[1] * acomp[1] + fcomp[2] * acomp[2])
        return (total, jnp.stack(fcomp))
    total, finals = lax.scan(one_group, jnp.zeros((NZ, X, Y), jnp.float32), (fwd_fields, adj_fields, source_pos, wave_idx))
    scale = 3.0 / (STEPS * math.sqrt(GROUPS))
    grad = scale * filter_xy(total)
    grad_owner = grad.reshape(NZ, NBLK, BX, Y)[:, block_ids].reshape(NZ, X, Y)
    return (finals, grad_owner)
```

```python
import functools
import math

import jax
import jax.numpy as jnp
from jax import lax
from jax.experimental import pallas as pl
from jax.experimental.pallas import tpu as pltpu
from jax.sharding import PartitionSpec as P

STEPS = 4
AMPLITUDE = 4.0
PAD = 8
F32 = jnp.float32

VMEM = pltpu.MemorySpace.VMEM
IN_VMEM = pl.BlockSpec(memory_space=pltpu.VMEM)
IN_SMEM = pl.BlockSpec(memory_space=pltpu.SMEM)
IN_HBM = pl.BlockSpec(memory_space=pltpu.MemorySpace.HBM)


def on_chip(*shape):
    return VMEM(shape, F32)


def held(array, spec):
    if spec is IN_SMEM:
        return array
    space = VMEM if spec is IN_VMEM else pltpu.MemorySpace.HBM
    return pltpu.with_memory_space_constraint(array, space)


def call(kernel, outs, out_specs, operands, specs, scratch=(), aliases=None, flops=0):
    operands = [held(a, s) for a, s in zip(operands, specs)]
    return pl.pallas_call(
        kernel,
        out_shape=outs,
        in_specs=specs,
        out_specs=out_specs,
        scratch_shapes=scratch,
        input_output_aliases=aliases or {},
        compiler_params=pltpu.CompilerParams(vmem_limit_bytes=8 << 20),
        cost_estimate=pl.CostEstimate(flops=flops, bytes_accessed=flops // 4, transcendentals=0),
    )(*operands)


def chunks(rows):
    size = 32 if rows % 32 == 0 else rows
    return [(first, size) for first in range(0, rows, size)]


def last_lane(shape):
    return lax.broadcasted_iota(jnp.int32, shape, 1) == shape[1] - 1


def first_lane(shape):
    return lax.broadcasted_iota(jnp.int32, shape, 1) == 0


def next_col(value):
    return jnp.where(last_lane(value.shape), 0.0, pltpu.roll(value, value.shape[1] - 1, 1))


def prev_col(value):
    return jnp.where(first_lane(value.shape), 0.0, pltpu.roll(value, 1, 1))


def update_h(state, evo, layer, upper, rows, double=False):
    for first, size in chunks(rows):
        here = pl.ds(PAD + first, size)
        after = pl.ds(PAD + first + 1, size)
        ex = state[evo, 0, layer, here, :]
        ey = state[evo, 1, layer, here, :]
        ez = state[evo, 2, layer, here, :]
        hx = state[evo, 3, layer, here, :]
        hy = state[evo, 4, layer, here, :]
        hz = state[evo, 5, layer, here, :]
        if double:
            hx, hy, hz = hx + hx, hy + hy, hz + hz
        if upper is None:
            rise_x, rise_y = -ex, -ey
        else:
            rise_x, rise_y = upper(0, first, size) - ex, upper(1, first, size) - ey
        ez_after = state[evo, 2, layer, after, :]
        ey_after = state[evo, 1, layer, after, :]
        state[evo, 3, layer, here, :] = hx - ((next_col(ez) - ez) - rise_y)
        state[evo, 4, layer, here, :] = hy - (rise_x - (ez_after - ez))
        state[evo, 5, layer, here, :] = hz - ((ey_after - ey) - (next_col(ex) - ex))


def inner_upper(state, evo, layer):
    return lambda comp, first, size: state[evo, comp, layer + 1, pl.ds(PAD + first, size), :]


def update_e(state, coef, total, layer, lower, rows, add):
    for first, size in chunks(rows):
        here = pl.ds(PAD + first, size)
        before = pl.ds(PAD + first - 1, size)
        cell = coef[layer, pl.ds(first, size), :]
        news = []
        for evo in range(2):
            hx = state[evo, 3, layer, here, :]
            hy = state[evo, 4, layer, here, :]
            hz = state[evo, 5, layer, here, :]
            hy_before = state[evo, 4, layer, before, :]
            hz_before = state[evo, 5, layer, before, :]
            hx_below = lower(evo, 0, first, size)
            hy_below = lower(evo, 1, first, size)
            ex = state[evo, 0, layer, here, :] + cell * ((hz - prev_col(hz)) - (hy - hy_below))
            ey = state[evo, 1, layer, here, :] + cell * ((hx - hx_below) - (hz - hz_before))
            ez = state[evo, 2, layer, here, :] + cell * ((hy - hy_before) - (hx - prev_col(hx)))
            news.append((ex, ey, ez))
        if add is not None:
            news[0] = (news[0][0], news[0][1], news[0][2] + add(first, size))
        for evo in range(2):
            for comp in range(3):
                state[evo, comp, layer, here, :] = news[evo][comp]
        part = (
            news[0][0] * news[1][0] + news[0][1] * news[1][1] + news[0][2] * news[1][2]
        )
        total[layer, here, :] = total[layer, here, :] + part


def inner_lower(state, layer):
    return lambda evo, comp, first, size: state[
        evo, 3 + comp, layer - 1, pl.ds(PAD + first, size), :
    ]


def driver(ints, drives, profile, layer, step):
    amount = jnp.where(ints[3] == layer, drives[step], 0.0)
    return lambda first, size: amount * profile[pl.ds(first, size), :]


def write_payload(state, pays, ints, rows):
    depth = state.shape[2]

    def up(pay):
        for evo in range(2):
            for comp in range(2):
                pay[evo, comp] = state[evo, 3 + comp, depth - 1, pl.ds(PAD, rows), :]

    def down(pay):
        for evo in range(2):
            for comp in range(2):
                pay[evo, comp] = state[evo, comp, 0, pl.ds(PAD, rows), :]

    if len(pays) == 2:
        up(pays[0])
        down(pays[1])
    else:
        pl.when(ints[0] == 1)(lambda: up(pays[0]))
        pl.when(ints[0] != 1)(lambda: down(pays[0]))


def load_kernel(swap, fwd, adj, ints, state, total, profile, *rest):
    pays, sems = rest[:-1], rest[-1]
    depth, width_x, width_y = fwd.shape[2:]
    copies = []
    for evo, source in enumerate((fwd, adj)):
        for comp in range(6):
            copies.append(
                pltpu.make_async_copy(
                    source.at[0, comp],
                    state.at[evo, comp, :, pl.ds(PAD, width_x), :],
                    sems.at[evo, comp],
                )
            )
    for copy in copies:
        copy.start()
    edge = jnp.zeros((PAD, width_y), F32)

    def clear(layer, carry):
        for evo in range(2):
            for comp in range(6):
                state[evo, comp, layer, pl.ds(0, PAD), :] = edge
                state[evo, comp, layer, pl.ds(PAD + width_x, PAD), :] = edge
        total[layer] = jnp.zeros((width_x + 2 * PAD, width_y), F32)
        return carry

    lax.fori_loop(0, depth, clear, 0)
    xcoord = lax.broadcasted_iota(jnp.int32, (width_x, width_y), 0)
    ycoord = lax.broadcasted_iota(jnp.int32, (width_x, width_y), 1)
    offset_x = (xcoord - ints[4]).astype(F32) / (width_x / 4.0)
    offset_y = (ycoord - ints[5]).astype(F32) / (width_y / 4.0)
    profile[...] = jnp.exp(-0.5 * (offset_x * offset_x + offset_y * offset_y))
    for copy in copies:
        copy.wait()
    for evo in range(2):
        update_h(state, evo, depth - 1, None, width_x, double=True)
    write_payload(state, pays, ints, width_x)


def first_kernel(state_in, state):
    depth = state.shape[2]
    rows = state.shape[3] - 2 * PAD

    def body(layer, carry):
        for evo in range(2):
            update_h(state, evo, layer, inner_upper(state, evo, layer), rows, double=True)
        return carry

    lax.fori_loop(0, depth - 1, body, 0)


def coef_kernel(layout, count, *refs):
    parts = refs[:count]
    block_ids, material_idx, material_eps, ints, coef, blocks, placed, wide = refs[count:]
    nblock = blocks.shape[0]
    depth, rows, width_y = coef.shape
    block_rows = rows // nblock
    for part, masks in zip(parts, layout):
        for slot, mask in enumerate(masks):
            blocks[block_ids[ints[2] ^ mask]] = part[slot]
    edge = jnp.zeros((PAD, width_y), F32)

    def layer_of(layer, carry):
        placed[pl.ds(0, PAD), :] = edge
        placed[pl.ds(PAD + rows, PAD), :] = edge
        for block in range(nblock):
            source = pl.ds(pl.multiple_of(layer * block_rows, block_rows), block_rows)
            placed[pl.ds(PAD + block * block_rows, block_rows), :] = blocks[block, source, :]
        smooth = filtered(placed, rows)
        wide[...] = smooth
        for block in range(nblock):
            base = material_eps[material_idx[block]]
            here = pl.ds(block * block_rows, block_rows)
            coef[layer, here, :] = 0.25 / (base + 3.0 * wide[here, :])
        return carry

    lax.fori_loop(0, depth, layer_of, 0)


def filtered(padded, rows):
    here = padded[pl.ds(PAD, rows), :]
    along = (
        padded[pl.ds(PAD - 1, rows), :] + 2.0 * here + padded[pl.ds(PAD + 1, rows), :]
    )
    return (prev_col(along) + 2.0 * along + next_col(along)) * 0.0625


def bulk_kernel(step, state_in, total_in, coef, ints, drives, profile, state, total):
    depth = state.shape[2]
    rows = state.shape[3] - 2 * PAD
    if step > 0:
        for evo in range(2):
            update_h(state, evo, 0, inner_upper(state, evo, 0), rows)

    def body(layer, carry):
        if step > 0:
            for evo in range(2):
                update_h(state, evo, layer, inner_upper(state, evo, layer), rows)
        update_e(
            state,
            coef,
            total,
            layer,
            inner_lower(state, layer),
            rows,
            driver(ints, drives, profile, layer, step),
        )
        return carry

    lax.fori_loop(1, depth - 1, body, 0)


def edge_kernel(step, swap, state_in, total_in, coef, ints, drives, profile, *rest):
    arrived = rest[: 1 if swap else 2]
    state, total = rest[len(arrived) : len(arrived) + 2]
    pays, below = rest[len(arrived) + 2 : -1], rest[-1]
    from_below, from_above = arrived[0], arrived[-1]
    depth = state.shape[2]
    rows = state.shape[3] - 2 * PAD
    has_up = ints[0].astype(F32)
    has_low = ints[1].astype(F32)
    every = pl.ds(PAD, rows)
    top = depth - 1
    for evo in range(2):
        state[evo, 3, top, every, :] += has_up * from_above[evo, 1]
        state[evo, 4, top, every, :] -= has_up * from_above[evo, 0]
        below[evo, 0] = has_low * (from_below[evo, 0] + state[evo, 1, 0, every, :])
        below[evo, 1] = has_low * (from_below[evo, 1] - state[evo, 0, 0, every, :])
    update_e(
        state, coef, total, top, inner_lower(state, top), rows,
        driver(ints, drives, profile, top, step),
    )
    update_e(
        state,
        coef,
        total,
        0,
        lambda evo, comp, first, size: below[evo, comp, pl.ds(first, size), :],
        rows,
        driver(ints, drives, profile, 0, step),
    )
    if pays:
        for evo in range(2):
            update_h(state, evo, top, None, rows)
        write_payload(state, pays, ints, rows)


def pack_kernel(*refs):
    out = refs[-1]
    for slot, ref in enumerate(refs[:-1]):
        out[slot] = ref[...]


def filter_kernel(layout, total, block_ids, ints, *rest):
    parts, blocks, wide = rest[:-2], rest[-2], rest[-1]
    nblock = blocks.shape[0]
    depth = total.shape[0]
    rows = total.shape[1] - 2 * PAD
    block_rows = rows // nblock

    def layer_of(layer, carry):
        wide[...] = filtered(total.at[layer], rows)
        for block in range(nblock):
            target = pl.ds(pl.multiple_of(layer * block_rows, block_rows), block_rows)
            blocks[block, target, :] = wide[pl.ds(block * block_rows, block_rows), :]
        return carry

    lax.fori_loop(0, depth, layer_of, 0)
    for part, masks in zip(parts, layout):
        for slot, mask in enumerate(masks):
            part[slot] = blocks[block_ids[ints[2] ^ mask]]


def add_kernel(*refs):
    half = len(refs) // 3
    for a, b, out in zip(refs[:half], refs[half : 2 * half], refs[2 * half :]):
        out[...] = a[...] + b[...]


def add_split_kernel(count, *refs):
    terms, outs = refs[:count], refs[count:]
    for slot, out in enumerate(outs):
        value = terms[0][slot]
        for term in terms[1:]:
            value = value + term[slot]
        out[...] = value


def last_kernel(scale, *refs):
    value = refs[0][...]
    for ref in refs[1:-1]:
        value = value + ref[...]
    refs[-1][...] = value * scale


def out_kernel(state, finals, halves, sems):
    depth = state.shape[2]
    rows = state.shape[3] - 2 * PAD
    every = pl.ds(PAD, rows)
    copies = [
        pltpu.make_async_copy(
            state.at[0, comp, :, every, :], finals.at[0, comp], sems.at[comp]
        )
        for comp in range(3)
    ]
    for copy in copies:
        copy.start()
    for comp in range(3):

        def body(layer, carry):
            halves[comp, layer] = 0.5 * state[0, 3 + comp, layer, every, :]
            return carry

        lax.fori_loop(0, depth, body, 0)
        copy = pltpu.make_async_copy(halves.at[comp], finals.at[0, 3 + comp], sems.at[3 + comp])
        copy.start()
        copies.append(copy)
    for copy in copies:
        copy.wait()


def swap_over(array, axis, mask):
    return lax.ppermute(array, axis, [(i, i ^ mask) for i in range(lax.axis_size(axis))])


def shift_over(array, axis, distance):
    size = lax.axis_size(axis)
    route = [(i, i + distance) for i in range(size) if 0 <= i + distance < size]
    return lax.ppermute(array, axis, route)


def trade(pays):
    if len(pays) == 1:
        return [swap_over(pays[0], "slab", 1)]
    return [shift_over(pays[0], "slab", 1), shift_over(pays[1], "slab", -1)]


def per_device(
    fwd_fields, adj_fields, density, block_ids, material_idx, material_eps, source_pos, wave_idx
):
    depth, width_x, width_y = fwd_fields.shape[2:]
    nblock = block_ids.shape[0]
    block_rows = width_x // nblock
    ngrp = lax.axis_size("grp")
    nslab = lax.axis_size("slab")
    swap = nslab == 2
    slab = lax.axis_index("slab")
    me = lax.axis_index("grp")
    ints = jnp.stack(
        [
            (slab < nslab - 1).astype(jnp.int32),
            (slab > 0).astype(jnp.int32),
            me.astype(jnp.int32),
            source_pos[0, 0] - slab * depth,
            source_pos[0, 1],
            source_pos[0, 2],
        ]
    )
    omega = 2.0 * math.pi / (6.0 + 2.0 * wave_idx[0].astype(F32))
    drives = AMPLITUDE * jnp.sin(omega * (jnp.arange(STEPS, dtype=F32) + 1.0))

    far = 4
    middle = ngrp // (2 * far)
    far_masks = [2 * middle * j for j in range(far)]
    middle_masks = [2 * j for j in range(middle)]
    layout = [
        [core + mid + top for top in far_masks] for core in (0, 1) for mid in middle_masks
    ]
    piece = (depth * block_rows, width_y)
    group = (far,) + piece

    own = density.reshape(piece)
    pieces = [own] + [swap_over(own, "grp", mask) for mask in far_masks[1:]]
    near = call(pack_kernel, on_chip(*group), IN_VMEM, pieces, [IN_VMEM] * far)
    parts = [near] + [swap_over(near, "grp", mask) for mask in middle_masks[1:]]
    parts = parts + [swap_over(part, "grp", 1) for part in parts]

    state_shape = on_chip(2, 6, depth, width_x + 2 * PAD, width_y)
    total_shape = on_chip(depth, width_x + 2 * PAD, width_y)
    plane = on_chip(width_x, width_y)
    pay_shape = on_chip(2, 2, width_x, width_y)
    npay = 1 if swap else 2
    state, total, profile, *pays = call(
        functools.partial(load_kernel, swap),
        [state_shape, total_shape, plane] + [pay_shape] * npay,
        [IN_VMEM] * (3 + npay),
        [fwd_fields, adj_fields, ints],
        [IN_HBM, IN_HBM, IN_SMEM],
        [pltpu.SemaphoreType.DMA((2, 6))],
    )
    arrived = trade(pays)
    state = call(first_kernel, state_shape, IN_VMEM, [state], [IN_VMEM], aliases={0: 0})

    coef = call(
        functools.partial(coef_kernel, layout, len(parts)),
        on_chip(depth, width_x, width_y),
        IN_VMEM,
        parts + [block_ids, material_idx, material_eps, ints],
        [IN_VMEM] * len(parts) + [IN_SMEM] * 4,
        [
            pltpu.VMEM((nblock,) + piece, F32),
            pltpu.VMEM((width_x + 2 * PAD, width_y), F32),
            pltpu.VMEM((width_x, width_y), F32),
        ],
    )

    for step in range(STEPS):
        more = step < STEPS - 1
        state, total = call(
            functools.partial(bulk_kernel, step),
            [state_shape, total_shape],
            [IN_VMEM] * 2,
            [state, total, coef, ints, drives, profile],
            [IN_VMEM, IN_VMEM, IN_VMEM, IN_SMEM, IN_SMEM, IN_VMEM],
            aliases={0: 0, 1: 1},
        )
        state, total, *pays = call(
            functools.partial(edge_kernel, step, swap),
            [state_shape, total_shape] + [pay_shape] * (npay if more else 0),
            [IN_VMEM] * (2 + (npay if more else 0)),
            [state, total, coef, ints, drives, profile] + arrived,
            [IN_VMEM, IN_VMEM, IN_VMEM, IN_SMEM, IN_SMEM, IN_VMEM] + [IN_VMEM] * npay,
            [pltpu.VMEM((2, 2, width_x, width_y), F32)],
            aliases={0: 0, 1: 1},
        )
        if more:
            arrived = trade(pays)

    parts = call(
        functools.partial(filter_kernel, layout),
        [on_chip(*group)] * len(layout),
        [IN_VMEM] * len(layout),
        [total, block_ids, ints],
        [IN_VMEM, IN_SMEM, IN_SMEM],
        [pltpu.VMEM((nblock,) + piece, F32), pltpu.VMEM((width_x, width_y), F32)],
    )
    kept, sent = parts[:middle], parts[middle:]
    got = [swap_over(part, "grp", 1) for part in sent]
    sums = call(
        add_kernel,
        [on_chip(*group)] * middle,
        [IN_VMEM] * middle,
        list(kept) + got,
        [IN_VMEM] * (2 * middle),
    )
    got = [swap_over(part, "grp", mask) for part, mask in zip(sums[1:], middle_masks[1:])]
    pieces = call(
        functools.partial(add_split_kernel, middle),
        [on_chip(*piece)] * far,
        [IN_VMEM] * far,
        [sums[0]] + got,
        [IN_VMEM] * middle,
    )
    got = [swap_over(part, "grp", mask) for part, mask in zip(pieces[1:], far_masks[1:])]
    scale = 3.0 / (STEPS * math.sqrt(ngrp))
    grad = call(
        functools.partial(last_kernel, scale),
        jax.ShapeDtypeStruct(piece, F32),
        IN_VMEM,
        [pieces[0]] + got,
        [IN_VMEM] * far,
    )
    finals = call(
        out_kernel,
        jax.ShapeDtypeStruct(fwd_fields.shape, F32),
        IN_HBM,
        [state],
        [IN_VMEM],
        [
            pltpu.VMEM((3, depth, width_x, width_y), F32),
            pltpu.SemaphoreType.DMA((6,)),
        ],
    )
    return finals, grad.reshape(density.shape)


def solution(mesh):
    placed = (
        P("grp", None, "slab", None, None),
        P("grp", None, "slab", None, None),
        P("slab", "grp", None),
        P(),
        P(),
        P(),
        P("grp", None),
        P("grp"),
    )
    return jax.shard_map(
        per_device,
        mesh=mesh,
        in_specs=placed,
        out_specs=(P("grp", None, "slab", None, None), P("slab", "grp", None)),
        check_vma=False,
    )
```

```python
import functools
import math

import jax
import jax.numpy as jnp
from jax import lax
from jax.experimental import pallas as pl
from jax.experimental.pallas import tpu as pltpu
from jax.sharding import PartitionSpec as P

STEPS = 4
AMPLITUDE = 4.0
PAD = 8
F32 = jnp.float32

VMEM = pltpu.MemorySpace.VMEM
IN_VMEM = pl.BlockSpec(memory_space=pltpu.VMEM)
IN_SMEM = pl.BlockSpec(memory_space=pltpu.SMEM)
IN_HBM = pl.BlockSpec(memory_space=pltpu.MemorySpace.HBM)


def on_chip(*shape):
    return VMEM(shape, F32)


def held(array, spec):
    if spec is IN_SMEM:
        return array
    space = VMEM if spec is IN_VMEM else pltpu.MemorySpace.HBM
    return pltpu.with_memory_space_constraint(array, space)


def call(kernel, outs, out_specs, operands, specs, scratch=(), aliases=None, flops=0):
    operands = [held(a, s) for a, s in zip(operands, specs)]
    return pl.pallas_call(
        kernel,
        out_shape=outs,
        in_specs=specs,
        out_specs=out_specs,
        scratch_shapes=scratch,
        input_output_aliases=aliases or {},
        compiler_params=pltpu.CompilerParams(vmem_limit_bytes=8 << 20),
        cost_estimate=pl.CostEstimate(flops=flops, bytes_accessed=flops // 4, transcendentals=0),
    )(*operands)


TOP_ALONE, BOTTOM_ALONE, ABOVE, BELOW, UNDER, SPARE = range(6)
EXTRA = 6
CHUNK = 16


def chunks(rows):
    size = CHUNK if rows % CHUNK == 0 else rows
    return [(first, size) for first in range(0, rows, size)]


def next_col(value):
    column = lax.broadcasted_iota(jnp.int32, value.shape, 1)
    moved = pltpu.roll(value, value.shape[1] - 1, 1)
    return jnp.where(column == value.shape[1] - 1, 0.0, moved)


def prev_col(value):
    column = lax.broadcasted_iota(jnp.int32, value.shape, 1)
    return jnp.where(column == 0, 0.0, pltpu.roll(value, 1, 1))


class Window:
    def __init__(self, state, coef=None, total=None, source=None, drives=None, profile=None):
        self.state, self.coef, self.total = state, coef, total
        self.source, self.drives, self.profile = source, drives, profile
        self.rows = state.shape[3] - 2 * PAD
        self.depth = state.shape[2] - EXTRA
        self.top = self.depth - 1
        self.slab = lax.axis_index("slab")
        self.has_up = self.slab < lax.axis_size("slab") - 1
        self.has_low = self.slab > 0

    def extra(self, which):
        return self.depth + which

    def read(self, evo, comp, layer, first, size, shift=0):
        return self.state[evo, comp, layer, pl.ds(PAD + first + shift, size), :]

    def write(self, evo, comp, layer, first, size, value):
        self.state[evo, comp, layer, pl.ds(PAD + first, size), :] = value

    def put_h(self, layer, upper, evos=(0, 1), e=None, h=None, flat=False):
        e = layer if e is None else e
        h = layer if h is None else h
        for evo in evos:
            for first, size in chunks(self.rows):
                ex, ey, ez = (self.read(evo, c, e, first, size) for c in range(3))
                if upper is None:
                    rise_x, rise_y = -ex, -ey
                else:
                    rise_x = self.read(evo, 0, upper, first, size) - ex
                    rise_y = self.read(evo, 1, upper, first, size) - ey
                ez_after = self.read(evo, 2, e, first, size, 1)
                hx = self.read(evo, 3, h, first, size) - ((next_col(ez) - ez) - rise_y)
                hy = self.read(evo, 4, h, first, size) - (rise_x - (ez_after - ez))
                self.write(evo, 3, layer, first, size, hx)
                self.write(evo, 4, layer, first, size, hy)
                if not flat:
                    ey_after = self.read(evo, 1, e, first, size, 1)
                    hz = self.read(evo, 5, h, first, size)
                    hz = hz - ((ey_after - ey) - (next_col(ex) - ex))
                    self.write(evo, 5, layer, first, size, hz)

    def curl_h(self, evo, h, lower, first, size):
        hx, hy, hz = (self.read(evo, c, h, first, size) for c in (3, 4, 5))
        if lower is None:
            step_x, step_y = hx, hy
        else:
            step_x = hx - self.read(evo, 3, lower, first, size)
            step_y = hy - self.read(evo, 4, lower, first, size)
        hy_before = self.read(evo, 4, h, first, size, -1)
        hz_before = self.read(evo, 5, h, first, size, -1)
        return (
            (hz - prev_col(hz)) - step_y,
            step_x - (hz - hz_before),
            (hy - hy_before) - (hx - prev_col(hx)),
        )

    def drive(self, step, layer, into=None):
        into = layer if into is None else into

        @pl.when(self.source[0, 0] - self.slab * self.depth == layer)
        def _():
            amount = self.drives[step]
            for first, size in chunks(self.rows):
                here = pl.ds(PAD + first, size)
                self.state[0, 2, into, here, :] += amount * self.profile[pl.ds(first, size), :]

    def put_e(self, layer, lower, step):
        self.drive(step, layer)
        for first, size in chunks(self.rows):
            cell = self.coef[layer, pl.ds(first, size), :]
            part = None
            news = []
            for evo in range(2):
                curl = self.curl_h(evo, layer, lower, first, size)
                news.append(
                    [self.read(evo, c, layer, first, size) + cell * curl[c] for c in range(3)]
                )
            for evo in range(2):
                for c in range(3):
                    self.write(evo, c, layer, first, size, news[evo][c])
            part = news[0][0] * news[1][0] + news[0][1] * news[1][1] + news[0][2] * news[1][2]
            self.total[layer, pl.ds(PAD + first, size), :] += part

    def put_e_of(self, out, e, h, lower, cell_layer):
        for evo in range(2):
            for first, size in chunks(self.rows):
                cell = self.coef[cell_layer, pl.ds(first, size), :]
                curl = self.curl_h(evo, h, lower, first, size)
                for c in range(3):
                    self.write(
                        evo, c, out, first, size, self.read(evo, c, e, first, size) + cell * curl[c]
                    )

    def lift_h(self, layer, edge, extra=None):
        for evo in range(2):
            for first, size in chunks(self.rows):
                here = pl.ds(first, size)
                ex, ey = edge[evo, 0, here, :], edge[evo, 1, here, :]
                if extra is not None:
                    ex = ex + self.read(evo, 0, extra, first, size)
                    ey = ey + self.read(evo, 1, extra, first, size)
                self.write(evo, 3, layer, first, size, self.read(evo, 3, layer, first, size) + ey)
                self.write(evo, 4, layer, first, size, self.read(evo, 4, layer, first, size) - ex)

    def spread(self, layer, e):
        for evo in range(2):
            for first, size in chunks(self.rows):
                self.write(evo, 3, layer, first, size, self.read(evo, 1, e, first, size))
                self.write(evo, 4, layer, first, size, -self.read(evo, 0, e, first, size))

    def set_under(self, edge):
        under, below = self.extra(UNDER), self.extra(BELOW)
        for evo in range(2):
            for c in range(2):
                for first, size in chunks(self.rows):
                    value = edge[evo, c, pl.ds(first, size), :]
                    value = value + self.read(evo, 3 + c, below, first, size)
                    self.write(evo, 3 + c, under, first, size, value)

    def send_h(self, pay, layer):
        for evo in range(2):
            for c in range(2):
                pay[evo, c] = self.state[evo, 3 + c, layer, pl.ds(PAD, self.rows), :]

    def send_e(self, pay, layer):
        for evo in range(2):
            for c in range(2):
                pay[evo, c] = self.state[evo, c, layer, pl.ds(PAD, self.rows), :]


def first_kernel(fwd, adj, state, total, *pays):
    win = Window(state)
    rows, width_y = win.rows, state.shape[4]
    edge = jnp.zeros((PAD, width_y), F32)

    def clear(layer, carry):
        for evo in range(2):
            for comp in range(6):
                state[evo, comp, layer, pl.ds(0, PAD), :] = edge
                state[evo, comp, layer, pl.ds(PAD + rows, PAD), :] = edge
        return carry

    lax.fori_loop(0, state.shape[2], clear, 0)
    for which in (ABOVE, BELOW, UNDER):
        for evo in range(2):
            for comp in range(6):
                state[evo, comp, win.extra(which)] = jnp.zeros((rows + 2 * PAD, width_y), F32)

    def copy(layer, carry):
        total[layer] = jnp.zeros((rows + 2 * PAD, width_y), F32)
        for evo, given in enumerate((fwd, adj)):
            for comp in range(6):
                for first, size in chunks(rows):
                    value = given[0, comp, layer, pl.ds(first, size), :]
                    win.write(evo, comp, layer, first, size, value + value if comp > 2 else value)
        return carry

    lax.fori_loop(0, win.depth, copy, 0)
    win.put_h(win.top, None)
    if len(pays) == 2:
        win.send_h(pays[0], win.top)
        win.send_e(pays[1], 0)
    else:
        pl.when(win.has_up)(lambda: win.send_h(pays[0], win.top))
        pl.when(win.has_low)(lambda: win.send_e(pays[0], 0))


def inner_kernel(state_in, source, state, profile):
    win = Window(state)
    rows, width_y = win.rows, state.shape[4]
    xcoord = lax.broadcasted_iota(jnp.int32, (rows, width_y), 0)
    ycoord = lax.broadcasted_iota(jnp.int32, (rows, width_y), 1)
    offset_x = (xcoord - source[0, 1]).astype(F32) / (rows / 4.0)
    offset_y = (ycoord - source[0, 2]).astype(F32) / (width_y / 4.0)
    profile[...] = jnp.exp(-0.5 * (offset_x * offset_x + offset_y * offset_y))

    def body(layer, carry):
        win.put_h(layer, layer + 1)
        return carry

    lax.fori_loop(0, win.top, body, 0)


def curl_kernel(state_in, from_below, from_above, state, curls):
    win = Window(state)
    pl.when(win.has_up)(lambda: win.lift_h(win.top, from_above))

    @pl.when(win.has_low)
    def _():
        win.spread(win.extra(BELOW), 0)
        win.set_under(from_below)

    def one(layer, lower):
        for evo in range(2):
            for first, size in chunks(win.rows):
                for c, value in enumerate(win.curl_h(evo, layer, lower, first, size)):
                    curls[evo, c, layer, pl.ds(first, size), :] = value

    def body(layer, carry):
        one(layer, layer - 1)
        return carry

    one(0, win.extra(UNDER))
    lax.fori_loop(1, win.depth, body, 0)


def coef_kernel(layout, count, depth, *refs):
    parts = refs[:count]
    block_ids, material_idx, material_eps, coef, blocks, placed, base = refs[count:]
    nblock = blocks.shape[0]
    rows, width_y = coef.shape[1:]
    block_rows = rows // nblock
    me = lax.axis_index("grp")
    for part, masks in zip(parts, layout):
        for slot, mask in enumerate(masks):
            blocks[block_ids[me ^ mask]] = part[slot]
    for block in range(nblock):
        level = jnp.full((block_rows, width_y), material_eps[material_idx[block]], F32)
        base[pl.ds(block * block_rows, block_rows), :] = level
    placed[pl.ds(0, PAD), :] = jnp.zeros((PAD, width_y), F32)
    placed[pl.ds(PAD + rows, PAD), :] = jnp.zeros((PAD, width_y), F32)

    def layer_of(layer, carry):
        for block in range(nblock):
            source = pl.ds(pl.multiple_of(layer * block_rows, block_rows), block_rows)
            placed[pl.ds(PAD + block * block_rows, block_rows), :] = blocks[block, source, :]
        for first, size in chunks(rows):
            here = pl.ds(first, size)
            smooth = filtered(placed, first, size)
            coef[layer, here, :] = 0.25 / (base[here, :] + 3.0 * smooth)
        return carry

    lax.fori_loop(0, depth, layer_of, 0)


def filtered(padded, first, size):
    here = padded[pl.ds(PAD + first, size), :]
    before = padded[pl.ds(PAD + first - 1, size), :]
    after = padded[pl.ds(PAD + first + 1, size), :]
    along = before + 2.0 * here + after
    return (prev_col(along) + 2.0 * along + next_col(along)) * 0.0625


def ahead_a_kernel(state_in, total_in, coef, curls, source, drives, profile, state, total, *pays):
    win = Window(state, coef, total, source, drives, profile)

    def body(layer, carry):
        win.drive(0, layer)
        for first, size in chunks(win.rows):
            here = pl.ds(first, size)
            cell = coef[layer, here, :]
            news = []
            for evo in range(2):
                news.append(
                    [
                        win.read(evo, c, layer, first, size) + cell * curls[evo, c, layer, here, :]
                        for c in range(3)
                    ]
                )
                for c in range(3):
                    win.write(evo, c, layer, first, size, news[evo][c])
            part = news[0][0] * news[1][0] + news[0][1] * news[1][1] + news[0][2] * news[1][2]
            total[layer, pl.ds(PAD + first, size), :] += part
        return carry

    lax.fori_loop(0, win.depth, body, 0)
    win.put_h(win.top, None)

    def up(pay, cells):
        win.send_h(pay, win.top)
        cells[...] = coef[win.top]

    def down(pay, cells):
        win.send_e(pay, 0)
        cells[...] = coef[0]

    half = len(pays) // 2
    if half == 2:
        up(pays[0], pays[2])
        down(pays[1], pays[3])
    else:
        pl.when(win.has_up)(lambda: up(*pays))
        pl.when(win.has_low)(lambda: down(*pays))


def ahead_b_kernel(state_in, coef, source, drives, profile, state, *pays):
    win = Window(state, coef, None, source, drives, profile)
    top = win.top
    win.put_h(top - 1, top)
    win.put_h(0, 1)

    def up(pay):
        alone = win.extra(TOP_ALONE)
        win.put_e_of(alone, top, top, top - 1, top)
        win.drive(1, top, alone)
        win.put_h(alone, None, h=top)
        win.send_h(pay, alone)

    def down(pay):
        alone = win.extra(BOTTOM_ALONE)
        win.put_e_of(alone, 0, 0, None, 0)
        win.drive(1, 0, alone)
        win.send_e(pay, alone)

    pl.when(win.has_up)(lambda: up(pays[0]))
    pl.when(win.has_low)(lambda: down(pays[-1]))


def ahead_c_kernel(state_in, total_in, coef, source, drives, profile, state, total, *pays):
    win = Window(state, coef, total, source, drives, profile)
    top = win.top
    win.put_h(top - 2, top - 1)
    win.put_h(1, 2)
    win.put_e(top - 1, top - 2, 1)
    win.put_e(1, 0, 1)

    def up(pay):
        alone, spare = win.extra(TOP_ALONE), win.extra(SPARE)
        win.put_h(spare, alone, e=top - 1, h=top - 1, flat=True)
        win.put_e_of(alone, alone, alone, spare, top)
        win.drive(2, top, alone)
        win.put_h(alone, None, flat=True)
        win.send_h(pay, alone)

    def down(pay):
        alone = win.extra(BOTTOM_ALONE)
        win.put_h(alone, 1, h=0)
        win.put_e_of(alone, alone, alone, None, 0)
        win.drive(2, 0, alone)
        win.send_e(pay, alone)

    pl.when(win.has_up)(lambda: up(pays[0]))
    pl.when(win.has_low)(lambda: down(pays[-1]))


def bulk_kernel(state_in, total_in, coef, source, drives, profile, state, total):
    win = Window(state, coef, total, source, drives, profile)
    top = win.top

    def sweep(step):
        def body(layer, carry):
            win.put_h(layer, layer + 1)
            win.put_e(layer, layer - 1, step)
            return carry

        return body

    lax.fori_loop(2, top - 2, sweep(1), 0)
    win.put_e(top - 2, top - 3, 1)
    win.put_h(1, 2)
    lax.fori_loop(2, top - 1, sweep(2), 0)
    win.put_h(2, 3)
    lax.fori_loop(3, top - 2, sweep(3), 0)


def behind_a_kernel(
    state_in, total_in, coef_in, below, above, below_cells, above_cells, source, drives, profile,
    state, total, coef,
):
    win = Window(state, coef, total, source, drives, profile)
    top, depth = win.top, win.depth

    @pl.when(win.has_up)
    def _():
        win.lift_h(top, above)
        coef[depth] = above_cells[...]

    @pl.when(win.has_low)
    def _():
        ghost = win.extra(BELOW)
        win.spread(ghost, 0)
        win.set_under(below)
        coef[depth + 1] = below_cells[...]
        for evo in range(2):
            for c in range(3):
                win.write(evo, c, ghost, 0, win.rows, jnp.zeros((win.rows, state.shape[4]), F32))
            win.write(evo, 5, ghost, 0, win.rows, jnp.zeros((win.rows, state.shape[4]), F32))
        win.put_e_of(ghost, ghost, ghost, None, depth + 1)

    win.put_e(top, top - 1, 1)
    win.put_e(0, win.extra(UNDER), 1)

    @pl.when(win.has_up)
    def _():
        ghost = win.extra(ABOVE)
        for evo in range(2):
            for first, size in chunks(win.rows):
                cell = coef[depth, pl.ds(first, size), :]
                win.write(evo, 0, ghost, first, size, cell * win.read(evo, 4, top, first, size))
                win.write(evo, 1, ghost, first, size, -cell * win.read(evo, 3, top, first, size))

    win.put_h(top - 1, top)
    win.put_h(top, None)
    win.put_h(0, 1)
    win.put_e(top - 1, top - 2, 2)
    win.put_e(1, 0, 2)


def behind_b_kernel(
    state_in, total_in, coef, below, above, source, drives, profile, state, total
):
    win = Window(state, coef, total, source, drives, profile)
    top, depth = win.top, win.depth

    @pl.when(win.has_up)
    def _():
        ghost = win.extra(ABOVE)
        win.lift_h(top, above, ghost)
        win.put_h(ghost, None)
        win.put_e_of(ghost, ghost, ghost, top, depth)

    @pl.when(win.has_low)
    def _():
        ghost, spare = win.extra(BELOW), win.extra(SPARE)
        win.put_h(ghost, 0)
        win.set_under(below)
        win.spread(spare, ghost)
        win.put_e_of(ghost, ghost, ghost, spare, depth + 1)

    win.put_e(top, top - 1, 2)
    win.put_e(0, win.extra(UNDER), 2)
    win.put_h(top - 1, top)
    win.put_h(top, None)
    win.put_h(top - 2, top - 1)
    win.put_h(0, 1)
    win.put_h(1, 2)
    win.put_e(top - 1, top - 2, 3)
    win.put_e(top - 2, top - 3, 3)
    win.put_e(1, 0, 3)
    win.put_e(2, 1, 3)


def behind_c_kernel(
    state_in, total_in, coef, below, above, source, drives, profile, state, total
):
    win = Window(state, coef, total, source, drives, profile)
    top = win.top
    pl.when(win.has_up)(lambda: win.lift_h(top, above, win.extra(ABOVE)))

    @pl.when(win.has_low)
    def _():
        win.put_h(win.extra(BELOW), 0, flat=True)
        win.set_under(below)

    win.put_e(top, top - 1, 3)
    win.put_e(0, win.extra(UNDER), 3)


def pack_kernel(*refs):
    out = refs[-1]
    for slot, ref in enumerate(refs[:-1]):
        out[slot] = ref[...]


def filter_kernel(layout, total, block_ids, *rest):
    parts, blocks, wide = rest[:-2], rest[-2], rest[-1]
    nblock = blocks.shape[0]
    depth = total.shape[0]
    rows = total.shape[1] - 2 * PAD
    block_rows = rows // nblock
    me = lax.axis_index("grp")

    def layer_of(layer, carry):
        for first, size in chunks(rows):
            wide[pl.ds(first, size), :] = filtered(total.at[layer], first, size)
        for block in range(nblock):
            target = pl.ds(pl.multiple_of(layer * block_rows, block_rows), block_rows)
            blocks[block, target, :] = wide[pl.ds(block * block_rows, block_rows), :]
        return carry

    lax.fori_loop(0, depth, layer_of, 0)
    for part, masks in zip(parts, layout):
        for slot, mask in enumerate(masks):
            part[slot] = blocks[block_ids[me ^ mask]]


def add_kernel(*refs):
    half = len(refs) // 3
    for a, b, out in zip(refs[:half], refs[half : 2 * half], refs[2 * half :]):
        out[...] = a[...] + b[...]


def add_split_kernel(count, *refs):
    terms, outs = refs[:count], refs[count:]
    for slot, out in enumerate(outs):
        value = terms[0][slot]
        for term in terms[1:]:
            value = value + term[slot]
        out[...] = value


def last_kernel(scale, *refs):
    value = refs[0][...]
    for ref in refs[1:-1]:
        value = value + ref[...]
    refs[-1][...] = value * scale


def out_kernel(state, finals, halves, sems):
    depth = state.shape[2] - EXTRA
    rows = state.shape[3] - 2 * PAD
    every = pl.ds(PAD, rows)
    copies = [
        pltpu.make_async_copy(
            state.at[0, comp, pl.ds(0, depth), every, :], finals.at[0, comp], sems.at[comp]
        )
        for comp in range(3)
    ]
    for copy in copies:
        copy.start()
    for comp in range(3):

        def body(layer, carry):
            halves[comp, layer] = 0.5 * state[0, 3 + comp, layer, every, :]
            return carry

        lax.fori_loop(0, depth, body, 0)
        copy = pltpu.make_async_copy(halves.at[comp], finals.at[0, 3 + comp], sems.at[3 + comp])
        copy.start()
        copies.append(copy)
    for copy in copies:
        copy.wait()


def swap_over(array, axis, mask):
    return lax.ppermute(array, axis, [(i, i ^ mask) for i in range(lax.axis_size(axis))])


def shift_over(array, axis, distance):
    size = lax.axis_size(axis)
    route = [(i, i + distance) for i in range(size) if 0 <= i + distance < size]
    return lax.ppermute(array, axis, route)


def trade(pays):
    if len(pays) == 1:
        return [swap_over(pays[0], "slab", 1)] * 2
    return [shift_over(pays[0], "slab", 1), shift_over(pays[1], "slab", -1)]


def per_device(
    fwd_fields, adj_fields, density, block_ids, material_idx, material_eps, source_pos, wave_idx
):
    depth, width_x, width_y = fwd_fields.shape[2:]
    nblock = block_ids.shape[0]
    block_rows = width_x // nblock
    ngrp = lax.axis_size("grp")
    npay = 1 if lax.axis_size("slab") == 2 else 2
    omega = 2.0 * math.pi / (6.0 + 2.0 * wave_idx[0].astype(F32))
    drives = AMPLITUDE * jnp.sin(omega * (jnp.arange(STEPS, dtype=F32) + 1.0))

    far = 4
    middle = ngrp // (2 * far)
    far_masks = [2 * middle * j for j in range(far)]
    middle_masks = [2 * j for j in range(middle)]
    layout = [
        [core + mid + top for top in far_masks] for core in (0, 1) for mid in middle_masks
    ]
    piece = (depth * block_rows, width_y)
    group = (far,) + piece

    state_shape = on_chip(2, 6, depth + EXTRA, width_x + 2 * PAD, width_y)
    total_shape = on_chip(depth, width_x + 2 * PAD, width_y)
    coef_shape = on_chip(depth + 2, width_x, width_y)
    plane = on_chip(width_x, width_y)
    pay_shape = on_chip(2, 2, width_x, width_y)

    own = density.reshape(piece)
    pieces = [own] + [swap_over(own, "grp", mask) for mask in far_masks[1:]]
    near = call(pack_kernel, on_chip(*group), IN_VMEM, pieces, [IN_VMEM] * far)
    parts = [near] + [swap_over(near, "grp", mask) for mask in middle_masks[1:]]
    parts = parts + [swap_over(part, "grp", 1) for part in parts]

    state, total, *pays = call(
        first_kernel,
        [state_shape, total_shape] + [pay_shape] * npay,
        [IN_VMEM] * (2 + npay),
        [fwd_fields, adj_fields],
        [IN_VMEM, IN_VMEM],
    )
    from_below, from_above = trade(pays)
    state, profile = call(
        inner_kernel, [state_shape, plane], [IN_VMEM] * 2, [state, source_pos],
        [IN_VMEM, IN_SMEM], aliases={0: 0},
    )
    state, curls = call(
        curl_kernel,
        [state_shape, on_chip(2, 3, depth, width_x, width_y)],
        [IN_VMEM] * 2,
        [state, from_below, from_above],
        [IN_VMEM] * 3,
        aliases={0: 0},
    )
    coef = call(
        functools.partial(coef_kernel, layout, len(parts), depth),
        coef_shape,
        IN_VMEM,
        parts + [block_ids, material_idx, material_eps],
        [IN_VMEM] * len(parts) + [IN_SMEM] * 3,
        [
            pltpu.VMEM((nblock,) + piece, F32),
            pltpu.VMEM((width_x + 2 * PAD, width_y), F32),
            pltpu.VMEM((width_x, width_y), F32),
        ],
    )

    about = [source_pos, drives, profile]
    about_specs = [IN_SMEM, IN_SMEM, IN_VMEM]
    state, total, *pays = call(
        ahead_a_kernel,
        [state_shape, total_shape] + [pay_shape] * npay + [plane] * npay,
        [IN_VMEM] * (2 + 2 * npay),
        [state, total, coef, curls] + about,
        [IN_VMEM] * 4 + about_specs,
        aliases={0: 0, 1: 1},
    )
    edges_a = trade(pays[:npay])
    cells = trade(pays[npay:])
    state, *pays = call(
        ahead_b_kernel,
        [state_shape] + [pay_shape] * npay,
        [IN_VMEM] * (1 + npay),
        [state, coef] + about,
        [IN_VMEM] * 2 + about_specs,
        aliases={0: 0},
    )
    edges_b = trade(pays)
    state, total, *pays = call(
        ahead_c_kernel,
        [state_shape, total_shape] + [pay_shape] * npay,
        [IN_VMEM] * (2 + npay),
        [state, total, coef] + about,
        [IN_VMEM] * 3 + about_specs,
        aliases={0: 0, 1: 1},
    )
    edges_c = trade(pays)
    state, total = call(
        bulk_kernel,
        [state_shape, total_shape],
        [IN_VMEM] * 2,
        [state, total, coef] + about,
        [IN_VMEM] * 3 + about_specs,
        aliases={0: 0, 1: 1},
    )
    state, total, coef = call(
        behind_a_kernel,
        [state_shape, total_shape, coef_shape],
        [IN_VMEM] * 3,
        [state, total, coef] + edges_a + cells + about,
        [IN_VMEM] * 7 + about_specs,
        aliases={0: 0, 1: 1, 2: 2},
    )
    for kernel, edges in ((behind_b_kernel, edges_b), (behind_c_kernel, edges_c)):
        state, total = call(
            kernel,
            [state_shape, total_shape],
            [IN_VMEM] * 2,
            [state, total, coef] + edges + about,
            [IN_VMEM] * 5 + about_specs,
            aliases={0: 0, 1: 1},
        )

    parts = call(
        functools.partial(filter_kernel, layout),
        [on_chip(*group)] * len(layout),
        [IN_VMEM] * len(layout),
        [total, block_ids],
        [IN_VMEM, IN_SMEM],
        [pltpu.VMEM((nblock,) + piece, F32), pltpu.VMEM((width_x, width_y), F32)],
    )
    kept, sent = parts[:middle], parts[middle:]
    got = [swap_over(part, "grp", 1) for part in sent]
    sums = call(
        add_kernel,
        [on_chip(*group)] * middle,
        [IN_VMEM] * middle,
        list(kept) + got,
        [IN_VMEM] * (2 * middle),
    )
    got = [swap_over(part, "grp", mask) for part, mask in zip(sums[1:], middle_masks[1:])]
    pieces = call(
        functools.partial(add_split_kernel, middle),
        [on_chip(*piece)] * far,
        [IN_VMEM] * far,
        [sums[0]] + got,
        [IN_VMEM] * middle,
    )
    got = [swap_over(part, "grp", mask) for part, mask in zip(pieces[1:], far_masks[1:])]
    scale = 3.0 / (STEPS * math.sqrt(ngrp))
    grad = call(
        functools.partial(last_kernel, scale),
        jax.ShapeDtypeStruct(piece, F32),
        IN_VMEM,
        [pieces[0]] + got,
        [IN_VMEM] * far,
    )
    finals = call(
        out_kernel,
        jax.ShapeDtypeStruct(fwd_fields.shape, F32),
        IN_HBM,
        [state],
        [IN_VMEM],
        [
            pltpu.VMEM((3, depth, width_x, width_y), F32),
            pltpu.SemaphoreType.DMA((6,)),
        ],
    )
    return finals, grad.reshape(density.shape)


def solution(mesh):
    placed = (
        P("grp", None, "slab", None, None),
        P("grp", None, "slab", None, None),
        P("slab", "grp", None),
        P(),
        P(),
        P(),
        P("grp", None),
        P("grp"),
    )
    return jax.shard_map(
        per_device,
        mesh=mesh,
        in_specs=placed,
        out_specs=(P("grp", None, "slab", None, None), P("slab", "grp", None)),
        check_vma=False,
    )
```

```python
import functools
import math

import jax
import jax.numpy as jnp
from jax import lax
from jax.experimental import pallas as pl
from jax.experimental.pallas import tpu as pltpu
from jax.sharding import PartitionSpec as P

STEPS = 4
AMPLITUDE = 4.0
PAD = 8
F32 = jnp.float32

VMEM = pltpu.MemorySpace.VMEM
IN_VMEM = pl.BlockSpec(memory_space=pltpu.VMEM)
IN_SMEM = pl.BlockSpec(memory_space=pltpu.SMEM)
IN_HBM = pl.BlockSpec(memory_space=pltpu.MemorySpace.HBM)


def on_chip(*shape):
    return VMEM(shape, F32)


def held(array, spec):
    if spec is IN_SMEM:
        return array
    space = VMEM if spec is IN_VMEM else pltpu.MemorySpace.HBM
    return pltpu.with_memory_space_constraint(array, space)


def call(kernel, outs, out_specs, operands, specs, scratch=(), aliases=None, flops=0):
    operands = [held(a, s) for a, s in zip(operands, specs)]
    return pl.pallas_call(
        kernel,
        out_shape=outs,
        in_specs=specs,
        out_specs=out_specs,
        scratch_shapes=scratch,
        input_output_aliases=aliases or {},
        compiler_params=pltpu.CompilerParams(vmem_limit_bytes=8 << 20),
        cost_estimate=pl.CostEstimate(flops=flops, bytes_accessed=flops // 4, transcendentals=0),
    )(*operands)


EXTRA = 1
CHUNK = 16


def chunks(rows):
    size = CHUNK if rows % CHUNK == 0 else rows
    return [(first, size) for first in range(0, rows, size)]


def next_col(value):
    column = lax.broadcasted_iota(jnp.int32, value.shape, 1)
    moved = pltpu.roll(value, value.shape[1] - 1, 1)
    return jnp.where(column == value.shape[1] - 1, 0.0, moved)


def prev_col(value):
    column = lax.broadcasted_iota(jnp.int32, value.shape, 1)
    return jnp.where(column == 0, 0.0, pltpu.roll(value, 1, 1))


class Window:
    def __init__(self, state, coef=None, total=None, source=None, drives=None, profile=None):
        self.state, self.coef, self.total = state, coef, total
        self.source, self.drives, self.profile = source, drives, profile
        self.rows = state.shape[3] - 2 * PAD
        self.depth = state.shape[2] - EXTRA
        self.top, self.under = self.depth - 1, self.depth
        self.slab = lax.axis_index("slab")
        self.has_up = self.slab < lax.axis_size("slab") - 1
        self.has_low = self.slab > 0

    def read(self, evo, comp, layer, first, size, shift=0):
        return self.state[evo, comp, layer, pl.ds(PAD + first + shift, size), :]

    def write(self, evo, comp, layer, first, size, value):
        self.state[evo, comp, layer, pl.ds(PAD + first, size), :] = value

    def put_h(self, evo, layer, upper):
        for first, size in chunks(self.rows):
            ex, ey, ez, hx, hy, hz = (self.read(evo, c, layer, first, size) for c in range(6))
            if upper is None:
                rise_x, rise_y = -ex, -ey
            else:
                rise_x = self.read(evo, 0, upper, first, size) - ex
                rise_y = self.read(evo, 1, upper, first, size) - ey
            ey_after = self.read(evo, 1, layer, first, size, 1)
            ez_after = self.read(evo, 2, layer, first, size, 1)
            self.write(evo, 3, layer, first, size, hx - ((next_col(ez) - ez) - rise_y))
            self.write(evo, 4, layer, first, size, hy - (rise_x - (ez_after - ez)))
            self.write(evo, 5, layer, first, size, hz - ((ey_after - ey) - (next_col(ex) - ex)))

    def curl_h(self, evo, h, lower, first, size):
        hx, hy, hz = (self.read(evo, c, h, first, size) for c in (3, 4, 5))
        if lower is None:
            step_x, step_y = hx, hy
        else:
            step_x = hx - self.read(evo, 3, lower, first, size)
            step_y = hy - self.read(evo, 4, lower, first, size)
        hy_before = self.read(evo, 4, h, first, size, -1)
        hz_before = self.read(evo, 5, h, first, size, -1)
        return (
            (hz - prev_col(hz)) - step_y,
            step_x - (hz - hz_before),
            (hy - hy_before) - (hx - prev_col(hx)),
        )

    def drive(self, step, layer):
        @pl.when(self.source[0, 0] - self.slab * self.depth == layer)
        def _():
            amount = self.drives[step]
            for first, size in chunks(self.rows):
                here = pl.ds(PAD + first, size)
                self.state[0, 2, layer, here, :] += amount * self.profile[pl.ds(first, size), :]

    def next_e(self, evo, layer, lower, first, size):
        cell = self.coef[layer, pl.ds(first, size), :]
        curl = self.curl_h(evo, layer, lower, first, size)
        return [self.read(evo, c, layer, first, size) + cell * curl[c] for c in range(3)]

    def put_e(self, evo, layer, lower, step):
        if evo == 0:
            self.drive(step, layer)
        for first, size in chunks(self.rows):
            for c, value in enumerate(self.next_e(evo, layer, lower, first, size)):
                self.write(evo, c, layer, first, size, value)

    def put_both_e(self, layer, lower, step):
        self.drive(step, layer)
        for first, size in chunks(self.rows):
            fwd, adj = (self.next_e(evo, layer, lower, first, size) for evo in range(2))
            for evo, news in enumerate((fwd, adj)):
                for c in range(3):
                    self.write(evo, c, layer, first, size, news[c])
            part = fwd[0] * adj[0] + fwd[1] * adj[1] + fwd[2] * adj[2]
            self.total[layer, pl.ds(PAD + first, size), :] += part

    def add_edge(self, edges, slot, layer):
        for first, size in chunks(self.rows):
            part = edges[slot, pl.ds(PAD + first, size), :]
            for c in range(3):
                part += self.read(0, c, layer, first, size) * self.read(1, c, layer, first, size)
            edges[slot, pl.ds(PAD + first, size), :] = part

    def take(self, evo, below, above):
        top, under = self.top, self.under

        @pl.when(self.has_up)
        def _():
            for first, size in chunks(self.rows):
                here = pl.ds(first, size)
                hx = self.read(evo, 3, top, first, size) + above[1, here, :]
                hy = self.read(evo, 4, top, first, size) - above[0, here, :]
                self.write(evo, 3, top, first, size, hx)
                self.write(evo, 4, top, first, size, hy)

        @pl.when(self.has_low)
        def _():
            for first, size in chunks(self.rows):
                here = pl.ds(first, size)
                hx = below[0, here, :] + self.read(evo, 1, 0, first, size)
                hy = below[1, here, :] - self.read(evo, 0, 0, first, size)
                self.write(evo, 3, under, first, size, hx)
                self.write(evo, 4, under, first, size, hy)

    def give(self, evo, pays):
        def up(pay):
            for c in range(2):
                pay[c] = self.state[evo, 3 + c, self.top, pl.ds(PAD, self.rows), :]

        def down(pay):
            for c in range(2):
                pay[c] = self.state[evo, c, 0, pl.ds(PAD, self.rows), :]

        if len(pays) == 2:
            up(pays[0])
            down(pays[1])
        else:
            pl.when(self.has_up)(lambda: up(pays[0]))
            pl.when(self.has_low)(lambda: down(pays[0]))


def opening_kernel(fwd, adj, density, own, *rest):
    pays, (planes, sems) = rest[:-2], rest[-2:]
    depth, rows, width_y = fwd.shape[2:]
    top = depth - 1
    slab = lax.axis_index("slab")
    has_up, has_low = slab < lax.axis_size("slab") - 1, slab > 0
    held_copy = pltpu.make_async_copy(density, own, sems.at[2, 0])
    held_copy.start()

    def up(pay):
        copies = []
        for evo, given in enumerate((fwd, adj)):
            for c in range(5):
                copies.append(
                    pltpu.make_async_copy(given.at[0, c, top], planes.at[evo, c], sems.at[evo, c])
                )
        for copy in copies:
            copy.start()
        for copy in copies:
            copy.wait()
        for evo in range(2):
            for first, size in chunks(rows):
                here = pl.ds(first, size)
                ex, ey, ez, hx, hy = (planes[evo, c, here, :] for c in range(5))
                if first + size < rows:
                    ez_after = planes[evo, 2, pl.ds(first + 1, size), :]
                else:
                    row = lax.broadcasted_iota(jnp.int32, ez.shape, 0)
                    ez_after = jnp.where(row == size - 1, 0.0, pltpu.roll(ez, size - 1, 0))
                pay[evo, 0, here, :] = (hx + hx) - ((next_col(ez) - ez) + ey)
                pay[evo, 1, here, :] = (hy + hy) + (ex + (ez_after - ez))

    def down(pay):
        copies = []
        for evo, given in enumerate((fwd, adj)):
            for c in range(2):
                copies.append(
                    pltpu.make_async_copy(given.at[0, c, 0], pay.at[evo, c], sems.at[evo, c])
                )
        for copy in copies:
            copy.start()
        for copy in copies:
            copy.wait()

    if len(pays) == 2:
        up(pays[0])
        down(pays[1])
    else:
        pl.when(has_up)(lambda: up(pays[0]))
        pl.when(has_low)(lambda: down(pays[0]))
    held_copy.wait()


def first_kernel(fwd, adj, source, state, total, edges, profile):
    win = Window(state)
    rows, width_y = win.rows, state.shape[4]
    margin = jnp.zeros((PAD, width_y), F32)
    empty = jnp.zeros((rows + 2 * PAD, width_y), F32)

    def clear(layer, carry):
        for evo in range(2):
            for comp in range(6):
                state[evo, comp, layer, pl.ds(0, PAD), :] = margin
                state[evo, comp, layer, pl.ds(PAD + rows, PAD), :] = margin
        return carry

    lax.fori_loop(0, state.shape[2], clear, 0)
    for evo in range(2):
        for comp in (3, 4):
            state[evo, comp, win.under] = empty
        edges[evo] = empty

    def copy(layer, carry):
        total[layer] = empty
        for evo, given in enumerate((fwd, adj)):
            for comp in range(6):
                for first, size in chunks(rows):
                    value = given[0, comp, layer, pl.ds(first, size), :]
                    win.write(evo, comp, layer, first, size, value + value if comp > 2 else value)
        return carry

    lax.fori_loop(0, win.depth, copy, 0)

    def body(layer, carry):
        for evo in range(2):
            win.put_h(evo, layer, layer + 1)
        return carry

    lax.fori_loop(0, win.top, body, 0)
    for evo in range(2):
        win.put_h(evo, win.top, None)
    xcoord = lax.broadcasted_iota(jnp.int32, (rows, width_y), 0)
    ycoord = lax.broadcasted_iota(jnp.int32, (rows, width_y), 1)
    offset_x = (xcoord - source[0, 1]).astype(F32) / (rows / 4.0)
    offset_y = (ycoord - source[0, 2]).astype(F32) / (width_y / 4.0)
    profile[...] = jnp.exp(-0.5 * (offset_x * offset_x + offset_y * offset_y))


def take_kernel(state_in, below, above, state):
    win = Window(state)
    for evo in range(2):
        win.take(evo, below.at[evo], above.at[evo])


def edge_kernel(
    step, evo, state_in, edges_in, coef, source, drives, profile, *rest
):
    rest = list(rest)
    arrived = [rest.pop(0) for _ in range(2 if step > 0 else 0)]
    state, edges, pays = rest[0], rest[1], rest[2:]
    win = Window(state, coef, None, source, drives, profile)
    if step > 0:
        win.take(evo, *arrived)
    win.put_e(evo, win.top, win.top - 1, step)
    win.put_e(evo, 0, win.under, step)
    if pays:
        if evo == 1:
            win.add_edge(edges, 0, 0)
            win.add_edge(edges, 1, win.top)
        win.put_h(evo, win.top, None)
        win.give(evo, pays)
    elif evo == 1:
        win.add_edge(edges, 0, 0)
        win.add_edge(edges, 1, win.top)


def inner_kernel(step, state_in, total_in, coef, source, drives, profile, state, total):
    win = Window(state, coef, total, source, drives, profile)

    def first(layer, carry):
        win.put_both_e(layer, layer - 1, 0)
        return carry

    if step == 1:
        lax.fori_loop(1, win.top, first, 0)
    for evo in range(2):
        win.put_h(evo, 0, 1)

    def body(layer, carry):
        for evo in range(2):
            win.put_h(evo, layer, layer + 1)
        win.put_both_e(layer, layer - 1, step)
        return carry

    lax.fori_loop(1, win.top, body, 0)


def coef_layer(layer, coef, blocks, placed, base):
    nblock = blocks.shape[0]
    rows = base.shape[0]
    block_rows = rows // nblock
    for block in range(nblock):
        source = pl.ds(pl.multiple_of(layer * block_rows, block_rows), block_rows)
        placed[pl.ds(PAD + block * block_rows, block_rows), :] = blocks[block, source, :]
    for first, size in chunks(rows):
        here = pl.ds(first, size)
        coef[layer, here, :] = 0.25 / (base[here, :] + 3.0 * filtered(placed, first, size))


def coef_edge_kernel(layout, count, *refs):
    parts = refs[:count]
    block_ids, material_idx, material_eps, coef, blocks, base, placed = refs[count:]
    nblock = blocks.shape[0]
    depth, rows, width_y = coef.shape
    block_rows = rows // nblock
    me = lax.axis_index("grp")
    for part, masks in zip(parts, layout):
        for slot, mask in enumerate(masks):
            blocks[block_ids[me ^ mask]] = part[slot]
    for block in range(nblock):
        level = jnp.full((block_rows, width_y), material_eps[material_idx[block]], F32)
        base[pl.ds(block * block_rows, block_rows), :] = level
    placed[pl.ds(0, PAD), :] = jnp.zeros((PAD, width_y), F32)
    placed[pl.ds(PAD + rows, PAD), :] = jnp.zeros((PAD, width_y), F32)
    coef_layer(0, coef, blocks, placed, base)
    coef_layer(depth - 1, coef, blocks, placed, base)


def coef_inner_kernel(coef_in, blocks, base, coef, placed):
    depth, rows, width_y = coef.shape
    placed[pl.ds(0, PAD), :] = jnp.zeros((PAD, width_y), F32)
    placed[pl.ds(PAD + rows, PAD), :] = jnp.zeros((PAD, width_y), F32)

    def body(layer, carry):
        coef_layer(layer, coef, blocks, placed, base)
        return carry

    lax.fori_loop(1, depth - 1, body, 0)


def filtered(padded, first, size):
    here = padded[pl.ds(PAD + first, size), :]
    before = padded[pl.ds(PAD + first - 1, size), :]
    after = padded[pl.ds(PAD + first + 1, size), :]
    along = before + 2.0 * here + after
    return (prev_col(along) + 2.0 * along + next_col(along)) * 0.0625


def pack_kernel(*refs):
    out = refs[-1]
    for slot, ref in enumerate(refs[:-1]):
        out[slot] = ref[...]


def filter_kernel(layout, skip, total, block_ids, *rest):
    parts, blocks, wide = rest[:-2], rest[-2], rest[-1]
    nblock = blocks.shape[0]
    rows = total.shape[1] - 2 * PAD
    block_rows = rows // nblock
    me = lax.axis_index("grp")

    def layer_of(layer, carry):
        for first, size in chunks(rows):
            wide[pl.ds(first, size), :] = filtered(total.at[layer + skip], first, size)
        for block in range(nblock):
            target = pl.ds(pl.multiple_of(layer * block_rows, block_rows), block_rows)
            blocks[block, target, :] = wide[pl.ds(block * block_rows, block_rows), :]
        return carry

    lax.fori_loop(0, total.shape[0] - 2 * skip, layer_of, 0)
    for part, masks in zip(parts, layout):
        for slot, mask in enumerate(masks):
            part[slot] = blocks[block_ids[me ^ mask]]


def add_kernel(*refs):
    half = len(refs) // 3
    for a, b, out in zip(refs[:half], refs[half : 2 * half], refs[2 * half :]):
        out[...] = a[...] + b[...]


def join_kernel(count, block_rows, *refs):
    inner, edge, outs = refs[:count], refs[count : 2 * count], refs[2 * count :]
    rows = outs[0].shape[0]
    for slot, out in enumerate(outs):
        middle, ends = inner[0][slot], edge[0][slot]
        for a, b in zip(inner[1:], edge[1:]):
            middle, ends = middle + a[slot], ends + b[slot]
        out[pl.ds(0, block_rows), :] = ends[:block_rows]
        out[pl.ds(block_rows, rows - 2 * block_rows), :] = middle
        out[pl.ds(rows - block_rows, block_rows), :] = ends[block_rows:]


def last_kernel(scale, *refs):
    value = refs[0][...]
    for ref in refs[1:-1]:
        value = value + ref[...]
    refs[-1][...] = value * scale


def out_kernel(state, finals, halves, sems):
    depth = state.shape[2] - EXTRA
    rows = state.shape[3] - 2 * PAD
    every = pl.ds(PAD, rows)
    copies = [
        pltpu.make_async_copy(
            state.at[0, comp, pl.ds(0, depth), every, :], finals.at[0, comp], sems.at[comp]
        )
        for comp in range(3)
    ]
    for copy in copies:
        copy.start()
    for comp in range(3):

        def body(layer, carry):
            halves[comp, layer] = 0.5 * state[0, 3 + comp, layer, every, :]
            return carry

        lax.fori_loop(0, depth, body, 0)
        copy = pltpu.make_async_copy(halves.at[comp], finals.at[0, 3 + comp], sems.at[3 + comp])
        copy.start()
        copies.append(copy)
    for copy in copies:
        copy.wait()


def swap_over(array, axis, mask):
    return lax.ppermute(array, axis, [(i, i ^ mask) for i in range(lax.axis_size(axis))])


def shift_over(array, axis, distance):
    size = lax.axis_size(axis)
    route = [(i, i + distance) for i in range(size) if 0 <= i + distance < size]
    return lax.ppermute(array, axis, route)


def trade(pays):
    if len(pays) == 1:
        return [swap_over(pays[0], "slab", 1)] * 2
    return [shift_over(pays[0], "slab", 1), shift_over(pays[1], "slab", -1)]


def per_device(
    fwd_fields, adj_fields, density, block_ids, material_idx, material_eps, source_pos, wave_idx
):
    depth, width_x, width_y = fwd_fields.shape[2:]
    nblock = block_ids.shape[0]
    block_rows = width_x // nblock
    ngrp = lax.axis_size("grp")
    npay = 1 if lax.axis_size("slab") == 2 else 2
    omega = 2.0 * math.pi / (6.0 + 2.0 * wave_idx[0].astype(F32))
    drives = AMPLITUDE * jnp.sin(omega * (jnp.arange(STEPS, dtype=F32) + 1.0))

    far = 4
    middle = ngrp // (2 * far)
    far_masks = [2 * middle * j for j in range(far)]
    middle_masks = [2 * j for j in range(middle)]
    layout = [
        [core + mid + top for top in far_masks] for core in (0, 1) for mid in middle_masks
    ]
    piece = (depth * block_rows, width_y)
    group = (far,) + piece

    state_shape = on_chip(2, 6, depth + EXTRA, width_x + 2 * PAD, width_y)
    total_shape = on_chip(depth, width_x + 2 * PAD, width_y)
    edges_shape = on_chip(2, width_x + 2 * PAD, width_y)
    coef_shape = on_chip(depth, width_x, width_y)
    blocks_shape = on_chip(nblock, *piece)
    plane = on_chip(width_x, width_y)
    padded = pltpu.VMEM((width_x + 2 * PAD, width_y), F32)

    design = density.reshape(piece)
    got = [swap_over(design, "grp", mask) for mask in far_masks[1:]]
    own, *pays = call(
        opening_kernel,
        [on_chip(*piece)] + [on_chip(2, 2, width_x, width_y)] * npay,
        [IN_VMEM] * (1 + npay),
        [fwd_fields, adj_fields, design],
        [IN_HBM] * 3,
        [pltpu.VMEM((2, 5, width_x, width_y), F32), pltpu.SemaphoreType.DMA((3, 5))],
    )
    below, above = trade(pays)

    near = call(pack_kernel, on_chip(*group), IN_VMEM, [own] + got, [IN_VMEM] * far)
    parts = [near] + [swap_over(near, "grp", mask) for mask in middle_masks[1:]]
    parts = parts + [swap_over(part, "grp", 1) for part in parts]

    state, total, edges, profile = call(
        first_kernel,
        [state_shape, total_shape, edges_shape, plane],
        [IN_VMEM] * 4,
        [fwd_fields, adj_fields, source_pos],
        [IN_VMEM, IN_VMEM, IN_SMEM],
    )
    state = call(
        take_kernel, state_shape, IN_VMEM, [state, below, above], [IN_VMEM] * 3, aliases={0: 0}
    )
    coef, blocks, base = call(
        functools.partial(coef_edge_kernel, layout, len(parts)),
        [coef_shape, blocks_shape, plane],
        [IN_VMEM] * 3,
        parts + [block_ids, material_idx, material_eps],
        [IN_VMEM] * len(parts) + [IN_SMEM] * 3,
        [padded],
    )

    about = [source_pos, drives, profile]
    about_specs = [IN_SMEM, IN_SMEM, IN_VMEM]
    arrived = [[], []]
    for step in range(STEPS):
        more = npay if step < STEPS - 1 else 0
        for evo in range(2):
            state, edges, *pays = call(
                functools.partial(edge_kernel, step, evo),
                [state_shape, edges_shape] + [on_chip(2, width_x, width_y)] * more,
                [IN_VMEM] * (2 + more),
                [state, edges, coef] + about + arrived[evo],
                [IN_VMEM] * 3 + about_specs + [IN_VMEM] * len(arrived[evo]),
                aliases={0: 0, 1: 1},
            )
            if more:
                arrived[evo] = trade(pays)
        if step == 0:
            coef = call(
                coef_inner_kernel, coef_shape, IN_VMEM, [coef, blocks, base], [IN_VMEM] * 3,
                [padded], aliases={0: 0},
            )
        if more:
            state, total = call(
                functools.partial(inner_kernel, step + 1),
                [state_shape, total_shape],
                [IN_VMEM] * 2,
                [state, total, coef] + about,
                [IN_VMEM] * 3 + about_specs,
                aliases={0: 0, 1: 1},
            )

    def by_owner(values, skip):
        layers = values.shape[0] - 2 * skip
        shape = (far, layers * block_rows, width_y)
        parts = call(
            functools.partial(filter_kernel, layout, skip),
            [on_chip(*shape)] * len(layout),
            [IN_VMEM] * len(layout),
            [values, block_ids],
            [IN_VMEM, IN_SMEM],
            [pltpu.VMEM((nblock,) + shape[1:], F32), pltpu.VMEM((width_x, width_y), F32)],
        )
        got = [swap_over(part, "grp", 1) for part in parts[middle:]]
        sums = call(
            add_kernel,
            [on_chip(*shape)] * middle,
            [IN_VMEM] * middle,
            list(parts[:middle]) + got,
            [IN_VMEM] * (2 * middle),
        )
        return [sums[0]] + [
            swap_over(part, "grp", mask) for part, mask in zip(sums[1:], middle_masks[1:])
        ]

    inner = by_owner(total, 1)
    ends = by_owner(edges, 0)
    pieces = call(
        functools.partial(join_kernel, middle, block_rows),
        [on_chip(*piece)] * far,
        [IN_VMEM] * far,
        inner + ends,
        [IN_VMEM] * (2 * middle),
    )
    got = [swap_over(part, "grp", mask) for part, mask in zip(pieces[1:], far_masks[1:])]
    scale = 3.0 / (STEPS * math.sqrt(ngrp))
    grad = call(
        functools.partial(last_kernel, scale),
        jax.ShapeDtypeStruct(piece, F32),
        IN_VMEM,
        [pieces[0]] + got,
        [IN_VMEM] * far,
    )
    finals = call(
        out_kernel,
        jax.ShapeDtypeStruct(fwd_fields.shape, F32),
        IN_HBM,
        [state],
        [IN_VMEM],
        [
            pltpu.VMEM((3, depth, width_x, width_y), F32),
            pltpu.SemaphoreType.DMA((6,)),
        ],
    )
    return finals, grad.reshape(density.shape)


def solution(mesh):
    placed = (
        P("grp", None, "slab", None, None),
        P("grp", None, "slab", None, None),
        P("slab", "grp", None),
        P(),
        P(),
        P(),
        P("grp", None),
        P("grp"),
    )
    return jax.shard_map(
        per_device,
        mesh=mesh,
        in_specs=placed,
        out_specs=(P("grp", None, "slab", None, None), P("slab", "grp", None)),
        check_vma=False,
    )
```

```python
import functools
import math

import jax
import jax.numpy as jnp
from jax import lax
from jax.experimental import pallas as pl
from jax.experimental.pallas import tpu as pltpu
from jax.sharding import PartitionSpec as P

STEPS = 4
AMPLITUDE = 4.0
PAD = 8
F32 = jnp.float32

VMEM = pltpu.MemorySpace.VMEM
IN_VMEM = pl.BlockSpec(memory_space=pltpu.VMEM)
IN_SMEM = pl.BlockSpec(memory_space=pltpu.SMEM)
IN_HBM = pl.BlockSpec(memory_space=pltpu.MemorySpace.HBM)


def on_chip(*shape):
    return VMEM(shape, F32)


def held(array, spec):
    if spec is IN_SMEM:
        return array
    space = VMEM if spec is IN_VMEM else pltpu.MemorySpace.HBM
    return pltpu.with_memory_space_constraint(array, space)


def call(kernel, outs, out_specs, operands, specs, scratch=(), aliases=None, flops=0):
    operands = [held(a, s) for a, s in zip(operands, specs)]
    return pl.pallas_call(
        kernel,
        out_shape=outs,
        in_specs=specs,
        out_specs=out_specs,
        scratch_shapes=scratch,
        input_output_aliases=aliases or {},
        compiler_params=pltpu.CompilerParams(vmem_limit_bytes=8 << 20),
        cost_estimate=pl.CostEstimate(flops=flops, bytes_accessed=flops // 4, transcendentals=0),
    )(*operands)


CHUNK = 16


def chunks(rows):
    size = CHUNK if rows % CHUNK == 0 else rows
    return [(first, size) for first in range(0, rows, size)]


def next_col(value):
    column = lax.broadcasted_iota(jnp.int32, value.shape, 1)
    moved = pltpu.roll(value, value.shape[1] - 1, 1)
    return jnp.where(column == value.shape[1] - 1, 0.0, moved)


def prev_col(value):
    column = lax.broadcasted_iota(jnp.int32, value.shape, 1)
    return jnp.where(column == 0, 0.0, pltpu.roll(value, 1, 1))


class Window:
    def __init__(self, e, h, coef=None, total=None, source=None, drives=None, profile=None):
        self.e, self.h, self.coef, self.total = e, h, coef, total
        self.source, self.drives, self.profile = source, drives, profile
        self.rows = e.shape[3] - 2 * PAD
        self.depth = e.shape[2] - 1
        self.top, self.under = self.depth - 1, self.depth
        self.slab = lax.axis_index("slab")
        self.has_up = self.slab < lax.axis_size("slab") - 1
        self.has_low = self.slab > 0

    def read_e(self, evo, layer, first, size, shift=0):
        rows = pl.ds(PAD + first + shift, size)
        return [self.e[evo, c, layer, rows, :] for c in range(3)]

    def read_h(self, evo, layer, first, size, shift=0):
        rows = pl.ds(PAD + first + shift, size)
        return [self.h[evo, c, layer, rows, :] for c in range(3)]

    def write(self, ref, evo, layer, first, size, values):
        for c, value in enumerate(values):
            ref[evo, c, layer, pl.ds(PAD + first, size), :] = value

    def put_h(self, evo, layer, double=False):
        for first, size in chunks(self.rows):
            rows = pl.ds(PAD + first, size)
            after = pl.ds(PAD + first + 1, size)
            ex, ey, ez = self.read_e(evo, layer, first, size)
            hx, hy, hz = self.read_h(evo, layer, first, size)
            if double:
                hx, hy, hz = hx + hx, hy + hy, hz + hz
            rise_x = self.e[evo, 0, layer + 1, rows, :] - ex
            rise_y = self.e[evo, 1, layer + 1, rows, :] - ey
            ey_after = self.e[evo, 1, layer, after, :]
            ez_after = self.e[evo, 2, layer, after, :]
            hx = hx - ((next_col(ez) - ez) - rise_y)
            hy = hy - (rise_x - (ez_after - ez))
            hz = hz - ((ey_after - ey) - (next_col(ex) - ex))
            self.write(self.h, evo, layer, first, size, (hx, hy, hz))

    def put_top_h(self, evo):
        layer = self.top
        for first, size in chunks(self.rows):
            after = pl.ds(PAD + first + 1, size)
            ex, ey, ez = self.read_e(evo, layer, first, size)
            hx, hy, hz = self.read_h(evo, layer, first, size)
            ey_after = self.e[evo, 1, layer, after, :]
            ez_after = self.e[evo, 2, layer, after, :]
            hx = hx - ((next_col(ez) - ez) + ey)
            hy = hy + (ex + (ez_after - ez))
            hz = hz - ((ey_after - ey) - (next_col(ex) - ex))
            self.write(self.h, evo, layer, first, size, (hx, hy, hz))

    def curl_h(self, evo, layer, lower, first, size):
        rows = pl.ds(PAD + first, size)
        before = pl.ds(PAD + first - 1, size)
        hx, hy, hz = self.read_h(evo, layer, first, size)
        step_x = hx - self.h[evo, 0, lower, rows, :]
        step_y = hy - self.h[evo, 1, lower, rows, :]
        hy_before = self.h[evo, 1, layer, before, :]
        hz_before = self.h[evo, 2, layer, before, :]
        return (
            (hz - prev_col(hz)) - step_y,
            step_x - (hz - hz_before),
            (hy - hy_before) - (hx - prev_col(hx)),
        )

    def drive(self, step, layer):
        @pl.when(self.source[0, 0] - self.slab * self.depth == layer)
        def _():
            amount = self.drives[step]
            for first, size in chunks(self.rows):
                here = pl.ds(PAD + first, size)
                self.e[0, 2, layer, here, :] += amount * self.profile[pl.ds(first, size), :]

    def next_e(self, evo, layer, lower, first, size, curls):
        cell = self.coef[layer, pl.ds(first, size), :]
        if curls is None:
            curl = self.curl_h(evo, layer, lower, first, size)
        else:
            curl = [curls[evo, c, layer, pl.ds(first, size), :] for c in range(3)]
        old = self.read_e(evo, layer, first, size)
        return [a + cell * b for a, b in zip(old, curl)]

    def put_e(self, evo, layer, lower, step, curls=None):
        if evo == 0:
            self.drive(step, layer)
        for first, size in chunks(self.rows):
            news = self.next_e(evo, layer, lower, first, size, curls)
            self.write(self.e, evo, layer, first, size, news)

    def put_both_e(self, layer, lower, curls=None):
        for first, size in chunks(self.rows):
            fwd, adj = (self.next_e(evo, layer, lower, first, size, curls) for evo in range(2))
            self.write(self.e, 0, layer, first, size, fwd)
            self.write(self.e, 1, layer, first, size, adj)
            part = fwd[0] * adj[0] + fwd[1] * adj[1] + fwd[2] * adj[2]
            self.total[layer, pl.ds(PAD + first, size), :] += part

    def add_edge(self, edges, slot, layer):
        for first, size in chunks(self.rows):
            part = edges[slot, pl.ds(PAD + first, size), :]
            for fwd, adj in zip(
                self.read_e(0, layer, first, size), self.read_e(1, layer, first, size)
            ):
                part += fwd * adj
            edges[slot, pl.ds(PAD + first, size), :] = part

    def take_above(self, evo, above):
        for first, size in chunks(self.rows):
            here, rows = pl.ds(first, size), pl.ds(PAD + first, size)
            self.h[evo, 0, self.top, rows, :] += above[1, here, :]
            self.h[evo, 1, self.top, rows, :] -= above[0, here, :]

    def take_below(self, evo, below):
        for first, size in chunks(self.rows):
            here, rows = pl.ds(first, size), pl.ds(PAD + first, size)
            self.h[evo, 0, self.under, rows, :] = below[0, here, :] + self.e[evo, 1, 0, rows, :]
            self.h[evo, 1, self.under, rows, :] = below[1, here, :] - self.e[evo, 0, 0, rows, :]


def opening_kernel(fwd, adj, density, own, *rest):
    pays, (planes, sems) = rest[:-2], rest[-2:]
    depth, rows, width_y = fwd.shape[2:]
    top = depth - 1
    slab = lax.axis_index("slab")
    has_up, has_low = slab < lax.axis_size("slab") - 1, slab > 0
    held_copy = pltpu.make_async_copy(density, own, sems.at[2, 0])
    held_copy.start()

    def up(pay):
        copies = []
        for evo, given in enumerate((fwd, adj)):
            for c in range(5):
                copies.append(
                    pltpu.make_async_copy(given.at[0, c, top], planes.at[evo, c], sems.at[evo, c])
                )
        for copy in copies:
            copy.start()
        for copy in copies:
            copy.wait()
        for evo in range(2):
            for first, size in chunks(rows):
                here = pl.ds(first, size)
                ex, ey, ez, hx, hy = (planes[evo, c, here, :] for c in range(5))
                if first + size < rows:
                    ez_after = planes[evo, 2, pl.ds(first + 1, size), :]
                else:
                    row = lax.broadcasted_iota(jnp.int32, ez.shape, 0)
                    ez_after = jnp.where(row == size - 1, 0.0, pltpu.roll(ez, size - 1, 0))
                pay[evo, 0, here, :] = (hx + hx) - ((next_col(ez) - ez) + ey)
                pay[evo, 1, here, :] = (hy + hy) + (ex + (ez_after - ez))

    def down(pay):
        copies = []
        for evo, given in enumerate((fwd, adj)):
            for c in range(2):
                copies.append(
                    pltpu.make_async_copy(given.at[0, c, 0], pay.at[evo, c], sems.at[evo, c])
                )
        for copy in copies:
            copy.start()
        for copy in copies:
            copy.wait()

    if len(pays) == 2:
        up(pays[0])
        down(pays[1])
    else:
        pl.when(has_up)(lambda: up(pays[0]))
        pl.when(has_low)(lambda: down(pays[0]))
    held_copy.wait()


def first_kernel(fwd, adj, near, source, e, h, total, edges, profile, curls, sems):
    win = Window(e, h)
    rows, width_y = win.rows, e.shape[4]
    copies = ([], [])
    for evo, given in enumerate((fwd, adj)):
        for comp in range(6):
            ref = e if comp < 3 else h
            copies[evo].append(
                pltpu.make_async_copy(
                    given.at[0, comp],
                    ref.at[evo, comp % 3, pl.ds(0, win.depth), pl.ds(PAD, rows), :],
                    sems.at[evo, comp],
                )
            )
    for copy in copies[0] + copies[1]:
        copy.start()
    margin = jnp.zeros((PAD, width_y), F32)
    empty = jnp.zeros((rows + 2 * PAD, width_y), F32)

    def clear(layer, carry):
        for ref in (e, h):
            for evo in range(2):
                for comp in range(3):
                    ref[evo, comp, layer, pl.ds(0, PAD), :] = margin
                    ref[evo, comp, layer, pl.ds(PAD + rows, PAD), :] = margin
        total[layer] = empty
        return carry

    lax.fori_loop(0, win.depth, clear, 0)
    for evo in range(2):
        for comp in range(3):
            e[evo, comp, win.depth] = empty
            h[evo, comp, win.depth] = empty
        edges[evo] = empty
    xcoord = lax.broadcasted_iota(jnp.int32, (rows, width_y), 0)
    ycoord = lax.broadcasted_iota(jnp.int32, (rows, width_y), 1)
    offset_x = (xcoord - source[0, 1]).astype(F32) / (rows / 4.0)
    offset_y = (ycoord - source[0, 2]).astype(F32) / (width_y / 4.0)
    profile[...] = jnp.exp(-0.5 * (offset_x * offset_x + offset_y * offset_y))
    for evo in range(2):
        for copy in copies[evo]:
            copy.wait()
        win.put_h(evo, 0, True)
        win.put_h(evo, 1, True)

        def body(layer, carry, evo=evo):
            win.put_h(evo, layer + 1, True)
            put_curl(win, curls, evo, layer, layer - 1)
            return carry

        lax.fori_loop(1, win.top, body, 0)


def put_curl(win, curls, evo, layer, lower):
    for first, size in chunks(win.rows):
        for c, value in enumerate(win.curl_h(evo, layer, lower, first, size)):
            curls[evo, c, layer, pl.ds(first, size), :] = value


def take_kernel(h_in, curls_in, e, below, above, h, curls):
    win = Window(e, h)
    for evo in range(2):
        pl.when(win.has_up)(lambda: win.take_above(evo, above.at[evo]))
        pl.when(win.has_low)(lambda: win.take_below(evo, below.at[evo]))
    for evo in range(2):
        put_curl(win, curls, evo, win.top, win.top - 1)
        put_curl(win, curls, evo, 0, win.under)


def edge_kernel(step, evo, e_in, h_in, edges_in, coef, source, drives, profile, *rest):
    rest = list(rest)
    curls = rest.pop(0) if step == 0 else None
    below, above = [rest.pop(0) for _ in range(2)] if step > 0 else (None, None)
    e, h, edges = rest[:3]
    pays = rest[3:]
    win = Window(e, h, coef, None, source, drives, profile)
    top = win.top

    @pl.when(win.has_up)
    def _():
        if step > 0:
            win.take_above(evo, above)
        win.put_e(evo, top, top - 1, step, curls)
        if pays:
            win.put_top_h(evo)
            for c in range(2):
                pays[0][c] = h[evo, c, top, pl.ds(PAD, win.rows), :]
        if evo == 1:
            win.add_edge(edges, 1, top)

    @pl.when(win.has_low)
    def _():
        if step > 0:
            win.take_below(evo, below)
        win.put_e(evo, 0, win.under, step, curls)
        if pays:
            for c in range(2):
                pays[-1][c] = e[evo, c, 0, pl.ds(PAD, win.rows), :]
        if evo == 1:
            win.add_edge(edges, 0, 0)


def inner_kernel(step, e_in, h_in, total_in, coef, source, drives, profile, *rest):
    rest = list(rest)
    curls = rest.pop(0) if step == 1 else None
    e, h, total = rest
    win = Window(e, h, coef, total, source, drives, profile)
    lowest = jnp.where(win.has_low, 1, 0)
    highest = jnp.where(win.has_up, win.top - 1, win.top)

    def first(layer, carry):
        win.drive(0, layer)
        win.put_both_e(layer, None, curls)
        return carry

    if step == 1:
        lax.fori_loop(lowest, highest + 1, first, 0)
    for evo in range(2):
        win.put_h(evo, 0)

    @pl.when(win.has_low)
    def _():
        for evo in range(2):
            win.put_h(evo, 1)

    def body(layer, carry):
        win.drive(step, layer)
        for evo in range(2):
            win.put_h(evo, layer + 1)
        win.put_both_e(layer, jnp.where(layer == 0, win.under, layer - 1))
        return carry

    lax.fori_loop(lowest, highest, body, 0)
    win.drive(step, highest)
    win.put_both_e(highest, highest - 1)


def coef_layer(layer, coef, blocks, placed, base):
    nblock = blocks.shape[0]
    rows = base.shape[0]
    block_rows = rows // nblock
    for block in range(nblock):
        source = pl.ds(pl.multiple_of(layer * block_rows, block_rows), block_rows)
        placed[pl.ds(PAD + block * block_rows, block_rows), :] = blocks[block, source, :]
    for first, size in chunks(rows):
        here = pl.ds(first, size)
        coef[layer, here, :] = 0.25 / (base[here, :] + 3.0 * filtered(placed, first, size))


def coef_edge_kernel(layout, count, *refs):
    parts = refs[:count]
    block_ids, material_idx, material_eps, coef, blocks, base, placed = refs[count:]
    nblock = blocks.shape[0]
    depth, rows, width_y = coef.shape
    block_rows = rows // nblock
    me = lax.axis_index("grp")
    for part, masks in zip(parts, layout):
        for slot, mask in enumerate(masks):
            blocks[block_ids[me ^ mask]] = part[slot]
    for block in range(nblock):
        level = jnp.full((block_rows, width_y), material_eps[material_idx[block]], F32)
        base[pl.ds(block * block_rows, block_rows), :] = level
    placed[pl.ds(0, PAD), :] = jnp.zeros((PAD, width_y), F32)
    placed[pl.ds(PAD + rows, PAD), :] = jnp.zeros((PAD, width_y), F32)
    coef_layer(0, coef, blocks, placed, base)
    coef_layer(depth - 1, coef, blocks, placed, base)


def coef_inner_kernel(coef_in, blocks, base, coef, placed):
    depth, rows, width_y = coef.shape
    placed[pl.ds(0, PAD), :] = jnp.zeros((PAD, width_y), F32)
    placed[pl.ds(PAD + rows, PAD), :] = jnp.zeros((PAD, width_y), F32)

    def body(layer, carry):
        coef_layer(layer, coef, blocks, placed, base)
        return carry

    lax.fori_loop(1, depth - 1, body, 0)


def filtered(padded, first, size):
    here = padded[pl.ds(PAD + first, size), :]
    before = padded[pl.ds(PAD + first - 1, size), :]
    after = padded[pl.ds(PAD + first + 1, size), :]
    along = before + 2.0 * here + after
    return (prev_col(along) + 2.0 * along + next_col(along)) * 0.0625


def pack_kernel(*refs):
    out = refs[-1]
    for slot, ref in enumerate(refs[:-1]):
        out[slot] = ref[...]


def filter_layer(values, layer, blocks, wide):
    nblock = blocks.shape[0]
    rows = wide.shape[0]
    block_rows = rows // nblock
    for first, size in chunks(rows):
        wide[pl.ds(first, size), :] = filtered(values, first, size)
    for block in range(nblock):
        target = pl.ds(pl.multiple_of(layer * block_rows, block_rows), block_rows)
        blocks[block, target, :] = wide[pl.ds(block * block_rows, block_rows), :]


def filter_inner_kernel(total, blocks, wide):
    def body(layer, carry):
        filter_layer(total.at[layer], layer, blocks, wide)
        return carry

    lax.fori_loop(1, total.shape[0] - 1, body, 0)


def filter_edge_kernel(layout, blocks_in, total, edges, block_ids, blocks, *rest):
    parts, wide, ends = rest[:-2], rest[-2], rest[-1]
    me = lax.axis_index("grp")
    for slot, layer in enumerate((0, total.shape[0] - 1)):
        ends[slot] = total[layer] + edges[slot]
        filter_layer(ends.at[slot], layer, blocks, wide.at[slot])
    for part, masks in zip(parts, layout):
        for slot, mask in enumerate(masks):
            part[slot] = blocks[block_ids[me ^ mask]]


def add_kernel(*refs):
    half = len(refs) // 3
    for a, b, out in zip(refs[:half], refs[half : 2 * half], refs[2 * half :]):
        out[...] = a[...] + b[...]


def add_split_kernel(count, *refs):
    terms, outs = refs[:count], refs[count:]
    for slot, out in enumerate(outs):
        value = terms[0][slot]
        for term in terms[1:]:
            value = value + term[slot]
        out[...] = value


def last_kernel(scale, *refs):
    value = refs[0][...]
    for ref in refs[1:-1]:
        value = value + ref[...]
    refs[-1][...] = value * scale


def out_kernel(e, h, finals, halves, sems):
    depth = e.shape[2] - 1
    rows = e.shape[3] - 2 * PAD
    every = pl.ds(PAD, rows)
    copies = [
        pltpu.make_async_copy(
            e.at[0, c, pl.ds(0, depth), every, :], finals.at[0, c], sems.at[c]
        )
        for c in range(3)
    ]
    for copy in copies:
        copy.start()
    for c in range(3):

        def body(layer, carry, c=c):
            halves[c, layer] = 0.5 * h[0, c, layer, every, :]
            return carry

        lax.fori_loop(0, depth, body, 0)
        copy = pltpu.make_async_copy(halves.at[c], finals.at[0, 3 + c], sems.at[3 + c])
        copy.start()
        copies.append(copy)
    for copy in copies:
        copy.wait()


def swap_over(array, axis, mask):
    return lax.ppermute(array, axis, [(i, i ^ mask) for i in range(lax.axis_size(axis))])


def shift_over(array, axis, distance):
    size = lax.axis_size(axis)
    route = [(i, i + distance) for i in range(size) if 0 <= i + distance < size]
    return lax.ppermute(array, axis, route)


def trade(pays):
    if len(pays) == 1:
        return [swap_over(pays[0], "slab", 1)] * 2
    return [shift_over(pays[0], "slab", 1), shift_over(pays[1], "slab", -1)]


def per_device(
    fwd_fields, adj_fields, density, block_ids, material_idx, material_eps, source_pos, wave_idx
):
    depth, width_x, width_y = fwd_fields.shape[2:]
    nblock = block_ids.shape[0]
    block_rows = width_x // nblock
    ngrp = lax.axis_size("grp")
    npay = 1 if lax.axis_size("slab") == 2 else 2
    omega = 2.0 * math.pi / (6.0 + 2.0 * wave_idx[0].astype(F32))
    drives = AMPLITUDE * jnp.sin(omega * (jnp.arange(STEPS, dtype=F32) + 1.0))

    far = 4
    middle = ngrp // (2 * far)
    far_masks = [2 * middle * j for j in range(far)]
    middle_masks = [2 * j for j in range(middle)]
    layout = [
        [core + mid + top for top in far_masks] for core in (0, 1) for mid in middle_masks
    ]
    piece = (depth * block_rows, width_y)
    group = (far,) + piece

    field_shape = on_chip(2, 3, depth + 1, width_x + 2 * PAD, width_y)
    curls_shape = on_chip(2, 3, depth, width_x, width_y)
    total_shape = on_chip(depth, width_x + 2 * PAD, width_y)
    edges_shape = on_chip(2, width_x + 2 * PAD, width_y)
    coef_shape = on_chip(depth, width_x, width_y)
    blocks_shape = on_chip(nblock, *piece)
    plane = on_chip(width_x, width_y)
    padded = pltpu.VMEM((width_x + 2 * PAD, width_y), F32)

    design = density.reshape(piece)
    got = [swap_over(design, "grp", mask) for mask in far_masks[1:]]
    own, *pays = call(
        opening_kernel,
        [on_chip(*piece)] + [on_chip(2, 2, width_x, width_y)] * npay,
        [IN_VMEM] * (1 + npay),
        [fwd_fields, adj_fields, design],
        [IN_HBM] * 3,
        [pltpu.VMEM((2, 5, width_x, width_y), F32), pltpu.SemaphoreType.DMA((3, 5))],
    )
    below, above = trade(pays)

    near = call(pack_kernel, on_chip(*group), IN_VMEM, [own] + got, [IN_VMEM] * far)
    parts = [near] + [swap_over(near, "grp", mask) for mask in middle_masks[1:]]
    parts = parts + [swap_over(part, "grp", 1) for part in parts]

    e, h, total, edges, profile, curls = call(
        first_kernel,
        [field_shape, field_shape, total_shape, edges_shape, plane, curls_shape],
        [IN_VMEM] * 6,
        [fwd_fields, adj_fields, near, source_pos],
        [IN_HBM, IN_HBM, IN_VMEM, IN_SMEM],
        [pltpu.SemaphoreType.DMA((2, 6))],
    )
    h, curls = call(
        take_kernel,
        [field_shape, curls_shape],
        [IN_VMEM] * 2,
        [h, curls, e, below, above],
        [IN_VMEM] * 5,
        aliases={0: 0, 1: 1},
    )
    coef, blocks, base = call(
        functools.partial(coef_edge_kernel, layout, len(parts)),
        [coef_shape, blocks_shape, plane],
        [IN_VMEM] * 3,
        parts + [block_ids, material_idx, material_eps],
        [IN_VMEM] * len(parts) + [IN_SMEM] * 3,
        [padded],
    )

    about = [source_pos, drives, profile]
    about_specs = [IN_SMEM, IN_SMEM, IN_VMEM]
    arrived = [[curls], [curls]]
    for step in range(STEPS):
        more = npay if step < STEPS - 1 else 0
        for evo in range(2):
            e, h, edges, *pays = call(
                functools.partial(edge_kernel, step, evo),
                [field_shape, field_shape, edges_shape] + [on_chip(2, width_x, width_y)] * more,
                [IN_VMEM] * (3 + more),
                [e, h, edges, coef] + about + arrived[evo],
                [IN_VMEM] * 4 + about_specs + [IN_VMEM] * len(arrived[evo]),
                aliases={0: 0, 1: 1, 2: 2},
            )
            if more:
                arrived[evo] = trade(pays)
        if step == 0:
            coef = call(
                coef_inner_kernel, coef_shape, IN_VMEM, [coef, blocks, base], [IN_VMEM] * 3,
                [padded], aliases={0: 0},
            )
        if more:
            late = [curls] if step == 0 else []
            e, h, total = call(
                functools.partial(inner_kernel, step + 1),
                [field_shape, field_shape, total_shape],
                [IN_VMEM] * 3,
                [e, h, total, coef] + about + late,
                [IN_VMEM] * 4 + about_specs + [IN_VMEM] * len(late),
                aliases={0: 0, 1: 1, 2: 2},
            )
        if step == STEPS - 2:
            blocks = call(
                filter_inner_kernel, blocks_shape, IN_VMEM, [total], [IN_VMEM],
                [pltpu.VMEM((width_x, width_y), F32)],
            )

    blocks, *parts = call(
        functools.partial(filter_edge_kernel, layout),
        [blocks_shape] + [on_chip(*group)] * len(layout),
        [IN_VMEM] * (1 + len(layout)),
        [blocks, total, edges, block_ids],
        [IN_VMEM] * 3 + [IN_SMEM],
        [
            pltpu.VMEM((2, width_x, width_y), F32),
            pltpu.VMEM((2, width_x + 2 * PAD, width_y), F32),
        ],
        aliases={0: 0},
    )
    got = [swap_over(part, "grp", 1) for part in parts[middle:]]
    sums = call(
        add_kernel,
        [on_chip(*group)] * middle,
        [IN_VMEM] * middle,
        list(parts[:middle]) + got,
        [IN_VMEM] * (2 * middle),
    )
    got = [swap_over(part, "grp", mask) for part, mask in zip(sums[1:], middle_masks[1:])]
    pieces = call(
        functools.partial(add_split_kernel, middle),
        [on_chip(*piece)] * far,
        [IN_VMEM] * far,
        [sums[0]] + got,
        [IN_VMEM] * middle,
    )
    got = [swap_over(part, "grp", mask) for part, mask in zip(pieces[1:], far_masks[1:])]
    scale = 3.0 / (STEPS * math.sqrt(ngrp))
    grad = call(
        functools.partial(last_kernel, scale),
        jax.ShapeDtypeStruct(piece, F32),
        IN_VMEM,
        [pieces[0]] + got,
        [IN_VMEM] * far,
    )
    finals = call(
        out_kernel,
        jax.ShapeDtypeStruct(fwd_fields.shape, F32),
        IN_HBM,
        [e, h],
        [IN_VMEM] * 2,
        [
            pltpu.VMEM((3, depth, width_x, width_y), F32),
            pltpu.SemaphoreType.DMA((6,)),
        ],
    )
    return finals, grad.reshape(density.shape)


def solution(mesh):
    placed = (
        P("grp", None, "slab", None, None),
        P("grp", None, "slab", None, None),
        P("slab", "grp", None),
        P(),
        P(),
        P(),
        P("grp", None),
        P("grp"),
    )
    return jax.shard_map(
        per_device,
        mesh=mesh,
        in_specs=placed,
        out_specs=(P("grp", None, "slab", None, None), P("slab", "grp", None)),
        check_vma=False,
    )
```

```python
import functools
import math

import jax
import jax.numpy as jnp
from jax import lax
from jax.experimental import pallas as pl
from jax.experimental.pallas import tpu as pltpu
from jax.sharding import PartitionSpec as P

STEPS = 4
AMPLITUDE = 4.0
PAD = 8
F32 = jnp.float32
HBM_PER_MICRO = 3.0e6

VMEM = pltpu.MemorySpace.VMEM
IN_VMEM = pl.BlockSpec(memory_space=pltpu.VMEM)
IN_SMEM = pl.BlockSpec(memory_space=pltpu.SMEM)
IN_HBM = pl.BlockSpec(memory_space=pltpu.MemorySpace.HBM)


def on_chip(*shape):
    return VMEM(shape, F32)


def held(array, spec):
    if spec is IN_SMEM:
        return array
    space = VMEM if spec is IN_VMEM else pltpu.MemorySpace.HBM
    return pltpu.with_memory_space_constraint(array, space)


def call(kernel, outs, out_specs, operands, specs, scratch=(), aliases=None, micros=0.3):
    operands = [held(a, s) for a, s in zip(operands, specs)]
    return pl.pallas_call(
        kernel,
        out_shape=outs,
        in_specs=specs,
        out_specs=out_specs,
        scratch_shapes=scratch,
        input_output_aliases=aliases or {},
        compiler_params=pltpu.CompilerParams(vmem_limit_bytes=8 << 20),
        cost_estimate=pl.CostEstimate(
            flops=0, bytes_accessed=int(micros * HBM_PER_MICRO), transcendentals=0
        ),
    )(*operands)


CHUNK = 16


def chunks(rows):
    size = CHUNK if rows % CHUNK == 0 else rows
    return [(first, size) for first in range(0, rows, size)]


def next_col(value):
    column = lax.broadcasted_iota(jnp.int32, value.shape, 1)
    moved = pltpu.roll(value, value.shape[1] - 1, 1)
    return jnp.where(column == value.shape[1] - 1, 0.0, moved)


def prev_col(value):
    column = lax.broadcasted_iota(jnp.int32, value.shape, 1)
    return jnp.where(column == 0, 0.0, pltpu.roll(value, 1, 1))


def neighbours():
    slab = lax.axis_index("slab")
    return slab < lax.axis_size("slab") - 1, slab > 0


class Window:
    def __init__(self, e, h, coef=None, force=None):
        self.e, self.h, self.coef, self.force = e, h, coef, force
        self.rows = e.shape[2] - 2 * PAD
        self.depth = e.shape[1] - 1
        self.top, self.under = self.depth - 1, self.depth

    def read(self, ref, layer, first, size):
        return [ref[c, layer, pl.ds(PAD + first, size), :] for c in range(3)]

    def write(self, ref, layer, first, size, values):
        for c, value in enumerate(values):
            ref[c, layer, pl.ds(PAD + first, size), :] = value

    def put_h(self, layer, double=False, alone=False):
        for first, size in chunks(self.rows):
            rows = pl.ds(PAD + first, size)
            after = pl.ds(PAD + first + 1, size)
            ex, ey, ez = self.read(self.e, layer, first, size)
            hx, hy, hz = self.read(self.h, layer, first, size)
            if double:
                hx, hy, hz = hx + hx, hy + hy, hz + hz
            if alone:
                rise_x, rise_y = -ex, -ey
            else:
                rise_x = self.e[0, layer + 1, rows, :] - ex
                rise_y = self.e[1, layer + 1, rows, :] - ey
            ey_after = self.e[1, layer, after, :]
            ez_after = self.e[2, layer, after, :]
            hx = hx - ((next_col(ez) - ez) - rise_y)
            hy = hy - (rise_x - (ez_after - ez))
            hz = hz - ((ey_after - ey) - (next_col(ex) - ex))
            self.write(self.h, layer, first, size, (hx, hy, hz))

    def curl_h(self, layer, lower, first, size):
        rows = pl.ds(PAD + first, size)
        before = pl.ds(PAD + first - 1, size)
        hx, hy, hz = self.read(self.h, layer, first, size)
        step_x = hx - self.h[0, lower, rows, :]
        step_y = hy - self.h[1, lower, rows, :]
        hy_before = self.h[1, layer, before, :]
        hz_before = self.h[2, layer, before, :]
        return (
            (hz - prev_col(hz)) - step_y,
            step_x - (hz - hz_before),
            (hy - hy_before) - (hx - prev_col(hx)),
        )

    def put_curl(self, curls, layer, lower):
        for first, size in chunks(self.rows):
            for c, value in enumerate(self.curl_h(layer, lower, first, size)):
                curls[c, layer, pl.ds(first, size), :] = value

    def next_e(self, layer, lower, first, size, curls=None):
        here = pl.ds(first, size)
        cell = self.coef[layer, here, :]
        if curls is None:
            curl = self.curl_h(layer, lower, first, size)
        else:
            curl = [curls[c, layer, here, :] for c in range(3)]
        ex, ey, ez = [a + cell * b for a, b in zip(self.read(self.e, layer, first, size), curl)]
        if self.force is not None:
            ez = ez + self.force(layer, here)
        return ex, ey, ez

    def put_e(self, layer, lower, curls=None, other=None, total=None, slot=None):
        for first, size in chunks(self.rows):
            news = self.next_e(layer, lower, first, size, curls)
            self.write(self.e, layer, first, size, news)
            if total is not None:
                rows = pl.ds(PAD + first, size)
                part = [a * other[c, layer, rows, :] for c, a in enumerate(news)]
                total[layer if slot is None else slot, rows, :] += part[0] + part[1] + part[2]

    def take_above(self, above):
        for first, size in chunks(self.rows):
            here, rows = pl.ds(first, size), pl.ds(PAD + first, size)
            self.h[0, self.top, rows, :] += above[1, here, :]
            self.h[1, self.top, rows, :] -= above[0, here, :]

    def take_below(self, below):
        for first, size in chunks(self.rows):
            here, rows = pl.ds(first, size), pl.ds(PAD + first, size)
            self.h[0, self.under, rows, :] = below[0, here, :] + self.e[1, 0, rows, :]
            self.h[1, self.under, rows, :] = below[1, here, :] - self.e[0, 0, rows, :]


def forcing(step, drives, forced):
    if drives is None:
        return None
    return lambda layer, here: drives[pl.ds(step, 1), :] * forced[layer, here, :]


def opening_kernel(fwd, adj, density, own, *rest):
    pays, (planes, sems) = rest[:-2], rest[-2:]
    depth, rows, width_y = fwd.shape[2:]
    top = depth - 1
    has_up, has_low = neighbours()
    held_copy = pltpu.make_async_copy(density, own, sems.at[2, 0])
    held_copy.start()

    def up(pay):
        copies = []
        for evo, given in enumerate((fwd, adj)):
            for c in range(5):
                copies.append(
                    pltpu.make_async_copy(given.at[0, c, top], planes.at[evo, c], sems.at[evo, c])
                )
        for copy in copies:
            copy.start()
        for copy in copies:
            copy.wait()
        for evo in range(2):
            for first, size in chunks(rows):
                here = pl.ds(first, size)
                ex, ey, ez, hx, hy = (planes[evo, c, here, :] for c in range(5))
                if first + size < rows:
                    ez_after = planes[evo, 2, pl.ds(first + 1, size), :]
                else:
                    row = lax.broadcasted_iota(jnp.int32, ez.shape, 0)
                    ez_after = jnp.where(row == size - 1, 0.0, pltpu.roll(ez, size - 1, 0))
                pay[evo, 0, here, :] = (hx + hx) - ((next_col(ez) - ez) + ey)
                pay[evo, 1, here, :] = (hy + hy) + (ex + (ez_after - ez))

    def down(pay):
        copies = []
        for evo, given in enumerate((fwd, adj)):
            for c in range(2):
                copies.append(
                    pltpu.make_async_copy(given.at[0, c, 0], pay.at[evo, c], sems.at[evo, c])
                )
        for copy in copies:
            copy.start()
        for copy in copies:
            copy.wait()

    if len(pays) == 2:
        up(pays[0])
        down(pays[1])
    else:
        pl.when(has_up)(lambda: up(pays[0]))
        pl.when(has_low)(lambda: down(pays[0]))
    held_copy.wait()


def prepare_kernel(source, total, edges, forced):
    depth, rows, width_y = forced.shape
    empty = jnp.zeros(total.shape[1:], F32)
    edges[0] = empty
    edges[1] = empty
    xcoord = lax.broadcasted_iota(jnp.int32, (rows, width_y), 0)
    ycoord = lax.broadcasted_iota(jnp.int32, (rows, width_y), 1)
    offset_x = (xcoord - source[0, 1]).astype(F32) / (rows / 4.0)
    offset_y = (ycoord - source[0, 2]).astype(F32) / (width_y / 4.0)
    profile = jnp.exp(-0.5 * (offset_x * offset_x + offset_y * offset_y))
    level = source[0, 0] - lax.axis_index("slab") * depth
    for layer in range(depth):
        total[layer] = empty
        forced[layer] = jnp.where(level == layer, 1.0, 0.0) * profile


def first_kernel(given, near, e, h, curls, sems):
    win = Window(e, h)
    rows, width_y = win.rows, e.shape[3]
    copies = [
        pltpu.make_async_copy(
            given.at[0, comp],
            (e if comp < 3 else h).at[comp % 3, pl.ds(0, win.depth), pl.ds(PAD, rows), :],
            sems.at[comp],
        )
        for comp in range(6)
    ]
    for copy in copies:
        copy.start()
    margin = jnp.zeros((PAD, width_y), F32)
    empty = jnp.zeros((rows + 2 * PAD, width_y), F32)

    def clear(layer, carry):
        for ref in (e, h):
            for comp in range(3):
                ref[comp, layer, pl.ds(0, PAD), :] = margin
                ref[comp, layer, pl.ds(PAD + rows, PAD), :] = margin
        return carry

    lax.fori_loop(0, win.depth, clear, 0)
    for comp in range(3):
        e[comp, win.depth] = empty
        h[comp, win.depth] = empty
    for copy in copies:
        copy.wait()
    win.put_h(0, True)
    win.put_h(1, True)

    def body(layer, carry):
        win.put_h(layer + 1, True)
        win.put_curl(curls, layer, layer - 1)
        return carry

    lax.fori_loop(1, win.top, body, 0)


def take_kernel(evo, h_in, curls_in, e, below, above, h, curls):
    win = Window(e, h)
    has_up, has_low = neighbours()
    pl.when(has_up)(lambda: win.take_above(above.at[evo]))
    pl.when(has_low)(lambda: win.take_below(below.at[evo]))
    win.put_curl(curls, win.top, win.top - 1)
    win.put_curl(curls, 0, win.under)


def edge_kernel(step, evo, *refs):
    refs = list(refs)
    e_in, h_in = refs.pop(0), refs.pop(0)
    if evo == 1:
        other_in, edges_in = refs.pop(0), refs.pop(0)
    coef = refs.pop(0)
    drives, forced = (refs.pop(0), refs.pop(0)) if evo == 0 else (None, None)
    curls = refs.pop(0) if step == 0 else None
    below, above = (refs.pop(0), refs.pop(0)) if step > 0 else (None, None)
    e, h = refs.pop(0), refs.pop(0)
    other, edges = (refs.pop(0), refs.pop(0)) if evo == 1 else (None, None)
    pays = refs
    win = Window(e, h, coef, forcing(step, drives, forced))
    top = win.top
    has_up, has_low = neighbours()

    @pl.when(has_up)
    def _():
        if step > 0:
            win.take_above(above)
        win.put_e(top, top - 1, curls, other, edges, 1)
        if pays:
            win.put_h(top, alone=True)
            for c in range(2):
                pays[0][c] = h[c, top, pl.ds(PAD, win.rows), :]

    @pl.when(has_low)
    def _():
        if step > 0:
            win.take_below(below)
        win.put_e(0, win.under, curls, other, edges, 0)
        if pays:
            for c in range(2):
                pays[-1][c] = e[c, 0, pl.ds(PAD, win.rows), :]


def inner_range(top):
    has_up, has_low = neighbours()
    return jnp.where(has_low, 1, 0), jnp.where(has_up, top - 1, top)


def begin_kernel(
    e_fwd_in, e_adj_in, total_in, coef, drives, forced, curls_fwd, curls_adj,
    e_fwd, e_adj, total,
):
    fwd = Window(e_fwd, None, coef, forcing(0, drives, forced))
    adj = Window(e_adj, None, coef)
    lowest, highest = inner_range(fwd.top)

    def body(layer, carry):
        fwd.put_e(layer, None, curls_fwd)
        adj.put_e(layer, None, curls_adj, e_fwd, total)
        return carry

    lax.fori_loop(lowest, highest + 1, body, 0)


def inner_kernel(step, evo, *refs):
    refs = list(refs)
    e_in, h_in = refs.pop(0), refs.pop(0)
    if evo == 1:
        other_in, total_in = refs.pop(0), refs.pop(0)
    coef = refs.pop(0)
    drives, forced = (refs.pop(0), refs.pop(0)) if evo == 0 else (None, None)
    e, h = refs.pop(0), refs.pop(0)
    other, total = (refs.pop(0), refs.pop(0)) if evo == 1 else (None, None)
    win = Window(e, h, coef, forcing(step, drives, forced))
    lowest, highest = inner_range(win.top)
    win.put_h(0)
    pl.when(lowest == 1)(lambda: win.put_h(1))

    def body(layer, carry):
        win.put_h(layer + 1)
        win.put_e(layer, jnp.where(layer == 0, win.under, layer - 1), None, other, total)
        return carry

    lax.fori_loop(lowest, highest, body, 0)
    win.put_e(highest, highest - 1, None, other, total)


def coef_layer(layer, coef, blocks, placed, base):
    nblock = blocks.shape[0]
    rows = base.shape[0]
    block_rows = rows // nblock
    for block in range(nblock):
        source = pl.ds(pl.multiple_of(layer * block_rows, block_rows), block_rows)
        placed[pl.ds(PAD + block * block_rows, block_rows), :] = blocks[block, source, :]
    for first, size in chunks(rows):
        here = pl.ds(first, size)
        coef[layer, here, :] = 0.25 / (base[here, :] + 3.0 * filtered(placed, first, size))


def coef_edge_kernel(layout, count, *refs):
    parts = refs[:count]
    block_ids, material_idx, material_eps, coef, blocks, base, placed = refs[count:]
    nblock = blocks.shape[0]
    depth, rows, width_y = coef.shape
    block_rows = rows // nblock
    me = lax.axis_index("grp")
    for part, masks in zip(parts, layout):
        for slot, mask in enumerate(masks):
            blocks[block_ids[me ^ mask]] = part[slot]
    for block in range(nblock):
        level = jnp.full((block_rows, width_y), material_eps[material_idx[block]], F32)
        base[pl.ds(block * block_rows, block_rows), :] = level
    placed[pl.ds(0, PAD), :] = jnp.zeros((PAD, width_y), F32)
    placed[pl.ds(PAD + rows, PAD), :] = jnp.zeros((PAD, width_y), F32)
    coef_layer(0, coef, blocks, placed, base)
    coef_layer(depth - 1, coef, blocks, placed, base)


def coef_inner_kernel(coef_in, blocks, base, coef, placed):
    depth, rows, width_y = coef.shape
    placed[pl.ds(0, PAD), :] = jnp.zeros((PAD, width_y), F32)
    placed[pl.ds(PAD + rows, PAD), :] = jnp.zeros((PAD, width_y), F32)

    def body(layer, carry):
        coef_layer(layer, coef, blocks, placed, base)
        return carry

    lax.fori_loop(1, depth - 1, body, 0)


def filtered(padded, first, size):
    here = padded[pl.ds(PAD + first, size), :]
    before = padded[pl.ds(PAD + first - 1, size), :]
    after = padded[pl.ds(PAD + first + 1, size), :]
    along = before + 2.0 * here + after
    return (prev_col(along) + 2.0 * along + next_col(along)) * 0.0625


def pack_kernel(*refs):
    out = refs[-1]
    for slot, ref in enumerate(refs[:-1]):
        out[slot] = ref[...]


def filter_layer(values, layer, blocks, wide):
    nblock = blocks.shape[0]
    rows = wide.shape[0]
    block_rows = rows // nblock
    for first, size in chunks(rows):
        wide[pl.ds(first, size), :] = filtered(values, first, size)
    for block in range(nblock):
        target = pl.ds(pl.multiple_of(layer * block_rows, block_rows), block_rows)
        blocks[block, target, :] = wide[pl.ds(block * block_rows, block_rows), :]


def filter_inner_kernel(total, blocks, wide):
    def body(layer, carry):
        filter_layer(total.at[layer], layer, blocks, wide)
        return carry

    lax.fori_loop(1, total.shape[0] - 1, body, 0)


def filter_edge_kernel(layout, blocks_in, total, edges, block_ids, blocks, *rest):
    parts, wide, ends = rest[:-2], rest[-2], rest[-1]
    me = lax.axis_index("grp")
    for slot, layer in enumerate((0, total.shape[0] - 1)):
        ends[slot] = total[layer] + edges[slot]
        filter_layer(ends.at[slot], layer, blocks, wide.at[slot])
    for part, masks in zip(parts, layout):
        for slot, mask in enumerate(masks):
            part[slot] = blocks[block_ids[me ^ mask]]


def add_kernel(*refs):
    half = len(refs) // 3
    for a, b, out in zip(refs[:half], refs[half : 2 * half], refs[2 * half :]):
        out[...] = a[...] + b[...]


def add_split_kernel(count, *refs):
    terms, outs = refs[:count], refs[count:]
    for slot, out in enumerate(outs):
        value = terms[0][slot]
        for term in terms[1:]:
            value = value + term[slot]
        out[...] = value


def last_kernel(scale, *refs):
    value = refs[0][...]
    for ref in refs[1:-1]:
        value = value + ref[...]
    refs[-1][...] = value * scale


def out_kernel(e, h, finals, halves, sems):
    depth = e.shape[1] - 1
    rows = e.shape[2] - 2 * PAD
    every = pl.ds(PAD, rows)
    copies = [
        pltpu.make_async_copy(e.at[c, pl.ds(0, depth), every, :], finals.at[0, c], sems.at[c])
        for c in range(3)
    ]
    for copy in copies:
        copy.start()
    for c in range(3):

        def body(layer, carry, c=c):
            halves[c, layer] = 0.5 * h[c, layer, every, :]
            return carry

        lax.fori_loop(0, depth, body, 0)
        copy = pltpu.make_async_copy(halves.at[c], finals.at[0, 3 + c], sems.at[3 + c])
        copy.start()
        copies.append(copy)
    for copy in copies:
        copy.wait()


def swap_over(array, axis, mask):
    return lax.ppermute(array, axis, [(i, i ^ mask) for i in range(lax.axis_size(axis))])


def shift_over(array, axis, distance):
    size = lax.axis_size(axis)
    route = [(i, i + distance) for i in range(size) if 0 <= i + distance < size]
    return lax.ppermute(array, axis, route)


def trade(pays):
    if len(pays) == 1:
        return [swap_over(pays[0], "slab", 1)] * 2
    return [shift_over(pays[0], "slab", 1), shift_over(pays[1], "slab", -1)]


def per_device(
    fwd_fields, adj_fields, density, block_ids, material_idx, material_eps, source_pos, wave_idx
):
    depth, width_x, width_y = fwd_fields.shape[2:]
    nblock = block_ids.shape[0]
    block_rows = width_x // nblock
    ngrp = lax.axis_size("grp")
    npay = 1 if lax.axis_size("slab") == 2 else 2
    omega = 2.0 * math.pi / (6.0 + 2.0 * wave_idx[0].astype(F32))
    steps = lax.broadcasted_iota(jnp.int32, (STEPS, width_y), 0).astype(F32)
    drives = AMPLITUDE * jnp.sin(omega * (steps + 1.0))

    far = 4
    middle = ngrp // (2 * far)
    far_masks = [2 * middle * j for j in range(far)]
    middle_masks = [2 * j for j in range(middle)]
    layout = [
        [core + mid + top for top in far_masks] for core in (0, 1) for mid in middle_masks
    ]
    piece = (depth * block_rows, width_y)
    group = (far,) + piece

    field_shape = on_chip(3, depth + 1, width_x + 2 * PAD, width_y)
    curls_shape = on_chip(3, depth, width_x, width_y)
    halo_shape = on_chip(2, width_x, width_y)
    total_shape = on_chip(depth, width_x + 2 * PAD, width_y)
    edges_shape = on_chip(2, width_x + 2 * PAD, width_y)
    coef_shape = on_chip(depth, width_x, width_y)
    blocks_shape = on_chip(nblock, *piece)
    plane = on_chip(width_x, width_y)
    padded = pltpu.VMEM((width_x + 2 * PAD, width_y), F32)

    design = density.reshape(piece)
    got = [swap_over(design, "grp", mask) for mask in far_masks[1:]]
    own, *pays = call(
        opening_kernel,
        [on_chip(*piece)] + [on_chip(2, 2, width_x, width_y)] * npay,
        [IN_VMEM] * (1 + npay),
        [fwd_fields, adj_fields, design],
        [IN_HBM] * 3,
        [pltpu.VMEM((2, 5, width_x, width_y), F32), pltpu.SemaphoreType.DMA((3, 5))],
    )
    below, above = trade(pays)

    near = call(pack_kernel, on_chip(*group), IN_VMEM, [own] + got, [IN_VMEM] * far)
    parts = [near] + [swap_over(near, "grp", mask) for mask in middle_masks[1:]]
    parts = parts + [swap_over(part, "grp", 1) for part in parts]

    total, edges, forced = call(
        prepare_kernel,
        [total_shape, edges_shape, on_chip(depth, width_x, width_y)],
        [IN_VMEM] * 3,
        [source_pos],
        [IN_SMEM],
    )
    fields = []
    for evo, given in enumerate((fwd_fields, adj_fields)):
        e, h, curls = call(
            first_kernel,
            [field_shape, field_shape, curls_shape],
            [IN_VMEM] * 3,
            [given, near],
            [IN_HBM, IN_VMEM],
            [pltpu.SemaphoreType.DMA((6,))],
            micros=2.3,
        )
        fields.append((e, h, curls))
    taken = []
    for evo, (e, h, curls) in enumerate(fields):
        h, curls = call(
            functools.partial(take_kernel, evo),
            [field_shape, curls_shape],
            [IN_VMEM] * 2,
            [h, curls, e, below, above],
            [IN_VMEM] * 5,
            aliases={0: 0, 1: 1},
        )
        taken.append((e, h, curls))
    (e_fwd, h_fwd, curls_fwd), (e_adj, h_adj, curls_adj) = taken
    coef, blocks, base = call(
        functools.partial(coef_edge_kernel, layout, len(parts)),
        [coef_shape, blocks_shape, plane],
        [IN_VMEM] * 3,
        parts + [block_ids, material_idx, material_eps],
        [IN_VMEM] * len(parts) + [IN_SMEM] * 3,
        [padded],
    )

    arrived_fwd, arrived_adj = [curls_fwd], [curls_adj]
    for step in range(STEPS):
        more = npay if step < STEPS - 1 else 0
        e_fwd, h_fwd, *pays = call(
            functools.partial(edge_kernel, step, 0),
            [field_shape] * 2 + [halo_shape] * more,
            [IN_VMEM] * (2 + more),
            [e_fwd, h_fwd, coef, drives, forced] + arrived_fwd,
            [IN_VMEM] * (5 + len(arrived_fwd)),
            aliases={0: 0, 1: 1},
        )
        if more:
            arrived_fwd = trade(pays)
        if step == 0:
            coef = call(
                coef_inner_kernel, coef_shape, IN_VMEM, [coef, blocks, base], [IN_VMEM] * 3,
                [padded], aliases={0: 0}, micros=0.7,
            )
            e_fwd, e_adj, total = call(
                begin_kernel,
                [field_shape, field_shape, total_shape],
                [IN_VMEM] * 3,
                [e_fwd, e_adj, total, coef, drives, forced, curls_fwd, curls_adj],
                [IN_VMEM] * 8,
                aliases={0: 0, 1: 1, 2: 2},
                micros=0.7,
            )
        else:
            e_adj, h_adj, e_fwd, total = call(
                functools.partial(inner_kernel, step, 1),
                [field_shape] * 3 + [total_shape],
                [IN_VMEM] * 4,
                [e_adj, h_adj, e_fwd, total, coef],
                [IN_VMEM] * 5,
                aliases={0: 0, 1: 1, 2: 2, 3: 3},
                micros=1.2,
            )
        if not more:
            blocks = call(
                filter_inner_kernel, blocks_shape, IN_VMEM, [total], [IN_VMEM],
                [pltpu.VMEM((width_x, width_y), F32)], micros=0.6,
            )
        e_adj, h_adj, e_fwd, edges, *pays = call(
            functools.partial(edge_kernel, step, 1),
            [field_shape] * 3 + [edges_shape] + [halo_shape] * more,
            [IN_VMEM] * (4 + more),
            [e_adj, h_adj, e_fwd, edges, coef] + arrived_adj,
            [IN_VMEM] * (5 + len(arrived_adj)),
            aliases={0: 0, 1: 1, 2: 2, 3: 3},
        )
        if more:
            arrived_adj = trade(pays)
            e_fwd, h_fwd = call(
                functools.partial(inner_kernel, step + 1, 0),
                [field_shape] * 2,
                [IN_VMEM] * 2,
                [e_fwd, h_fwd, coef, drives, forced],
                [IN_VMEM] * 5,
                aliases={0: 0, 1: 1},
                micros=1.1,
            )

    blocks, *parts = call(
        functools.partial(filter_edge_kernel, layout),
        [blocks_shape] + [on_chip(*group)] * len(layout),
        [IN_VMEM] * (1 + len(layout)),
        [blocks, total, edges, block_ids],
        [IN_VMEM] * 3 + [IN_SMEM],
        [
            pltpu.VMEM((2, width_x, width_y), F32),
            pltpu.VMEM((2, width_x + 2 * PAD, width_y), F32),
        ],
        aliases={0: 0},
    )
    got = [swap_over(part, "grp", 1) for part in parts[middle:]]
    sums = call(
        add_kernel,
        [on_chip(*group)] * middle,
        [IN_VMEM] * middle,
        list(parts[:middle]) + got,
        [IN_VMEM] * (2 * middle),
    )
    got = [swap_over(part, "grp", mask) for part, mask in zip(sums[1:], middle_masks[1:])]
    pieces = call(
        functools.partial(add_split_kernel, middle),
        [on_chip(*piece)] * far,
        [IN_VMEM] * far,
        [sums[0]] + got,
        [IN_VMEM] * middle,
    )
    got = [swap_over(part, "grp", mask) for part, mask in zip(pieces[1:], far_masks[1:])]
    scale = 3.0 / (STEPS * math.sqrt(ngrp))
    grad = call(
        functools.partial(last_kernel, scale),
        jax.ShapeDtypeStruct(piece, F32),
        IN_VMEM,
        [pieces[0]] + got,
        [IN_VMEM] * far,
    )
    finals = call(
        out_kernel,
        jax.ShapeDtypeStruct(fwd_fields.shape, F32),
        IN_HBM,
        [e_fwd, h_fwd],
        [IN_VMEM] * 2,
        [
            pltpu.VMEM((3, depth, width_x, width_y), F32),
            pltpu.SemaphoreType.DMA((6,)),
        ],
        micros=1.7,
    )
    return finals, grad.reshape(density.shape)


def solution(mesh):
    placed = (
        P("grp", None, "slab", None, None),
        P("grp", None, "slab", None, None),
        P("slab", "grp", None),
        P(),
        P(),
        P(),
        P("grp", None),
        P("grp"),
    )
    return jax.shard_map(
        per_device,
        mesh=mesh,
        in_specs=placed,
        out_specs=(P("grp", None, "slab", None, None), P("slab", "grp", None)),
        check_vma=False,
    )
```

```python
import functools
import math

import jax
import jax.numpy as jnp
from jax import lax
from jax.experimental import pallas as pl
from jax.experimental.pallas import tpu as pltpu
from jax.sharding import PartitionSpec as P

STEPS = 4
AMPLITUDE = 4.0
PAD = 8
F32 = jnp.float32
HBM_PER_MICRO = 3.0e6

VMEM = pltpu.MemorySpace.VMEM
IN_VMEM = pl.BlockSpec(memory_space=pltpu.VMEM)
IN_SMEM = pl.BlockSpec(memory_space=pltpu.SMEM)
IN_HBM = pl.BlockSpec(memory_space=pltpu.MemorySpace.HBM)


def on_chip(*shape):
    return VMEM(shape, F32)


def held(array, spec):
    if spec is IN_SMEM:
        return array
    space = VMEM if spec is IN_VMEM else pltpu.MemorySpace.HBM
    return pltpu.with_memory_space_constraint(array, space)


def call(kernel, outs, out_specs, operands, specs, scratch=(), aliases=None, micros=0.3):
    operands = [held(a, s) for a, s in zip(operands, specs)]
    return pl.pallas_call(
        kernel,
        out_shape=outs,
        in_specs=specs,
        out_specs=out_specs,
        scratch_shapes=scratch,
        input_output_aliases=aliases or {},
        compiler_params=pltpu.CompilerParams(vmem_limit_bytes=8 << 20),
        cost_estimate=pl.CostEstimate(
            flops=0, bytes_accessed=int(micros * HBM_PER_MICRO), transcendentals=0
        ),
    )(*operands)


CHUNK = 16


def chunks(rows):
    size = CHUNK if rows % CHUNK == 0 else rows
    return [(first, size) for first in range(0, rows, size)]


def next_col(value):
    column = lax.broadcasted_iota(jnp.int32, value.shape, 1)
    moved = pltpu.roll(value, value.shape[1] - 1, 1)
    return jnp.where(column == value.shape[1] - 1, 0.0, moved)


def prev_col(value):
    column = lax.broadcasted_iota(jnp.int32, value.shape, 1)
    return jnp.where(column == 0, 0.0, pltpu.roll(value, 1, 1))


def neighbours():
    slab = lax.axis_index("slab")
    return slab < lax.axis_size("slab") - 1, slab > 0


class Window:
    def __init__(self, e, h, coef=None, force=None):
        self.e, self.h, self.coef, self.force = e, h, coef, force
        self.rows = e.shape[2] - 2 * PAD
        self.depth = e.shape[1] - 1
        self.top, self.under = self.depth - 1, self.depth

    def read(self, ref, layer, first, size):
        return [ref[c, layer, pl.ds(PAD + first, size), :] for c in range(3)]

    def write(self, ref, layer, first, size, values):
        for c, value in enumerate(values):
            ref[c, layer, pl.ds(PAD + first, size), :] = value

    def put_h(self, layer, given=None, alone=False):
        for first, size in chunks(self.rows):
            rows = pl.ds(PAD + first, size)
            after = pl.ds(PAD + first + 1, size)
            ex, ey, ez = self.read(self.e, layer, first, size)
            if given is None:
                hx, hy, hz = self.read(self.h, layer, first, size)
            else:
                hx, hy, hz = (value + value for value in given(layer, first, size))
            if alone:
                rise_x, rise_y = -ex, -ey
            else:
                rise_x = self.e[0, layer + 1, rows, :] - ex
                rise_y = self.e[1, layer + 1, rows, :] - ey
            ey_after = self.e[1, layer, after, :]
            ez_after = self.e[2, layer, after, :]
            hx = hx - ((next_col(ez) - ez) - rise_y)
            hy = hy - (rise_x - (ez_after - ez))
            hz = hz - ((ey_after - ey) - (next_col(ex) - ex))
            self.write(self.h, layer, first, size, (hx, hy, hz))

    def curl_h(self, layer, lower, first, size):
        rows = pl.ds(PAD + first, size)
        before = pl.ds(PAD + first - 1, size)
        hx, hy, hz = self.read(self.h, layer, first, size)
        step_x = hx - self.h[0, lower, rows, :]
        step_y = hy - self.h[1, lower, rows, :]
        hy_before = self.h[1, layer, before, :]
        hz_before = self.h[2, layer, before, :]
        return (
            (hz - prev_col(hz)) - step_y,
            step_x - (hz - hz_before),
            (hy - hy_before) - (hx - prev_col(hx)),
        )

    def put_curl(self, curls, layer, lower):
        for first, size in chunks(self.rows):
            for c, value in enumerate(self.curl_h(layer, lower, first, size)):
                curls[c, layer, pl.ds(first, size), :] = value

    def next_e(self, layer, lower, first, size, curls=None):
        here = pl.ds(first, size)
        cell = self.coef[layer, here, :]
        if curls is None:
            curl = self.curl_h(layer, lower, first, size)
        else:
            curl = [curls[c, layer, here, :] for c in range(3)]
        ex, ey, ez = [a + cell * b for a, b in zip(self.read(self.e, layer, first, size), curl)]
        if self.force is not None:
            ez = ez + self.force(layer, here)
        return ex, ey, ez

    def put_e(self, layer, lower, curls=None, other=None, total=None, slot=None):
        for first, size in chunks(self.rows):
            news = self.next_e(layer, lower, first, size, curls)
            self.write(self.e, layer, first, size, news)
            if total is not None:
                rows = pl.ds(PAD + first, size)
                part = [a * other[c, layer, rows, :] for c, a in enumerate(news)]
                total[layer if slot is None else slot, rows, :] += part[0] + part[1] + part[2]

    def take_above(self, above):
        for first, size in chunks(self.rows):
            here, rows = pl.ds(first, size), pl.ds(PAD + first, size)
            self.h[0, self.top, rows, :] += above[1, here, :]
            self.h[1, self.top, rows, :] -= above[0, here, :]

    def take_below(self, below):
        for first, size in chunks(self.rows):
            here, rows = pl.ds(first, size), pl.ds(PAD + first, size)
            self.h[0, self.under, rows, :] = below[0, here, :] + self.e[1, 0, rows, :]
            self.h[1, self.under, rows, :] = below[1, here, :] - self.e[0, 0, rows, :]


def forcing(step, drives, forced):
    if drives is None:
        return None
    return lambda layer, here: drives[pl.ds(step, 1), :] * forced[layer, here, :]


def opening_kernel(fwd, adj, density, own, *rest):
    pays, (planes, sems) = rest[:-2], rest[-2:]
    depth, rows, width_y = fwd.shape[2:]
    top = depth - 1
    has_up, has_low = neighbours()
    held_copy = pltpu.make_async_copy(density, own, sems.at[2, 0])
    held_copy.start()

    def up(pay):
        copies = []
        for evo, given in enumerate((fwd, adj)):
            for c in range(5):
                copies.append(
                    pltpu.make_async_copy(given.at[0, c, top], planes.at[evo, c], sems.at[evo, c])
                )
        for copy in copies:
            copy.start()
        for copy in copies:
            copy.wait()
        for evo in range(2):
            for first, size in chunks(rows):
                here = pl.ds(first, size)
                ex, ey, ez, hx, hy = (planes[evo, c, here, :] for c in range(5))
                if first + size < rows:
                    ez_after = planes[evo, 2, pl.ds(first + 1, size), :]
                else:
                    row = lax.broadcasted_iota(jnp.int32, ez.shape, 0)
                    ez_after = jnp.where(row == size - 1, 0.0, pltpu.roll(ez, size - 1, 0))
                pay[evo, 0, here, :] = (hx + hx) - ((next_col(ez) - ez) + ey)
                pay[evo, 1, here, :] = (hy + hy) + (ex + (ez_after - ez))

    def down(pay):
        copies = []
        for evo, given in enumerate((fwd, adj)):
            for c in range(2):
                copies.append(
                    pltpu.make_async_copy(given.at[0, c, 0], pay.at[evo, c], sems.at[evo, c])
                )
        for copy in copies:
            copy.start()
        for copy in copies:
            copy.wait()

    if len(pays) == 2:
        up(pays[0])
        down(pays[1])
    else:
        pl.when(has_up)(lambda: up(pays[0]))
        pl.when(has_low)(lambda: down(pays[0]))
    held_copy.wait()


def prepare_kernel(
    layout, source, block_ids, material_idx, material_eps, total, edges, forced, base, place
):
    depth, rows, width_y = forced.shape
    nblock = block_ids.shape[0]
    block_rows = rows // nblock
    empty = jnp.zeros(total.shape[1:], F32)
    edges[0] = empty
    edges[1] = empty
    xcoord = lax.broadcasted_iota(jnp.int32, (rows, width_y), 0)
    ycoord = lax.broadcasted_iota(jnp.int32, (rows, width_y), 1)
    offset_x = (xcoord - source[0, 1]).astype(F32) / (rows / 4.0)
    offset_y = (ycoord - source[0, 2]).astype(F32) / (width_y / 4.0)
    profile = jnp.exp(-0.5 * (offset_x * offset_x + offset_y * offset_y))
    level = source[0, 0] - lax.axis_index("slab") * depth
    for layer in range(depth):
        total[layer] = empty
        forced[layer] = jnp.where(level == layer, 1.0, 0.0) * profile
    for block in range(nblock):
        value = jnp.full((block_rows, width_y), material_eps[material_idx[block]], F32)
        base[pl.ds(block * block_rows, block_rows), :] = value
    me = lax.axis_index("grp")
    block = lax.broadcasted_iota(jnp.int32, (nblock, width_y), 0)
    for slot, mask in enumerate(mask for masks in layout for mask in masks):
        place[slot] = jnp.where(block == block_ids[me ^ mask], 1.0, 0.0)


def first_kernel(given, near, e, h, curls):
    win = Window(e, h)
    rows, width_y = win.rows, e.shape[3]
    margin = jnp.zeros((PAD, width_y), F32)
    empty = jnp.zeros((rows + 2 * PAD, width_y), F32)
    for comp in range(3):
        e[comp, win.depth] = empty
        h[comp, win.depth] = empty

    def copy(layer):
        for comp in range(3):
            for ref in (e, h):
                ref[comp, layer, pl.ds(0, PAD), :] = margin
                ref[comp, layer, pl.ds(PAD + rows, PAD), :] = margin
            for first, size in chunks(rows):
                here = pl.ds(first, size)
                e[comp, layer, pl.ds(PAD + first, size), :] = given[0, comp, layer, here, :]

    def from_given(layer, first, size):
        return [given[0, 3 + c, layer, pl.ds(first, size), :] for c in range(3)]

    copy(0)
    copy(1)
    win.put_h(0, from_given)
    copy(2)
    win.put_h(1, from_given)

    def body(layer, carry):
        pl.when(layer + 2 < win.depth)(lambda: copy(layer + 2))
        win.put_h(layer + 1, from_given)
        win.put_curl(curls, layer, layer - 1)
        return carry

    lax.fori_loop(1, win.top, body, 0)


def take_kernel(evo, h_in, curls_in, e, below, above, h, curls):
    win = Window(e, h)
    has_up, has_low = neighbours()
    pl.when(has_up)(lambda: win.take_above(above.at[evo]))
    pl.when(has_low)(lambda: win.take_below(below.at[evo]))
    win.put_curl(curls, win.top, win.top - 1)
    win.put_curl(curls, 0, win.under)


def edge_kernel(step, evo, *refs):
    refs = list(refs)
    e_in, h_in = refs.pop(0), refs.pop(0)
    if evo == 1:
        other_in, edges_in = refs.pop(0), refs.pop(0)
    coef = refs.pop(0)
    drives, forced = (refs.pop(0), refs.pop(0)) if evo == 0 else (None, None)
    curls = refs.pop(0) if step == 0 else None
    below, above = (refs.pop(0), refs.pop(0)) if step > 0 else (None, None)
    e, h = refs.pop(0), refs.pop(0)
    other, edges = (refs.pop(0), refs.pop(0)) if evo == 1 else (None, None)
    pays = refs
    win = Window(e, h, coef, forcing(step, drives, forced))
    top = win.top
    has_up, has_low = neighbours()

    @pl.when(has_up)
    def _():
        if step > 0:
            win.take_above(above)
        win.put_e(top, top - 1, curls, other, edges, 1)
        if pays:
            win.put_h(top, alone=True)
            for c in range(2):
                pays[0][c] = h[c, top, pl.ds(PAD, win.rows), :]

    @pl.when(has_low)
    def _():
        if step > 0:
            win.take_below(below)
        win.put_e(0, win.under, curls, other, edges, 0)
        if pays:
            for c in range(2):
                pays[-1][c] = e[c, 0, pl.ds(PAD, win.rows), :]


def inner_range(top):
    has_up, has_low = neighbours()
    return jnp.where(has_low, 1, 0), jnp.where(has_up, top - 1, top)


def begin_kernel(
    e_fwd_in, e_adj_in, total_in, coef, drives, forced, curls_fwd, curls_adj,
    e_fwd, e_adj, total,
):
    fwd = Window(e_fwd, None, coef, forcing(0, drives, forced))
    adj = Window(e_adj, None, coef)
    lowest, highest = inner_range(fwd.top)

    def body(layer, carry):
        fwd.put_e(layer, None, curls_fwd)
        adj.put_e(layer, None, curls_adj, e_fwd, total)
        return carry

    lax.fori_loop(lowest, highest + 1, body, 0)


def inner_kernel(step, evo, *refs):
    refs = list(refs)
    e_in, h_in = refs.pop(0), refs.pop(0)
    if evo == 1:
        other_in, total_in = refs.pop(0), refs.pop(0)
    coef = refs.pop(0)
    drives, forced = (refs.pop(0), refs.pop(0)) if evo == 0 else (None, None)
    e, h = refs.pop(0), refs.pop(0)
    other, total = (refs.pop(0), refs.pop(0)) if evo == 1 else (None, None)
    win = Window(e, h, coef, forcing(step, drives, forced))
    lowest, highest = inner_range(win.top)
    win.put_h(0)
    pl.when(lowest == 1)(lambda: win.put_h(1))

    def body(layer, carry):
        win.put_h(layer + 1)
        win.put_e(layer, jnp.where(layer == 0, win.under, layer - 1), None, other, total)
        return carry

    lax.fori_loop(lowest, highest, body, 0)
    win.put_e(highest, highest - 1, None, other, total)


def coef_layer(layer, coef, placed, base):
    for first, size in chunks(base.shape[0]):
        here = pl.ds(first, size)
        coef[layer, here, :] = 0.25 / (base[here, :] + 3.0 * filtered(placed, first, size))


def clear_margins(placed):
    rows = placed.shape[0] - 2 * PAD
    margin = jnp.zeros((PAD, placed.shape[1]), F32)
    placed[pl.ds(0, PAD), :] = margin
    placed[pl.ds(PAD + rows, PAD), :] = margin


def coef_edge_kernel(count, *refs):
    parts, (place, base, coef, placed) = refs[:count], refs[count:]
    depth, rows, width_y = coef.shape
    nblock = place.shape[0]
    block_rows = rows // nblock
    for which, layer in enumerate((0, depth - 1)):
        there = placed.at[which]
        clear_margins(there)
        source = pl.ds(layer * block_rows, block_rows)
        pieces = [part[slot, source, :] for part in parts for slot in range(part.shape[0])]
        for block in range(nblock):
            value = None
            for slot, piece in enumerate(pieces):
                term = place[slot, pl.ds(block, 1), :] * piece
                value = term if value is None else value + term
            there[pl.ds(PAD + block * block_rows, block_rows), :] = value
    for which, layer in enumerate((0, depth - 1)):
        coef_layer(layer, coef, placed.at[which], base)


def coef_inner_kernel(layout, coef_in, *refs):
    parts, (block_ids, base, coef, blocks, placed) = refs[: len(layout)], refs[len(layout) :]
    depth, rows, width_y = coef.shape
    nblock = blocks.shape[0]
    block_rows = rows // nblock
    me = lax.axis_index("grp")
    clear_margins(placed)
    for part, masks in zip(parts, layout):
        for slot, mask in enumerate(masks):
            blocks[block_ids[me ^ mask]] = part[slot]

    def body(layer, carry):
        for block in range(nblock):
            source = pl.ds(pl.multiple_of(layer * block_rows, block_rows), block_rows)
            placed[pl.ds(PAD + block * block_rows, block_rows), :] = blocks[block, source, :]
        coef_layer(layer, coef, placed, base)
        return carry

    lax.fori_loop(1, depth - 1, body, 0)


def filtered(padded, first, size):
    here = padded[pl.ds(PAD + first, size), :]
    before = padded[pl.ds(PAD + first - 1, size), :]
    after = padded[pl.ds(PAD + first + 1, size), :]
    along = before + 2.0 * here + after
    return (prev_col(along) + 2.0 * along + next_col(along)) * 0.0625


def tie_kernel(*refs):
    pass


def tie(array, others):
    return call(
        tie_kernel, on_chip(*array.shape), IN_VMEM, [array] + others,
        [IN_VMEM] * (1 + len(others)), aliases={0: 0},
    )


def pack_kernel(*refs):
    out = refs[-1]
    for slot, ref in enumerate(refs[:-1]):
        out[slot] = ref[...]


def filter_inner_kernel(layout, total, block_ids, *rest):
    parts, (blocks, wide) = rest[:-2], rest[-2:]
    depth = total.shape[0]
    nblock = blocks.shape[0]
    rows = wide.shape[0]
    block_rows = rows // nblock
    me = lax.axis_index("grp")

    def body(layer, carry):
        for first, size in chunks(rows):
            wide[pl.ds(first, size), :] = filtered(total.at[layer], first, size)
        for block in range(nblock):
            target = pl.ds(pl.multiple_of(layer * block_rows, block_rows), block_rows)
            blocks[block, target, :] = wide[pl.ds(block * block_rows, block_rows), :]
        return carry

    lax.fori_loop(1, depth - 1, body, 0)
    inner = pl.ds(block_rows, (depth - 2) * block_rows)
    for part, masks in zip(parts, layout):
        for slot, mask in enumerate(masks):
            part[slot, inner, :] = blocks[block_ids[me ^ mask], inner, :]


def filter_edge_kernel(count, *refs):
    total, edges, place = refs[count : count + 3]
    parts, (sums, wide) = refs[count + 3 : -2], refs[-2:]
    depth = total.shape[0]
    nblock = place.shape[0]
    rows = wide.shape[1]
    block_rows = rows // nblock
    for which, layer in enumerate((0, depth - 1)):
        sums[which] = total[layer] + edges[which]
        for first, size in chunks(rows):
            wide[which, pl.ds(first, size), :] = filtered(sums.at[which], first, size)
    for which, layer in enumerate((0, depth - 1)):
        blocks = [
            wide[which, pl.ds(block * block_rows, block_rows), :] for block in range(nblock)
        ]
        target = pl.ds(layer * block_rows, block_rows)
        for slot in range(nblock):
            value = None
            for block, piece in enumerate(blocks):
                term = place[slot, pl.ds(block, 1), :] * piece
                value = term if value is None else value + term
            parts[slot // parts[0].shape[0]][slot % parts[0].shape[0], target, :] = value


def add_kernel(*refs):
    half = len(refs) // 3
    for a, b, out in zip(refs[:half], refs[half : 2 * half], refs[2 * half :]):
        out[...] = a[...] + b[...]


def add_split_kernel(count, *refs):
    terms, outs = refs[:count], refs[count:]
    for slot, out in enumerate(outs):
        value = terms[0][slot]
        for term in terms[1:]:
            value = value + term[slot]
        out[...] = value


def last_kernel(scale, *refs):
    value = refs[0][...]
    for ref in refs[1:-1]:
        value = value + ref[...]
    refs[-1][...] = value * scale


def out_kernel(e, h, finals, halves, sems):
    depth = e.shape[1] - 1
    rows = e.shape[2] - 2 * PAD
    every = pl.ds(PAD, rows)
    copies = [
        pltpu.make_async_copy(e.at[c, pl.ds(0, depth), every, :], finals.at[0, c], sems.at[c])
        for c in range(3)
    ]
    for copy in copies:
        copy.start()
    for c in range(3):

        def body(layer, carry, c=c):
            halves[c, layer] = 0.5 * h[c, layer, every, :]
            return carry

        lax.fori_loop(0, depth, body, 0)
        copy = pltpu.make_async_copy(halves.at[c], finals.at[0, 3 + c], sems.at[3 + c])
        copy.start()
        copies.append(copy)
    for copy in copies:
        copy.wait()


def swap_over(array, axis, mask):
    return lax.ppermute(array, axis, [(i, i ^ mask) for i in range(lax.axis_size(axis))])


def shift_over(array, axis, distance):
    size = lax.axis_size(axis)
    route = [(i, i + distance) for i in range(size) if 0 <= i + distance < size]
    return lax.ppermute(array, axis, route)


def trade(pays):
    if len(pays) == 1:
        return [swap_over(pays[0], "slab", 1)] * 2
    return [shift_over(pays[0], "slab", 1), shift_over(pays[1], "slab", -1)]


def per_device(
    fwd_fields, adj_fields, density, block_ids, material_idx, material_eps, source_pos, wave_idx
):
    depth, width_x, width_y = fwd_fields.shape[2:]
    nblock = block_ids.shape[0]
    block_rows = width_x // nblock
    ngrp = lax.axis_size("grp")
    npay = 1 if lax.axis_size("slab") == 2 else 2
    omega = 2.0 * math.pi / (6.0 + 2.0 * wave_idx[0].astype(F32))
    steps = lax.broadcasted_iota(jnp.int32, (STEPS, width_y), 0).astype(F32)
    drives = AMPLITUDE * jnp.sin(omega * (steps + 1.0))

    far = 4
    middle = ngrp // (2 * far)
    far_masks = [2 * middle * j for j in range(far)]
    middle_masks = [2 * j for j in range(middle)]
    layout = [
        [core + mid + top for top in far_masks] for core in (0, 1) for mid in middle_masks
    ]
    piece = (depth * block_rows, width_y)
    group = (far,) + piece

    field_shape = on_chip(3, depth + 1, width_x + 2 * PAD, width_y)
    curls_shape = on_chip(3, depth, width_x, width_y)
    halo_shape = on_chip(2, width_x, width_y)
    total_shape = on_chip(depth, width_x + 2 * PAD, width_y)
    edges_shape = on_chip(2, width_x + 2 * PAD, width_y)
    coef_shape = on_chip(depth, width_x, width_y)
    plane = on_chip(width_x, width_y)
    padded = pltpu.VMEM((width_x + 2 * PAD, width_y), F32)

    design = density.reshape(piece)
    got = [swap_over(design, "grp", mask) for mask in far_masks[1:]]
    own, *pays = call(
        opening_kernel,
        [on_chip(*piece)] + [on_chip(2, 2, width_x, width_y)] * npay,
        [IN_VMEM] * (1 + npay),
        [fwd_fields, adj_fields, design],
        [IN_HBM] * 3,
        [pltpu.VMEM((2, 5, width_x, width_y), F32), pltpu.SemaphoreType.DMA((3, 5))],
    )
    below, above = trade(pays)

    near = call(pack_kernel, on_chip(*group), IN_VMEM, [own] + got, [IN_VMEM] * far)
    others = [swap_over(near, "grp", mask) for mask in middle_masks[1:]]
    near_across = swap_over(near, "grp", 1)

    place_shape = on_chip(nblock, nblock, width_y)
    total, edges, forced, base, place = call(
        functools.partial(prepare_kernel, layout),
        [total_shape, edges_shape, on_chip(depth, width_x, width_y), plane, place_shape],
        [IN_VMEM] * 5,
        [source_pos, block_ids, material_idx, material_eps],
        [IN_SMEM] * 4,
    )
    fields = []
    for evo, given in enumerate((fwd_fields, adj_fields)):
        e, h, curls = call(
            first_kernel,
            [field_shape, field_shape, curls_shape],
            [IN_VMEM] * 3,
            [given, near],
            [IN_VMEM, IN_VMEM],
            micros=1.5,
        )
        fields.append((e, h, curls))
    others = [tie(part, [forced] + [e for e, _, _ in fields]) for part in others]
    parts = [near] + others + [near_across] + [swap_over(part, "grp", 1) for part in others]

    taken = []
    for evo, (e, h, curls) in enumerate(fields):
        h, curls = call(
            functools.partial(take_kernel, evo),
            [field_shape, curls_shape],
            [IN_VMEM] * 2,
            [h, curls, e, below, above],
            [IN_VMEM] * 5,
            aliases={0: 0, 1: 1},
        )
        taken.append((e, h, curls))
    (e_fwd, h_fwd, curls_fwd), (e_adj, h_adj, curls_adj) = taken
    coef = call(
        functools.partial(coef_edge_kernel, len(parts)),
        coef_shape,
        IN_VMEM,
        parts + [place, base],
        [IN_VMEM] * (len(parts) + 2),
        [pltpu.VMEM((2, width_x + 2 * PAD, width_y), F32)],
    )

    arrived_fwd, arrived_adj = [curls_fwd], [curls_adj]
    for step in range(STEPS):
        more = npay if step < STEPS - 1 else 0
        e_fwd, h_fwd, *pays = call(
            functools.partial(edge_kernel, step, 0),
            [field_shape] * 2 + [halo_shape] * more,
            [IN_VMEM] * (2 + more),
            [e_fwd, h_fwd, coef, drives, forced] + arrived_fwd,
            [IN_VMEM] * (5 + len(arrived_fwd)),
            aliases={0: 0, 1: 1},
        )
        if more:
            arrived_fwd = trade(pays)
        if step == 0:
            coef = call(
                functools.partial(coef_inner_kernel, layout),
                coef_shape,
                IN_VMEM,
                [coef] + parts + [block_ids, base],
                [IN_VMEM] * (1 + len(parts)) + [IN_SMEM, IN_VMEM],
                [pltpu.VMEM((nblock,) + piece, F32), padded],
                aliases={0: 0},
                micros=0.9,
            )
            e_fwd, e_adj, total = call(
                begin_kernel,
                [field_shape, field_shape, total_shape],
                [IN_VMEM] * 3,
                [e_fwd, e_adj, total, coef, drives, forced, curls_fwd, curls_adj],
                [IN_VMEM] * 8,
                aliases={0: 0, 1: 1, 2: 2},
                micros=0.7,
            )
        else:
            e_adj, h_adj, e_fwd, total = call(
                functools.partial(inner_kernel, step, 1),
                [field_shape] * 3 + [total_shape],
                [IN_VMEM] * 4,
                [e_adj, h_adj, e_fwd, total, coef],
                [IN_VMEM] * 5,
                aliases={0: 0, 1: 1, 2: 2, 3: 3},
                micros=1.2,
            )
        if not more:
            parts = call(
                functools.partial(filter_inner_kernel, layout),
                [on_chip(*group)] * len(layout),
                [IN_VMEM] * len(layout),
                [total, block_ids],
                [IN_VMEM, IN_SMEM],
                [pltpu.VMEM((nblock,) + piece, F32), pltpu.VMEM((width_x, width_y), F32)],
                micros=1.1,
            )
        e_adj, h_adj, e_fwd, edges, *pays = call(
            functools.partial(edge_kernel, step, 1),
            [field_shape] * 3 + [edges_shape] + [halo_shape] * more,
            [IN_VMEM] * (4 + more),
            [e_adj, h_adj, e_fwd, edges, coef] + arrived_adj,
            [IN_VMEM] * (5 + len(arrived_adj)),
            aliases={0: 0, 1: 1, 2: 2, 3: 3},
        )
        if more:
            arrived_adj = trade(pays)
            e_fwd, h_fwd = call(
                functools.partial(inner_kernel, step + 1, 0),
                [field_shape] * 2,
                [IN_VMEM] * 2,
                [e_fwd, h_fwd, coef, drives, forced],
                [IN_VMEM] * 5,
                aliases={0: 0, 1: 1},
                micros=1.1,
            )

    parts = call(
        functools.partial(filter_edge_kernel, len(layout)),
        [on_chip(*group)] * len(layout),
        [IN_VMEM] * len(layout),
        list(parts) + [total, edges, place],
        [IN_VMEM] * (len(layout) + 3),
        [
            pltpu.VMEM((2, width_x + 2 * PAD, width_y), F32),
            pltpu.VMEM((2, width_x, width_y), F32),
        ],
        aliases={slot: slot for slot in range(len(layout))},
    )
    got = [swap_over(part, "grp", 1) for part in parts[middle:]]
    sums = call(
        add_kernel,
        [on_chip(*group)] * middle,
        [IN_VMEM] * middle,
        list(parts[:middle]) + got,
        [IN_VMEM] * (2 * middle),
    )
    got = [swap_over(part, "grp", mask) for part, mask in zip(sums[1:], middle_masks[1:])]
    pieces = call(
        functools.partial(add_split_kernel, middle),
        [on_chip(*piece)] * far,
        [IN_VMEM] * far,
        [sums[0]] + got,
        [IN_VMEM] * middle,
    )
    got = [swap_over(part, "grp", mask) for part, mask in zip(pieces[1:], far_masks[1:])]
    scale = 3.0 / (STEPS * math.sqrt(ngrp))
    grad = call(
        functools.partial(last_kernel, scale),
        jax.ShapeDtypeStruct(piece, F32),
        IN_VMEM,
        [pieces[0]] + got,
        [IN_VMEM] * far,
    )
    finals = call(
        out_kernel,
        jax.ShapeDtypeStruct(fwd_fields.shape, F32),
        IN_HBM,
        [e_fwd, h_fwd],
        [IN_VMEM] * 2,
        [
            pltpu.VMEM((3, depth, width_x, width_y), F32),
            pltpu.SemaphoreType.DMA((6,)),
        ],
        micros=1.7,
    )
    return finals, grad.reshape(density.shape)


def solution(mesh):
    placed = (
        P("grp", None, "slab", None, None),
        P("grp", None, "slab", None, None),
        P("slab", "grp", None),
        P(),
        P(),
        P(),
        P("grp", None),
        P("grp"),
    )
    return jax.shard_map(
        per_device,
        mesh=mesh,
        in_specs=placed,
        out_specs=(P("grp", None, "slab", None, None), P("slab", "grp", None)),
        check_vma=False,
    )
```

```python
import functools
import math

import jax
import jax.numpy as jnp
from jax import lax
from jax.experimental import pallas as pl
from jax.experimental.pallas import tpu as pltpu
from jax.sharding import PartitionSpec as P

STEPS = 4
AMPLITUDE = 4.0
PAD = 8
F32 = jnp.float32
HBM_PER_MICRO = 3.0e6

VMEM = pltpu.MemorySpace.VMEM
IN_VMEM = pl.BlockSpec(memory_space=pltpu.VMEM)
IN_SMEM = pl.BlockSpec(memory_space=pltpu.SMEM)
IN_HBM = pl.BlockSpec(memory_space=pltpu.MemorySpace.HBM)


def on_chip(*shape):
    return VMEM(shape, F32)


def held(array, spec):
    if spec is IN_SMEM:
        return array
    space = VMEM if spec is IN_VMEM else pltpu.MemorySpace.HBM
    return pltpu.with_memory_space_constraint(array, space)


def call(kernel, outs, out_specs, operands, specs, scratch=(), aliases=None, micros=0.3):
    operands = [held(a, s) for a, s in zip(operands, specs)]
    return pl.pallas_call(
        kernel,
        out_shape=outs,
        in_specs=specs,
        out_specs=out_specs,
        scratch_shapes=scratch,
        input_output_aliases=aliases or {},
        compiler_params=pltpu.CompilerParams(vmem_limit_bytes=8 << 20),
        cost_estimate=pl.CostEstimate(
            flops=0, bytes_accessed=int(micros * HBM_PER_MICRO), transcendentals=0
        ),
    )(*operands)


CHUNK = 16


def chunks(rows):
    size = CHUNK if rows % CHUNK == 0 else rows
    return [(first, size) for first in range(0, rows, size)]


def next_col(value):
    column = lax.broadcasted_iota(jnp.int32, value.shape, 1)
    moved = pltpu.roll(value, value.shape[1] - 1, 1)
    return jnp.where(column == value.shape[1] - 1, 0.0, moved)


def prev_col(value):
    column = lax.broadcasted_iota(jnp.int32, value.shape, 1)
    return jnp.where(column == 0, 0.0, pltpu.roll(value, 1, 1))


def neighbours():
    slab = lax.axis_index("slab")
    return slab < lax.axis_size("slab") - 1, slab > 0


class Window:
    def __init__(self, e, h, coef=None, force=None):
        self.e, self.h, self.coef, self.force = e, h, coef, force
        self.rows = e.shape[2] - 2 * PAD
        self.depth = e.shape[1] - 1
        self.top, self.under = self.depth - 1, self.depth

    def read(self, ref, layer, first, size):
        return [ref[c, layer, pl.ds(PAD + first, size), :] for c in range(3)]

    def write(self, ref, layer, first, size, values):
        for c, value in enumerate(values):
            ref[c, layer, pl.ds(PAD + first, size), :] = value

    def put_h(self, layer, given=None, alone=False):
        for first, size in chunks(self.rows):
            rows = pl.ds(PAD + first, size)
            after = pl.ds(PAD + first + 1, size)
            ex, ey, ez = self.read(self.e, layer, first, size)
            if given is None:
                hx, hy, hz = self.read(self.h, layer, first, size)
            else:
                hx, hy, hz = (value + value for value in given(layer, first, size))
            if alone:
                rise_x, rise_y = -ex, -ey
            else:
                rise_x = self.e[0, layer + 1, rows, :] - ex
                rise_y = self.e[1, layer + 1, rows, :] - ey
            ey_after = self.e[1, layer, after, :]
            ez_after = self.e[2, layer, after, :]
            hx = hx - ((next_col(ez) - ez) - rise_y)
            hy = hy - (rise_x - (ez_after - ez))
            hz = hz - ((ey_after - ey) - (next_col(ex) - ex))
            self.write(self.h, layer, first, size, (hx, hy, hz))

    def curl_h(self, layer, lower, first, size):
        rows = pl.ds(PAD + first, size)
        before = pl.ds(PAD + first - 1, size)
        hx, hy, hz = self.read(self.h, layer, first, size)
        step_x = hx - self.h[0, lower, rows, :]
        step_y = hy - self.h[1, lower, rows, :]
        hy_before = self.h[1, layer, before, :]
        hz_before = self.h[2, layer, before, :]
        return (
            (hz - prev_col(hz)) - step_y,
            step_x - (hz - hz_before),
            (hy - hy_before) - (hx - prev_col(hx)),
        )

    def put_curl(self, curls, layer, lower):
        for first, size in chunks(self.rows):
            for c, value in enumerate(self.curl_h(layer, lower, first, size)):
                curls[c, layer, pl.ds(first, size), :] = value

    def next_e(self, layer, lower, first, size, curls=None):
        here = pl.ds(first, size)
        cell = self.coef[layer, here, :]
        if curls is None:
            curl = self.curl_h(layer, lower, first, size)
        else:
            curl = [curls[c, layer, here, :] for c in range(3)]
        ex, ey, ez = [a + cell * b for a, b in zip(self.read(self.e, layer, first, size), curl)]
        if self.force is not None:
            ez = ez + self.force(layer, here)
        return ex, ey, ez

    def put_e(self, layer, lower, curls=None, other=None, total=None, slot=None):
        for first, size in chunks(self.rows):
            news = self.next_e(layer, lower, first, size, curls)
            self.write(self.e, layer, first, size, news)
            if total is not None:
                rows = pl.ds(PAD + first, size)
                part = [a * other[c, layer, rows, :] for c, a in enumerate(news)]
                total[layer if slot is None else slot, rows, :] += part[0] + part[1] + part[2]

    def take_above(self, above):
        for first, size in chunks(self.rows):
            here, rows = pl.ds(first, size), pl.ds(PAD + first, size)
            self.h[0, self.top, rows, :] += above[1, here, :]
            self.h[1, self.top, rows, :] -= above[0, here, :]

    def take_below(self, below):
        for first, size in chunks(self.rows):
            here, rows = pl.ds(first, size), pl.ds(PAD + first, size)
            self.h[0, self.under, rows, :] = below[0, here, :] + self.e[1, 0, rows, :]
            self.h[1, self.under, rows, :] = below[1, here, :] - self.e[0, 0, rows, :]


def forcing(step, drives, forced):
    if drives is None:
        return None
    return lambda layer, here: drives[pl.ds(step, 1), :] * forced[layer, here, :]


def opening_kernel(fwd, adj, density, own, *rest):
    pays, (planes, sems) = rest[:-2], rest[-2:]
    depth, rows, width_y = fwd.shape[2:]
    top = depth - 1
    has_up, has_low = neighbours()
    held_copy = pltpu.make_async_copy(density, own, sems.at[2, 0])
    held_copy.start()

    def up(pay):
        copies = []
        for evo, given in enumerate((fwd, adj)):
            for c in range(5):
                copies.append(
                    pltpu.make_async_copy(given.at[0, c, top], planes.at[evo, c], sems.at[evo, c])
                )
        for copy in copies:
            copy.start()
        for copy in copies:
            copy.wait()
        for evo in range(2):
            for first, size in chunks(rows):
                here = pl.ds(first, size)
                ex, ey, ez, hx, hy = (planes[evo, c, here, :] for c in range(5))
                if first + size < rows:
                    ez_after = planes[evo, 2, pl.ds(first + 1, size), :]
                else:
                    row = lax.broadcasted_iota(jnp.int32, ez.shape, 0)
                    ez_after = jnp.where(row == size - 1, 0.0, pltpu.roll(ez, size - 1, 0))
                pay[evo, 0, here, :] = (hx + hx) - ((next_col(ez) - ez) + ey)
                pay[evo, 1, here, :] = (hy + hy) + (ex + (ez_after - ez))

    def down(pay):
        copies = []
        for evo, given in enumerate((fwd, adj)):
            for c in range(2):
                copies.append(
                    pltpu.make_async_copy(given.at[0, c, 0], pay.at[evo, c], sems.at[evo, c])
                )
        for copy in copies:
            copy.start()
        for copy in copies:
            copy.wait()

    if len(pays) == 2:
        up(pays[0])
        down(pays[1])
    else:
        pl.when(has_up)(lambda: up(pays[0]))
        pl.when(has_low)(lambda: down(pays[0]))
    held_copy.wait()


def prepare_kernel(
    layout, source, wave_idx, block_ids, material_idx, material_eps,
    total, edges, forced, drives, base, place,
):
    depth, rows, width_y = forced.shape
    nblock = block_ids.shape[0]
    block_rows = rows // nblock
    empty = jnp.zeros(total.shape[1:], F32)
    edges[0] = empty
    edges[1] = empty
    xcoord = lax.broadcasted_iota(jnp.int32, (rows, width_y), 0)
    ycoord = lax.broadcasted_iota(jnp.int32, (rows, width_y), 1)
    offset_x = (xcoord - source[0, 1]).astype(F32) / (rows / 4.0)
    offset_y = (ycoord - source[0, 2]).astype(F32) / (width_y / 4.0)
    profile = jnp.exp(-0.5 * (offset_x * offset_x + offset_y * offset_y))
    step = lax.broadcasted_iota(jnp.int32, drives.shape, 0).astype(F32) + 1.0
    wave = jnp.full(drives.shape, wave_idx[0], jnp.int32).astype(F32)
    drives[...] = AMPLITUDE * jnp.sin(2.0 * math.pi / (6.0 + 2.0 * wave) * step)
    level = source[0, 0] - lax.axis_index("slab") * depth
    for layer in range(depth):
        total[layer] = empty
        forced[layer] = jnp.where(level == layer, 1.0, 0.0) * profile
    for block in range(nblock):
        value = jnp.full((block_rows, width_y), material_eps[material_idx[block]], F32)
        base[pl.ds(block * block_rows, block_rows), :] = value
    me = lax.axis_index("grp")
    block = lax.broadcasted_iota(jnp.int32, (nblock, width_y), 0)
    for slot, mask in enumerate(mask for masks in layout for mask in masks):
        place[slot] = jnp.where(block == block_ids[me ^ mask], 1.0, 0.0)


def first_kernel(given, near, e, h, curls):
    win = Window(e, h)
    rows, width_y = win.rows, e.shape[3]
    margin = jnp.zeros((PAD, width_y), F32)
    empty = jnp.zeros((rows + 2 * PAD, width_y), F32)
    for comp in range(3):
        e[comp, win.depth] = empty
        h[comp, win.depth] = empty

    def copy(layer):
        for comp in range(3):
            for ref in (e, h):
                ref[comp, layer, pl.ds(0, PAD), :] = margin
                ref[comp, layer, pl.ds(PAD + rows, PAD), :] = margin
            for first, size in chunks(rows):
                here = pl.ds(first, size)
                e[comp, layer, pl.ds(PAD + first, size), :] = given[0, comp, layer, here, :]

    def from_given(layer, first, size):
        return [given[0, 3 + c, layer, pl.ds(first, size), :] for c in range(3)]

    copy(0)
    copy(1)
    win.put_h(0, from_given)
    copy(2)
    win.put_h(1, from_given)

    def body(layer, carry):
        pl.when(layer + 2 < win.depth)(lambda: copy(layer + 2))
        win.put_h(layer + 1, from_given)
        win.put_curl(curls, layer, layer - 1)
        return carry

    lax.fori_loop(1, win.top, body, 0)


def take_kernel(evo, h_in, curls_in, e, below, above, h, curls):
    win = Window(e, h)
    has_up, has_low = neighbours()
    pl.when(has_up)(lambda: win.take_above(above.at[evo]))
    pl.when(has_low)(lambda: win.take_below(below.at[evo]))
    win.put_curl(curls, win.top, win.top - 1)
    win.put_curl(curls, 0, win.under)


def edge_kernel(step, evo, *refs):
    refs = list(refs)
    e_in, h_in = refs.pop(0), refs.pop(0)
    if evo == 1:
        other_in, edges_in = refs.pop(0), refs.pop(0)
    coef = refs.pop(0)
    drives, forced = (refs.pop(0), refs.pop(0)) if evo == 0 else (None, None)
    curls = refs.pop(0) if step == 0 else None
    below, above = (refs.pop(0), refs.pop(0)) if step > 0 else (None, None)
    e, h = refs.pop(0), refs.pop(0)
    other, edges = (refs.pop(0), refs.pop(0)) if evo == 1 else (None, None)
    pays = refs
    win = Window(e, h, coef, forcing(step, drives, forced))
    top = win.top
    has_up, has_low = neighbours()

    @pl.when(has_up)
    def _():
        if step > 0:
            win.take_above(above)
        win.put_e(top, top - 1, curls, other, edges, 1)
        if pays:
            win.put_h(top, alone=True)
            for c in range(2):
                pays[0][c] = h[c, top, pl.ds(PAD, win.rows), :]

    @pl.when(has_low)
    def _():
        if step > 0:
            win.take_below(below)
        win.put_e(0, win.under, curls, other, edges, 0)
        if pays:
            for c in range(2):
                pays[-1][c] = e[c, 0, pl.ds(PAD, win.rows), :]


def inner_range(top):
    has_up, has_low = neighbours()
    return jnp.where(has_low, 1, 0), jnp.where(has_up, top - 1, top)


def begin_kernel(
    e_fwd_in, e_adj_in, total_in, coef, drives, forced, curls_fwd, curls_adj,
    e_fwd, e_adj, total,
):
    fwd = Window(e_fwd, None, coef, forcing(0, drives, forced))
    adj = Window(e_adj, None, coef)
    lowest, highest = inner_range(fwd.top)

    def body(layer, carry):
        fwd.put_e(layer, None, curls_fwd)
        adj.put_e(layer, None, curls_adj, e_fwd, total)
        return carry

    lax.fori_loop(lowest, highest + 1, body, 0)


def inner_kernel(step, evo, *refs):
    refs = list(refs)
    e_in, h_in = refs.pop(0), refs.pop(0)
    if evo == 1:
        other_in, total_in = refs.pop(0), refs.pop(0)
    coef = refs.pop(0)
    drives, forced = (refs.pop(0), refs.pop(0)) if evo == 0 else (None, None)
    e, h = refs.pop(0), refs.pop(0)
    other, total = (refs.pop(0), refs.pop(0)) if evo == 1 else (None, None)
    win = Window(e, h, coef, forcing(step, drives, forced))
    lowest, highest = inner_range(win.top)
    win.put_h(0)
    pl.when(lowest == 1)(lambda: win.put_h(1))

    def body(layer, carry):
        win.put_h(layer + 1)
        win.put_e(layer, jnp.where(layer == 0, win.under, layer - 1), None, other, total)
        return carry

    if lax.axis_size("slab") == 2:
        lax.fori_loop(0, win.depth - 2, lambda i, carry: body(lowest + i, carry), 0, unroll=2)
    else:
        lax.fori_loop(lowest, highest, body, 0)
    win.put_e(highest, highest - 1, None, other, total)


def coef_layer(layer, coef, placed, base):
    for first, size in chunks(base.shape[0]):
        here = pl.ds(first, size)
        coef[layer, here, :] = 0.25 / (base[here, :] + 3.0 * filtered(placed, first, size))


def clear_margins(placed):
    rows = placed.shape[0] - 2 * PAD
    margin = jnp.zeros((PAD, placed.shape[1]), F32)
    placed[pl.ds(0, PAD), :] = margin
    placed[pl.ds(PAD + rows, PAD), :] = margin


def scatter_kernel(layout, *refs):
    parts, (block_ids, blocks) = refs[: len(layout)], refs[len(layout) :]
    me = lax.axis_index("grp")
    nothing = jnp.zeros(blocks.shape[1:], F32)
    for block in range(blocks.shape[0]):
        blocks[block] = nothing
    for part, masks in zip(parts, layout):
        for slot, mask in enumerate(masks):
            blocks[block_ids[me ^ mask]] = part[slot]


def place_layer(layer, first_slot, parts, place, blocks, placed):
    nblock = blocks.shape[0]
    block_rows = (placed.shape[0] - 2 * PAD) // nblock
    clear_margins(placed)
    start = layer * block_rows
    source = pl.ds(start if isinstance(layer, int) else pl.multiple_of(start, block_rows), block_rows)
    pieces = [part[slot, source, :] for part in parts for slot in range(part.shape[0])]
    for block in range(nblock):
        value = blocks[block, source, :]
        for slot, piece in enumerate(pieces):
            value = value + place[first_slot + slot, pl.ds(block, 1), :] * piece
        placed[pl.ds(PAD + block * block_rows, block_rows), :] = value


def coef_edge_kernel(first_slot, count, *refs):
    parts, (place, base, blocks, coef, placed) = refs[:count], refs[count:]
    edge_layers = (0, coef.shape[0] - 1)
    for which, layer in enumerate(edge_layers):
        place_layer(layer, first_slot, parts, place, blocks, placed.at[which])
    for which, layer in enumerate(edge_layers):
        coef_layer(layer, coef, placed.at[which], base)


def coef_inner_kernel(first_slot, count, coef_in, *refs):
    parts, (place, base, blocks, coef, placed) = refs[:count], refs[count:]

    def body(layer, carry):
        there = placed.at[lax.rem(layer, 2)]
        place_layer(layer, first_slot, parts, place, blocks, there)
        coef_layer(layer, coef, there, base)
        return carry

    lax.fori_loop(1, coef.shape[0] - 1, body, 0, unroll=2)


def filtered(padded, first, size):
    here = padded[pl.ds(PAD + first, size), :]
    before = padded[pl.ds(PAD + first - 1, size), :]
    after = padded[pl.ds(PAD + first + 1, size), :]
    along = before + 2.0 * here + after
    return (prev_col(along) + 2.0 * along + next_col(along)) * 0.0625


def tie_kernel(*refs):
    pass


def tie(array, others):
    return call(
        tie_kernel, on_chip(*array.shape), IN_VMEM, [array] + others,
        [IN_VMEM] * (1 + len(others)), aliases={0: 0},
    )


def pack_kernel(*refs):
    out = refs[-1]
    for slot, ref in enumerate(refs[:-1]):
        out[slot] = ref[...]


def filter_inner_kernel(layout, total, block_ids_far, *rest):
    parts, (blocks, wide, block_ids, sem) = rest[:-4], rest[-4:]
    fetch = pltpu.make_async_copy(block_ids_far, block_ids, sem)
    fetch.start()
    depth = total.shape[0]
    nblock = blocks.shape[0]
    rows = wide.shape[1]
    block_rows = rows // nblock
    me = lax.axis_index("grp")

    def body(layer, carry):
        there = wide.at[lax.rem(layer, 2)]
        for first, size in chunks(rows):
            there[pl.ds(first, size), :] = filtered(total.at[layer], first, size)
        for block in range(nblock):
            target = pl.ds(pl.multiple_of(layer * block_rows, block_rows), block_rows)
            blocks[block, target, :] = there[pl.ds(block * block_rows, block_rows), :]
        return carry

    lax.fori_loop(1, depth - 1, body, 0, unroll=2)
    fetch.wait()
    inner = pl.ds(block_rows, (depth - 2) * block_rows)
    for part, masks in zip(parts, layout):
        for slot, mask in enumerate(masks):
            part[slot, inner, :] = blocks[block_ids[me ^ mask], inner, :]


def filter_edge_kernel(count, *refs):
    total, edges, place = refs[count : count + 3]
    parts, (sums, wide) = refs[count + 3 : -2], refs[-2:]
    depth = total.shape[0]
    nblock = place.shape[0]
    rows = wide.shape[1]
    block_rows = rows // nblock
    for which, layer in enumerate((0, depth - 1)):
        sums[which] = total[layer] + edges[which]
        for first, size in chunks(rows):
            wide[which, pl.ds(first, size), :] = filtered(sums.at[which], first, size)
    for which, layer in enumerate((0, depth - 1)):
        blocks = [
            wide[which, pl.ds(block * block_rows, block_rows), :] for block in range(nblock)
        ]
        target = pl.ds(layer * block_rows, block_rows)
        for slot in range(nblock):
            value = None
            for block, piece in enumerate(blocks):
                term = place[slot, pl.ds(block, 1), :] * piece
                value = term if value is None else value + term
            parts[slot // parts[0].shape[0]][slot % parts[0].shape[0], target, :] = value


def add_kernel(*refs):
    half = len(refs) // 3
    for a, b, out in zip(refs[:half], refs[half : 2 * half], refs[2 * half :]):
        out[...] = a[...] + b[...]


def add_split_kernel(count, *refs):
    terms, outs = refs[:count], refs[count:]
    for slot, out in enumerate(outs):
        value = terms[0][slot]
        for term in terms[1:]:
            value = value + term[slot]
        out[...] = value


def last_kernel(scale, *refs):
    value = refs[0][...]
    for ref in refs[1:-1]:
        value = value + ref[...]
    refs[-1][...] = value * scale


def out_kernel(e, h, finals, halves, sems):
    depth = e.shape[1] - 1
    rows = e.shape[2] - 2 * PAD
    every = pl.ds(PAD, rows)
    copies = [
        pltpu.make_async_copy(e.at[c, pl.ds(0, depth), every, :], finals.at[0, c], sems.at[c])
        for c in range(3)
    ]
    for copy in copies:
        copy.start()
    for c in range(3):

        def body(layer, carry, c=c):
            halves[c, layer] = 0.5 * h[c, layer, every, :]
            return carry

        lax.fori_loop(0, depth, body, 0)
        copy = pltpu.make_async_copy(halves.at[c], finals.at[0, 3 + c], sems.at[3 + c])
        copy.start()
        copies.append(copy)
    for copy in copies:
        copy.wait()


def swap_over(array, axis, mask):
    return lax.ppermute(array, axis, [(i, i ^ mask) for i in range(lax.axis_size(axis))])


def shift_over(array, axis, distance):
    size = lax.axis_size(axis)
    route = [(i, i + distance) for i in range(size) if 0 <= i + distance < size]
    return lax.ppermute(array, axis, route)


def trade(pays):
    if len(pays) == 1:
        return [swap_over(pays[0], "slab", 1)] * 2
    return [shift_over(pays[0], "slab", 1), shift_over(pays[1], "slab", -1)]


def per_device(
    fwd_fields, adj_fields, density, block_ids, material_idx, material_eps, source_pos, wave_idx
):
    depth, width_x, width_y = fwd_fields.shape[2:]
    nblock = block_ids.shape[0]
    block_rows = width_x // nblock
    ngrp = lax.axis_size("grp")
    npay = 1 if lax.axis_size("slab") == 2 else 2

    far = 4
    middle = ngrp // (2 * far)
    far_masks = [2 * middle * j for j in range(far)]
    middle_masks = [2 * j for j in range(middle)]
    layout = [
        [core + mid + top for top in far_masks] for core in (0, 1) for mid in middle_masks
    ]
    piece = (depth * block_rows, width_y)
    group = (far,) + piece

    field_shape = on_chip(3, depth + 1, width_x + 2 * PAD, width_y)
    curls_shape = on_chip(3, depth, width_x, width_y)
    halo_shape = on_chip(2, width_x, width_y)
    total_shape = on_chip(depth, width_x + 2 * PAD, width_y)
    edges_shape = on_chip(2, width_x + 2 * PAD, width_y)
    coef_shape = on_chip(depth, width_x, width_y)
    plane = on_chip(width_x, width_y)

    design = density.reshape(piece)
    got = [swap_over(design, "grp", mask) for mask in far_masks[1:]]
    own, *pays = call(
        opening_kernel,
        [on_chip(*piece)] + [on_chip(2, 2, width_x, width_y)] * npay,
        [IN_VMEM] * (1 + npay),
        [fwd_fields, adj_fields, design],
        [IN_HBM] * 3,
        [pltpu.VMEM((2, 5, width_x, width_y), F32), pltpu.SemaphoreType.DMA((3, 5))],
    )
    below, above = trade(pays)

    near = call(pack_kernel, on_chip(*group), IN_VMEM, [own] + got, [IN_VMEM] * far)
    others = [swap_over(near, "grp", mask) for mask in middle_masks[1:]]
    near_across = swap_over(near, "grp", 1)

    place_shape = on_chip(nblock, nblock, width_y)
    total, edges, forced, drives, base, place = call(
        functools.partial(prepare_kernel, layout),
        [
            total_shape,
            edges_shape,
            on_chip(depth, width_x, width_y),
            on_chip(STEPS, width_y),
            plane,
            place_shape,
        ],
        [IN_VMEM] * 6,
        [source_pos, wave_idx, block_ids, material_idx, material_eps],
        [IN_SMEM] * 5,
    )
    fields = []
    for evo, given in enumerate((fwd_fields, adj_fields)):
        e, h, curls = call(
            first_kernel,
            [field_shape, field_shape, curls_shape],
            [IN_VMEM] * 3,
            [given, near],
            [IN_VMEM, IN_VMEM],
            micros=1.5,
        )
        fields.append((e, h, curls))
    others = [tie(part, [forced] + [e for e, _, _ in fields]) for part in others]
    early = [near] + others + [near_across]
    last = [swap_over(part, "grp", 1) for part in others]
    blocks = call(
        functools.partial(scatter_kernel, layout[: len(early)]),
        on_chip(nblock, *piece),
        IN_VMEM,
        early + [block_ids],
        [IN_VMEM] * len(early) + [IN_SMEM],
        micros=0.7,
    )
    first_slot = far * len(early)

    taken = []
    for evo, (e, h, curls) in enumerate(fields):
        h, curls = call(
            functools.partial(take_kernel, evo),
            [field_shape, curls_shape],
            [IN_VMEM] * 2,
            [h, curls, e, below, above],
            [IN_VMEM] * 5,
            aliases={0: 0, 1: 1},
        )
        taken.append((e, h, curls))
    (e_fwd, h_fwd, curls_fwd), (e_adj, h_adj, curls_adj) = taken
    placed = pltpu.VMEM((2, width_x + 2 * PAD, width_y), F32)
    coef = call(
        functools.partial(coef_edge_kernel, first_slot, len(last)),
        coef_shape,
        IN_VMEM,
        last + [place, base, blocks],
        [IN_VMEM] * (len(last) + 3),
        [placed],
    )

    arrived_fwd, arrived_adj = [curls_fwd], [curls_adj]
    for step in range(STEPS):
        more = npay if step < STEPS - 1 else 0
        e_fwd, h_fwd, *pays = call(
            functools.partial(edge_kernel, step, 0),
            [field_shape] * 2 + [halo_shape] * more,
            [IN_VMEM] * (2 + more),
            [e_fwd, h_fwd, coef, drives, forced] + arrived_fwd,
            [IN_VMEM] * (5 + len(arrived_fwd)),
            aliases={0: 0, 1: 1},
        )
        if more:
            arrived_fwd = trade(pays)
        if step == 0:
            coef = call(
                functools.partial(coef_inner_kernel, first_slot, len(last)),
                coef_shape,
                IN_VMEM,
                [coef] + last + [place, base, blocks],
                [IN_VMEM] * (len(last) + 4),
                [placed],
                aliases={0: 0},
                micros=0.9,
            )
            e_fwd, e_adj, total = call(
                begin_kernel,
                [field_shape, field_shape, total_shape],
                [IN_VMEM] * 3,
                [e_fwd, e_adj, total, coef, drives, forced, curls_fwd, curls_adj],
                [IN_VMEM] * 8,
                aliases={0: 0, 1: 1, 2: 2},
                micros=0.7,
            )
        else:
            e_adj, h_adj, e_fwd, total = call(
                functools.partial(inner_kernel, step, 1),
                [field_shape] * 3 + [total_shape],
                [IN_VMEM] * 4,
                [e_adj, h_adj, e_fwd, total, coef],
                [IN_VMEM] * 5,
                aliases={0: 0, 1: 1, 2: 2, 3: 3},
                micros=1.2,
            )
        if not more:
            parts = call(
                functools.partial(filter_inner_kernel, layout),
                [on_chip(*group)] * len(layout),
                [IN_VMEM] * len(layout),
                [total, block_ids],
                [IN_VMEM, IN_HBM],
                [
                    pltpu.VMEM((nblock,) + piece, F32),
                    pltpu.VMEM((2, width_x, width_y), F32),
                    pltpu.SMEM(block_ids.shape, jnp.int32),
                    pltpu.SemaphoreType.DMA,
                ],
                micros=0.8,
            )
        e_adj, h_adj, e_fwd, edges, *pays = call(
            functools.partial(edge_kernel, step, 1),
            [field_shape] * 3 + [edges_shape] + [halo_shape] * more,
            [IN_VMEM] * (4 + more),
            [e_adj, h_adj, e_fwd, edges, coef] + arrived_adj,
            [IN_VMEM] * (5 + len(arrived_adj)),
            aliases={0: 0, 1: 1, 2: 2, 3: 3},
        )
        if more:
            arrived_adj = trade(pays)
            e_fwd, h_fwd = call(
                functools.partial(inner_kernel, step + 1, 0),
                [field_shape] * 2,
                [IN_VMEM] * 2,
                [e_fwd, h_fwd, coef, drives, forced],
                [IN_VMEM] * 5,
                aliases={0: 0, 1: 1},
                micros=1.1,
            )

    parts = call(
        functools.partial(filter_edge_kernel, len(layout)),
        [on_chip(*group)] * len(layout),
        [IN_VMEM] * len(layout),
        list(parts) + [total, edges, place],
        [IN_VMEM] * (len(layout) + 3),
        [
            pltpu.VMEM((2, width_x + 2 * PAD, width_y), F32),
            pltpu.VMEM((2, width_x, width_y), F32),
        ],
        aliases={slot: slot for slot in range(len(layout))},
    )
    got = [swap_over(part, "grp", 1) for part in parts[middle:]]
    sums = call(
        add_kernel,
        [on_chip(*group)] * middle,
        [IN_VMEM] * middle,
        list(parts[:middle]) + got,
        [IN_VMEM] * (2 * middle),
    )
    got = [swap_over(part, "grp", mask) for part, mask in zip(sums[1:], middle_masks[1:])]
    pieces = call(
        functools.partial(add_split_kernel, middle),
        [on_chip(*piece)] * far,
        [IN_VMEM] * far,
        [sums[0]] + got,
        [IN_VMEM] * middle,
    )
    got = [swap_over(part, "grp", mask) for part, mask in zip(pieces[1:], far_masks[1:])]
    scale = 3.0 / (STEPS * math.sqrt(ngrp))
    grad = call(
        functools.partial(last_kernel, scale),
        jax.ShapeDtypeStruct(piece, F32),
        IN_VMEM,
        [pieces[0]] + got,
        [IN_VMEM] * far,
    )
    finals = call(
        out_kernel,
        jax.ShapeDtypeStruct(fwd_fields.shape, F32),
        IN_HBM,
        [e_fwd, h_fwd],
        [IN_VMEM] * 2,
        [
            pltpu.VMEM((3, depth, width_x, width_y), F32),
            pltpu.SemaphoreType.DMA((6,)),
        ],
        micros=1.7,
    )
    return finals, grad.reshape(density.shape)


def solution(mesh):
    placed = (
        P("grp", None, "slab", None, None),
        P("grp", None, "slab", None, None),
        P("slab", "grp", None),
        P(),
        P(),
        P(),
        P("grp", None),
        P("grp"),
    )
    return jax.shard_map(
        per_device,
        mesh=mesh,
        in_specs=placed,
        out_specs=(P("grp", None, "slab", None, None), P("slab", "grp", None)),
        check_vma=False,
    )
```

```python
import functools
import math

import jax
import jax.numpy as jnp
from jax import lax
from jax.experimental import pallas as pl
from jax.experimental.pallas import tpu as pltpu
from jax.sharding import PartitionSpec as P

STEPS = 4
AMPLITUDE = 4.0
PAD = 8
F32 = jnp.float32
HBM_PER_MICRO = 3.0e6

VMEM = pltpu.MemorySpace.VMEM
IN_VMEM = pl.BlockSpec(memory_space=pltpu.VMEM)
IN_SMEM = pl.BlockSpec(memory_space=pltpu.SMEM)
IN_HBM = pl.BlockSpec(memory_space=pltpu.MemorySpace.HBM)


def on_chip(*shape):
    return VMEM(shape, F32)


def held(array, spec):
    if spec is IN_SMEM:
        return array
    space = VMEM if spec is IN_VMEM else pltpu.MemorySpace.HBM
    return pltpu.with_memory_space_constraint(array, space)


def call(kernel, outs, out_specs, operands, specs, scratch=(), aliases=None, micros=0.3):
    operands = [held(a, s) for a, s in zip(operands, specs)]
    return pl.pallas_call(
        kernel,
        out_shape=outs,
        in_specs=specs,
        out_specs=out_specs,
        scratch_shapes=scratch,
        input_output_aliases=aliases or {},
        compiler_params=pltpu.CompilerParams(vmem_limit_bytes=8 << 20),
        cost_estimate=pl.CostEstimate(
            flops=0, bytes_accessed=int(micros * HBM_PER_MICRO), transcendentals=0
        ),
    )(*operands)


CHUNK = 16


def chunks(rows):
    size = CHUNK if rows % CHUNK == 0 else rows
    return [(first, size) for first in range(0, rows, size)]


def next_col(value):
    column = lax.broadcasted_iota(jnp.int32, value.shape, 1)
    moved = pltpu.roll(value, value.shape[1] - 1, 1)
    return jnp.where(column == value.shape[1] - 1, 0.0, moved)


def prev_col(value):
    column = lax.broadcasted_iota(jnp.int32, value.shape, 1)
    return jnp.where(column == 0, 0.0, pltpu.roll(value, 1, 1))


def neighbours():
    slab = lax.axis_index("slab")
    return slab < lax.axis_size("slab") - 1, slab > 0


class Window:
    def __init__(self, e, h, coef=None, force=None):
        self.e, self.h, self.coef, self.force = e, h, coef, force
        self.rows = e.shape[2] - 2 * PAD
        self.depth = e.shape[1] - 1
        self.top, self.under = self.depth - 1, self.depth

    def read(self, ref, layer, first, size):
        return [ref[c, layer, pl.ds(PAD + first, size), :] for c in range(3)]

    def write(self, ref, layer, first, size, values):
        for c, value in enumerate(values):
            ref[c, layer, pl.ds(PAD + first, size), :] = value

    def put_h(self, layer, given=None, alone=False):
        for first, size in chunks(self.rows):
            rows = pl.ds(PAD + first, size)
            after = pl.ds(PAD + first + 1, size)
            ex, ey, ez = self.read(self.e, layer, first, size)
            if given is None:
                hx, hy, hz = self.read(self.h, layer, first, size)
            else:
                hx, hy, hz = (value + value for value in given(layer, first, size))
            if alone:
                rise_x, rise_y = -ex, -ey
            else:
                rise_x = self.e[0, layer + 1, rows, :] - ex
                rise_y = self.e[1, layer + 1, rows, :] - ey
            ey_after = self.e[1, layer, after, :]
            ez_after = self.e[2, layer, after, :]
            hx = hx - ((next_col(ez) - ez) - rise_y)
            hy = hy - (rise_x - (ez_after - ez))
            hz = hz - ((ey_after - ey) - (next_col(ex) - ex))
            self.write(self.h, layer, first, size, (hx, hy, hz))

    def curl_h(self, layer, lower, first, size):
        rows = pl.ds(PAD + first, size)
        before = pl.ds(PAD + first - 1, size)
        hx, hy, hz = self.read(self.h, layer, first, size)
        step_x = hx - self.h[0, lower, rows, :]
        step_y = hy - self.h[1, lower, rows, :]
        hy_before = self.h[1, layer, before, :]
        hz_before = self.h[2, layer, before, :]
        return (
            (hz - prev_col(hz)) - step_y,
            step_x - (hz - hz_before),
            (hy - hy_before) - (hx - prev_col(hx)),
        )

    def put_curl(self, curls, layer, lower):
        for first, size in chunks(self.rows):
            for c, value in enumerate(self.curl_h(layer, lower, first, size)):
                curls[c, layer, pl.ds(first, size), :] = value

    def next_e(self, layer, lower, first, size, curls=None):
        here = pl.ds(first, size)
        cell = self.coef[layer, here, :]
        if curls is None:
            curl = self.curl_h(layer, lower, first, size)
        else:
            curl = [curls[c, layer, here, :] for c in range(3)]
        ex, ey, ez = [a + cell * b for a, b in zip(self.read(self.e, layer, first, size), curl)]
        if self.force is not None:
            ez = ez + self.force(layer, here)
        return ex, ey, ez

    def put_e(self, layer, lower, curls=None, other=None, total=None, slot=None):
        for first, size in chunks(self.rows):
            news = self.next_e(layer, lower, first, size, curls)
            self.write(self.e, layer, first, size, news)
            if total is not None:
                rows = pl.ds(PAD + first, size)
                part = [a * other[c, layer, rows, :] for c, a in enumerate(news)]
                total[layer if slot is None else slot, rows, :] += part[0] + part[1] + part[2]

    def take_above(self, above):
        for first, size in chunks(self.rows):
            here, rows = pl.ds(first, size), pl.ds(PAD + first, size)
            self.h[0, self.top, rows, :] += above[1, here, :]
            self.h[1, self.top, rows, :] -= above[0, here, :]

    def take_below(self, below):
        for first, size in chunks(self.rows):
            here, rows = pl.ds(first, size), pl.ds(PAD + first, size)
            self.h[0, self.under, rows, :] = below[0, here, :] + self.e[1, 0, rows, :]
            self.h[1, self.under, rows, :] = below[1, here, :] - self.e[0, 0, rows, :]


def forcing(step, drives, forced):
    if drives is None:
        return None
    return lambda layer, here: drives[pl.ds(step, 1), :] * forced[layer, here, :]


def opening_kernel(fwd, adj, density, own, *rest):
    pays, (planes, sems) = rest[:-2], rest[-2:]
    depth, rows, width_y = fwd.shape[2:]
    top = depth - 1
    has_up, has_low = neighbours()
    held_copy = pltpu.make_async_copy(density, own, sems.at[2, 0])
    held_copy.start()

    def up(pay):
        copies = []
        for evo, given in enumerate((fwd, adj)):
            for c in range(5):
                copies.append(
                    pltpu.make_async_copy(given.at[0, c, top], planes.at[evo, c], sems.at[evo, c])
                )
        for copy in copies:
            copy.start()
        for copy in copies:
            copy.wait()
        for evo in range(2):
            for first, size in chunks(rows):
                here = pl.ds(first, size)
                ex, ey, ez, hx, hy = (planes[evo, c, here, :] for c in range(5))
                if first + size < rows:
                    ez_after = planes[evo, 2, pl.ds(first + 1, size), :]
                else:
                    row = lax.broadcasted_iota(jnp.int32, ez.shape, 0)
                    ez_after = jnp.where(row == size - 1, 0.0, pltpu.roll(ez, size - 1, 0))
                pay[evo, 0, here, :] = (hx + hx) - ((next_col(ez) - ez) + ey)
                pay[evo, 1, here, :] = (hy + hy) + (ex + (ez_after - ez))

    def down(pay):
        copies = []
        for evo, given in enumerate((fwd, adj)):
            for c in range(2):
                copies.append(
                    pltpu.make_async_copy(given.at[0, c, 0], pay.at[evo, c], sems.at[evo, c])
                )
        for copy in copies:
            copy.start()
        for copy in copies:
            copy.wait()

    if len(pays) == 2:
        up(pays[0])
        down(pays[1])
    else:
        pl.when(has_up)(lambda: up(pays[0]))
        pl.when(has_low)(lambda: down(pays[0]))
    held_copy.wait()


def owners(count):
    core = lax.rem(lax.axis_index("grp"), 2)
    return [2 * chip + side for side in (core, 1 - core) for chip in range(count // 2)]


def prepare_kernel(
    masks, source, wave_idx, block_ids, material_idx, material_eps,
    total, edges, forced, drives, base, place, owned,
):
    depth, rows, width_y = forced.shape
    nblock = block_ids.shape[0]
    block_rows = rows // nblock
    empty = jnp.zeros(total.shape[1:], F32)
    edges[0] = empty
    edges[1] = empty
    xcoord = lax.broadcasted_iota(jnp.int32, (rows, width_y), 0)
    ycoord = lax.broadcasted_iota(jnp.int32, (rows, width_y), 1)
    offset_x = (xcoord - source[0, 1]).astype(F32) / (rows / 4.0)
    offset_y = (ycoord - source[0, 2]).astype(F32) / (width_y / 4.0)
    profile = jnp.exp(-0.5 * (offset_x * offset_x + offset_y * offset_y))
    step = lax.broadcasted_iota(jnp.int32, drives.shape, 0).astype(F32) + 1.0
    wave = jnp.full(drives.shape, wave_idx[0], jnp.int32).astype(F32)
    drives[...] = AMPLITUDE * jnp.sin(2.0 * math.pi / (6.0 + 2.0 * wave) * step)
    level = source[0, 0] - lax.axis_index("slab") * depth
    for layer in range(depth):
        total[layer] = empty
        forced[layer] = jnp.where(level == layer, 1.0, 0.0) * profile
    for block in range(nblock):
        value = jnp.full((block_rows, width_y), material_eps[material_idx[block]], F32)
        base[pl.ds(block * block_rows, block_rows), :] = value
    me = lax.axis_index("grp")
    block = lax.broadcasted_iota(jnp.int32, (nblock, width_y), 0)
    for slot, mask in enumerate(masks):
        place[slot] = jnp.where(block == block_ids[me ^ mask], 1.0, 0.0)
    for slot, owner in enumerate(owners(nblock)):
        owned[slot] = jnp.where(block == block_ids[owner], 1.0, 0.0)


def first_kernel(given, near, e, h, curls):
    win = Window(e, h)
    rows, width_y = win.rows, e.shape[3]
    margin = jnp.zeros((PAD, width_y), F32)
    empty = jnp.zeros((rows + 2 * PAD, width_y), F32)
    for comp in range(3):
        e[comp, win.depth] = empty
        h[comp, win.depth] = empty

    def copy(layer):
        for comp in range(3):
            for ref in (e, h):
                ref[comp, layer, pl.ds(0, PAD), :] = margin
                ref[comp, layer, pl.ds(PAD + rows, PAD), :] = margin
            for first, size in chunks(rows):
                here = pl.ds(first, size)
                e[comp, layer, pl.ds(PAD + first, size), :] = given[0, comp, layer, here, :]

    def from_given(layer, first, size):
        return [given[0, 3 + c, layer, pl.ds(first, size), :] for c in range(3)]

    copy(0)
    copy(1)
    win.put_h(0, from_given)
    copy(2)
    win.put_h(1, from_given)

    def body(layer, carry):
        pl.when(layer + 2 < win.depth)(lambda: copy(layer + 2))
        win.put_h(layer + 1, from_given)
        win.put_curl(curls, layer, layer - 1)
        return carry

    lax.fori_loop(1, win.top, body, 0)


def take_kernel(evo, h_in, curls_in, e, below, above, h, curls):
    win = Window(e, h)
    has_up, has_low = neighbours()
    pl.when(has_up)(lambda: win.take_above(above.at[evo]))
    pl.when(has_low)(lambda: win.take_below(below.at[evo]))
    win.put_curl(curls, win.top, win.top - 1)
    win.put_curl(curls, 0, win.under)


def edge_kernel(step, *refs):
    refs = list(refs)
    del refs[:5]
    coef, drives, forced = (refs.pop(0) for _ in range(3))
    first_curls = (refs.pop(0), refs.pop(0)) if step == 0 else (None, None)
    below, above = (refs.pop(0), refs.pop(0)) if step > 0 else (None, None)
    e_fwd, h_fwd, e_adj, h_adj, edges = refs[:5]
    pays = refs[5:]
    fwd = Window(e_fwd, h_fwd, coef, forcing(step, drives, forced))
    adj = Window(e_adj, h_adj, coef)
    top = fwd.top
    every = pl.ds(PAD, fwd.rows)
    has_up, has_low = neighbours()

    @pl.when(has_up)
    def _():
        if step > 0:
            for evo, win in enumerate((fwd, adj)):
                win.take_above(above.at[evo])
        fwd.put_e(top, top - 1, first_curls[0])
        adj.put_e(top, top - 1, first_curls[1], e_fwd, edges, 1)
        if pays:
            for evo, win in enumerate((fwd, adj)):
                win.put_h(top, alone=True)
                for c in range(2):
                    pays[0][evo, c] = win.h[c, top, every, :]

    @pl.when(has_low)
    def _():
        if step > 0:
            for evo, win in enumerate((fwd, adj)):
                win.take_below(below.at[evo])
        fwd.put_e(0, fwd.under, first_curls[0])
        adj.put_e(0, fwd.under, first_curls[1], e_fwd, edges, 0)
        if pays:
            for evo, win in enumerate((fwd, adj)):
                for c in range(2):
                    pays[-1][evo, c] = win.e[c, 0, every, :]


def inner_range(top):
    has_up, has_low = neighbours()
    return jnp.where(has_low, 1, 0), jnp.where(has_up, top - 1, top)


def begin_kernel(
    e_fwd_in, e_adj_in, total_in, coef, drives, forced, curls_fwd, curls_adj,
    e_fwd, e_adj, total,
):
    fwd = Window(e_fwd, None, coef, forcing(0, drives, forced))
    adj = Window(e_adj, None, coef)
    lowest, highest = inner_range(fwd.top)

    def body(layer, carry):
        fwd.put_e(layer, None, curls_fwd)
        adj.put_e(layer, None, curls_adj, e_fwd, total)
        return carry

    lax.fori_loop(lowest, highest + 1, body, 0)


def inner_kernel(step, *refs):
    coef, drives, forced, e_fwd, h_fwd, e_adj, h_adj, total = refs[5:]
    fwd = Window(e_fwd, h_fwd, coef, forcing(step, drives, forced))
    adj = Window(e_adj, h_adj, coef)
    lowest, highest = inner_range(fwd.top)

    def put_h(layer):
        fwd.put_h(layer)
        adj.put_h(layer)

    def put_e(layer, lower):
        fwd.put_e(layer, lower)
        adj.put_e(layer, lower, None, e_fwd, total)

    def body(layer, carry):
        put_h(layer + 1)
        put_e(layer, jnp.where(layer == 0, fwd.under, layer - 1))
        return carry

    put_h(0)
    pl.when(lowest == 1)(lambda: put_h(1))
    if lax.axis_size("slab") == 2:
        lax.fori_loop(0, fwd.depth - 2, lambda i, carry: body(lowest + i, carry), 0, unroll=2)
    else:
        lax.fori_loop(lowest, highest, body, 0)
    put_e(highest, highest - 1)


def coef_layer(layer, coef, placed, base):
    for first, size in chunks(base.shape[0]):
        here = pl.ds(first, size)
        coef[layer, here, :] = 0.25 / (base[here, :] + 3.0 * filtered(placed, first, size))


def clear_margins(placed):
    rows = placed.shape[0] - 2 * PAD
    margin = jnp.zeros((PAD, placed.shape[1]), F32)
    placed[pl.ds(0, PAD), :] = margin
    placed[pl.ds(PAD + rows, PAD), :] = margin


def scatter_kernel(layout, *refs):
    parts, (block_ids, blocks) = refs[: len(layout)], refs[len(layout) :]
    me = lax.axis_index("grp")
    nothing = jnp.zeros(blocks.shape[1:], F32)
    for block in range(blocks.shape[0]):
        blocks[block] = nothing
    for part, masks in zip(parts, layout):
        for slot, mask in enumerate(masks):
            blocks[block_ids[me ^ mask]] = part[slot]


def place_layer(layer, parts, place, blocks, placed):
    nblock = blocks.shape[0]
    block_rows = (placed.shape[0] - 2 * PAD) // nblock
    clear_margins(placed)
    start = layer * block_rows
    source = pl.ds(start if isinstance(layer, int) else pl.multiple_of(start, block_rows), block_rows)
    pieces = [part[slot, source, :] for part in parts for slot in range(part.shape[0])]
    for block in range(nblock):
        value = blocks[block, source, :]
        for slot, piece in enumerate(pieces):
            value = value + place[slot, pl.ds(block, 1), :] * piece
        placed[pl.ds(PAD + block * block_rows, block_rows), :] = value


def coef_edge_kernel(count, *refs):
    parts, (place, base, blocks, coef, placed) = refs[:count], refs[count:]
    edge_layers = (0, coef.shape[0] - 1)
    for which, layer in enumerate(edge_layers):
        place_layer(layer, parts, place, blocks, placed.at[which])
    for which, layer in enumerate(edge_layers):
        coef_layer(layer, coef, placed.at[which], base)


def coef_inner_kernel(count, coef_in, *refs):
    parts, (place, base, blocks, coef, placed) = refs[:count], refs[count:]

    def body(layer, carry):
        there = placed.at[lax.rem(layer, 2)]
        place_layer(layer, parts, place, blocks, there)
        coef_layer(layer, coef, there, base)
        return carry

    lax.fori_loop(1, coef.shape[0] - 1, body, 0, unroll=2)


def filtered(padded, first, size):
    here = padded[pl.ds(PAD + first, size), :]
    before = padded[pl.ds(PAD + first - 1, size), :]
    after = padded[pl.ds(PAD + first + 1, size), :]
    along = before + 2.0 * here + after
    return (prev_col(along) + 2.0 * along + next_col(along)) * 0.0625


def tie_kernel(*refs):
    pass


def tie(array, others):
    return call(
        tie_kernel, on_chip(*array.shape), IN_VMEM, [array] + others,
        [IN_VMEM] * (1 + len(others)), aliases={0: 0},
    )


def pack_kernel(*refs):
    out = refs[-1]
    for slot, ref in enumerate(refs[:-1]):
        out[slot] = ref[...]


def filter_inner_kernel(total, block_ids_far, kept, sent, blocks, wide, block_ids, sem):
    fetch = pltpu.make_async_copy(block_ids_far, block_ids, sem)
    fetch.start()
    depth = total.shape[0]
    nblock = blocks.shape[0]
    rows = wide.shape[1]
    block_rows = rows // nblock

    def body(layer, carry):
        there = wide.at[lax.rem(layer, 2)]
        for first, size in chunks(rows):
            there[pl.ds(first, size), :] = filtered(total.at[layer], first, size)
        for block in range(nblock):
            target = pl.ds(pl.multiple_of(layer * block_rows, block_rows), block_rows)
            blocks[block, target, :] = there[pl.ds(block * block_rows, block_rows), :]
        return carry

    lax.fori_loop(1, depth - 1, body, 0, unroll=2)
    fetch.wait()
    inner = pl.ds(block_rows, (depth - 2) * block_rows)
    chips = nblock // 2
    for slot, owner in enumerate(owners(nblock)):
        part = kept if slot < chips else sent
        part[slot % chips, inner, :] = blocks[block_ids[owner], inner, :]


def filter_edge_kernel(kept_in, sent_in, total, edges, owned, kept, sent, sums, wide):
    depth = total.shape[0]
    nblock = owned.shape[0]
    chips = nblock // 2
    rows = wide.shape[1]
    block_rows = rows // nblock
    for which, layer in enumerate((0, depth - 1)):
        sums[which] = total[layer] + edges[which]
        for first, size in chunks(rows):
            wide[which, pl.ds(first, size), :] = filtered(sums.at[which], first, size)
    for which, layer in enumerate((0, depth - 1)):
        blocks = [
            wide[which, pl.ds(block * block_rows, block_rows), :] for block in range(nblock)
        ]
        target = pl.ds(layer * block_rows, block_rows)
        for slot in range(nblock):
            value = None
            for block, piece in enumerate(blocks):
                term = owned[slot, pl.ds(block, 1), :] * piece
                value = term if value is None else value + term
            part = kept if slot < chips else sent
            part[slot % chips, target, :] = value


def add_kernel(kept, got, out):
    out[...] = kept[...] + got[...]


def last_kernel(scale, got, out):
    value = got[0]
    for slot in range(1, got.shape[0]):
        value = value + got[slot]
    out[...] = value * scale


def out_kernel(lowest, stride, count, e, h, *refs):
    finals, halves, sems = refs[-5], refs[-2], refs[-1]
    rows = e.shape[2] - 2 * PAD
    every = pl.ds(PAD, rows)
    runs = [(lowest, count)] if stride == 1 else [(lowest + stride * i, 1) for i in range(count)]
    copies = []
    for run, (first, size) in enumerate(runs):
        layers = pl.ds(first, size)
        for c in range(3):
            source = e.at[c, layers, every, :]
            copies.append(pltpu.make_async_copy(source, finals.at[0, c, layers], sems.at[run, c]))
            copies[-1].start()
    for run, (first, size) in enumerate(runs):
        for c in range(3):
            for layer in range(first, first + size):
                halves[c, layer] = 0.5 * h[c, layer, every, :]
            layers = pl.ds(first, size)
            source = halves.at[c, layers]
            target = finals.at[0, 3 + c, layers]
            copies.append(pltpu.make_async_copy(source, target, sems.at[run, 3 + c]))
            copies[-1].start()
    for copy in copies:
        copy.wait()


def swap_over(array, axis, mask):
    return lax.ppermute(array, axis, [(i, i ^ mask) for i in range(lax.axis_size(axis))])


def shift_over(array, axis, distance):
    size = lax.axis_size(axis)
    route = [(i, i + distance) for i in range(size) if 0 <= i + distance < size]
    return lax.ppermute(array, axis, route)


def trade(pays):
    if len(pays) == 1:
        return [swap_over(pays[0], "slab", 1)] * 2
    return [shift_over(pays[0], "slab", 1), shift_over(pays[1], "slab", -1)]


def per_device(
    fwd_fields, adj_fields, density, block_ids, material_idx, material_eps, source_pos, wave_idx
):
    depth, width_x, width_y = fwd_fields.shape[2:]
    nblock = block_ids.shape[0]
    block_rows = width_x // nblock
    ngrp = lax.axis_size("grp")
    npay = 1 if lax.axis_size("slab") == 2 else 2

    far = 4
    middle = ngrp // (2 * far)
    far_masks = [2 * middle * j for j in range(far)]
    middle_masks = [2 * j for j in range(middle)]
    layout = [
        [core + mid + top for top in far_masks] for core in (0, 1) for mid in middle_masks
    ]
    piece = (depth * block_rows, width_y)
    group = (far,) + piece
    chips = nblock // 2

    field_shape = on_chip(3, depth + 1, width_x + 2 * PAD, width_y)
    curls_shape = on_chip(3, depth, width_x, width_y)
    pay_shape = on_chip(2, 2, width_x, width_y)
    total_shape = on_chip(depth, width_x + 2 * PAD, width_y)
    edges_shape = on_chip(2, width_x + 2 * PAD, width_y)
    coef_shape = on_chip(depth, width_x, width_y)
    plane = on_chip(width_x, width_y)

    def write_out(lowest, stride, count, fields, finals, micros):
        finals, fields[0], fields[1] = call(
            functools.partial(out_kernel, lowest, stride, count),
            [jax.ShapeDtypeStruct(fwd_fields.shape, F32), field_shape, field_shape],
            [IN_HBM, IN_VMEM, IN_VMEM],
            fields[:2] + finals,
            [IN_VMEM] * 2 + [IN_HBM] * len(finals),
            [
                pltpu.VMEM((3, depth, width_x, width_y), F32),
                pltpu.SemaphoreType.DMA((2, 6)),
            ],
            aliases={0: 1, 1: 2, 2: 0} if finals else {0: 1, 1: 2},
            micros=micros,
        )
        return finals

    design = density.reshape(piece)
    got = [swap_over(design, "grp", mask) for mask in far_masks[1:]]
    own, *pays = call(
        opening_kernel,
        [on_chip(*piece)] + [pay_shape] * npay,
        [IN_VMEM] * (1 + npay),
        [fwd_fields, adj_fields, design],
        [IN_HBM] * 3,
        [pltpu.VMEM((2, 5, width_x, width_y), F32), pltpu.SemaphoreType.DMA((3, 5))],
    )
    below, above = trade(pays)

    near = call(pack_kernel, on_chip(*group), IN_VMEM, [own] + got, [IN_VMEM] * far)
    others = [swap_over(near, "grp", mask) for mask in middle_masks[1:]]
    near_across = swap_over(near, "grp", 1)

    total, edges, forced, drives, base, place, owned = call(
        functools.partial(prepare_kernel, [m for masks in layout[middle + 1 :] for m in masks]),
        [
            total_shape,
            edges_shape,
            on_chip(depth, width_x, width_y),
            on_chip(STEPS, width_y),
            plane,
            on_chip(far * (middle - 1), nblock, width_y),
            on_chip(nblock, nblock, width_y),
        ],
        [IN_VMEM] * 7,
        [source_pos, wave_idx, block_ids, material_idx, material_eps],
        [IN_SMEM] * 5,
    )
    fields = []
    for evo, given in enumerate((fwd_fields, adj_fields)):
        e, h, curls = call(
            first_kernel,
            [field_shape, field_shape, curls_shape],
            [IN_VMEM] * 3,
            [given, near],
            [IN_VMEM, IN_VMEM],
            micros=1.5,
        )
        fields.append((e, h, curls))
    others = [tie(part, [forced] + [e for e, _, _ in fields]) for part in others]
    early = [near] + others + [near_across]
    last = [swap_over(part, "grp", 1) for part in others]
    blocks = call(
        functools.partial(scatter_kernel, layout[: len(early)]),
        on_chip(nblock, *piece),
        IN_VMEM,
        early + [block_ids],
        [IN_VMEM] * len(early) + [IN_SMEM],
        micros=0.7,
    )

    taken = []
    for evo, (e, h, curls) in enumerate(fields):
        h, curls = call(
            functools.partial(take_kernel, evo),
            [field_shape, curls_shape],
            [IN_VMEM] * 2,
            [h, curls, e, below, above],
            [IN_VMEM] * 5,
            aliases={0: 0, 1: 1},
        )
        taken.append((e, h, curls))
    (e_fwd, h_fwd, curls_fwd), (e_adj, h_adj, curls_adj) = taken
    placed = pltpu.VMEM((2, width_x + 2 * PAD, width_y), F32)
    coef = call(
        functools.partial(coef_edge_kernel, len(last)),
        coef_shape,
        IN_VMEM,
        last + [place, base, blocks],
        [IN_VMEM] * (len(last) + 3),
        [placed],
    )

    fields = [e_fwd, h_fwd, e_adj, h_adj]
    about = [drives, forced]
    late = [curls_fwd, curls_adj]
    for step in range(STEPS):
        more = npay if step < STEPS - 1 else 0
        outcome = call(
            functools.partial(edge_kernel, step),
            [field_shape] * 4 + [edges_shape] + [pay_shape] * more,
            [IN_VMEM] * (5 + more),
            fields + [edges, coef] + about + late,
            [IN_VMEM] * 10,
            aliases={slot: slot for slot in range(5)},
        )
        fields, edges, pays = list(outcome[:4]), outcome[4], outcome[5:]
        if not more:
            break
        late = trade(pays)
        if step == 0:
            coef = call(
                functools.partial(coef_inner_kernel, len(last)),
                coef_shape,
                IN_VMEM,
                [coef] + last + [place, base, blocks],
                [IN_VMEM] * (len(last) + 4),
                [placed],
                aliases={0: 0},
                micros=0.6,
            )
            fields[0], fields[2], total = call(
                begin_kernel,
                [field_shape, field_shape, total_shape],
                [IN_VMEM] * 3,
                [fields[0], fields[2], total, coef] + about + [curls_fwd, curls_adj],
                [IN_VMEM] * 8,
                aliases={0: 0, 1: 1, 2: 2},
                micros=0.5,
            )
        *fields, total = call(
            functools.partial(inner_kernel, step + 1),
            [field_shape] * 4 + [total_shape],
            [IN_VMEM] * 5,
            fields + [total, coef] + about,
            [IN_VMEM] * 8,
            aliases={slot: slot for slot in range(5)},
            micros=2.3,
        )
        if step == STEPS - 2:
            kept, sent = call(
                filter_inner_kernel,
                [on_chip(chips, *piece)] * 2,
                [IN_VMEM] * 2,
                [total, block_ids],
                [IN_VMEM, IN_HBM],
                [
                    pltpu.VMEM((nblock,) + piece, F32),
                    pltpu.VMEM((2, width_x, width_y), F32),
                    pltpu.SMEM(block_ids.shape, jnp.int32),
                    pltpu.SemaphoreType.DMA,
                ],
                micros=0.8,
            )
            finals = write_out(1, 1, depth - 2, fields, [], 1.3)
    finals = write_out(0, depth - 1, 2, fields, [finals], 0.7)

    kept, sent = call(
        filter_edge_kernel,
        [on_chip(chips, *piece)] * 2,
        [IN_VMEM] * 2,
        [kept, sent, total, edges, owned],
        [IN_VMEM] * 5,
        [
            pltpu.VMEM((2, width_x + 2 * PAD, width_y), F32),
            pltpu.VMEM((2, width_x, width_y), F32),
        ],
        aliases={0: 0, 1: 1},
    )
    got = swap_over(sent, "grp", 1)
    sums = call(add_kernel, on_chip(chips, *piece), IN_VMEM, [kept, got], [IN_VMEM] * 2)
    got = lax.all_to_all(
        sums, "grp", 0, 0, axis_index_groups=[list(range(core, ngrp, 2)) for core in (0, 1)]
    )
    scale = 3.0 / (STEPS * math.sqrt(ngrp))
    grad = call(
        functools.partial(last_kernel, scale),
        jax.ShapeDtypeStruct(piece, F32),
        IN_VMEM,
        [got],
        [IN_VMEM],
    )
    return finals, grad.reshape(density.shape)


def solution(mesh):
    placed = (
        P("grp", None, "slab", None, None),
        P("grp", None, "slab", None, None),
        P("slab", "grp", None),
        P(),
        P(),
        P(),
        P("grp", None),
        P("grp"),
    )
    return jax.shard_map(
        per_device,
        mesh=mesh,
        in_specs=placed,
        out_specs=(P("grp", None, "slab", None, None), P("slab", "grp", None)),
        check_vma=False,
    )
```

```python
import functools
import math

import jax
import jax.numpy as jnp
from jax import lax
from jax.experimental import pallas as pl
from jax.experimental.pallas import tpu as pltpu
from jax.sharding import PartitionSpec as P

STEPS = 4
AMPLITUDE = 4.0
PAD = 8
F32 = jnp.float32
HBM_PER_MICRO = 3.0e6

VMEM = pltpu.MemorySpace.VMEM
IN_VMEM = pl.BlockSpec(memory_space=pltpu.VMEM)
IN_SMEM = pl.BlockSpec(memory_space=pltpu.SMEM)
IN_HBM = pl.BlockSpec(memory_space=pltpu.MemorySpace.HBM)


def on_chip(*shape):
    return VMEM(shape, F32)


def held(array, spec):
    if spec is IN_SMEM:
        return array
    space = VMEM if spec is IN_VMEM else pltpu.MemorySpace.HBM
    return pltpu.with_memory_space_constraint(array, space)


def call(kernel, outs, out_specs, operands, specs, scratch=(), aliases=None, micros=0.3):
    operands = [held(a, s) for a, s in zip(operands, specs)]
    return pl.pallas_call(
        kernel,
        out_shape=outs,
        in_specs=specs,
        out_specs=out_specs,
        scratch_shapes=scratch,
        input_output_aliases=aliases or {},
        compiler_params=pltpu.CompilerParams(vmem_limit_bytes=8 << 20),
        cost_estimate=pl.CostEstimate(
            flops=0, bytes_accessed=int(micros * HBM_PER_MICRO), transcendentals=0
        ),
    )(*operands)


CHUNK = 16


def chunks(rows):
    size = CHUNK if rows % CHUNK == 0 else rows
    return [(first, size) for first in range(0, rows, size)]


def next_col(value):
    column = lax.broadcasted_iota(jnp.int32, value.shape, 1)
    moved = pltpu.roll(value, value.shape[1] - 1, 1)
    return jnp.where(column == value.shape[1] - 1, 0.0, moved)


def prev_col(value):
    column = lax.broadcasted_iota(jnp.int32, value.shape, 1)
    return jnp.where(column == 0, 0.0, pltpu.roll(value, 1, 1))


def neighbours():
    slab = lax.axis_index("slab")
    return slab < lax.axis_size("slab") - 1, slab > 0


class Window:
    def __init__(self, e, h, coef=None, force=None):
        self.e, self.h, self.coef, self.force = e, h, coef, force
        self.rows = e.shape[2] - 2 * PAD
        self.depth = e.shape[1] - 1
        self.top, self.under = self.depth - 1, self.depth

    def read(self, ref, layer, first, size):
        return [ref[c, layer, pl.ds(PAD + first, size), :] for c in range(3)]

    def write(self, ref, layer, first, size, values):
        for c, value in enumerate(values):
            ref[c, layer, pl.ds(PAD + first, size), :] = value

    def put_h(self, layer, given=None, alone=False):
        for first, size in chunks(self.rows):
            rows = pl.ds(PAD + first, size)
            after = pl.ds(PAD + first + 1, size)
            ex, ey, ez = self.read(self.e, layer, first, size)
            if given is None:
                hx, hy, hz = self.read(self.h, layer, first, size)
            else:
                hx, hy, hz = (value + value for value in given(layer, first, size))
            if alone:
                rise_x, rise_y = -ex, -ey
            else:
                rise_x = self.e[0, layer + 1, rows, :] - ex
                rise_y = self.e[1, layer + 1, rows, :] - ey
            ey_after = self.e[1, layer, after, :]
            ez_after = self.e[2, layer, after, :]
            hx = hx - ((next_col(ez) - ez) - rise_y)
            hy = hy - (rise_x - (ez_after - ez))
            hz = hz - ((ey_after - ey) - (next_col(ex) - ex))
            self.write(self.h, layer, first, size, (hx, hy, hz))

    def curl_h(self, layer, lower, first, size):
        rows = pl.ds(PAD + first, size)
        before = pl.ds(PAD + first - 1, size)
        hx, hy, hz = self.read(self.h, layer, first, size)
        step_x = hx - self.h[0, lower, rows, :]
        step_y = hy - self.h[1, lower, rows, :]
        hy_before = self.h[1, layer, before, :]
        hz_before = self.h[2, layer, before, :]
        return (
            (hz - prev_col(hz)) - step_y,
            step_x - (hz - hz_before),
            (hy - hy_before) - (hx - prev_col(hx)),
        )

    def put_curl(self, curls, layer, lower):
        for first, size in chunks(self.rows):
            for c, value in enumerate(self.curl_h(layer, lower, first, size)):
                curls[c, layer, pl.ds(first, size), :] = value

    def next_e(self, layer, lower, first, size, curls=None):
        here = pl.ds(first, size)
        cell = self.coef[layer, here, :]
        if curls is None:
            curl = self.curl_h(layer, lower, first, size)
        else:
            curl = [curls[c, layer, here, :] for c in range(3)]
        ex, ey, ez = [a + cell * b for a, b in zip(self.read(self.e, layer, first, size), curl)]
        if self.force is not None:
            ez = ez + self.force(layer, here)
        return ex, ey, ez

    def put_e(self, layer, lower, curls=None, other=None, total=None, slot=None):
        for first, size in chunks(self.rows):
            news = self.next_e(layer, lower, first, size, curls)
            self.write(self.e, layer, first, size, news)
            if total is not None:
                rows = pl.ds(PAD + first, size)
                part = [a * other[c, layer, rows, :] for c, a in enumerate(news)]
                total[layer if slot is None else slot, rows, :] += part[0] + part[1] + part[2]

    def take_above(self, above):
        for first, size in chunks(self.rows):
            here, rows = pl.ds(first, size), pl.ds(PAD + first, size)
            self.h[0, self.top, rows, :] += above[1, here, :]
            self.h[1, self.top, rows, :] -= above[0, here, :]

    def take_below(self, below):
        for first, size in chunks(self.rows):
            here, rows = pl.ds(first, size), pl.ds(PAD + first, size)
            self.h[0, self.under, rows, :] = below[0, here, :] + self.e[1, 0, rows, :]
            self.h[1, self.under, rows, :] = below[1, here, :] - self.e[0, 0, rows, :]


def forcing(step, drives, forced):
    if drives is None:
        return None
    return lambda layer, here: drives[pl.ds(step, 1), :] * forced[layer, here, :]


def opening_kernel(fwd, adj, density, own, *rest):
    pays, (planes, sems) = rest[:-2], rest[-2:]
    depth, rows, width_y = fwd.shape[2:]
    top = depth - 1
    has_up, has_low = neighbours()
    held_copy = pltpu.make_async_copy(density, own, sems.at[2, 0])
    held_copy.start()

    def up(pay):
        copies = []
        for evo, given in enumerate((fwd, adj)):
            for c in range(5):
                copies.append(
                    pltpu.make_async_copy(given.at[0, c, top], planes.at[evo, c], sems.at[evo, c])
                )
        for copy in copies:
            copy.start()
        for copy in copies:
            copy.wait()
        for evo in range(2):
            for first, size in chunks(rows):
                here = pl.ds(first, size)
                ex, ey, ez, hx, hy = (planes[evo, c, here, :] for c in range(5))
                if first + size < rows:
                    ez_after = planes[evo, 2, pl.ds(first + 1, size), :]
                else:
                    row = lax.broadcasted_iota(jnp.int32, ez.shape, 0)
                    ez_after = jnp.where(row == size - 1, 0.0, pltpu.roll(ez, size - 1, 0))
                pay[evo, 0, here, :] = (hx + hx) - ((next_col(ez) - ez) + ey)
                pay[evo, 1, here, :] = (hy + hy) + (ex + (ez_after - ez))

    def down(pay):
        copies = []
        for evo, given in enumerate((fwd, adj)):
            for c in range(2):
                copies.append(
                    pltpu.make_async_copy(given.at[0, c, 0], pay.at[evo, c], sems.at[evo, c])
                )
        for copy in copies:
            copy.start()
        for copy in copies:
            copy.wait()

    if len(pays) == 2:
        up(pays[0])
        down(pays[1])
    else:
        pl.when(has_up)(lambda: up(pays[0]))
        pl.when(has_low)(lambda: down(pays[0]))
    held_copy.wait()


def prepare_kernel(
    layout, wave_idx, source_far, ids_far, idx_far, eps_far,
    total, edges, forced, drives, base, place,
    source, block_ids, material_idx, material_eps, sems,
):
    depth, rows, width_y = forced.shape
    fetches = [
        pltpu.make_async_copy(far, near, sems.at[slot])
        for slot, (far, near) in enumerate(
            (
                (source_far, source),
                (ids_far, block_ids),
                (idx_far, material_idx),
                (eps_far, material_eps),
            )
        )
    ]
    for fetch in fetches:
        fetch.start()
    nblock = block_ids.shape[0]
    block_rows = rows // nblock
    empty = jnp.zeros(total.shape[1:], F32)
    edges[0] = empty
    edges[1] = empty
    for layer in range(depth):
        total[layer] = empty
    for fetch in fetches:
        fetch.wait()
    xcoord = lax.broadcasted_iota(jnp.int32, (rows, width_y), 0)
    ycoord = lax.broadcasted_iota(jnp.int32, (rows, width_y), 1)
    offset_x = (xcoord - source[0, 1]).astype(F32) / (rows / 4.0)
    offset_y = (ycoord - source[0, 2]).astype(F32) / (width_y / 4.0)
    profile = jnp.exp(-0.5 * (offset_x * offset_x + offset_y * offset_y))
    step = lax.broadcasted_iota(jnp.int32, drives.shape, 0).astype(F32) + 1.0
    wave = jnp.full(drives.shape, wave_idx[0], jnp.int32).astype(F32)
    drives[...] = AMPLITUDE * jnp.sin(2.0 * math.pi / (6.0 + 2.0 * wave) * step)
    level = source[0, 0] - lax.axis_index("slab") * depth
    for layer in range(depth):
        forced[layer] = jnp.where(level == layer, 1.0, 0.0) * profile
    for block in range(nblock):
        value = jnp.full((block_rows, width_y), material_eps[material_idx[block]], F32)
        base[pl.ds(block * block_rows, block_rows), :] = value
    me = lax.axis_index("grp")
    block = lax.broadcasted_iota(jnp.int32, (nblock, width_y), 0)
    for slot, mask in enumerate(mask for masks in layout for mask in masks):
        place[slot] = jnp.where(block == block_ids[me ^ mask], 1.0, 0.0)


def first_kernel(given, near, e, h, curls):
    win = Window(e, h)
    rows, width_y = win.rows, e.shape[3]
    margin = jnp.zeros((PAD, width_y), F32)
    empty = jnp.zeros((rows + 2 * PAD, width_y), F32)
    for comp in range(3):
        e[comp, win.depth] = empty
        h[comp, win.depth] = empty

    def copy(layer):
        for comp in range(3):
            for ref in (e, h):
                ref[comp, layer, pl.ds(0, PAD), :] = margin
                ref[comp, layer, pl.ds(PAD + rows, PAD), :] = margin
            for first, size in chunks(rows):
                here = pl.ds(first, size)
                e[comp, layer, pl.ds(PAD + first, size), :] = given[0, comp, layer, here, :]

    def from_given(layer, first, size):
        return [given[0, 3 + c, layer, pl.ds(first, size), :] for c in range(3)]

    copy(0)
    copy(1)
    win.put_h(0, from_given)
    copy(2)
    win.put_h(1, from_given)

    def body(layer, carry):
        pl.when(layer + 2 < win.depth)(lambda: copy(layer + 2))
        win.put_h(layer + 1, from_given)
        win.put_curl(curls, layer, layer - 1)
        return carry

    lax.fori_loop(1, win.top, body, 0)


def settle_kernel(layout, *refs):
    refs = list(refs)
    del refs[:4]
    e_fwd, e_adj, below, above = (refs.pop(0) for _ in range(4))
    parts = [refs.pop(0) for _ in layout]
    ids_far, h_fwd, curls_fwd, h_adj, curls_adj, blocks, block_ids, sem = refs
    fetch = pltpu.make_async_copy(ids_far, block_ids, sem)
    fetch.start()
    nothing = jnp.zeros(blocks.shape[1:], F32)
    for block in range(blocks.shape[0]):
        blocks[block] = nothing
    has_up, has_low = neighbours()
    for evo, (e, h, curls) in enumerate(((e_fwd, h_fwd, curls_fwd), (e_adj, h_adj, curls_adj))):
        win = Window(e, h)
        pl.when(has_up)(lambda: win.take_above(above.at[evo]))
        pl.when(has_low)(lambda: win.take_below(below.at[evo]))
        win.put_curl(curls, win.top, win.top - 1)
        win.put_curl(curls, 0, win.under)
    fetch.wait()
    me = lax.axis_index("grp")
    for part, masks in zip(parts, layout):
        for slot, mask in enumerate(masks):
            blocks[block_ids[me ^ mask]] = part[slot]


def edge_kernel(step, evo, *refs):
    refs = list(refs)
    e_in, h_in = refs.pop(0), refs.pop(0)
    if evo == 1:
        other_in, edges_in = refs.pop(0), refs.pop(0)
    coef = refs.pop(0)
    drives, forced = (refs.pop(0), refs.pop(0)) if evo == 0 else (None, None)
    curls = refs.pop(0) if step == 0 else None
    below, above = (refs.pop(0), refs.pop(0)) if step > 0 else (None, None)
    e, h = refs.pop(0), refs.pop(0)
    other, edges = (refs.pop(0), refs.pop(0)) if evo == 1 else (None, None)
    pays = refs
    win = Window(e, h, coef, forcing(step, drives, forced))
    top = win.top
    has_up, has_low = neighbours()

    @pl.when(has_up)
    def _():
        if step > 0:
            win.take_above(above)
        win.put_e(top, top - 1, curls, other, edges, 1)
        if pays:
            win.put_h(top, alone=True)
            for c in range(2):
                pays[0][c] = h[c, top, pl.ds(PAD, win.rows), :]

    @pl.when(has_low)
    def _():
        if step > 0:
            win.take_below(below)
        win.put_e(0, win.under, curls, other, edges, 0)
        if pays:
            for c in range(2):
                pays[-1][c] = e[c, 0, pl.ds(PAD, win.rows), :]


def inner_range(top):
    has_up, has_low = neighbours()
    return jnp.where(has_low, 1, 0), jnp.where(has_up, top - 1, top)


def begin_kernel(
    e_fwd_in, e_adj_in, total_in, coef, drives, forced, curls_fwd, curls_adj,
    e_fwd, e_adj, total,
):
    fwd = Window(e_fwd, None, coef, forcing(0, drives, forced))
    adj = Window(e_adj, None, coef)
    lowest, highest = inner_range(fwd.top)

    def body(layer, carry):
        fwd.put_e(layer, None, curls_fwd)
        adj.put_e(layer, None, curls_adj, e_fwd, total)
        return carry

    lax.fori_loop(lowest, highest + 1, body, 0)


def inner_kernel(step, evo, *refs):
    refs = list(refs)
    e_in, h_in = refs.pop(0), refs.pop(0)
    if evo == 1:
        other_in, total_in = refs.pop(0), refs.pop(0)
    coef = refs.pop(0)
    drives, forced = (refs.pop(0), refs.pop(0)) if evo == 0 else (None, None)
    e, h = refs.pop(0), refs.pop(0)
    other, total = (refs.pop(0), refs.pop(0)) if evo == 1 else (None, None)
    win = Window(e, h, coef, forcing(step, drives, forced))
    lowest, highest = inner_range(win.top)
    win.put_h(0)
    pl.when(lowest == 1)(lambda: win.put_h(1))

    def body(layer, carry):
        win.put_h(layer + 1)
        win.put_e(layer, jnp.where(layer == 0, win.under, layer - 1), None, other, total)
        return carry

    if lax.axis_size("slab") == 2:
        lax.fori_loop(0, win.depth - 2, lambda i, carry: body(lowest + i, carry), 0, unroll=2)
    else:
        lax.fori_loop(lowest, highest, body, 0)
    win.put_e(highest, highest - 1, None, other, total)


def coef_layer(layer, coef, placed, base):
    for first, size in chunks(base.shape[0]):
        here = pl.ds(first, size)
        coef[layer, here, :] = 0.25 / (base[here, :] + 3.0 * filtered(placed, first, size))


def clear_margins(placed):
    rows = placed.shape[0] - 2 * PAD
    margin = jnp.zeros((PAD, placed.shape[1]), F32)
    placed[pl.ds(0, PAD), :] = margin
    placed[pl.ds(PAD + rows, PAD), :] = margin


def place_layer(layer, first_slot, parts, place, blocks, placed):
    nblock = blocks.shape[0]
    block_rows = (placed.shape[0] - 2 * PAD) // nblock
    clear_margins(placed)
    start = layer * block_rows
    source = pl.ds(start if isinstance(layer, int) else pl.multiple_of(start, block_rows), block_rows)
    pieces = [part[slot, source, :] for part in parts for slot in range(part.shape[0])]
    for block in range(nblock):
        value = blocks[block, source, :]
        for slot, piece in enumerate(pieces):
            value = value + place[first_slot + slot, pl.ds(block, 1), :] * piece
        placed[pl.ds(PAD + block * block_rows, block_rows), :] = value


def coef_edge_kernel(first_slot, count, *refs):
    parts, (place, base, blocks, coef, placed) = refs[:count], refs[count:]
    edge_layers = (0, coef.shape[0] - 1)
    for which, layer in enumerate(edge_layers):
        place_layer(layer, first_slot, parts, place, blocks, placed.at[which])
    for which, layer in enumerate(edge_layers):
        coef_layer(layer, coef, placed.at[which], base)


def coef_inner_kernel(first_slot, count, coef_in, *refs):
    parts, (place, base, blocks, coef, placed) = refs[:count], refs[count:]

    def body(layer, carry):
        there = placed.at[lax.rem(layer, 2)]
        place_layer(layer, first_slot, parts, place, blocks, there)
        coef_layer(layer, coef, there, base)
        return carry

    lax.fori_loop(1, coef.shape[0] - 1, body, 0, unroll=2)


def filtered(padded, first, size):
    here = padded[pl.ds(PAD + first, size), :]
    before = padded[pl.ds(PAD + first - 1, size), :]
    after = padded[pl.ds(PAD + first + 1, size), :]
    along = before + 2.0 * here + after
    return (prev_col(along) + 2.0 * along + next_col(along)) * 0.0625


def tie_kernel(*refs):
    pass


def tie(array, others):
    return call(
        tie_kernel, on_chip(*array.shape), IN_VMEM, [array] + others,
        [IN_VMEM] * (1 + len(others)), aliases={0: 0},
    )


def pack_kernel(*refs):
    out = refs[-1]
    for slot, ref in enumerate(refs[:-1]):
        out[slot] = ref[...]


def filter_inner_kernel(layout, total, block_ids_far, *rest):
    parts, (blocks, wide, block_ids, sem) = rest[:-4], rest[-4:]
    fetch = pltpu.make_async_copy(block_ids_far, block_ids, sem)
    fetch.start()
    depth = total.shape[0]
    nblock = blocks.shape[0]
    rows = wide.shape[1]
    block_rows = rows // nblock
    me = lax.axis_index("grp")

    def body(layer, carry):
        there = wide.at[lax.rem(layer, 2)]
        for first, size in chunks(rows):
            there[pl.ds(first, size), :] = filtered(total.at[layer], first, size)
        for block in range(nblock):
            target = pl.ds(pl.multiple_of((layer - 1) * block_rows, block_rows), block_rows)
            blocks[block, target, :] = there[pl.ds(block * block_rows, block_rows), :]
        return carry

    lax.fori_loop(1, depth - 1, body, 0, unroll=2)
    fetch.wait()
    inner = pl.ds(0, (depth - 2) * block_rows)
    for part, masks in zip(parts, layout):
        for slot, mask in enumerate(masks):
            part[slot] = blocks[block_ids[me ^ mask], inner, :]


def filter_edge_kernel(layout, total, edges, place, *rest):
    parts, (sums, wide) = rest[:-2], rest[-2:]
    depth = total.shape[0]
    nblock = place.shape[0]
    rows = wide.shape[1]
    block_rows = rows // nblock
    for which, layer in enumerate((0, depth - 1)):
        sums[which] = total[layer] + edges[which]
        for first, size in chunks(rows):
            wide[which, pl.ds(first, size), :] = filtered(sums.at[which], first, size)
    for which in range(2):
        blocks = [
            wide[which, pl.ds(block * block_rows, block_rows), :] for block in range(nblock)
        ]
        target = pl.ds(which * block_rows, block_rows)
        for slot in range(nblock):
            value = None
            for block, piece in enumerate(blocks):
                term = place[slot, pl.ds(block, 1), :] * piece
                value = term if value is None else value + term
            parts[slot // parts[0].shape[0]][slot % parts[0].shape[0], target, :] = value


def add_kernel(*refs):
    half = len(refs) // 3
    for a, b, out in zip(refs[:half], refs[half : 2 * half], refs[2 * half :]):
        out[...] = a[...] + b[...]


def join_kernel(count, block_rows, *refs):
    inner, edge, outs = refs[:count], refs[count : 2 * count], refs[2 * count :]
    rows = outs[0].shape[0]
    for slot, out in enumerate(outs):
        middle, ends = inner[0][slot], edge[0][slot]
        for a, b in zip(inner[1:], edge[1:]):
            middle, ends = middle + a[slot], ends + b[slot]
        out[pl.ds(0, block_rows), :] = ends[:block_rows]
        out[pl.ds(block_rows, rows - 2 * block_rows), :] = middle
        out[pl.ds(rows - block_rows, block_rows), :] = ends[block_rows:]


def last_kernel(scale, *refs):
    value = refs[0][...]
    for ref in refs[1:-1]:
        value = value + ref[...]
    refs[-1][...] = value * scale


def out_kernel(e, h, finals, halves, sems):
    depth = e.shape[1] - 1
    rows = e.shape[2] - 2 * PAD
    every = pl.ds(PAD, rows)
    copies = [
        pltpu.make_async_copy(e.at[c, pl.ds(0, depth), every, :], finals.at[0, c], sems.at[c])
        for c in range(3)
    ]
    for copy in copies:
        copy.start()
    for c in range(3):

        def body(layer, carry, c=c):
            halves[c, layer] = 0.5 * h[c, layer, every, :]
            return carry

        lax.fori_loop(0, depth, body, 0)
        copy = pltpu.make_async_copy(halves.at[c], finals.at[0, 3 + c], sems.at[3 + c])
        copy.start()
        copies.append(copy)
    for copy in copies:
        copy.wait()


def swap_over(array, axis, mask):
    return lax.ppermute(array, axis, [(i, i ^ mask) for i in range(lax.axis_size(axis))])


def shift_over(array, axis, distance):
    size = lax.axis_size(axis)
    route = [(i, i + distance) for i in range(size) if 0 <= i + distance < size]
    return lax.ppermute(array, axis, route)


def trade(pays):
    if len(pays) == 1:
        return [swap_over(pays[0], "slab", 1)] * 2
    return [shift_over(pays[0], "slab", 1), shift_over(pays[1], "slab", -1)]


def per_device(
    fwd_fields, adj_fields, density, block_ids, material_idx, material_eps, source_pos, wave_idx
):
    depth, width_x, width_y = fwd_fields.shape[2:]
    nblock = block_ids.shape[0]
    block_rows = width_x // nblock
    ngrp = lax.axis_size("grp")
    npay = 1 if lax.axis_size("slab") == 2 else 2

    far = 4
    middle = ngrp // (2 * far)
    far_masks = [2 * middle * j for j in range(far)]
    middle_masks = [2 * j for j in range(middle)]
    layout = [
        [core + mid + top for top in far_masks] for core in (0, 1) for mid in middle_masks
    ]
    piece = (depth * block_rows, width_y)
    group = (far,) + piece

    field_shape = on_chip(3, depth + 1, width_x + 2 * PAD, width_y)
    curls_shape = on_chip(3, depth, width_x, width_y)
    halo_shape = on_chip(2, width_x, width_y)
    total_shape = on_chip(depth, width_x + 2 * PAD, width_y)
    edges_shape = on_chip(2, width_x + 2 * PAD, width_y)
    coef_shape = on_chip(depth, width_x, width_y)
    plane = on_chip(width_x, width_y)

    def by_owner(kernel, layers, operands, specs, scratch, micros):
        shape = on_chip(far, layers * block_rows, width_y)
        parts = call(
            kernel,
            [shape] * len(layout),
            [IN_VMEM] * len(layout),
            operands,
            specs,
            scratch,
            micros=micros,
        )
        got = [swap_over(part, "grp", 1) for part in parts[middle:]]
        sums = call(
            add_kernel,
            [shape] * middle,
            [IN_VMEM] * middle,
            list(parts[:middle]) + got,
            [IN_VMEM] * (2 * middle),
        )
        return [sums[0]] + [
            swap_over(part, "grp", mask) for part, mask in zip(sums[1:], middle_masks[1:])
        ]

    design = density.reshape(piece)
    got = [swap_over(design, "grp", mask) for mask in far_masks[1:]]
    own, *pays = call(
        opening_kernel,
        [on_chip(*piece)] + [on_chip(2, 2, width_x, width_y)] * npay,
        [IN_VMEM] * (1 + npay),
        [fwd_fields, adj_fields, design],
        [IN_HBM] * 3,
        [pltpu.VMEM((2, 5, width_x, width_y), F32), pltpu.SemaphoreType.DMA((3, 5))],
    )
    below, above = trade(pays)

    near = call(pack_kernel, on_chip(*group), IN_VMEM, [own] + got, [IN_VMEM] * far)
    others = [swap_over(near, "grp", mask) for mask in middle_masks[1:]]
    near_across = swap_over(near, "grp", 1)

    place_shape = on_chip(nblock, nblock, width_y)
    total, edges, forced, drives, base, place = call(
        functools.partial(prepare_kernel, layout),
        [
            total_shape,
            edges_shape,
            on_chip(depth, width_x, width_y),
            on_chip(STEPS, width_y),
            plane,
            place_shape,
        ],
        [IN_VMEM] * 6,
        [wave_idx, source_pos, block_ids, material_idx, material_eps],
        [IN_SMEM] + [IN_HBM] * 4,
        [
            pltpu.SMEM(source_pos.shape, jnp.int32),
            pltpu.SMEM(block_ids.shape, jnp.int32),
            pltpu.SMEM(material_idx.shape, jnp.int32),
            pltpu.SMEM(material_eps.shape, F32),
            pltpu.SemaphoreType.DMA((4,)),
        ],
    )
    fields = []
    for evo, given in enumerate((fwd_fields, adj_fields)):
        e, h, curls = call(
            first_kernel,
            [field_shape, field_shape, curls_shape],
            [IN_VMEM] * 3,
            [given, near],
            [IN_VMEM, IN_VMEM],
            micros=1.5,
        )
        fields.append((e, h, curls))
    others = [tie(part, [forced] + [e for e, _, _ in fields]) for part in others]
    early = [near] + others + [near_across]
    last = [swap_over(part, "grp", 1) for part in others]
    first_slot = far * len(early)

    (e_fwd, h_fwd, curls_fwd), (e_adj, h_adj, curls_adj) = fields
    h_fwd, curls_fwd, h_adj, curls_adj, blocks = call(
        functools.partial(settle_kernel, layout[: len(early)]),
        [field_shape, curls_shape] * 2 + [on_chip(nblock, *piece)],
        [IN_VMEM] * 5,
        [h_fwd, curls_fwd, h_adj, curls_adj, e_fwd, e_adj, below, above] + early + [block_ids],
        [IN_VMEM] * (8 + len(early)) + [IN_HBM],
        [pltpu.SMEM(block_ids.shape, jnp.int32), pltpu.SemaphoreType.DMA],
        aliases={0: 0, 1: 1, 2: 2, 3: 3},
        micros=0.6,
    )
    placed = pltpu.VMEM((2, width_x + 2 * PAD, width_y), F32)
    coef = call(
        functools.partial(coef_edge_kernel, first_slot, len(last)),
        coef_shape,
        IN_VMEM,
        last + [place, base, blocks],
        [IN_VMEM] * (len(last) + 3),
        [placed],
    )

    arrived_fwd, arrived_adj = [curls_fwd], [curls_adj]
    for step in range(STEPS):
        more = npay if step < STEPS - 1 else 0

        def edge_fwd(e_fwd, h_fwd):
            return call(
                functools.partial(edge_kernel, step, 0),
                [field_shape] * 2 + [halo_shape] * more,
                [IN_VMEM] * (2 + more),
                [e_fwd, h_fwd, coef, drives, forced] + arrived_fwd,
                [IN_VMEM] * (5 + len(arrived_fwd)),
                aliases={0: 0, 1: 1},
            )

        if more:
            e_fwd, h_fwd, *pays = edge_fwd(e_fwd, h_fwd)
            arrived_fwd_next = trade(pays)
        if step > 0:
            e_adj, h_adj, e_fwd, total = call(
                functools.partial(inner_kernel, step, 1),
                [field_shape] * 3 + [total_shape],
                [IN_VMEM] * 4,
                [e_adj, h_adj, e_fwd, total, coef],
                [IN_VMEM] * 5,
                aliases={0: 0, 1: 1, 2: 2, 3: 3},
                micros=1.2,
            )
        if not more:
            inner = by_owner(
                functools.partial(filter_inner_kernel, layout),
                depth - 2,
                [total, block_ids],
                [IN_VMEM, IN_HBM],
                [
                    pltpu.VMEM((nblock,) + piece, F32),
                    pltpu.VMEM((2, width_x, width_y), F32),
                    pltpu.SMEM(block_ids.shape, jnp.int32),
                    pltpu.SemaphoreType.DMA,
                ],
                0.8,
            )
            e_fwd, h_fwd = edge_fwd(e_fwd, h_fwd)
        e_adj, h_adj, e_fwd, edges, *pays = call(
            functools.partial(edge_kernel, step, 1),
            [field_shape] * 3 + [edges_shape] + [halo_shape] * more,
            [IN_VMEM] * (4 + more),
            [e_adj, h_adj, e_fwd, edges, coef] + arrived_adj,
            [IN_VMEM] * (5 + len(arrived_adj)),
            aliases={0: 0, 1: 1, 2: 2, 3: 3},
        )
        if not more:
            break
        arrived_fwd, arrived_adj = arrived_fwd_next, trade(pays)
        if step == 0:
            coef = call(
                functools.partial(coef_inner_kernel, first_slot, len(last)),
                coef_shape,
                IN_VMEM,
                [coef] + last + [place, base, blocks],
                [IN_VMEM] * (len(last) + 4),
                [placed],
                aliases={0: 0},
                micros=0.6,
            )
            e_fwd, e_adj, total = call(
                begin_kernel,
                [field_shape, field_shape, total_shape],
                [IN_VMEM] * 3,
                [e_fwd, e_adj, total, coef, drives, forced, curls_fwd, curls_adj],
                [IN_VMEM] * 8,
                aliases={0: 0, 1: 1, 2: 2},
                micros=0.5,
            )
        e_fwd, h_fwd = call(
            functools.partial(inner_kernel, step + 1, 0),
            [field_shape] * 2,
            [IN_VMEM] * 2,
            [e_fwd, h_fwd, coef, drives, forced],
            [IN_VMEM] * 5,
            aliases={0: 0, 1: 1},
            micros=1.1,
        )

    ends = by_owner(
        functools.partial(filter_edge_kernel, layout),
        2,
        [total, edges, place],
        [IN_VMEM] * 3,
        [
            pltpu.VMEM((2, width_x + 2 * PAD, width_y), F32),
            pltpu.VMEM((2, width_x, width_y), F32),
        ],
        0.3,
    )
    pieces = call(
        functools.partial(join_kernel, middle, block_rows),
        [on_chip(*piece)] * far,
        [IN_VMEM] * far,
        inner + ends,
        [IN_VMEM] * (2 * middle),
    )
    got = [swap_over(part, "grp", mask) for part, mask in zip(pieces[1:], far_masks[1:])]
    scale = 3.0 / (STEPS * math.sqrt(ngrp))
    grad = call(
        functools.partial(last_kernel, scale),
        jax.ShapeDtypeStruct(piece, F32),
        IN_VMEM,
        [pieces[0]] + got,
        [IN_VMEM] * far,
    )
    finals = call(
        out_kernel,
        jax.ShapeDtypeStruct(fwd_fields.shape, F32),
        IN_HBM,
        [e_fwd, h_fwd],
        [IN_VMEM] * 2,
        [
            pltpu.VMEM((3, depth, width_x, width_y), F32),
            pltpu.SemaphoreType.DMA((6,)),
        ],
        micros=1.7,
    )
    return finals, grad.reshape(density.shape)


def solution(mesh):
    placed = (
        P("grp", None, "slab", None, None),
        P("grp", None, "slab", None, None),
        P("slab", "grp", None),
        P(),
        P(),
        P(),
        P("grp", None),
        P("grp"),
    )
    return jax.shard_map(
        per_device,
        mesh=mesh,
        in_specs=placed,
        out_specs=(P("grp", None, "slab", None, None), P("slab", "grp", None)),
        check_vma=False,
    )
```

```python
import functools
import math

import jax
import jax.numpy as jnp
from jax import lax
from jax.experimental import pallas as pl
from jax.experimental.pallas import tpu as pltpu
from jax.sharding import PartitionSpec as P

STEPS = 4
AMPLITUDE = 4.0
PAD = 8
F32 = jnp.float32
HBM_PER_MICRO = 1.0e5

VMEM = pltpu.MemorySpace.VMEM
IN_VMEM = pl.BlockSpec(memory_space=pltpu.VMEM)
IN_SMEM = pl.BlockSpec(memory_space=pltpu.SMEM)
IN_HBM = pl.BlockSpec(memory_space=pltpu.MemorySpace.HBM)


def on_chip(*shape):
    return VMEM(shape, F32)


def held(array, spec):
    if spec is IN_SMEM:
        return array
    space = VMEM if spec is IN_VMEM else pltpu.MemorySpace.HBM
    return pltpu.with_memory_space_constraint(array, space)


def call(kernel, outs, out_specs, operands, specs, scratch=(), aliases=None, micros=0.3):
    operands = [held(a, s) for a, s in zip(operands, specs)]
    return pl.pallas_call(
        kernel,
        out_shape=outs,
        in_specs=specs,
        out_specs=out_specs,
        scratch_shapes=scratch,
        input_output_aliases=aliases or {},
        compiler_params=pltpu.CompilerParams(vmem_limit_bytes=8 << 20),
        cost_estimate=pl.CostEstimate(
            flops=0, bytes_accessed=int(micros * HBM_PER_MICRO), transcendentals=0
        ),
    )(*operands)


CHUNK = 16


def chunks(rows):
    size = CHUNK if rows % CHUNK == 0 else rows
    return [(first, size) for first in range(0, rows, size)]


def next_col(value):
    column = lax.broadcasted_iota(jnp.int32, value.shape, 1)
    moved = pltpu.roll(value, value.shape[1] - 1, 1)
    return jnp.where(column == value.shape[1] - 1, 0.0, moved)


def prev_col(value):
    column = lax.broadcasted_iota(jnp.int32, value.shape, 1)
    return jnp.where(column == 0, 0.0, pltpu.roll(value, 1, 1))


def neighbours():
    slab = lax.axis_index("slab")
    return slab < lax.axis_size("slab") - 1, slab > 0


class Window:
    def __init__(self, e, h, coef=None, force=None):
        self.e, self.h, self.coef, self.force = e, h, coef, force
        self.rows = e.shape[2] - 2 * PAD
        self.depth = e.shape[1] - 1
        self.top, self.under = self.depth - 1, self.depth

    def read(self, ref, layer, first, size):
        return [ref[c, layer, pl.ds(PAD + first, size), :] for c in range(3)]

    def write(self, ref, layer, first, size, values):
        for c, value in enumerate(values):
            ref[c, layer, pl.ds(PAD + first, size), :] = value

    def put_h(self, layer, given=None, alone=False):
        for first, size in chunks(self.rows):
            rows = pl.ds(PAD + first, size)
            after = pl.ds(PAD + first + 1, size)
            ex, ey, ez = self.read(self.e, layer, first, size)
            if given is None:
                hx, hy, hz = self.read(self.h, layer, first, size)
            else:
                hx, hy, hz = (value + value for value in given(layer, first, size))
            if alone:
                rise_x, rise_y = -ex, -ey
            else:
                rise_x = self.e[0, layer + 1, rows, :] - ex
                rise_y = self.e[1, layer + 1, rows, :] - ey
            ey_after = self.e[1, layer, after, :]
            ez_after = self.e[2, layer, after, :]
            hx = hx - ((next_col(ez) - ez) - rise_y)
            hy = hy - (rise_x - (ez_after - ez))
            hz = hz - ((ey_after - ey) - (next_col(ex) - ex))
            self.write(self.h, layer, first, size, (hx, hy, hz))

    def curl_h(self, layer, lower, first, size):
        rows = pl.ds(PAD + first, size)
        before = pl.ds(PAD + first - 1, size)
        hx, hy, hz = self.read(self.h, layer, first, size)
        step_x = hx - self.h[0, lower, rows, :]
        step_y = hy - self.h[1, lower, rows, :]
        hy_before = self.h[1, layer, before, :]
        hz_before = self.h[2, layer, before, :]
        return (
            (hz - prev_col(hz)) - step_y,
            step_x - (hz - hz_before),
            (hy - hy_before) - (hx - prev_col(hx)),
        )

    def put_curl(self, curls, layer, lower):
        for first, size in chunks(self.rows):
            for c, value in enumerate(self.curl_h(layer, lower, first, size)):
                curls[c, layer, pl.ds(first, size), :] = value

    def next_e(self, layer, lower, first, size, curls=None):
        here = pl.ds(first, size)
        cell = self.coef[layer, here, :]
        if curls is None:
            curl = self.curl_h(layer, lower, first, size)
        else:
            curl = [curls[c, layer, here, :] for c in range(3)]
        ex, ey, ez = [a + cell * b for a, b in zip(self.read(self.e, layer, first, size), curl)]
        if self.force is not None:
            ez = ez + self.force(layer, here)
        return ex, ey, ez

    def put_e(self, layer, lower, curls=None, other=None, total=None, slot=None):
        for first, size in chunks(self.rows):
            news = self.next_e(layer, lower, first, size, curls)
            self.write(self.e, layer, first, size, news)
            if total is not None:
                rows = pl.ds(PAD + first, size)
                part = [a * other[c, layer, rows, :] for c, a in enumerate(news)]
                total[layer if slot is None else slot, rows, :] += part[0] + part[1] + part[2]

    def take_above(self, above):
        for first, size in chunks(self.rows):
            here, rows = pl.ds(first, size), pl.ds(PAD + first, size)
            self.h[0, self.top, rows, :] += above[1, here, :]
            self.h[1, self.top, rows, :] -= above[0, here, :]

    def take_below(self, below):
        for first, size in chunks(self.rows):
            here, rows = pl.ds(first, size), pl.ds(PAD + first, size)
            self.h[0, self.under, rows, :] = below[0, here, :] + self.e[1, 0, rows, :]
            self.h[1, self.under, rows, :] = below[1, here, :] - self.e[0, 0, rows, :]


def forcing(step, drives, forced):
    if drives is None:
        return None
    return lambda layer, here: drives[pl.ds(step, 1), :] * forced[layer, here, :]


def opening_kernel(fwd, adj, density, wave_idx, own, drives, *rest):
    pays, (planes, sems) = rest[:-2], rest[-2:]
    depth, rows, width_y = fwd.shape[2:]
    top = depth - 1
    has_up, has_low = neighbours()
    held_copy = pltpu.make_async_copy(density, own, sems.at[2, 0])
    held_copy.start()
    step = lax.broadcasted_iota(jnp.int32, drives.shape, 0).astype(F32) + 1.0
    wave = jnp.full(drives.shape, wave_idx[0], jnp.int32).astype(F32)
    drives[...] = AMPLITUDE * jnp.sin(2.0 * math.pi / (6.0 + 2.0 * wave) * step)

    def up(pay):
        copies = []
        for evo, given in enumerate((fwd, adj)):
            for c in range(5):
                copies.append(
                    pltpu.make_async_copy(given.at[0, c, top], planes.at[evo, c], sems.at[evo, c])
                )
        for copy in copies:
            copy.start()
        for copy in copies:
            copy.wait()
        for evo in range(2):
            for first, size in chunks(rows):
                here = pl.ds(first, size)
                ex, ey, ez, hx, hy = (planes[evo, c, here, :] for c in range(5))
                if first + size < rows:
                    ez_after = planes[evo, 2, pl.ds(first + 1, size), :]
                else:
                    row = lax.broadcasted_iota(jnp.int32, ez.shape, 0)
                    ez_after = jnp.where(row == size - 1, 0.0, pltpu.roll(ez, size - 1, 0))
                pay[evo, 0, here, :] = (hx + hx) - ((next_col(ez) - ez) + ey)
                pay[evo, 1, here, :] = (hy + hy) + (ex + (ez_after - ez))

    def down(pay):
        copies = []
        for evo, given in enumerate((fwd, adj)):
            for c in range(2):
                copies.append(
                    pltpu.make_async_copy(given.at[0, c, 0], pay.at[evo, c], sems.at[evo, c])
                )
        for copy in copies:
            copy.start()
        for copy in copies:
            copy.wait()

    if len(pays) == 2:
        up(pays[0])
        down(pays[1])
    else:
        pl.when(has_up)(lambda: up(pays[0]))
        pl.when(has_low)(lambda: down(pays[0]))
    held_copy.wait()


def first_fwd_kernel(
    layout, given, near, source_far, ids_far, idx_far, eps_far,
    e, h, curls, total, edges, forced, base, place,
    source, block_ids, material_idx, material_eps, sems,
):
    fetches = [
        pltpu.make_async_copy(far, here, sems.at[slot])
        for slot, (far, here) in enumerate(
            (
                (source_far, source),
                (ids_far, block_ids),
                (idx_far, material_idx),
                (eps_far, material_eps),
            )
        )
    ]
    for fetch in fetches:
        fetch.start()
    first_kernel(given, near, e, h, curls)
    depth, rows, width_y = forced.shape
    nblock = block_ids.shape[0]
    block_rows = rows // nblock
    empty = jnp.zeros(total.shape[1:], F32)
    edges[0] = empty
    edges[1] = empty
    for layer in range(depth):
        total[layer] = empty
    for fetch in fetches:
        fetch.wait()
    xcoord = lax.broadcasted_iota(jnp.int32, (rows, width_y), 0)
    ycoord = lax.broadcasted_iota(jnp.int32, (rows, width_y), 1)
    offset_x = (xcoord - source[0, 1]).astype(F32) / (rows / 4.0)
    offset_y = (ycoord - source[0, 2]).astype(F32) / (width_y / 4.0)
    profile = jnp.exp(-0.5 * (offset_x * offset_x + offset_y * offset_y))
    level = source[0, 0] - lax.axis_index("slab") * depth
    for layer in range(depth):
        forced[layer] = jnp.where(level == layer, 1.0, 0.0) * profile
    for block in range(nblock):
        value = jnp.full((block_rows, width_y), material_eps[material_idx[block]], F32)
        base[pl.ds(block * block_rows, block_rows), :] = value
    me = lax.axis_index("grp")
    block = lax.broadcasted_iota(jnp.int32, (nblock, width_y), 0)
    for slot, mask in enumerate(mask for masks in layout for mask in masks):
        place[slot] = jnp.where(block == block_ids[me ^ mask], 1.0, 0.0)


def first_kernel(given, near, e, h, curls):
    win = Window(e, h)
    rows, width_y = win.rows, e.shape[3]
    margin = jnp.zeros((PAD, width_y), F32)
    empty = jnp.zeros((rows + 2 * PAD, width_y), F32)
    for comp in range(3):
        e[comp, win.depth] = empty
        h[comp, win.depth] = empty

    def copy(layer):
        for comp in range(3):
            for ref in (e, h):
                ref[comp, layer, pl.ds(0, PAD), :] = margin
                ref[comp, layer, pl.ds(PAD + rows, PAD), :] = margin
            for first, size in chunks(rows):
                here = pl.ds(first, size)
                e[comp, layer, pl.ds(PAD + first, size), :] = given[0, comp, layer, here, :]

    def from_given(layer, first, size):
        return [given[0, 3 + c, layer, pl.ds(first, size), :] for c in range(3)]

    copy(0)
    copy(1)
    win.put_h(0, from_given)
    copy(2)
    win.put_h(1, from_given)

    def body(layer, carry):
        pl.when(layer + 2 < win.depth)(lambda: copy(layer + 2))
        win.put_h(layer + 1, from_given)
        win.put_curl(curls, layer, layer - 1)
        return carry

    lax.fori_loop(1, win.top, body, 0)


def settle_kernel(layout, *refs):
    refs = list(refs)
    del refs[:4]
    e_fwd, e_adj, below, above = (refs.pop(0) for _ in range(4))
    parts = [refs.pop(0) for _ in layout]
    ids_far, h_fwd, curls_fwd, h_adj, curls_adj, blocks, block_ids, sem = refs
    fetch = pltpu.make_async_copy(ids_far, block_ids, sem)
    fetch.start()
    nothing = jnp.zeros(blocks.shape[1:], F32)
    for block in range(blocks.shape[0]):
        blocks[block] = nothing
    has_up, has_low = neighbours()
    for evo, (e, h, curls) in enumerate(((e_fwd, h_fwd, curls_fwd), (e_adj, h_adj, curls_adj))):
        win = Window(e, h)
        pl.when(has_up)(lambda: win.take_above(above.at[evo]))
        pl.when(has_low)(lambda: win.take_below(below.at[evo]))
        win.put_curl(curls, win.top, win.top - 1)
        win.put_curl(curls, 0, win.under)
    fetch.wait()
    me = lax.axis_index("grp")
    for part, masks in zip(parts, layout):
        for slot, mask in enumerate(masks):
            blocks[block_ids[me ^ mask]] = part[slot]


def edge_kernel(step, evo, *refs):
    refs = list(refs)
    e_in, h_in = refs.pop(0), refs.pop(0)
    if evo == 1:
        other_in, edges_in = refs.pop(0), refs.pop(0)
    coef = refs.pop(0)
    drives, forced = (refs.pop(0), refs.pop(0)) if evo == 0 else (None, None)
    curls = refs.pop(0) if step == 0 else None
    below, above = (refs.pop(0), refs.pop(0)) if step > 0 else (None, None)
    e, h = refs.pop(0), refs.pop(0)
    other, edges = (refs.pop(0), refs.pop(0)) if evo == 1 else (None, None)
    pays = refs
    win = Window(e, h, coef, forcing(step, drives, forced))
    top = win.top
    has_up, has_low = neighbours()

    @pl.when(has_up)
    def _():
        if step > 0:
            win.take_above(above)
        win.put_e(top, top - 1, curls, other, edges, 1)
        if pays:
            win.put_h(top, alone=True)
            for c in range(2):
                pays[0][c] = h[c, top, pl.ds(PAD, win.rows), :]

    @pl.when(has_low)
    def _():
        if step > 0:
            win.take_below(below)
        win.put_e(0, win.under, curls, other, edges, 0)
        if pays:
            for c in range(2):
                pays[-1][c] = e[c, 0, pl.ds(PAD, win.rows), :]


def inner_range(top):
    has_up, has_low = neighbours()
    return jnp.where(has_low, 1, 0), jnp.where(has_up, top - 1, top)


def begin_kernel(
    e_fwd_in, e_adj_in, total_in, coef, drives, forced, curls_fwd, curls_adj,
    e_fwd, e_adj, total,
):
    fwd = Window(e_fwd, None, coef, forcing(0, drives, forced))
    adj = Window(e_adj, None, coef)
    lowest, highest = inner_range(fwd.top)

    def body(layer, carry):
        fwd.put_e(layer, None, curls_fwd)
        adj.put_e(layer, None, curls_adj, e_fwd, total)
        return carry

    lax.fori_loop(lowest, highest + 1, body, 0)


def inner_kernel(step, evo, *refs):
    refs = list(refs)
    e_in, h_in = refs.pop(0), refs.pop(0)
    if evo == 1:
        other_in, total_in = refs.pop(0), refs.pop(0)
    coef = refs.pop(0)
    drives, forced = (refs.pop(0), refs.pop(0)) if evo == 0 else (None, None)
    e, h = refs.pop(0), refs.pop(0)
    other, total = (refs.pop(0), refs.pop(0)) if evo == 1 else (None, None)
    win = Window(e, h, coef, forcing(step, drives, forced))
    lowest, highest = inner_range(win.top)
    win.put_h(0)
    pl.when(lowest == 1)(lambda: win.put_h(1))

    def body(layer, carry):
        win.put_h(layer + 1)
        win.put_e(layer, jnp.where(layer == 0, win.under, layer - 1), None, other, total)
        return carry

    if lax.axis_size("slab") == 2:
        lax.fori_loop(0, win.depth - 2, lambda i, carry: body(lowest + i, carry), 0, unroll=2)
    else:
        lax.fori_loop(lowest, highest, body, 0)
    win.put_e(highest, highest - 1, None, other, total)


def coef_layer(layer, coef, placed, base):
    for first, size in chunks(base.shape[0]):
        here = pl.ds(first, size)
        coef[layer, here, :] = 0.25 / (base[here, :] + 3.0 * filtered(placed, first, size))


def clear_margins(placed):
    rows = placed.shape[0] - 2 * PAD
    margin = jnp.zeros((PAD, placed.shape[1]), F32)
    placed[pl.ds(0, PAD), :] = margin
    placed[pl.ds(PAD + rows, PAD), :] = margin


def place_layer(layer, first_slot, parts, place, blocks, placed):
    nblock = blocks.shape[0]
    block_rows = (placed.shape[0] - 2 * PAD) // nblock
    clear_margins(placed)
    start = layer * block_rows
    source = pl.ds(start if isinstance(layer, int) else pl.multiple_of(start, block_rows), block_rows)
    pieces = [part[slot, source, :] for part in parts for slot in range(part.shape[0])]
    for block in range(nblock):
        value = blocks[block, source, :]
        for slot, piece in enumerate(pieces):
            value = value + place[first_slot + slot, pl.ds(block, 1), :] * piece
        placed[pl.ds(PAD + block * block_rows, block_rows), :] = value


def coef_edge_kernel(first_slot, count, *refs):
    parts, (place, base, blocks, coef, placed) = refs[:count], refs[count:]
    edge_layers = (0, coef.shape[0] - 1)
    for which, layer in enumerate(edge_layers):
        place_layer(layer, first_slot, parts, place, blocks, placed.at[which])
    for which, layer in enumerate(edge_layers):
        coef_layer(layer, coef, placed.at[which], base)


def coef_inner_kernel(first_slot, count, coef_in, *refs):
    parts, (place, base, blocks, coef, placed) = refs[:count], refs[count:]

    def body(layer, carry):
        there = placed.at[lax.rem(layer, 2)]
        place_layer(layer, first_slot, parts, place, blocks, there)
        coef_layer(layer, coef, there, base)
        return carry

    lax.fori_loop(1, coef.shape[0] - 1, body, 0, unroll=2)


def filtered(padded, first, size):
    here = padded[pl.ds(PAD + first, size), :]
    before = padded[pl.ds(PAD + first - 1, size), :]
    after = padded[pl.ds(PAD + first + 1, size), :]
    along = before + 2.0 * here + after
    return (prev_col(along) + 2.0 * along + next_col(along)) * 0.0625


def tie_kernel(*refs):
    pass


def tie(array, others):
    return call(
        tie_kernel, on_chip(*array.shape), IN_VMEM, [array] + others,
        [IN_VMEM] * (1 + len(others)), aliases={0: 0},
    )


def pack_kernel(*refs):
    out = refs[-1]
    for slot, ref in enumerate(refs[:-1]):
        out[slot] = ref[...]


def filter_inner_kernel(layout, total, after, block_ids_far, *rest):
    parts, (blocks, wide, block_ids, sem) = rest[:-4], rest[-4:]
    fetch = pltpu.make_async_copy(block_ids_far, block_ids, sem)
    fetch.start()
    depth = total.shape[0]
    nblock = blocks.shape[0]
    rows = wide.shape[1]
    block_rows = rows // nblock
    me = lax.axis_index("grp")

    def body(layer, carry):
        there = wide.at[lax.rem(layer, 2)]
        for first, size in chunks(rows):
            there[pl.ds(first, size), :] = filtered(total.at[layer], first, size)
        for block in range(nblock):
            target = pl.ds(pl.multiple_of((layer - 1) * block_rows, block_rows), block_rows)
            blocks[block, target, :] = there[pl.ds(block * block_rows, block_rows), :]
        return carry

    lax.fori_loop(1, depth - 1, body, 0, unroll=2)
    fetch.wait()
    inner = pl.ds(0, (depth - 2) * block_rows)
    for part, masks in zip(parts, layout):
        for slot, mask in enumerate(masks):
            part[slot] = blocks[block_ids[me ^ mask], inner, :]


def filter_edge_kernel(layout, total, edges, place, *rest):
    parts, (sums, wide) = rest[:-2], rest[-2:]
    depth = total.shape[0]
    nblock = place.shape[0]
    rows = wide.shape[1]
    block_rows = rows // nblock
    for which, layer in enumerate((0, depth - 1)):
        sums[which] = total[layer] + edges[which]
        for first, size in chunks(rows):
            wide[which, pl.ds(first, size), :] = filtered(sums.at[which], first, size)
    for which in range(2):
        blocks = [
            wide[which, pl.ds(block * block_rows, block_rows), :] for block in range(nblock)
        ]
        target = pl.ds(which * block_rows, block_rows)
        for slot in range(nblock):
            value = None
            for block, piece in enumerate(blocks):
                term = place[slot, pl.ds(block, 1), :] * piece
                value = term if value is None else value + term
            parts[slot // parts[0].shape[0]][slot % parts[0].shape[0], target, :] = value


def add_kernel(*refs):
    half = len(refs) // 3
    for a, b, out in zip(refs[:half], refs[half : 2 * half], refs[2 * half :]):
        out[...] = a[...] + b[...]


def join_kernel(count, block_rows, *refs):
    inner, edge, outs = refs[:count], refs[count : 2 * count], refs[2 * count :]
    rows = outs[0].shape[0]
    for slot, out in enumerate(outs):
        middle, ends = inner[0][slot], edge[0][slot]
        for a, b in zip(inner[1:], edge[1:]):
            middle, ends = middle + a[slot], ends + b[slot]
        out[pl.ds(0, block_rows), :] = ends[:block_rows]
        out[pl.ds(block_rows, rows - 2 * block_rows), :] = middle
        out[pl.ds(rows - block_rows, block_rows), :] = ends[block_rows:]


def last_kernel(scale, *refs):
    value = refs[0][...]
    for ref in refs[1:-1]:
        value = value + ref[...]
    refs[-1][...] = value * scale


def out_kernel(e, h, finals, halves, sems):
    depth = e.shape[1] - 1
    rows = e.shape[2] - 2 * PAD
    every = pl.ds(PAD, rows)
    copies = [
        pltpu.make_async_copy(e.at[c, pl.ds(0, depth), every, :], finals.at[0, c], sems.at[c])
        for c in range(3)
    ]
    for copy in copies:
        copy.start()
    for c in range(3):

        def body(layer, carry, c=c):
            halves[c, layer] = 0.5 * h[c, layer, every, :]
            return carry

        lax.fori_loop(0, depth, body, 0)
        copy = pltpu.make_async_copy(halves.at[c], finals.at[0, 3 + c], sems.at[3 + c])
        copy.start()
        copies.append(copy)
    for copy in copies:
        copy.wait()


def swap_over(array, axis, mask):
    return lax.ppermute(array, axis, [(i, i ^ mask) for i in range(lax.axis_size(axis))])


def shift_over(array, axis, distance):
    size = lax.axis_size(axis)
    route = [(i, i + distance) for i in range(size) if 0 <= i + distance < size]
    return lax.ppermute(array, axis, route)


def trade(pays):
    if len(pays) == 1:
        return [swap_over(pays[0], "slab", 1)] * 2
    return [shift_over(pays[0], "slab", 1), shift_over(pays[1], "slab", -1)]


def per_device(
    fwd_fields, adj_fields, density, block_ids, material_idx, material_eps, source_pos, wave_idx
):
    depth, width_x, width_y = fwd_fields.shape[2:]
    nblock = block_ids.shape[0]
    block_rows = width_x // nblock
    ngrp = lax.axis_size("grp")
    npay = 1 if lax.axis_size("slab") == 2 else 2

    far = 4
    middle = ngrp // (2 * far)
    far_masks = [2 * middle * j for j in range(far)]
    middle_masks = [2 * j for j in range(middle)]
    layout = [
        [core + mid + top for top in far_masks] for core in (0, 1) for mid in middle_masks
    ]
    piece = (depth * block_rows, width_y)
    group = (far,) + piece

    field_shape = on_chip(3, depth + 1, width_x + 2 * PAD, width_y)
    curls_shape = on_chip(3, depth, width_x, width_y)
    halo_shape = on_chip(2, width_x, width_y)
    total_shape = on_chip(depth, width_x + 2 * PAD, width_y)
    edges_shape = on_chip(2, width_x + 2 * PAD, width_y)
    coef_shape = on_chip(depth, width_x, width_y)
    plane = on_chip(width_x, width_y)

    def by_owner(kernel, layers, operands, specs, scratch, micros):
        shape = on_chip(far, layers * block_rows, width_y)
        parts = call(
            kernel,
            [shape] * len(layout),
            [IN_VMEM] * len(layout),
            operands,
            specs,
            scratch,
            micros=micros,
        )
        got = [swap_over(part, "grp", 1) for part in parts[middle:]]
        sums = call(
            add_kernel,
            [shape] * middle,
            [IN_VMEM] * middle,
            list(parts[:middle]) + got,
            [IN_VMEM] * (2 * middle),
        )
        return [sums[0]] + [
            swap_over(part, "grp", mask) for part, mask in zip(sums[1:], middle_masks[1:])
        ]

    design = density.reshape(piece)
    got = [swap_over(design, "grp", mask) for mask in far_masks[1:]]
    own, drives, *pays = call(
        opening_kernel,
        [on_chip(*piece), on_chip(STEPS, width_y)] + [on_chip(2, 2, width_x, width_y)] * npay,
        [IN_VMEM] * (2 + npay),
        [fwd_fields, adj_fields, design, wave_idx],
        [IN_HBM] * 3 + [IN_SMEM],
        [pltpu.VMEM((2, 5, width_x, width_y), F32), pltpu.SemaphoreType.DMA((3, 5))],
    )
    below, above = trade(pays)

    near = call(pack_kernel, on_chip(*group), IN_VMEM, [own] + got, [IN_VMEM] * far)
    others = [swap_over(near, "grp", mask) for mask in middle_masks[1:]]
    near_across = swap_over(near, "grp", 1)

    e_fwd, h_fwd, curls_fwd, total, edges, forced, base, place = call(
        functools.partial(first_fwd_kernel, layout),
        [
            field_shape,
            field_shape,
            curls_shape,
            total_shape,
            edges_shape,
            on_chip(depth, width_x, width_y),
            plane,
            on_chip(nblock, nblock, width_y),
        ],
        [IN_VMEM] * 8,
        [fwd_fields, near, source_pos, block_ids, material_idx, material_eps],
        [IN_VMEM] * 2 + [IN_HBM] * 4,
        [
            pltpu.SMEM(source_pos.shape, jnp.int32),
            pltpu.SMEM(block_ids.shape, jnp.int32),
            pltpu.SMEM(material_idx.shape, jnp.int32),
            pltpu.SMEM(material_eps.shape, F32),
            pltpu.SemaphoreType.DMA((4,)),
        ],
        micros=1.5,
    )
    e_adj, h_adj, curls_adj = call(
        first_kernel,
        [field_shape, field_shape, curls_shape],
        [IN_VMEM] * 3,
        [adj_fields, near],
        [IN_VMEM, IN_VMEM],
        micros=1.2,
    )
    others = [tie(part, [e_fwd, e_adj]) for part in others]
    early = [near] + others + [near_across]
    last = [swap_over(part, "grp", 1) for part in others]
    first_slot = far * len(early)

    h_fwd, curls_fwd, h_adj, curls_adj, blocks = call(
        functools.partial(settle_kernel, layout[: len(early)]),
        [field_shape, curls_shape] * 2 + [on_chip(nblock, *piece)],
        [IN_VMEM] * 5,
        [h_fwd, curls_fwd, h_adj, curls_adj, e_fwd, e_adj, below, above] + early + [block_ids],
        [IN_VMEM] * (8 + len(early)) + [IN_HBM],
        [pltpu.SMEM(block_ids.shape, jnp.int32), pltpu.SemaphoreType.DMA],
        aliases={0: 0, 1: 1, 2: 2, 3: 3},
        micros=0.6,
    )
    placed = pltpu.VMEM((2, width_x + 2 * PAD, width_y), F32)
    coef = call(
        functools.partial(coef_edge_kernel, first_slot, len(last)),
        coef_shape,
        IN_VMEM,
        last + [place, base, blocks],
        [IN_VMEM] * (len(last) + 3),
        [placed],
    )

    arrived_fwd, arrived_adj = [curls_fwd], [curls_adj]
    for step in range(STEPS):
        more = npay if step < STEPS - 1 else 0

        def edge_fwd(e_fwd, h_fwd):
            return call(
                functools.partial(edge_kernel, step, 0),
                [field_shape] * 2 + [halo_shape] * more,
                [IN_VMEM] * (2 + more),
                [e_fwd, h_fwd, coef, drives, forced] + arrived_fwd,
                [IN_VMEM] * (5 + len(arrived_fwd)),
                aliases={0: 0, 1: 1},
            )

        if more:
            e_fwd, h_fwd, *pays = edge_fwd(e_fwd, h_fwd)
            arrived_fwd_next = trade(pays)
        if step > 0:
            e_adj, h_adj, e_fwd, total = call(
                functools.partial(inner_kernel, step, 1),
                [field_shape] * 3 + [total_shape],
                [IN_VMEM] * 4,
                [e_adj, h_adj, e_fwd, total, coef],
                [IN_VMEM] * 5,
                aliases={0: 0, 1: 1, 2: 2, 3: 3},
                micros=1.2,
            )
        if not more:
            e_fwd, h_fwd = edge_fwd(e_fwd, h_fwd)
            inner = by_owner(
                functools.partial(filter_inner_kernel, layout),
                depth - 2,
                [total, e_fwd, block_ids],
                [IN_VMEM, IN_VMEM, IN_HBM],
                [
                    pltpu.VMEM((nblock,) + piece, F32),
                    pltpu.VMEM((2, width_x, width_y), F32),
                    pltpu.SMEM(block_ids.shape, jnp.int32),
                    pltpu.SemaphoreType.DMA,
                ],
                0.8,
            )
        e_adj, h_adj, e_fwd, edges, *pays = call(
            functools.partial(edge_kernel, step, 1),
            [field_shape] * 3 + [edges_shape] + [halo_shape] * more,
            [IN_VMEM] * (4 + more),
            [e_adj, h_adj, e_fwd, edges, coef] + arrived_adj,
            [IN_VMEM] * (5 + len(arrived_adj)),
            aliases={0: 0, 1: 1, 2: 2, 3: 3},
        )
        if not more:
            break
        arrived_fwd, arrived_adj = arrived_fwd_next, trade(pays)
        if step == 0:
            coef = call(
                functools.partial(coef_inner_kernel, first_slot, len(last)),
                coef_shape,
                IN_VMEM,
                [coef] + last + [place, base, blocks],
                [IN_VMEM] * (len(last) + 4),
                [placed],
                aliases={0: 0},
                micros=0.6,
            )
            e_fwd, e_adj, total = call(
                begin_kernel,
                [field_shape, field_shape, total_shape],
                [IN_VMEM] * 3,
                [e_fwd, e_adj, total, coef, drives, forced, curls_fwd, curls_adj],
                [IN_VMEM] * 8,
                aliases={0: 0, 1: 1, 2: 2},
                micros=0.5,
            )
        e_fwd, h_fwd = call(
            functools.partial(inner_kernel, step + 1, 0),
            [field_shape] * 2,
            [IN_VMEM] * 2,
            [e_fwd, h_fwd, coef, drives, forced],
            [IN_VMEM] * 5,
            aliases={0: 0, 1: 1},
            micros=1.1,
        )

    ends = by_owner(
        functools.partial(filter_edge_kernel, layout),
        2,
        [total, edges, place],
        [IN_VMEM] * 3,
        [
            pltpu.VMEM((2, width_x + 2 * PAD, width_y), F32),
            pltpu.VMEM((2, width_x, width_y), F32),
        ],
        0.3,
    )
    pieces = call(
        functools.partial(join_kernel, middle, block_rows),
        [on_chip(*piece)] * far,
        [IN_VMEM] * far,
        inner + ends,
        [IN_VMEM] * (2 * middle),
    )
    got = [swap_over(part, "grp", mask) for part, mask in zip(pieces[1:], far_masks[1:])]
    scale = 3.0 / (STEPS * math.sqrt(ngrp))
    grad = call(
        functools.partial(last_kernel, scale),
        jax.ShapeDtypeStruct(piece, F32),
        IN_VMEM,
        [pieces[0]] + got,
        [IN_VMEM] * far,
    )
    finals = call(
        out_kernel,
        jax.ShapeDtypeStruct(fwd_fields.shape, F32),
        IN_HBM,
        [e_fwd, h_fwd],
        [IN_VMEM] * 2,
        [
            pltpu.VMEM((3, depth, width_x, width_y), F32),
            pltpu.SemaphoreType.DMA((6,)),
        ],
        micros=1.7,
    )
    return finals, grad.reshape(density.shape)


def solution(mesh):
    placed = (
        P("grp", None, "slab", None, None),
        P("grp", None, "slab", None, None),
        P("slab", "grp", None),
        P(),
        P(),
        P(),
        P("grp", None),
        P("grp"),
    )
    return jax.shard_map(
        per_device,
        mesh=mesh,
        in_specs=placed,
        out_specs=(P("grp", None, "slab", None, None), P("slab", "grp", None)),
        check_vma=False,
    )
```

```python
import functools
import math

import jax
import jax.numpy as jnp
from jax import lax
from jax.experimental import pallas as pl
from jax.experimental.pallas import tpu as pltpu
from jax.sharding import PartitionSpec as P

STEPS = 4
AMPLITUDE = 4.0
PAD = 8
F32 = jnp.float32
HBM_PER_MICRO = 1.0e5

VMEM = pltpu.MemorySpace.VMEM
IN_VMEM = pl.BlockSpec(memory_space=pltpu.VMEM)
IN_SMEM = pl.BlockSpec(memory_space=pltpu.SMEM)
IN_HBM = pl.BlockSpec(memory_space=pltpu.MemorySpace.HBM)


def on_chip(*shape):
    return VMEM(shape, F32)


def held(array, spec):
    if spec is IN_SMEM:
        return array
    space = VMEM if spec is IN_VMEM else pltpu.MemorySpace.HBM
    return pltpu.with_memory_space_constraint(array, space)


def call(kernel, outs, out_specs, operands, specs, scratch=(), aliases=None, micros=0.3):
    operands = [held(a, s) for a, s in zip(operands, specs)]
    return pl.pallas_call(
        kernel,
        out_shape=outs,
        in_specs=specs,
        out_specs=out_specs,
        scratch_shapes=scratch,
        input_output_aliases=aliases or {},
        compiler_params=pltpu.CompilerParams(vmem_limit_bytes=8 << 20),
        cost_estimate=pl.CostEstimate(
            flops=0, bytes_accessed=int(micros * HBM_PER_MICRO), transcendentals=0
        ),
    )(*operands)


CHUNK = 16


def chunks(rows):
    size = CHUNK if rows % CHUNK == 0 else rows
    return [(first, size) for first in range(0, rows, size)]


def next_col(value):
    column = lax.broadcasted_iota(jnp.int32, value.shape, 1)
    moved = pltpu.roll(value, value.shape[1] - 1, 1)
    return jnp.where(column == value.shape[1] - 1, 0.0, moved)


def prev_col(value):
    column = lax.broadcasted_iota(jnp.int32, value.shape, 1)
    return jnp.where(column == 0, 0.0, pltpu.roll(value, 1, 1))


def neighbours():
    slab = lax.axis_index("slab")
    return slab < lax.axis_size("slab") - 1, slab > 0


class Window:
    def __init__(self, e, h, coef=None, force=None):
        self.e, self.h, self.coef, self.force = e, h, coef, force
        self.rows = e.shape[2] - 2 * PAD
        self.depth = e.shape[1] - 1
        self.top, self.under = self.depth - 1, self.depth

    def read(self, ref, layer, first, size):
        return [ref[c, layer, pl.ds(PAD + first, size), :] for c in range(3)]

    def write(self, ref, layer, first, size, values):
        for c, value in enumerate(values):
            ref[c, layer, pl.ds(PAD + first, size), :] = value

    def put_h(self, layer, given=None, alone=False):
        for first, size in chunks(self.rows):
            rows = pl.ds(PAD + first, size)
            after = pl.ds(PAD + first + 1, size)
            ex, ey, ez = self.read(self.e, layer, first, size)
            if given is None:
                hx, hy, hz = self.read(self.h, layer, first, size)
            else:
                hx, hy, hz = (value + value for value in given(layer, first, size))
            if alone:
                rise_x, rise_y = -ex, -ey
            else:
                rise_x = self.e[0, layer + 1, rows, :] - ex
                rise_y = self.e[1, layer + 1, rows, :] - ey
            ey_after = self.e[1, layer, after, :]
            ez_after = self.e[2, layer, after, :]
            hx = hx - ((next_col(ez) - ez) - rise_y)
            hy = hy - (rise_x - (ez_after - ez))
            hz = hz - ((ey_after - ey) - (next_col(ex) - ex))
            self.write(self.h, layer, first, size, (hx, hy, hz))

    def curl_h(self, layer, lower, first, size):
        rows = pl.ds(PAD + first, size)
        before = pl.ds(PAD + first - 1, size)
        hx, hy, hz = self.read(self.h, layer, first, size)
        step_x = hx - self.h[0, lower, rows, :]
        step_y = hy - self.h[1, lower, rows, :]
        hy_before = self.h[1, layer, before, :]
        hz_before = self.h[2, layer, before, :]
        return (
            (hz - prev_col(hz)) - step_y,
            step_x - (hz - hz_before),
            (hy - hy_before) - (hx - prev_col(hx)),
        )

    def put_curl(self, curls, layer, lower):
        for first, size in chunks(self.rows):
            for c, value in enumerate(self.curl_h(layer, lower, first, size)):
                curls[c, layer, pl.ds(first, size), :] = value

    def next_e(self, layer, lower, first, size, curls=None):
        here = pl.ds(first, size)
        cell = self.coef[layer, here, :]
        if curls is None:
            curl = self.curl_h(layer, lower, first, size)
        else:
            curl = [curls[c, layer, here, :] for c in range(3)]
        ex, ey, ez = [a + cell * b for a, b in zip(self.read(self.e, layer, first, size), curl)]
        if self.force is not None:
            ez = ez + self.force(layer, here)
        return ex, ey, ez

    def put_e(self, layer, lower, curls=None, other=None, total=None, slot=None):
        for first, size in chunks(self.rows):
            news = self.next_e(layer, lower, first, size, curls)
            self.write(self.e, layer, first, size, news)
            if total is not None:
                rows = pl.ds(PAD + first, size)
                part = [a * other[c, layer, rows, :] for c, a in enumerate(news)]
                total[layer if slot is None else slot, rows, :] += part[0] + part[1] + part[2]

    def take_above(self, above):
        for first, size in chunks(self.rows):
            here, rows = pl.ds(first, size), pl.ds(PAD + first, size)
            self.h[0, self.top, rows, :] += above[1, here, :]
            self.h[1, self.top, rows, :] -= above[0, here, :]

    def take_below(self, below):
        for first, size in chunks(self.rows):
            here, rows = pl.ds(first, size), pl.ds(PAD + first, size)
            self.h[0, self.under, rows, :] = below[0, here, :] + self.e[1, 0, rows, :]
            self.h[1, self.under, rows, :] = below[1, here, :] - self.e[0, 0, rows, :]


def forcing(step, drives, forced):
    if drives is None:
        return None
    return lambda layer, here: drives[pl.ds(step, 1), :] * forced[layer, here, :]


def opening_kernel(fwd, adj, density, own, *rest):
    pays, (planes, sems) = rest[:-2], rest[-2:]
    depth, rows, width_y = fwd.shape[2:]
    top = depth - 1
    has_up, has_low = neighbours()
    held_copy = pltpu.make_async_copy(density, own, sems.at[2, 0])
    held_copy.start()

    def up(pay):
        copies = []
        for evo, given in enumerate((fwd, adj)):
            for c in range(5):
                copies.append(
                    pltpu.make_async_copy(given.at[0, c, top], planes.at[evo, c], sems.at[evo, c])
                )
        for copy in copies:
            copy.start()
        for copy in copies:
            copy.wait()
        for evo in range(2):
            for first, size in chunks(rows):
                here = pl.ds(first, size)
                ex, ey, ez, hx, hy = (planes[evo, c, here, :] for c in range(5))
                if first + size < rows:
                    ez_after = planes[evo, 2, pl.ds(first + 1, size), :]
                else:
                    row = lax.broadcasted_iota(jnp.int32, ez.shape, 0)
                    ez_after = jnp.where(row == size - 1, 0.0, pltpu.roll(ez, size - 1, 0))
                pay[evo, 0, here, :] = (hx + hx) - ((next_col(ez) - ez) + ey)
                pay[evo, 1, here, :] = (hy + hy) + (ex + (ez_after - ez))

    def down(pay):
        copies = []
        for evo, given in enumerate((fwd, adj)):
            for c in range(2):
                copies.append(
                    pltpu.make_async_copy(given.at[0, c, 0], pay.at[evo, c], sems.at[evo, c])
                )
        for copy in copies:
            copy.start()
        for copy in copies:
            copy.wait()

    if len(pays) == 2:
        up(pays[0])
        down(pays[1])
    else:
        pl.when(has_up)(lambda: up(pays[0]))
        pl.when(has_low)(lambda: down(pays[0]))
    held_copy.wait()


def first_fwd_kernel(
    layout, given, near, wave_idx, source_far, ids_far, idx_far, eps_far,
    e, h, curls, total, edges, forced, drives, base, place,
    source, block_ids, material_idx, material_eps, sems,
):
    fetches = [
        pltpu.make_async_copy(far, here, sems.at[slot])
        for slot, (far, here) in enumerate(
            (
                (source_far, source),
                (ids_far, block_ids),
                (idx_far, material_idx),
                (eps_far, material_eps),
            )
        )
    ]
    for fetch in fetches:
        fetch.start()
    first_kernel(given, near, e, h, curls)
    depth, rows, width_y = forced.shape
    nblock = block_ids.shape[0]
    block_rows = rows // nblock
    empty = jnp.zeros(total.shape[1:], F32)
    edges[0] = empty
    edges[1] = empty
    for layer in range(depth):
        total[layer] = empty
    for fetch in fetches:
        fetch.wait()
    xcoord = lax.broadcasted_iota(jnp.int32, (rows, width_y), 0)
    ycoord = lax.broadcasted_iota(jnp.int32, (rows, width_y), 1)
    offset_x = (xcoord - source[0, 1]).astype(F32) / (rows / 4.0)
    offset_y = (ycoord - source[0, 2]).astype(F32) / (width_y / 4.0)
    profile = jnp.exp(-0.5 * (offset_x * offset_x + offset_y * offset_y))
    step = lax.broadcasted_iota(jnp.int32, drives.shape, 0).astype(F32) + 1.0
    wave = jnp.full(drives.shape, wave_idx[0], jnp.int32).astype(F32)
    drives[...] = AMPLITUDE * jnp.sin(2.0 * math.pi / (6.0 + 2.0 * wave) * step)
    level = source[0, 0] - lax.axis_index("slab") * depth
    for layer in range(depth):
        forced[layer] = jnp.where(level == layer, 1.0, 0.0) * profile
    for block in range(nblock):
        value = jnp.full((block_rows, width_y), material_eps[material_idx[block]], F32)
        base[pl.ds(block * block_rows, block_rows), :] = value
    me = lax.axis_index("grp")
    block = lax.broadcasted_iota(jnp.int32, (nblock, width_y), 0)
    for slot, mask in enumerate(mask for masks in layout for mask in masks):
        place[slot] = jnp.where(block == block_ids[me ^ mask], 1.0, 0.0)


def first_kernel(given, near, e, h, curls):
    win = Window(e, h)
    rows, width_y = win.rows, e.shape[3]
    margin = jnp.zeros((PAD, width_y), F32)
    empty = jnp.zeros((rows + 2 * PAD, width_y), F32)
    for comp in range(3):
        e[comp, win.depth] = empty
        h[comp, win.depth] = empty

    def copy(layer):
        for comp in range(3):
            for ref in (e, h):
                ref[comp, layer, pl.ds(0, PAD), :] = margin
                ref[comp, layer, pl.ds(PAD + rows, PAD), :] = margin
            for first, size in chunks(rows):
                here = pl.ds(first, size)
                e[comp, layer, pl.ds(PAD + first, size), :] = given[0, comp, layer, here, :]

    def from_given(layer, first, size):
        return [given[0, 3 + c, layer, pl.ds(first, size), :] for c in range(3)]

    copy(0)
    copy(1)
    win.put_h(0, from_given)
    copy(2)
    win.put_h(1, from_given)

    def body(layer, carry):
        pl.when(layer + 2 < win.depth)(lambda: copy(layer + 2))
        win.put_h(layer + 1, from_given)
        win.put_curl(curls, layer, layer - 1)
        return carry

    lax.fori_loop(1, win.top, body, 0)


def settle_kernel(layout, *refs):
    refs = list(refs)
    del refs[:4]
    e_fwd, e_adj, below, above = (refs.pop(0) for _ in range(4))
    parts = [refs.pop(0) for _ in layout]
    ids_far, h_fwd, curls_fwd, h_adj, curls_adj, blocks, block_ids, sem = refs
    fetch = pltpu.make_async_copy(ids_far, block_ids, sem)
    fetch.start()
    nothing = jnp.zeros(blocks.shape[1:], F32)
    for block in range(blocks.shape[0]):
        blocks[block] = nothing
    has_up, has_low = neighbours()
    for evo, (e, h, curls) in enumerate(((e_fwd, h_fwd, curls_fwd), (e_adj, h_adj, curls_adj))):
        win = Window(e, h)
        pl.when(has_up)(lambda: win.take_above(above.at[evo]))
        pl.when(has_low)(lambda: win.take_below(below.at[evo]))
        win.put_curl(curls, win.top, win.top - 1)
        win.put_curl(curls, 0, win.under)
    fetch.wait()
    me = lax.axis_index("grp")
    for part, masks in zip(parts, layout):
        for slot, mask in enumerate(masks):
            blocks[block_ids[me ^ mask]] = part[slot]


def edge_kernel(step, evo, *refs):
    refs = list(refs)
    e_in, h_in = refs.pop(0), refs.pop(0)
    if evo == 1:
        other_in, edges_in = refs.pop(0), refs.pop(0)
    coef = refs.pop(0)
    drives, forced = (refs.pop(0), refs.pop(0)) if evo == 0 else (None, None)
    curls = refs.pop(0) if step == 0 else None
    below, above = (refs.pop(0), refs.pop(0)) if step > 0 else (None, None)
    e, h = refs.pop(0), refs.pop(0)
    other, edges = (refs.pop(0), refs.pop(0)) if evo == 1 else (None, None)
    pays = refs
    win = Window(e, h, coef, forcing(step, drives, forced))
    top = win.top
    has_up, has_low = neighbours()

    @pl.when(has_up)
    def _():
        if step > 0:
            win.take_above(above)
        win.put_e(top, top - 1, curls, other, edges, 1)
        if pays:
            win.put_h(top, alone=True)
            for c in range(2):
                pays[0][c] = h[c, top, pl.ds(PAD, win.rows), :]

    @pl.when(has_low)
    def _():
        if step > 0:
            win.take_below(below)
        win.put_e(0, win.under, curls, other, edges, 0)
        if pays:
            for c in range(2):
                pays[-1][c] = e[c, 0, pl.ds(PAD, win.rows), :]


def inner_range(top):
    has_up, has_low = neighbours()
    return jnp.where(has_low, 1, 0), jnp.where(has_up, top - 1, top)


def begin_kernel(
    e_fwd_in, e_adj_in, total_in, coef, drives, forced, curls_fwd, curls_adj,
    e_fwd, e_adj, total,
):
    fwd = Window(e_fwd, None, coef, forcing(0, drives, forced))
    adj = Window(e_adj, None, coef)
    lowest, highest = inner_range(fwd.top)

    def body(layer, carry):
        fwd.put_e(layer, None, curls_fwd)
        adj.put_e(layer, None, curls_adj, e_fwd, total)
        return carry

    lax.fori_loop(lowest, highest + 1, body, 0)


def inner_kernel(step, evo, *refs):
    refs = list(refs)
    e_in, h_in = refs.pop(0), refs.pop(0)
    if evo == 1:
        other_in, total_in = refs.pop(0), refs.pop(0)
    coef = refs.pop(0)
    drives, forced = (refs.pop(0), refs.pop(0)) if evo == 0 else (None, None)
    e, h = refs.pop(0), refs.pop(0)
    other, total = (refs.pop(0), refs.pop(0)) if evo == 1 else (None, None)
    win = Window(e, h, coef, forcing(step, drives, forced))
    lowest, highest = inner_range(win.top)
    win.put_h(0)
    pl.when(lowest == 1)(lambda: win.put_h(1))

    def body(layer, carry):
        win.put_h(layer + 1)
        win.put_e(layer, jnp.where(layer == 0, win.under, layer - 1), None, other, total)
        return carry

    if lax.axis_size("slab") == 2:
        lax.fori_loop(0, win.depth - 2, lambda i, carry: body(lowest + i, carry), 0, unroll=2)
    else:
        lax.fori_loop(lowest, highest, body, 0)
    win.put_e(highest, highest - 1, None, other, total)


def coef_layer(layer, coef, placed, base):
    for first, size in chunks(base.shape[0]):
        here = pl.ds(first, size)
        coef[layer, here, :] = 0.25 / (base[here, :] + 3.0 * filtered(placed, first, size))


def clear_margins(placed):
    rows = placed.shape[0] - 2 * PAD
    margin = jnp.zeros((PAD, placed.shape[1]), F32)
    placed[pl.ds(0, PAD), :] = margin
    placed[pl.ds(PAD + rows, PAD), :] = margin


def place_layer(layer, first_slot, parts, place, blocks, placed):
    nblock = blocks.shape[0]
    block_rows = (placed.shape[0] - 2 * PAD) // nblock
    clear_margins(placed)
    start = layer * block_rows
    source = pl.ds(start if isinstance(layer, int) else pl.multiple_of(start, block_rows), block_rows)
    pieces = [part[slot, source, :] for part in parts for slot in range(part.shape[0])]
    for block in range(nblock):
        value = blocks[block, source, :]
        for slot, piece in enumerate(pieces):
            value = value + place[first_slot + slot, pl.ds(block, 1), :] * piece
        placed[pl.ds(PAD + block * block_rows, block_rows), :] = value


def coef_edge_kernel(first_slot, count, *refs):
    parts, (place, base, blocks, coef, placed) = refs[:count], refs[count:]
    edge_layers = (0, coef.shape[0] - 1)
    for which, layer in enumerate(edge_layers):
        place_layer(layer, first_slot, parts, place, blocks, placed.at[which])
    for which, layer in enumerate(edge_layers):
        coef_layer(layer, coef, placed.at[which], base)


def coef_inner_kernel(first_slot, count, coef_in, *refs):
    parts, (place, base, blocks, coef, placed) = refs[:count], refs[count:]

    def body(layer, carry):
        there = placed.at[lax.rem(layer, 2)]
        place_layer(layer, first_slot, parts, place, blocks, there)
        coef_layer(layer, coef, there, base)
        return carry

    lax.fori_loop(1, coef.shape[0] - 1, body, 0, unroll=2)


def filtered(padded, first, size):
    here = padded[pl.ds(PAD + first, size), :]
    before = padded[pl.ds(PAD + first - 1, size), :]
    after = padded[pl.ds(PAD + first + 1, size), :]
    along = before + 2.0 * here + after
    return (prev_col(along) + 2.0 * along + next_col(along)) * 0.0625


def tie_kernel(*refs):
    pass


def tie(array, others):
    return call(
        tie_kernel, on_chip(*array.shape), IN_VMEM, [array] + others,
        [IN_VMEM] * (1 + len(others)), aliases={0: 0},
    )


def pack_kernel(*refs):
    out = refs[-1]
    for slot, ref in enumerate(refs[:-1]):
        out[slot] = ref[...]


def filter_inner_kernel(layout, total, after, block_ids_far, *rest):
    parts, (blocks, wide, block_ids, sem) = rest[:-4], rest[-4:]
    fetch = pltpu.make_async_copy(block_ids_far, block_ids, sem)
    fetch.start()
    depth = total.shape[0]
    nblock = blocks.shape[0]
    rows = wide.shape[1]
    block_rows = rows // nblock
    me = lax.axis_index("grp")

    def body(layer, carry):
        there = wide.at[lax.rem(layer, 2)]
        for first, size in chunks(rows):
            there[pl.ds(first, size), :] = filtered(total.at[layer], first, size)
        for block in range(nblock):
            target = pl.ds(pl.multiple_of((layer - 1) * block_rows, block_rows), block_rows)
            blocks[block, target, :] = there[pl.ds(block * block_rows, block_rows), :]
        return carry

    lax.fori_loop(1, depth - 1, body, 0, unroll=2)
    fetch.wait()
    inner = pl.ds(0, (depth - 2) * block_rows)
    for part, masks in zip(parts, layout):
        for slot, mask in enumerate(masks):
            part[slot] = blocks[block_ids[me ^ mask], inner, :]


def filter_edge_kernel(layout, total, edges, place, *rest):
    parts, (sums, wide) = rest[:-2], rest[-2:]
    depth = total.shape[0]
    nblock = place.shape[0]
    rows = wide.shape[1]
    block_rows = rows // nblock
    for which, layer in enumerate((0, depth - 1)):
        sums[which] = total[layer] + edges[which]
        for first, size in chunks(rows):
            wide[which, pl.ds(first, size), :] = filtered(sums.at[which], first, size)
    for which in range(2):
        blocks = [
            wide[which, pl.ds(block * block_rows, block_rows), :] for block in range(nblock)
        ]
        target = pl.ds(which * block_rows, block_rows)
        for slot in range(nblock):
            value = None
            for block, piece in enumerate(blocks):
                term = place[slot, pl.ds(block, 1), :] * piece
                value = term if value is None else value + term
            parts[slot // parts[0].shape[0]][slot % parts[0].shape[0], target, :] = value


def add_kernel(count, *refs):
    for a, b, out in zip(refs[:count], refs[count : 2 * count], refs[-count:]):
        out[...] = a[...] + b[...]


def join_kernel(count, block_rows, *refs):
    inner, edge, outs = refs[:count], refs[count : 2 * count], refs[2 * count :]
    rows = outs[0].shape[0]
    for slot, out in enumerate(outs):
        middle, ends = inner[0][slot], edge[0][slot]
        for a, b in zip(inner[1:], edge[1:]):
            middle, ends = middle + a[slot], ends + b[slot]
        out[pl.ds(0, block_rows), :] = ends[:block_rows]
        out[pl.ds(block_rows, rows - 2 * block_rows), :] = middle
        out[pl.ds(rows - block_rows, block_rows), :] = ends[block_rows:]


def last_kernel(scale, *refs):
    value = refs[0][...]
    for ref in refs[1:-1]:
        value = value + ref[...]
    refs[-1][...] = value * scale


def out_kernel(e, h, finals, halves, sems):
    depth = e.shape[1] - 1
    rows = e.shape[2] - 2 * PAD
    every = pl.ds(PAD, rows)
    copies = [
        pltpu.make_async_copy(e.at[c, pl.ds(0, depth), every, :], finals.at[0, c], sems.at[c])
        for c in range(3)
    ]
    for copy in copies:
        copy.start()
    for c in range(3):

        def body(layer, carry, c=c):
            halves[c, layer] = 0.5 * h[c, layer, every, :]
            return carry

        lax.fori_loop(0, depth, body, 0)
        copy = pltpu.make_async_copy(halves.at[c], finals.at[0, 3 + c], sems.at[3 + c])
        copy.start()
        copies.append(copy)
    for copy in copies:
        copy.wait()


def swap_over(array, axis, mask):
    return lax.ppermute(array, axis, [(i, i ^ mask) for i in range(lax.axis_size(axis))])


def shift_over(array, axis, distance):
    size = lax.axis_size(axis)
    route = [(i, i + distance) for i in range(size) if 0 <= i + distance < size]
    return lax.ppermute(array, axis, route)


def trade(pays):
    if len(pays) == 1:
        return [swap_over(pays[0], "slab", 1)] * 2
    return [shift_over(pays[0], "slab", 1), shift_over(pays[1], "slab", -1)]


def per_device(
    fwd_fields, adj_fields, density, block_ids, material_idx, material_eps, source_pos, wave_idx
):
    depth, width_x, width_y = fwd_fields.shape[2:]
    nblock = block_ids.shape[0]
    block_rows = width_x // nblock
    ngrp = lax.axis_size("grp")
    npay = 1 if lax.axis_size("slab") == 2 else 2

    far = 4
    middle = ngrp // (2 * far)
    far_masks = [2 * middle * j for j in range(far)]
    middle_masks = [2 * j for j in range(middle)]
    layout = [
        [core + mid + top for top in far_masks] for core in (0, 1) for mid in middle_masks
    ]
    piece = (depth * block_rows, width_y)
    group = (far,) + piece

    field_shape = on_chip(3, depth + 1, width_x + 2 * PAD, width_y)
    curls_shape = on_chip(3, depth, width_x, width_y)
    halo_shape = on_chip(2, width_x, width_y)
    total_shape = on_chip(depth, width_x + 2 * PAD, width_y)
    edges_shape = on_chip(2, width_x + 2 * PAD, width_y)
    coef_shape = on_chip(depth, width_x, width_y)
    plane = on_chip(width_x, width_y)

    def by_owner(kernel, layers, operands, specs, scratch, micros):
        shape = on_chip(far, layers * block_rows, width_y)
        parts = call(
            kernel,
            [shape] * len(layout),
            [IN_VMEM] * len(layout),
            operands,
            specs,
            scratch,
            micros=micros,
        )
        return list(parts[:middle]), [swap_over(part, "grp", 1) for part in parts[middle:]]

    def add_middle(kept, got, after):
        sums = call(
            functools.partial(add_kernel, middle),
            [on_chip(*part.shape) for part in kept],
            [IN_VMEM] * middle,
            kept + got + after,
            [IN_VMEM] * (2 * middle + len(after)),
        )
        return [sums[0]] + [
            swap_over(part, "grp", mask) for part, mask in zip(sums[1:], middle_masks[1:])
        ]

    design = density.reshape(piece)
    got = [swap_over(design, "grp", mask) for mask in far_masks[1:]]
    own, *pays = call(
        opening_kernel,
        [on_chip(*piece)] + [on_chip(2, 2, width_x, width_y)] * npay,
        [IN_VMEM] * (1 + npay),
        [fwd_fields, adj_fields, design],
        [IN_HBM] * 3,
        [pltpu.VMEM((2, 5, width_x, width_y), F32), pltpu.SemaphoreType.DMA((3, 5))],
    )
    below, above = trade(pays)

    near = call(pack_kernel, on_chip(*group), IN_VMEM, [own] + got, [IN_VMEM] * far)
    others = [swap_over(near, "grp", mask) for mask in middle_masks[1:]]
    near_across = swap_over(near, "grp", 1)

    e_fwd, h_fwd, curls_fwd, total, edges, forced, drives, base, place = call(
        functools.partial(first_fwd_kernel, layout),
        [
            field_shape,
            field_shape,
            curls_shape,
            total_shape,
            edges_shape,
            on_chip(depth, width_x, width_y),
            on_chip(STEPS, width_y),
            plane,
            on_chip(nblock, nblock, width_y),
        ],
        [IN_VMEM] * 9,
        [fwd_fields, near, wave_idx, source_pos, block_ids, material_idx, material_eps],
        [IN_VMEM] * 2 + [IN_SMEM] + [IN_HBM] * 4,
        [
            pltpu.SMEM(source_pos.shape, jnp.int32),
            pltpu.SMEM(block_ids.shape, jnp.int32),
            pltpu.SMEM(material_idx.shape, jnp.int32),
            pltpu.SMEM(material_eps.shape, F32),
            pltpu.SemaphoreType.DMA((4,)),
        ],
        micros=1.5,
    )
    e_adj, h_adj, curls_adj = call(
        first_kernel,
        [field_shape, field_shape, curls_shape],
        [IN_VMEM] * 3,
        [adj_fields, near],
        [IN_VMEM, IN_VMEM],
        micros=1.2,
    )
    others = [tie(part, [e_fwd, e_adj]) for part in others]
    early = [near] + others + [near_across]
    last = [swap_over(part, "grp", 1) for part in others]
    first_slot = far * len(early)

    h_fwd, curls_fwd, h_adj, curls_adj, blocks = call(
        functools.partial(settle_kernel, layout[: len(early)]),
        [field_shape, curls_shape] * 2 + [on_chip(nblock, *piece)],
        [IN_VMEM] * 5,
        [h_fwd, curls_fwd, h_adj, curls_adj, e_fwd, e_adj, below, above] + early + [block_ids],
        [IN_VMEM] * (8 + len(early)) + [IN_HBM],
        [pltpu.SMEM(block_ids.shape, jnp.int32), pltpu.SemaphoreType.DMA],
        aliases={0: 0, 1: 1, 2: 2, 3: 3},
        micros=0.6,
    )
    placed = pltpu.VMEM((2, width_x + 2 * PAD, width_y), F32)
    coef = call(
        functools.partial(coef_edge_kernel, first_slot, len(last)),
        coef_shape,
        IN_VMEM,
        last + [place, base, blocks],
        [IN_VMEM] * (len(last) + 3),
        [placed],
    )

    arrived_fwd, arrived_adj = [curls_fwd], [curls_adj]
    for step in range(STEPS):
        more = npay if step < STEPS - 1 else 0

        def edge_fwd(e_fwd, h_fwd):
            return call(
                functools.partial(edge_kernel, step, 0),
                [field_shape] * 2 + [halo_shape] * more,
                [IN_VMEM] * (2 + more),
                [e_fwd, h_fwd, coef, drives, forced] + arrived_fwd,
                [IN_VMEM] * (5 + len(arrived_fwd)),
                aliases={0: 0, 1: 1},
            )

        if more:
            e_fwd, h_fwd, *pays = edge_fwd(e_fwd, h_fwd)
            arrived_fwd_next = trade(pays)
        if step > 0:
            e_adj, h_adj, e_fwd, total = call(
                functools.partial(inner_kernel, step, 1),
                [field_shape] * 3 + [total_shape],
                [IN_VMEM] * 4,
                [e_adj, h_adj, e_fwd, total, coef],
                [IN_VMEM] * 5,
                aliases={0: 0, 1: 1, 2: 2, 3: 3},
                micros=1.2,
            )
        if not more:
            e_fwd, h_fwd = edge_fwd(e_fwd, h_fwd)
            inner = by_owner(
                functools.partial(filter_inner_kernel, layout),
                depth - 2,
                [total, e_fwd, block_ids],
                [IN_VMEM, IN_VMEM, IN_HBM],
                [
                    pltpu.VMEM((nblock,) + piece, F32),
                    pltpu.VMEM((2, width_x, width_y), F32),
                    pltpu.SMEM(block_ids.shape, jnp.int32),
                    pltpu.SemaphoreType.DMA,
                ],
                0.8,
            )
        if step == 0:
            coef = call(
                functools.partial(coef_inner_kernel, first_slot, len(last)),
                coef_shape,
                IN_VMEM,
                [coef] + last + [place, base, blocks],
                [IN_VMEM] * (len(last) + 4),
                [placed],
                aliases={0: 0},
                micros=0.6,
            )
            e_fwd, e_adj, total = call(
                begin_kernel,
                [field_shape, field_shape, total_shape],
                [IN_VMEM] * 3,
                [e_fwd, e_adj, total, coef, drives, forced, curls_fwd, curls_adj],
                [IN_VMEM] * 8,
                aliases={0: 0, 1: 1, 2: 2},
                micros=0.5,
            )
        e_adj, h_adj, e_fwd, edges, *pays = call(
            functools.partial(edge_kernel, step, 1),
            [field_shape] * 3 + [edges_shape] + [halo_shape] * more,
            [IN_VMEM] * (4 + more),
            [e_adj, h_adj, e_fwd, edges, coef] + arrived_adj,
            [IN_VMEM] * (5 + len(arrived_adj)),
            aliases={0: 0, 1: 1, 2: 2, 3: 3},
        )
        if not more:
            break
        arrived_fwd, arrived_adj = arrived_fwd_next, trade(pays)
        e_fwd, h_fwd = call(
            functools.partial(inner_kernel, step + 1, 0),
            [field_shape] * 2,
            [IN_VMEM] * 2,
            [e_fwd, h_fwd, coef, drives, forced],
            [IN_VMEM] * 5,
            aliases={0: 0, 1: 1},
            micros=1.1,
        )

    ends = by_owner(
        functools.partial(filter_edge_kernel, layout),
        2,
        [total, edges, place],
        [IN_VMEM] * 3,
        [
            pltpu.VMEM((2, width_x + 2 * PAD, width_y), F32),
            pltpu.VMEM((2, width_x, width_y), F32),
        ],
        0.3,
    )
    inner = add_middle(*inner, ends[0][:1])
    ends = add_middle(*ends, [])
    pieces = call(
        functools.partial(join_kernel, middle, block_rows),
        [on_chip(*piece)] * far,
        [IN_VMEM] * far,
        inner + ends,
        [IN_VMEM] * (2 * middle),
    )
    got = [swap_over(part, "grp", mask) for part, mask in zip(pieces[1:], far_masks[1:])]
    scale = 3.0 / (STEPS * math.sqrt(ngrp))
    grad = call(
        functools.partial(last_kernel, scale),
        jax.ShapeDtypeStruct(piece, F32),
        IN_VMEM,
        [pieces[0]] + got,
        [IN_VMEM] * far,
    )
    finals = call(
        out_kernel,
        jax.ShapeDtypeStruct(fwd_fields.shape, F32),
        IN_HBM,
        [e_fwd, h_fwd],
        [IN_VMEM] * 2,
        [
            pltpu.VMEM((3, depth, width_x, width_y), F32),
            pltpu.SemaphoreType.DMA((6,)),
        ],
        micros=1.7,
    )
    return finals, grad.reshape(density.shape)


def solution(mesh):
    placed = (
        P("grp", None, "slab", None, None),
        P("grp", None, "slab", None, None),
        P("slab", "grp", None),
        P(),
        P(),
        P(),
        P("grp", None),
        P("grp"),
    )
    return jax.shard_map(
        per_device,
        mesh=mesh,
        in_specs=placed,
        out_specs=(P("grp", None, "slab", None, None), P("slab", "grp", None)),
        check_vma=False,
    )
```

```python
import functools
import math

import jax
import jax.numpy as jnp
from jax import lax
from jax.experimental import pallas as pl
from jax.experimental.pallas import tpu as pltpu
from jax.sharding import PartitionSpec as P

STEPS = 4
AMPLITUDE = 4.0
PAD = 8
F32 = jnp.float32
HBM_PER_MICRO = 1.0e5

VMEM = pltpu.MemorySpace.VMEM
IN_VMEM = pl.BlockSpec(memory_space=pltpu.VMEM)
IN_SMEM = pl.BlockSpec(memory_space=pltpu.SMEM)
IN_HBM = pl.BlockSpec(memory_space=pltpu.MemorySpace.HBM)


def on_chip(*shape):
    return VMEM(shape, F32)


def held(array, spec):
    if spec is IN_SMEM:
        return array
    space = VMEM if spec is IN_VMEM else pltpu.MemorySpace.HBM
    return pltpu.with_memory_space_constraint(array, space)


def call(kernel, outs, out_specs, operands, specs, scratch=(), aliases=None, micros=0.3):
    operands = [held(a, s) for a, s in zip(operands, specs)]
    return pl.pallas_call(
        kernel,
        out_shape=outs,
        in_specs=specs,
        out_specs=out_specs,
        scratch_shapes=scratch,
        input_output_aliases=aliases or {},
        compiler_params=pltpu.CompilerParams(vmem_limit_bytes=8 << 20),
        cost_estimate=pl.CostEstimate(
            flops=0, bytes_accessed=int(micros * HBM_PER_MICRO), transcendentals=0
        ),
    )(*operands)


CHUNK = 16


def chunks(rows):
    size = CHUNK if rows % CHUNK == 0 else rows
    return [(first, size) for first in range(0, rows, size)]


def next_col(value):
    column = lax.broadcasted_iota(jnp.int32, value.shape, 1)
    moved = pltpu.roll(value, value.shape[1] - 1, 1)
    return jnp.where(column == value.shape[1] - 1, 0.0, moved)


def prev_col(value):
    column = lax.broadcasted_iota(jnp.int32, value.shape, 1)
    return jnp.where(column == 0, 0.0, pltpu.roll(value, 1, 1))


def neighbours():
    slab = lax.axis_index("slab")
    return slab < lax.axis_size("slab") - 1, slab > 0


class Window:
    def __init__(self, e, h, coef=None, force=None):
        self.e, self.h, self.coef, self.force = e, h, coef, force
        self.rows = e.shape[2] - 2 * PAD
        self.depth = e.shape[1] - 1
        self.top, self.under = self.depth - 1, self.depth

    def read(self, ref, layer, first, size):
        return [ref[c, layer, pl.ds(PAD + first, size), :] for c in range(3)]

    def write(self, ref, layer, first, size, values):
        for c, value in enumerate(values):
            ref[c, layer, pl.ds(PAD + first, size), :] = value

    def put_h(self, layer, given=None, alone=False):
        for first, size in chunks(self.rows):
            rows = pl.ds(PAD + first, size)
            after = pl.ds(PAD + first + 1, size)
            ex, ey, ez = self.read(self.e, layer, first, size)
            if given is None:
                hx, hy, hz = self.read(self.h, layer, first, size)
            else:
                hx, hy, hz = (value + value for value in given(layer, first, size))
            if alone:
                rise_x, rise_y = -ex, -ey
            else:
                rise_x = self.e[0, layer + 1, rows, :] - ex
                rise_y = self.e[1, layer + 1, rows, :] - ey
            ey_after = self.e[1, layer, after, :]
            ez_after = self.e[2, layer, after, :]
            hx = hx - ((next_col(ez) - ez) - rise_y)
            hy = hy - (rise_x - (ez_after - ez))
            hz = hz - ((ey_after - ey) - (next_col(ex) - ex))
            self.write(self.h, layer, first, size, (hx, hy, hz))

    def curl_h(self, layer, lower, first, size):
        rows = pl.ds(PAD + first, size)
        before = pl.ds(PAD + first - 1, size)
        hx, hy, hz = self.read(self.h, layer, first, size)
        step_x = hx - self.h[0, lower, rows, :]
        step_y = hy - self.h[1, lower, rows, :]
        hy_before = self.h[1, layer, before, :]
        hz_before = self.h[2, layer, before, :]
        return (
            (hz - prev_col(hz)) - step_y,
            step_x - (hz - hz_before),
            (hy - hy_before) - (hx - prev_col(hx)),
        )

    def put_curl(self, curls, layer, lower):
        for first, size in chunks(self.rows):
            for c, value in enumerate(self.curl_h(layer, lower, first, size)):
                curls[c, layer, pl.ds(first, size), :] = value

    def next_e(self, layer, lower, first, size, curls=None):
        here = pl.ds(first, size)
        cell = self.coef[layer, here, :]
        if curls is None:
            curl = self.curl_h(layer, lower, first, size)
        else:
            curl = [curls[c, layer, here, :] for c in range(3)]
        ex, ey, ez = [a + cell * b for a, b in zip(self.read(self.e, layer, first, size), curl)]
        if self.force is not None:
            ez = ez + self.force(layer, here)
        return ex, ey, ez

    def put_e(self, layer, lower, curls=None, other=None, total=None, slot=None):
        for first, size in chunks(self.rows):
            news = self.next_e(layer, lower, first, size, curls)
            self.write(self.e, layer, first, size, news)
            if total is not None:
                rows = pl.ds(PAD + first, size)
                part = [a * other[c, layer, rows, :] for c, a in enumerate(news)]
                total[layer if slot is None else slot, rows, :] += part[0] + part[1] + part[2]

    def take_above(self, above):
        for first, size in chunks(self.rows):
            here, rows = pl.ds(first, size), pl.ds(PAD + first, size)
            self.h[0, self.top, rows, :] += above[1, here, :]
            self.h[1, self.top, rows, :] -= above[0, here, :]

    def take_below(self, below):
        for first, size in chunks(self.rows):
            here, rows = pl.ds(first, size), pl.ds(PAD + first, size)
            self.h[0, self.under, rows, :] = below[0, here, :] + self.e[1, 0, rows, :]
            self.h[1, self.under, rows, :] = below[1, here, :] - self.e[0, 0, rows, :]


def forcing(step, drives, forced):
    if drives is None:
        return None
    return lambda layer, here: drives[pl.ds(step, 1), :] * forced[layer, here, :]


def opening_kernel(fwd, adj, density, own, *rest):
    pays, (planes, sems) = rest[:-2], rest[-2:]
    depth, rows, width_y = fwd.shape[2:]
    top = depth - 1
    has_up, has_low = neighbours()
    held_copy = pltpu.make_async_copy(density, own, sems.at[2, 0])
    held_copy.start()

    def up(pay):
        copies = []
        for evo, given in enumerate((fwd, adj)):
            for c in range(5):
                copies.append(
                    pltpu.make_async_copy(given.at[0, c, top], planes.at[evo, c], sems.at[evo, c])
                )
        for copy in copies:
            copy.start()
        for copy in copies:
            copy.wait()
        for evo in range(2):
            for first, size in chunks(rows):
                here = pl.ds(first, size)
                ex, ey, ez, hx, hy = (planes[evo, c, here, :] for c in range(5))
                if first + size < rows:
                    ez_after = planes[evo, 2, pl.ds(first + 1, size), :]
                else:
                    row = lax.broadcasted_iota(jnp.int32, ez.shape, 0)
                    ez_after = jnp.where(row == size - 1, 0.0, pltpu.roll(ez, size - 1, 0))
                pay[evo, 0, here, :] = (hx + hx) - ((next_col(ez) - ez) + ey)
                pay[evo, 1, here, :] = (hy + hy) + (ex + (ez_after - ez))

    def down(pay):
        copies = []
        for evo, given in enumerate((fwd, adj)):
            for c in range(2):
                copies.append(
                    pltpu.make_async_copy(given.at[0, c, 0], pay.at[evo, c], sems.at[evo, c])
                )
        for copy in copies:
            copy.start()
        for copy in copies:
            copy.wait()

    if len(pays) == 2:
        up(pays[0])
        down(pays[1])
    else:
        pl.when(has_up)(lambda: up(pays[0]))
        pl.when(has_low)(lambda: down(pays[0]))
    held_copy.wait()


def first_fwd_kernel(
    layout, given, near, wave_idx, source_far, ids_far, idx_far, eps_far,
    e, h, curls, total, edges, forced, drives, base, place,
    source, block_ids, material_idx, material_eps, sems,
):
    fetches = [
        pltpu.make_async_copy(far, here, sems.at[slot])
        for slot, (far, here) in enumerate(
            (
                (source_far, source),
                (ids_far, block_ids),
                (idx_far, material_idx),
                (eps_far, material_eps),
            )
        )
    ]
    for fetch in fetches:
        fetch.start()
    first_kernel(given, near, e, h, curls)
    depth, rows, width_y = forced.shape
    nblock = block_ids.shape[0]
    block_rows = rows // nblock
    empty = jnp.zeros(total.shape[1:], F32)
    edges[0] = empty
    edges[1] = empty
    for layer in range(depth):
        total[layer] = empty
    for fetch in fetches:
        fetch.wait()
    xcoord = lax.broadcasted_iota(jnp.int32, (rows, width_y), 0)
    ycoord = lax.broadcasted_iota(jnp.int32, (rows, width_y), 1)
    offset_x = (xcoord - source[0, 1]).astype(F32) / (rows / 4.0)
    offset_y = (ycoord - source[0, 2]).astype(F32) / (width_y / 4.0)
    profile = jnp.exp(-0.5 * (offset_x * offset_x + offset_y * offset_y))
    step = lax.broadcasted_iota(jnp.int32, drives.shape, 0).astype(F32) + 1.0
    wave = jnp.full(drives.shape, wave_idx[0], jnp.int32).astype(F32)
    drives[...] = AMPLITUDE * jnp.sin(2.0 * math.pi / (6.0 + 2.0 * wave) * step)
    level = source[0, 0] - lax.axis_index("slab") * depth
    for layer in range(depth):
        forced[layer] = jnp.where(level == layer, 1.0, 0.0) * profile
    for block in range(nblock):
        value = jnp.full((block_rows, width_y), material_eps[material_idx[block]], F32)
        base[pl.ds(block * block_rows, block_rows), :] = value
    me = lax.axis_index("grp")
    block = lax.broadcasted_iota(jnp.int32, (nblock, width_y), 0)
    for slot, mask in enumerate(mask for masks in layout for mask in masks):
        place[slot] = jnp.where(block == block_ids[me ^ mask], 1.0, 0.0)


def first_kernel(given, near, e, h, curls):
    win = Window(e, h)
    rows, width_y = win.rows, e.shape[3]
    margin = jnp.zeros((PAD, width_y), F32)
    empty = jnp.zeros((rows + 2 * PAD, width_y), F32)
    for comp in range(3):
        e[comp, win.depth] = empty
        h[comp, win.depth] = empty

    def copy(layer):
        for comp in range(3):
            for ref in (e, h):
                ref[comp, layer, pl.ds(0, PAD), :] = margin
                ref[comp, layer, pl.ds(PAD + rows, PAD), :] = margin
            for first, size in chunks(rows):
                here = pl.ds(first, size)
                e[comp, layer, pl.ds(PAD + first, size), :] = given[0, comp, layer, here, :]

    def from_given(layer, first, size):
        return [given[0, 3 + c, layer, pl.ds(first, size), :] for c in range(3)]

    copy(0)
    copy(1)
    win.put_h(0, from_given)
    copy(2)
    win.put_h(1, from_given)

    def body(layer, carry):
        pl.when(layer + 2 < win.depth)(lambda: copy(layer + 2))
        win.put_h(layer + 1, from_given)
        win.put_curl(curls, layer, layer - 1)
        return carry

    lax.fori_loop(1, win.top, body, 0)


def settle_kernel(layout, *refs):
    refs = list(refs)
    del refs[:4]
    e_fwd, e_adj, below, above = (refs.pop(0) for _ in range(4))
    parts = [refs.pop(0) for _ in layout]
    ids_far, h_fwd, curls_fwd, h_adj, curls_adj, blocks, block_ids, sem = refs
    fetch = pltpu.make_async_copy(ids_far, block_ids, sem)
    fetch.start()
    nothing = jnp.zeros(blocks.shape[1:], F32)
    for block in range(blocks.shape[0]):
        blocks[block] = nothing
    has_up, has_low = neighbours()
    for evo, (e, h, curls) in enumerate(((e_fwd, h_fwd, curls_fwd), (e_adj, h_adj, curls_adj))):
        win = Window(e, h)
        pl.when(has_up)(lambda: win.take_above(above.at[evo]))
        pl.when(has_low)(lambda: win.take_below(below.at[evo]))
        win.put_curl(curls, win.top, win.top - 1)
        win.put_curl(curls, 0, win.under)
    fetch.wait()
    me = lax.axis_index("grp")
    for part, masks in zip(parts, layout):
        for slot, mask in enumerate(masks):
            blocks[block_ids[me ^ mask]] = part[slot]


def edge_kernel(step, evo, *refs):
    refs = list(refs)
    e_in, h_in = refs.pop(0), refs.pop(0)
    if evo == 1:
        other_in, edges_in = refs.pop(0), refs.pop(0)
    coef = refs.pop(0)
    drives, forced = (refs.pop(0), refs.pop(0)) if evo == 0 else (None, None)
    curls = refs.pop(0) if step == 0 else None
    below, above = (refs.pop(0), refs.pop(0)) if step > 0 else (None, None)
    e, h = refs.pop(0), refs.pop(0)
    other, edges = (refs.pop(0), refs.pop(0)) if evo == 1 else (None, None)
    pays = refs
    win = Window(e, h, coef, forcing(step, drives, forced))
    top = win.top
    has_up, has_low = neighbours()

    @pl.when(has_up)
    def _():
        if step > 0:
            win.take_above(above)
        win.put_e(top, top - 1, curls, other, edges, 1)
        if pays:
            win.put_h(top, alone=True)
            for c in range(2):
                pays[0][c] = h[c, top, pl.ds(PAD, win.rows), :]

    @pl.when(has_low)
    def _():
        if step > 0:
            win.take_below(below)
        win.put_e(0, win.under, curls, other, edges, 0)
        if pays:
            for c in range(2):
                pays[-1][c] = e[c, 0, pl.ds(PAD, win.rows), :]


def inner_range(top):
    has_up, has_low = neighbours()
    return jnp.where(has_low, 1, 0), jnp.where(has_up, top - 1, top)


def begin_kernel(
    e_fwd_in, e_adj_in, total_in, coef, drives, forced, curls_fwd, curls_adj,
    e_fwd, e_adj, total,
):
    fwd = Window(e_fwd, None, coef, forcing(0, drives, forced))
    adj = Window(e_adj, None, coef)
    lowest, highest = inner_range(fwd.top)

    def body(layer, carry):
        fwd.put_e(layer, None, curls_fwd)
        adj.put_e(layer, None, curls_adj, e_fwd, total)
        return carry

    lax.fori_loop(lowest, highest + 1, body, 0)


def inner_kernel(step, evo, *refs):
    refs = list(refs)
    e_in, h_in = refs.pop(0), refs.pop(0)
    if evo == 1:
        other_in, total_in = refs.pop(0), refs.pop(0)
    coef = refs.pop(0)
    drives, forced = (refs.pop(0), refs.pop(0)) if evo == 0 else (None, None)
    e, h = refs.pop(0), refs.pop(0)
    other, total = (refs.pop(0), refs.pop(0)) if evo == 1 else (None, None)
    win = Window(e, h, coef, forcing(step, drives, forced))
    lowest, highest = inner_range(win.top)
    win.put_h(0)
    pl.when(lowest == 1)(lambda: win.put_h(1))

    def body(layer, carry):
        win.put_h(layer + 1)
        win.put_e(layer, jnp.where(layer == 0, win.under, layer - 1), None, other, total)
        return carry

    if lax.axis_size("slab") == 2:
        lax.fori_loop(0, win.depth - 2, lambda i, carry: body(lowest + i, carry), 0, unroll=2)
    else:
        lax.fori_loop(lowest, highest, body, 0)
    win.put_e(highest, highest - 1, None, other, total)


def coef_layer(layer, coef, placed, base):
    for first, size in chunks(base.shape[0]):
        here = pl.ds(first, size)
        coef[layer, here, :] = 0.25 / (base[here, :] + 3.0 * filtered(placed, first, size))


def clear_margins(placed):
    rows = placed.shape[0] - 2 * PAD
    margin = jnp.zeros((PAD, placed.shape[1]), F32)
    placed[pl.ds(0, PAD), :] = margin
    placed[pl.ds(PAD + rows, PAD), :] = margin


def place_layer(layer, first_slot, parts, place, blocks, placed):
    nblock = blocks.shape[0]
    block_rows = (placed.shape[0] - 2 * PAD) // nblock
    clear_margins(placed)
    start = layer * block_rows
    source = pl.ds(start if isinstance(layer, int) else pl.multiple_of(start, block_rows), block_rows)
    pieces = [part[slot, source, :] for part in parts for slot in range(part.shape[0])]
    for block in range(nblock):
        value = blocks[block, source, :]
        for slot, piece in enumerate(pieces):
            value = value + place[first_slot + slot, pl.ds(block, 1), :] * piece
        placed[pl.ds(PAD + block * block_rows, block_rows), :] = value


def coef_edge_kernel(first_slot, count, *refs):
    parts, (place, base, blocks, coef, placed) = refs[:count], refs[count:]
    edge_layers = (0, coef.shape[0] - 1)
    for which, layer in enumerate(edge_layers):
        place_layer(layer, first_slot, parts, place, blocks, placed.at[which])
    for which, layer in enumerate(edge_layers):
        coef_layer(layer, coef, placed.at[which], base)


def coef_inner_kernel(first_slot, count, coef_in, *refs):
    parts, (place, base, blocks, coef, placed) = refs[:count], refs[count:]

    def body(layer, carry):
        there = placed.at[lax.rem(layer, 2)]
        place_layer(layer, first_slot, parts, place, blocks, there)
        coef_layer(layer, coef, there, base)
        return carry

    lax.fori_loop(1, coef.shape[0] - 1, body, 0, unroll=2)


def filtered(padded, first, size):
    here = padded[pl.ds(PAD + first, size), :]
    before = padded[pl.ds(PAD + first - 1, size), :]
    after = padded[pl.ds(PAD + first + 1, size), :]
    along = before + 2.0 * here + after
    return (prev_col(along) + 2.0 * along + next_col(along)) * 0.0625


def tie_kernel(*refs):
    pass


def tie(array, others):
    return call(
        tie_kernel, on_chip(*array.shape), IN_VMEM, [array] + others,
        [IN_VMEM] * (1 + len(others)), aliases={0: 0},
    )


def pack_kernel(*refs):
    out = refs[-1]
    for slot, ref in enumerate(refs[:-1]):
        out[slot] = ref[...]


def filter_inner_kernel(layout, total, after, block_ids_far, *rest):
    parts, (blocks, wide, block_ids, sem) = rest[:-4], rest[-4:]
    fetch = pltpu.make_async_copy(block_ids_far, block_ids, sem)
    fetch.start()
    depth = total.shape[0]
    nblock = blocks.shape[0]
    rows = wide.shape[1]
    block_rows = rows // nblock
    me = lax.axis_index("grp")

    def body(layer, carry):
        there = wide.at[lax.rem(layer, 2)]
        for first, size in chunks(rows):
            there[pl.ds(first, size), :] = filtered(total.at[layer], first, size)
        for block in range(nblock):
            target = pl.ds(pl.multiple_of((layer - 1) * block_rows, block_rows), block_rows)
            blocks[block, target, :] = there[pl.ds(block * block_rows, block_rows), :]
        return carry

    lax.fori_loop(1, depth - 1, body, 0, unroll=2)
    fetch.wait()
    inner = pl.ds(0, (depth - 2) * block_rows)
    for slot, mask in enumerate(mask for masks in layout for mask in masks):
        part = parts[slot // parts[0].shape[0]]
        part[slot % part.shape[0]] = blocks[block_ids[me ^ mask], inner, :]


def filter_edge_kernel(layout, total, edges, place, *rest):
    parts, (sums, wide) = rest[:-2], rest[-2:]
    depth = total.shape[0]
    nblock = place.shape[0]
    rows = wide.shape[1]
    block_rows = rows // nblock
    for which, layer in enumerate((0, depth - 1)):
        sums[which] = total[layer] + edges[which]
        for first, size in chunks(rows):
            wide[which, pl.ds(first, size), :] = filtered(sums.at[which], first, size)
    for which in range(2):
        blocks = [
            wide[which, pl.ds(block * block_rows, block_rows), :] for block in range(nblock)
        ]
        target = pl.ds(which * block_rows, block_rows)
        for slot in range(nblock):
            value = None
            for block, piece in enumerate(blocks):
                term = place[slot, pl.ds(block, 1), :] * piece
                value = term if value is None else value + term
            parts[slot // parts[0].shape[0]][slot % parts[0].shape[0], target, :] = value


def add_kernel(pairs, count, *refs):
    outs = refs[-count:]
    size, per = refs[0].shape[0], outs[0].shape[0]
    for pair in range(pairs):
        kept, got = refs[pair], refs[pairs + pair]
        for first in range(0, size, per):
            part = pl.ds(first, per)
            outs[(pair * size + first) // per][...] = kept[part] + got[part]


def join_kernel(count, block_rows, *refs):
    inner, edge, outs = refs[:count], refs[count : 2 * count], refs[2 * count :]
    rows = outs[0].shape[0]
    for slot, out in enumerate(outs):
        middle, ends = inner[0][slot], edge[0][slot]
        for a, b in zip(inner[1:], edge[1:]):
            middle, ends = middle + a[slot], ends + b[slot]
        out[pl.ds(0, block_rows), :] = ends[:block_rows]
        out[pl.ds(block_rows, rows - 2 * block_rows), :] = middle
        out[pl.ds(rows - block_rows, block_rows), :] = ends[block_rows:]


def last_kernel(scale, *refs):
    value = refs[0][...]
    for ref in refs[1:-1]:
        value = value + ref[...]
    refs[-1][...] = value * scale


def out_kernel(e, h, finals, halves, sems):
    depth = e.shape[1] - 1
    rows = e.shape[2] - 2 * PAD
    every = pl.ds(PAD, rows)
    copies = [
        pltpu.make_async_copy(e.at[c, pl.ds(0, depth), every, :], finals.at[0, c], sems.at[c])
        for c in range(3)
    ]
    for copy in copies:
        copy.start()
    for c in range(3):

        def body(layer, carry, c=c):
            halves[c, layer] = 0.5 * h[c, layer, every, :]
            return carry

        lax.fori_loop(0, depth, body, 0)
        copy = pltpu.make_async_copy(halves.at[c], finals.at[0, 3 + c], sems.at[3 + c])
        copy.start()
        copies.append(copy)
    for copy in copies:
        copy.wait()


def swap_over(array, axis, mask):
    return lax.ppermute(array, axis, [(i, i ^ mask) for i in range(lax.axis_size(axis))])


def shift_over(array, axis, distance):
    size = lax.axis_size(axis)
    route = [(i, i + distance) for i in range(size) if 0 <= i + distance < size]
    return lax.ppermute(array, axis, route)


def trade(pays):
    if len(pays) == 1:
        return [swap_over(pays[0], "slab", 1)] * 2
    return [shift_over(pays[0], "slab", 1), shift_over(pays[1], "slab", -1)]


def per_device(
    fwd_fields, adj_fields, density, block_ids, material_idx, material_eps, source_pos, wave_idx
):
    depth, width_x, width_y = fwd_fields.shape[2:]
    nblock = block_ids.shape[0]
    block_rows = width_x // nblock
    ngrp = lax.axis_size("grp")
    npay = 1 if lax.axis_size("slab") == 2 else 2

    far = 4
    middle = ngrp // (2 * far)
    far_masks = [2 * middle * j for j in range(far)]
    middle_masks = [2 * j for j in range(middle)]
    layout = [
        [core + mid + top for top in far_masks] for core in (0, 1) for mid in middle_masks
    ]
    piece = (depth * block_rows, width_y)
    group = (far,) + piece

    field_shape = on_chip(3, depth + 1, width_x + 2 * PAD, width_y)
    curls_shape = on_chip(3, depth, width_x, width_y)
    halo_shape = on_chip(2, width_x, width_y)
    total_shape = on_chip(depth, width_x + 2 * PAD, width_y)
    edges_shape = on_chip(2, width_x + 2 * PAD, width_y)
    coef_shape = on_chip(depth, width_x, width_y)
    plane = on_chip(width_x, width_y)

    def by_owner(kernel, layers, operands, specs, scratch, micros, messages):
        slots = middle * far // messages
        parts = call(
            kernel,
            [on_chip(slots, layers * block_rows, width_y)] * (2 * messages),
            [IN_VMEM] * (2 * messages),
            operands,
            specs,
            scratch,
            micros=micros,
        )
        return list(parts[:messages]), [swap_over(part, "grp", 1) for part in parts[messages:]]

    def add_middle(kept, got, after):
        sums = call(
            functools.partial(add_kernel, len(kept), middle),
            [on_chip(far, *kept[0].shape[1:])] * middle,
            [IN_VMEM] * middle,
            kept + got + after,
            [IN_VMEM] * (len(kept + got + after)),
        )
        return [sums[0]] + [
            swap_over(part, "grp", mask) for part, mask in zip(sums[1:], middle_masks[1:])
        ]

    design = density.reshape(piece)
    got = [swap_over(design, "grp", mask) for mask in far_masks[1:]]
    own, *pays = call(
        opening_kernel,
        [on_chip(*piece)] + [on_chip(2, 2, width_x, width_y)] * npay,
        [IN_VMEM] * (1 + npay),
        [fwd_fields, adj_fields, design],
        [IN_HBM] * 3,
        [pltpu.VMEM((2, 5, width_x, width_y), F32), pltpu.SemaphoreType.DMA((3, 5))],
    )
    below, above = trade(pays)

    near = call(pack_kernel, on_chip(*group), IN_VMEM, [own] + got, [IN_VMEM] * far)
    others = [swap_over(near, "grp", mask) for mask in middle_masks[1:]]
    near_across = swap_over(near, "grp", 1)

    e_fwd, h_fwd, curls_fwd, total, edges, forced, drives, base, place = call(
        functools.partial(first_fwd_kernel, layout),
        [
            field_shape,
            field_shape,
            curls_shape,
            total_shape,
            edges_shape,
            on_chip(depth, width_x, width_y),
            on_chip(STEPS, width_y),
            plane,
            on_chip(nblock, nblock, width_y),
        ],
        [IN_VMEM] * 9,
        [fwd_fields, near, wave_idx, source_pos, block_ids, material_idx, material_eps],
        [IN_VMEM] * 2 + [IN_SMEM] + [IN_HBM] * 4,
        [
            pltpu.SMEM(source_pos.shape, jnp.int32),
            pltpu.SMEM(block_ids.shape, jnp.int32),
            pltpu.SMEM(material_idx.shape, jnp.int32),
            pltpu.SMEM(material_eps.shape, F32),
            pltpu.SemaphoreType.DMA((4,)),
        ],
        micros=1.5,
    )
    e_adj, h_adj, curls_adj = call(
        first_kernel,
        [field_shape, field_shape, curls_shape],
        [IN_VMEM] * 3,
        [adj_fields, near],
        [IN_VMEM, IN_VMEM],
        micros=1.2,
    )
    others = [tie(part, [e_fwd, e_adj]) for part in others]
    early = [near] + others + [near_across]
    last = [swap_over(part, "grp", 1) for part in others]
    first_slot = far * len(early)

    h_fwd, curls_fwd, h_adj, curls_adj, blocks = call(
        functools.partial(settle_kernel, layout[: len(early)]),
        [field_shape, curls_shape] * 2 + [on_chip(nblock, *piece)],
        [IN_VMEM] * 5,
        [h_fwd, curls_fwd, h_adj, curls_adj, e_fwd, e_adj, below, above] + early + [block_ids],
        [IN_VMEM] * (8 + len(early)) + [IN_HBM],
        [pltpu.SMEM(block_ids.shape, jnp.int32), pltpu.SemaphoreType.DMA],
        aliases={0: 0, 1: 1, 2: 2, 3: 3},
        micros=0.6,
    )
    placed = pltpu.VMEM((2, width_x + 2 * PAD, width_y), F32)
    coef = call(
        functools.partial(coef_edge_kernel, first_slot, len(last)),
        coef_shape,
        IN_VMEM,
        last + [place, base, blocks],
        [IN_VMEM] * (len(last) + 3),
        [placed],
    )

    arrived_fwd, arrived_adj = [curls_fwd], [curls_adj]
    for step in range(STEPS):
        more = npay if step < STEPS - 1 else 0

        def edge_fwd(e_fwd, h_fwd):
            return call(
                functools.partial(edge_kernel, step, 0),
                [field_shape] * 2 + [halo_shape] * more,
                [IN_VMEM] * (2 + more),
                [e_fwd, h_fwd, coef, drives, forced] + arrived_fwd,
                [IN_VMEM] * (5 + len(arrived_fwd)),
                aliases={0: 0, 1: 1},
            )

        if more:
            e_fwd, h_fwd, *pays = edge_fwd(e_fwd, h_fwd)
            arrived_fwd_next = trade(pays)
        if step > 0:
            e_adj, h_adj, e_fwd, total = call(
                functools.partial(inner_kernel, step, 1),
                [field_shape] * 3 + [total_shape],
                [IN_VMEM] * 4,
                [e_adj, h_adj, e_fwd, total, coef],
                [IN_VMEM] * 5,
                aliases={0: 0, 1: 1, 2: 2, 3: 3},
                micros=1.2,
            )
        if not more:
            e_fwd, h_fwd = edge_fwd(e_fwd, h_fwd)
            inner = by_owner(
                functools.partial(filter_inner_kernel, layout),
                depth - 2,
                [total, e_fwd, block_ids],
                [IN_VMEM, IN_VMEM, IN_HBM],
                [
                    pltpu.VMEM((nblock,) + piece, F32),
                    pltpu.VMEM((2, width_x, width_y), F32),
                    pltpu.SMEM(block_ids.shape, jnp.int32),
                    pltpu.SemaphoreType.DMA,
                ],
                0.8,
                middle,
            )
        if step == 0:
            coef = call(
                functools.partial(coef_inner_kernel, first_slot, len(last)),
                coef_shape,
                IN_VMEM,
                [coef] + last + [place, base, blocks],
                [IN_VMEM] * (len(last) + 4),
                [placed],
                aliases={0: 0},
                micros=0.6,
            )
            e_fwd, e_adj, total = call(
                begin_kernel,
                [field_shape, field_shape, total_shape],
                [IN_VMEM] * 3,
                [e_fwd, e_adj, total, coef, drives, forced, curls_fwd, curls_adj],
                [IN_VMEM] * 8,
                aliases={0: 0, 1: 1, 2: 2},
                micros=0.5,
            )
        e_adj, h_adj, e_fwd, edges, *pays = call(
            functools.partial(edge_kernel, step, 1),
            [field_shape] * 3 + [edges_shape] + [halo_shape] * more,
            [IN_VMEM] * (4 + more),
            [e_adj, h_adj, e_fwd, edges, coef] + arrived_adj,
            [IN_VMEM] * (5 + len(arrived_adj)),
            aliases={0: 0, 1: 1, 2: 2, 3: 3},
        )
        if not more:
            break
        arrived_fwd, arrived_adj = arrived_fwd_next, trade(pays)
        e_fwd, h_fwd = call(
            functools.partial(inner_kernel, step + 1, 0),
            [field_shape] * 2,
            [IN_VMEM] * 2,
            [e_fwd, h_fwd, coef, drives, forced],
            [IN_VMEM] * 5,
            aliases={0: 0, 1: 1},
            micros=1.1,
        )

    ends = by_owner(
        functools.partial(filter_edge_kernel, layout),
        2,
        [total, edges, place],
        [IN_VMEM] * 3,
        [
            pltpu.VMEM((2, width_x + 2 * PAD, width_y), F32),
            pltpu.VMEM((2, width_x, width_y), F32),
        ],
        0.3,
        1,
    )
    inner = add_middle(*inner, ends[0][:1])
    ends = add_middle(*ends, [])
    pieces = call(
        functools.partial(join_kernel, middle, block_rows),
        [on_chip(*piece)] * far,
        [IN_VMEM] * far,
        inner + ends,
        [IN_VMEM] * (2 * middle),
    )
    got = [swap_over(part, "grp", mask) for part, mask in zip(pieces[:0:-1], far_masks[:0:-1])]
    scale = 3.0 / (STEPS * math.sqrt(ngrp))
    grad = call(
        functools.partial(last_kernel, scale),
        jax.ShapeDtypeStruct(piece, F32),
        IN_VMEM,
        [pieces[0]] + got,
        [IN_VMEM] * far,
    )
    finals = call(
        out_kernel,
        jax.ShapeDtypeStruct(fwd_fields.shape, F32),
        IN_HBM,
        [e_fwd, h_fwd],
        [IN_VMEM] * 2,
        [
            pltpu.VMEM((3, depth, width_x, width_y), F32),
            pltpu.SemaphoreType.DMA((6,)),
        ],
        micros=1.7,
    )
    return finals, grad.reshape(density.shape)


def solution(mesh):
    placed = (
        P("grp", None, "slab", None, None),
        P("grp", None, "slab", None, None),
        P("slab", "grp", None),
        P(),
        P(),
        P(),
        P("grp", None),
        P("grp"),
    )
    return jax.shard_map(
        per_device,
        mesh=mesh,
        in_specs=placed,
        out_specs=(P("grp", None, "slab", None, None), P("slab", "grp", None)),
        check_vma=False,
    )
```

```python
import functools
import math

import jax
import jax.numpy as jnp
from jax import lax
from jax.experimental import pallas as pl
from jax.experimental.pallas import tpu as pltpu
from jax.sharding import PartitionSpec as P

STEPS = 4
AMPLITUDE = 4.0
PAD = 8
F32 = jnp.float32
HBM_PER_MICRO = 1.0e5

VMEM = pltpu.MemorySpace.VMEM
IN_VMEM = pl.BlockSpec(memory_space=pltpu.VMEM)
IN_SMEM = pl.BlockSpec(memory_space=pltpu.SMEM)
IN_HBM = pl.BlockSpec(memory_space=pltpu.MemorySpace.HBM)


def on_chip(*shape):
    return VMEM(shape, F32)


def held(array, spec):
    if spec is IN_SMEM:
        return array
    space = VMEM if spec is IN_VMEM else pltpu.MemorySpace.HBM
    return pltpu.with_memory_space_constraint(array, space)


def call(kernel, outs, out_specs, operands, specs, scratch=(), aliases=None, micros=0.3):
    operands = [held(a, s) for a, s in zip(operands, specs)]
    return pl.pallas_call(
        kernel,
        out_shape=outs,
        in_specs=specs,
        out_specs=out_specs,
        scratch_shapes=scratch,
        input_output_aliases=aliases or {},
        compiler_params=pltpu.CompilerParams(vmem_limit_bytes=8 << 20),
        cost_estimate=pl.CostEstimate(
            flops=0, bytes_accessed=int(micros * HBM_PER_MICRO), transcendentals=0
        ),
    )(*operands)


CHUNK = 16


def chunks(rows):
    size = CHUNK if rows % CHUNK == 0 else rows
    return [(first, size) for first in range(0, rows, size)]


def next_col(value):
    column = lax.broadcasted_iota(jnp.int32, value.shape, 1)
    moved = pltpu.roll(value, value.shape[1] - 1, 1)
    return jnp.where(column == value.shape[1] - 1, 0.0, moved)


def prev_col(value):
    column = lax.broadcasted_iota(jnp.int32, value.shape, 1)
    return jnp.where(column == 0, 0.0, pltpu.roll(value, 1, 1))


def neighbours():
    slab = lax.axis_index("slab")
    return slab < lax.axis_size("slab") - 1, slab > 0


class Window:
    def __init__(self, e, h, coef=None, force=None):
        self.e, self.h, self.coef, self.force = e, h, coef, force
        self.rows = e.shape[2] - 2 * PAD
        self.depth = e.shape[1] - 1
        self.top, self.under = self.depth - 1, self.depth

    def read(self, ref, layer, first, size):
        return [ref[c, layer, pl.ds(PAD + first, size), :] for c in range(3)]

    def write(self, ref, layer, first, size, values):
        for c, value in enumerate(values):
            ref[c, layer, pl.ds(PAD + first, size), :] = value

    def put_h(self, layer, given=None, alone=False):
        for first, size in chunks(self.rows):
            rows = pl.ds(PAD + first, size)
            after = pl.ds(PAD + first + 1, size)
            ex, ey, ez = self.read(self.e, layer, first, size)
            if given is None:
                hx, hy, hz = self.read(self.h, layer, first, size)
            else:
                hx, hy, hz = (value + value for value in given(layer, first, size))
            if alone:
                rise_x, rise_y = -ex, -ey
            else:
                rise_x = self.e[0, layer + 1, rows, :] - ex
                rise_y = self.e[1, layer + 1, rows, :] - ey
            ey_after = self.e[1, layer, after, :]
            ez_after = self.e[2, layer, after, :]
            hx = hx - ((next_col(ez) - ez) - rise_y)
            hy = hy - (rise_x - (ez_after - ez))
            hz = hz - ((ey_after - ey) - (next_col(ex) - ex))
            self.write(self.h, layer, first, size, (hx, hy, hz))

    def curl_h(self, layer, lower, first, size):
        rows = pl.ds(PAD + first, size)
        before = pl.ds(PAD + first - 1, size)
        hx, hy, hz = self.read(self.h, layer, first, size)
        step_x = hx - self.h[0, lower, rows, :]
        step_y = hy - self.h[1, lower, rows, :]
        hy_before = self.h[1, layer, before, :]
        hz_before = self.h[2, layer, before, :]
        return (
            (hz - prev_col(hz)) - step_y,
            step_x - (hz - hz_before),
            (hy - hy_before) - (hx - prev_col(hx)),
        )

    def put_curl(self, curls, layer, lower):
        for first, size in chunks(self.rows):
            for c, value in enumerate(self.curl_h(layer, lower, first, size)):
                curls[c, layer, pl.ds(first, size), :] = value

    def next_e(self, layer, lower, first, size, curls=None):
        here = pl.ds(first, size)
        cell = self.coef[layer, here, :]
        if curls is None:
            curl = self.curl_h(layer, lower, first, size)
        else:
            curl = [curls[c, layer, here, :] for c in range(3)]
        ex, ey, ez = [a + cell * b for a, b in zip(self.read(self.e, layer, first, size), curl)]
        if self.force is not None:
            ez = ez + self.force(layer, here)
        return ex, ey, ez

    def put_e(self, layer, lower, curls=None, other=None, total=None, slot=None):
        for first, size in chunks(self.rows):
            news = self.next_e(layer, lower, first, size, curls)
            self.write(self.e, layer, first, size, news)
            if total is not None:
                rows = pl.ds(PAD + first, size)
                part = [a * other[c, layer, rows, :] for c, a in enumerate(news)]
                total[layer if slot is None else slot, rows, :] += part[0] + part[1] + part[2]

    def take_above(self, above):
        for first, size in chunks(self.rows):
            here, rows = pl.ds(first, size), pl.ds(PAD + first, size)
            self.h[0, self.top, rows, :] += above[1, here, :]
            self.h[1, self.top, rows, :] -= above[0, here, :]

    def take_below(self, below):
        for first, size in chunks(self.rows):
            here, rows = pl.ds(first, size), pl.ds(PAD + first, size)
            self.h[0, self.under, rows, :] = below[0, here, :] + self.e[1, 0, rows, :]
            self.h[1, self.under, rows, :] = below[1, here, :] - self.e[0, 0, rows, :]


def forcing(step, drives, forced):
    if drives is None:
        return None
    return lambda layer, here: drives[pl.ds(step, 1), :] * forced[layer, here, :]


def opening_kernel(fwd, adj, density, own, *rest):
    pays, (planes, sems) = rest[:-2], rest[-2:]
    depth, rows, width_y = fwd.shape[2:]
    top = depth - 1
    has_up, has_low = neighbours()
    held_copy = pltpu.make_async_copy(density, own, sems.at[2, 0])
    held_copy.start()

    def up(pay):
        copies = []
        for evo, given in enumerate((fwd, adj)):
            for c in range(5):
                copies.append(
                    pltpu.make_async_copy(given.at[0, c, top], planes.at[evo, c], sems.at[evo, c])
                )
        for copy in copies:
            copy.start()
        for copy in copies:
            copy.wait()
        for evo in range(2):
            for first, size in chunks(rows):
                here = pl.ds(first, size)
                ex, ey, ez, hx, hy = (planes[evo, c, here, :] for c in range(5))
                if first + size < rows:
                    ez_after = planes[evo, 2, pl.ds(first + 1, size), :]
                else:
                    row = lax.broadcasted_iota(jnp.int32, ez.shape, 0)
                    ez_after = jnp.where(row == size - 1, 0.0, pltpu.roll(ez, size - 1, 0))
                pay[evo, 0, here, :] = (hx + hx) - ((next_col(ez) - ez) + ey)
                pay[evo, 1, here, :] = (hy + hy) + (ex + (ez_after - ez))

    def down(pay):
        copies = []
        for evo, given in enumerate((fwd, adj)):
            for c in range(2):
                copies.append(
                    pltpu.make_async_copy(given.at[0, c, 0], pay.at[evo, c], sems.at[evo, c])
                )
        for copy in copies:
            copy.start()
        for copy in copies:
            copy.wait()

    if len(pays) == 2:
        up(pays[0])
        down(pays[1])
    else:
        pl.when(has_up)(lambda: up(pays[0]))
        pl.when(has_low)(lambda: down(pays[0]))
    held_copy.wait()


def first_fwd_kernel(
    layout, given, near, wave_idx, source_far, ids_far, idx_far, eps_far,
    e, h, curls, total, edges, forced, drives, base, place,
    source, block_ids, material_idx, material_eps, sems,
):
    fetches = [
        pltpu.make_async_copy(far, here, sems.at[slot])
        for slot, (far, here) in enumerate(
            (
                (source_far, source),
                (ids_far, block_ids),
                (idx_far, material_idx),
                (eps_far, material_eps),
            )
        )
    ]
    for fetch in fetches:
        fetch.start()
    first_kernel(given, near, e, h, curls)
    depth, rows, width_y = forced.shape
    nblock = block_ids.shape[0]
    block_rows = rows // nblock
    empty = jnp.zeros(total.shape[1:], F32)
    edges[0] = empty
    edges[1] = empty
    for layer in range(depth):
        total[layer] = empty
    for fetch in fetches:
        fetch.wait()
    xcoord = lax.broadcasted_iota(jnp.int32, (rows, width_y), 0)
    ycoord = lax.broadcasted_iota(jnp.int32, (rows, width_y), 1)
    offset_x = (xcoord - source[0, 1]).astype(F32) / (rows / 4.0)
    offset_y = (ycoord - source[0, 2]).astype(F32) / (width_y / 4.0)
    profile = jnp.exp(-0.5 * (offset_x * offset_x + offset_y * offset_y))
    step = lax.broadcasted_iota(jnp.int32, drives.shape, 0).astype(F32) + 1.0
    wave = jnp.full(drives.shape, wave_idx[0], jnp.int32).astype(F32)
    drives[...] = AMPLITUDE * jnp.sin(2.0 * math.pi / (6.0 + 2.0 * wave) * step)
    level = source[0, 0] - lax.axis_index("slab") * depth
    for layer in range(depth):
        forced[layer] = jnp.where(level == layer, 1.0, 0.0) * profile
    for block in range(nblock):
        value = jnp.full((block_rows, width_y), material_eps[material_idx[block]], F32)
        base[pl.ds(block * block_rows, block_rows), :] = value
    me = lax.axis_index("grp")
    block = lax.broadcasted_iota(jnp.int32, (nblock, width_y), 0)
    for slot, mask in enumerate(mask for masks in layout for mask in masks):
        place[slot] = jnp.where(block == block_ids[me ^ mask], 1.0, 0.0)


def first_kernel(given, near, e, h, curls):
    win = Window(e, h)
    rows, width_y = win.rows, e.shape[3]
    margin = jnp.zeros((PAD, width_y), F32)
    empty = jnp.zeros((rows + 2 * PAD, width_y), F32)
    for comp in range(3):
        e[comp, win.depth] = empty
        h[comp, win.depth] = empty

    def copy(layer):
        for comp in range(3):
            for ref in (e, h):
                ref[comp, layer, pl.ds(0, PAD), :] = margin
                ref[comp, layer, pl.ds(PAD + rows, PAD), :] = margin
            for first, size in chunks(rows):
                here = pl.ds(first, size)
                e[comp, layer, pl.ds(PAD + first, size), :] = given[0, comp, layer, here, :]

    def from_given(layer, first, size):
        return [given[0, 3 + c, layer, pl.ds(first, size), :] for c in range(3)]

    copy(0)
    copy(1)
    win.put_h(0, from_given)
    copy(2)
    win.put_h(1, from_given)

    def body(layer, carry):
        pl.when(layer + 2 < win.depth)(lambda: copy(layer + 2))
        win.put_h(layer + 1, from_given)
        win.put_curl(curls, layer, layer - 1)
        return carry

    lax.fori_loop(1, win.top, body, 0)


def settle_kernel(layout, *refs):
    refs = list(refs)
    del refs[:4]
    e_fwd, e_adj, below, above = (refs.pop(0) for _ in range(4))
    parts = [refs.pop(0) for _ in layout]
    ids_far, h_fwd, curls_fwd, h_adj, curls_adj, blocks, block_ids, sem = refs
    fetch = pltpu.make_async_copy(ids_far, block_ids, sem)
    fetch.start()
    nothing = jnp.zeros(blocks.shape[1:], F32)
    for block in range(blocks.shape[0]):
        blocks[block] = nothing
    has_up, has_low = neighbours()
    for evo, (e, h, curls) in enumerate(((e_fwd, h_fwd, curls_fwd), (e_adj, h_adj, curls_adj))):
        win = Window(e, h)
        pl.when(has_up)(lambda: win.take_above(above.at[evo]))
        pl.when(has_low)(lambda: win.take_below(below.at[evo]))
        win.put_curl(curls, win.top, win.top - 1)
        win.put_curl(curls, 0, win.under)
    fetch.wait()
    me = lax.axis_index("grp")
    for part, masks in zip(parts, layout):
        for slot, mask in enumerate(masks):
            blocks[block_ids[me ^ mask]] = part[slot]


def edge_kernel(step, evo, *refs):
    refs = list(refs)
    e_in, h_in = refs.pop(0), refs.pop(0)
    if evo == 1:
        other_in, edges_in = refs.pop(0), refs.pop(0)
    coef = refs.pop(0)
    drives, forced = (refs.pop(0), refs.pop(0)) if evo == 0 else (None, None)
    curls = refs.pop(0) if step == 0 else None
    below, above = (refs.pop(0), refs.pop(0)) if step > 0 else (None, None)
    e, h = refs.pop(0), refs.pop(0)
    other, edges = (refs.pop(0), refs.pop(0)) if evo == 1 else (None, None)
    pays = refs
    win = Window(e, h, coef, forcing(step, drives, forced))
    top = win.top
    has_up, has_low = neighbours()

    @pl.when(has_up)
    def _():
        if step > 0:
            win.take_above(above)
        win.put_e(top, top - 1, curls, other, edges, 1)
        if pays:
            win.put_h(top, alone=True)
            for c in range(2):
                pays[0][c] = h[c, top, pl.ds(PAD, win.rows), :]

    @pl.when(has_low)
    def _():
        if step > 0:
            win.take_below(below)
        win.put_e(0, win.under, curls, other, edges, 0)
        if pays:
            for c in range(2):
                pays[-1][c] = e[c, 0, pl.ds(PAD, win.rows), :]


def inner_range(top):
    has_up, has_low = neighbours()
    return jnp.where(has_low, 1, 0), jnp.where(has_up, top - 1, top)


def begin_kernel(
    e_fwd_in, e_adj_in, total_in, coef, drives, forced, curls_fwd, curls_adj,
    e_fwd, e_adj, total,
):
    fwd = Window(e_fwd, None, coef, forcing(0, drives, forced))
    adj = Window(e_adj, None, coef)
    lowest, highest = inner_range(fwd.top)

    def body(layer, carry):
        fwd.put_e(layer, None, curls_fwd)
        adj.put_e(layer, None, curls_adj, e_fwd, total)
        return carry

    lax.fori_loop(lowest, highest + 1, body, 0)


def inner_kernel(step, evo, *refs):
    refs = list(refs)
    e_in, h_in = refs.pop(0), refs.pop(0)
    if evo == 1:
        other_in, total_in = refs.pop(0), refs.pop(0)
    coef = refs.pop(0)
    drives, forced = (refs.pop(0), refs.pop(0)) if evo == 0 else (None, None)
    e, h = refs.pop(0), refs.pop(0)
    other, total = (refs.pop(0), refs.pop(0)) if evo == 1 else (None, None)
    win = Window(e, h, coef, forcing(step, drives, forced))
    lowest, highest = inner_range(win.top)
    win.put_h(0)
    pl.when(lowest == 1)(lambda: win.put_h(1))

    def body(layer, carry):
        win.put_h(layer + 1)
        win.put_e(layer, jnp.where(layer == 0, win.under, layer - 1), None, other, total)
        return carry

    if lax.axis_size("slab") == 2:
        lax.fori_loop(0, win.depth - 2, lambda i, carry: body(lowest + i, carry), 0, unroll=2)
    else:
        lax.fori_loop(lowest, highest, body, 0)
    win.put_e(highest, highest - 1, None, other, total)


def coef_layer(layer, coef, placed, base):
    for first, size in chunks(base.shape[0]):
        here = pl.ds(first, size)
        coef[layer, here, :] = 0.25 / (base[here, :] + 3.0 * filtered(placed, first, size))


def clear_margins(placed):
    rows = placed.shape[0] - 2 * PAD
    margin = jnp.zeros((PAD, placed.shape[1]), F32)
    placed[pl.ds(0, PAD), :] = margin
    placed[pl.ds(PAD + rows, PAD), :] = margin


def place_layer(layer, first_slot, parts, place, blocks, placed):
    nblock = blocks.shape[0]
    block_rows = (placed.shape[0] - 2 * PAD) // nblock
    clear_margins(placed)
    start = layer * block_rows
    source = pl.ds(start if isinstance(layer, int) else pl.multiple_of(start, block_rows), block_rows)
    pieces = [part[slot, source, :] for part in parts for slot in range(part.shape[0])]
    for block in range(nblock):
        value = blocks[block, source, :]
        for slot, piece in enumerate(pieces):
            value = value + place[first_slot + slot, pl.ds(block, 1), :] * piece
        placed[pl.ds(PAD + block * block_rows, block_rows), :] = value


def coef_edge_kernel(first_slot, count, *refs):
    parts, (place, base, blocks, coef, placed) = refs[:count], refs[count:]
    edge_layers = (0, coef.shape[0] - 1)
    for which, layer in enumerate(edge_layers):
        place_layer(layer, first_slot, parts, place, blocks, placed.at[which])
    for which, layer in enumerate(edge_layers):
        coef_layer(layer, coef, placed.at[which], base)


def coef_inner_kernel(first_slot, count, coef_in, *refs):
    parts, (place, base, blocks, coef, placed) = refs[:count], refs[count:]

    def body(layer, carry):
        there = placed.at[lax.rem(layer, 2)]
        place_layer(layer, first_slot, parts, place, blocks, there)
        coef_layer(layer, coef, there, base)
        return carry

    lax.fori_loop(1, coef.shape[0] - 1, body, 0, unroll=2)


def filtered(padded, first, size):
    here = padded[pl.ds(PAD + first, size), :]
    before = padded[pl.ds(PAD + first - 1, size), :]
    after = padded[pl.ds(PAD + first + 1, size), :]
    along = before + 2.0 * here + after
    return (prev_col(along) + 2.0 * along + next_col(along)) * 0.0625


def tie_kernel(*refs):
    pass


def tie(array, others):
    return call(
        tie_kernel, on_chip(*array.shape), IN_VMEM, [array] + others,
        [IN_VMEM] * (1 + len(others)), aliases={0: 0},
    )


def pack_kernel(*refs):
    out = refs[-1]
    for slot, ref in enumerate(refs[:-1]):
        out[slot] = ref[...]


def filter_inner_kernel(layout, total, after, block_ids_far, *rest):
    parts, (blocks, wide, block_ids, sem) = rest[:-4], rest[-4:]
    fetch = pltpu.make_async_copy(block_ids_far, block_ids, sem)
    fetch.start()
    depth = total.shape[0]
    nblock = blocks.shape[0]
    rows = wide.shape[1]
    block_rows = rows // nblock
    me = lax.axis_index("grp")

    def body(layer, carry):
        there = wide.at[lax.rem(layer, 2)]
        for first, size in chunks(rows):
            there[pl.ds(first, size), :] = filtered(total.at[layer], first, size)
        for block in range(nblock):
            target = pl.ds(pl.multiple_of((layer - 1) * block_rows, block_rows), block_rows)
            blocks[block, target, :] = there[pl.ds(block * block_rows, block_rows), :]
        return carry

    lax.fori_loop(1, depth - 1, body, 0, unroll=2)
    fetch.wait()
    inner = pl.ds(0, (depth - 2) * block_rows)
    for slot, mask in enumerate(mask for masks in layout for mask in masks):
        part = parts[slot // parts[0].shape[0]]
        part[slot % part.shape[0]] = blocks[block_ids[me ^ mask], inner, :]


def filter_edge_kernel(layout, total, edges, place, *rest):
    parts, (sums, wide) = rest[:-2], rest[-2:]
    depth = total.shape[0]
    nblock = place.shape[0]
    rows = wide.shape[1]
    block_rows = rows // nblock
    for which, layer in enumerate((0, depth - 1)):
        sums[which] = total[layer] + edges[which]
        for first, size in chunks(rows):
            wide[which, pl.ds(first, size), :] = filtered(sums.at[which], first, size)
    for which in range(2):
        blocks = [
            wide[which, pl.ds(block * block_rows, block_rows), :] for block in range(nblock)
        ]
        target = pl.ds(which * block_rows, block_rows)
        for slot in range(nblock):
            value = None
            for block, piece in enumerate(blocks):
                term = place[slot, pl.ds(block, 1), :] * piece
                value = term if value is None else value + term
            parts[slot // parts[0].shape[0]][slot % parts[0].shape[0], target, :] = value


def add_kernel(pairs, count, *refs):
    outs = refs[-count:]
    size, per = refs[0].shape[0], outs[0].shape[0]
    for pair in range(pairs):
        kept, got = refs[pair], refs[pairs + pair]
        for first in range(0, size, per):
            part = pl.ds(first, per)
            outs[(pair * size + first) // per][...] = kept[part] + got[part]


def join_kernel(count, block_rows, *refs):
    inner, edge, joined = refs[:count], refs[count : 2 * count], refs[2 * count]
    rows = joined.shape[1]
    mine = lax.axis_index("grp") // (2 * count)
    for slot in range(joined.shape[0]):
        out = joined.at[mine ^ slot]
        middle, ends = inner[0][slot], edge[0][slot]
        for a, b in zip(inner[1:], edge[1:]):
            middle, ends = middle + a[slot], ends + b[slot]
        out[pl.ds(0, block_rows), :] = ends[:block_rows]
        out[pl.ds(block_rows, rows - 2 * block_rows), :] = middle
        out[pl.ds(rows - block_rows, block_rows), :] = ends[block_rows:]


def last_kernel(scale, got, out):
    value = got[0]
    for slot in range(1, got.shape[0]):
        value = value + got[slot]
    out[...] = value * scale


def out_kernel(e, h, finals, halves, sems):
    depth = e.shape[1] - 1
    rows = e.shape[2] - 2 * PAD
    every = pl.ds(PAD, rows)
    copies = [
        pltpu.make_async_copy(e.at[c, pl.ds(0, depth), every, :], finals.at[0, c], sems.at[c])
        for c in range(3)
    ]
    for copy in copies:
        copy.start()
    for c in range(3):

        def body(layer, carry, c=c):
            halves[c, layer] = 0.5 * h[c, layer, every, :]
            return carry

        lax.fori_loop(0, depth, body, 0)
        copy = pltpu.make_async_copy(halves.at[c], finals.at[0, 3 + c], sems.at[3 + c])
        copy.start()
        copies.append(copy)
    for copy in copies:
        copy.wait()


def swap_over(array, axis, mask):
    return lax.ppermute(array, axis, [(i, i ^ mask) for i in range(lax.axis_size(axis))])


def shift_over(array, axis, distance):
    size = lax.axis_size(axis)
    route = [(i, i + distance) for i in range(size) if 0 <= i + distance < size]
    return lax.ppermute(array, axis, route)


def trade(pays):
    if len(pays) == 1:
        return [swap_over(pays[0], "slab", 1)] * 2
    return [shift_over(pays[0], "slab", 1), shift_over(pays[1], "slab", -1)]


def per_device(
    fwd_fields, adj_fields, density, block_ids, material_idx, material_eps, source_pos, wave_idx
):
    depth, width_x, width_y = fwd_fields.shape[2:]
    nblock = block_ids.shape[0]
    block_rows = width_x // nblock
    ngrp = lax.axis_size("grp")
    npay = 1 if lax.axis_size("slab") == 2 else 2

    far = 4
    middle = ngrp // (2 * far)
    far_masks = [2 * middle * j for j in range(far)]
    middle_masks = [2 * j for j in range(middle)]
    layout = [
        [core + mid + top for top in far_masks] for core in (0, 1) for mid in middle_masks
    ]
    piece = (depth * block_rows, width_y)
    group = (far,) + piece

    field_shape = on_chip(3, depth + 1, width_x + 2 * PAD, width_y)
    curls_shape = on_chip(3, depth, width_x, width_y)
    halo_shape = on_chip(2, width_x, width_y)
    total_shape = on_chip(depth, width_x + 2 * PAD, width_y)
    edges_shape = on_chip(2, width_x + 2 * PAD, width_y)
    coef_shape = on_chip(depth, width_x, width_y)
    plane = on_chip(width_x, width_y)

    def by_owner(kernel, layers, operands, specs, scratch, micros, messages):
        slots = middle * far // messages
        parts = call(
            kernel,
            [on_chip(slots, layers * block_rows, width_y)] * (2 * messages),
            [IN_VMEM] * (2 * messages),
            operands,
            specs,
            scratch,
            micros=micros,
        )
        return list(parts[:messages]), [swap_over(part, "grp", 1) for part in parts[messages:]]

    def add_middle(kept, got, after):
        sums = call(
            functools.partial(add_kernel, len(kept), middle),
            [on_chip(far, *kept[0].shape[1:])] * middle,
            [IN_VMEM] * middle,
            kept + got + after,
            [IN_VMEM] * (len(kept + got + after)),
        )
        return [sums[0]] + [
            swap_over(part, "grp", mask) for part, mask in zip(sums[1:], middle_masks[1:])
        ]

    design = density.reshape(piece)
    got = [swap_over(design, "grp", mask) for mask in far_masks[1:]]
    own, *pays = call(
        opening_kernel,
        [on_chip(*piece)] + [on_chip(2, 2, width_x, width_y)] * npay,
        [IN_VMEM] * (1 + npay),
        [fwd_fields, adj_fields, design],
        [IN_HBM] * 3,
        [pltpu.VMEM((2, 5, width_x, width_y), F32), pltpu.SemaphoreType.DMA((3, 5))],
    )
    below, above = trade(pays)

    near = call(pack_kernel, on_chip(*group), IN_VMEM, [own] + got, [IN_VMEM] * far)
    others = [swap_over(near, "grp", mask) for mask in middle_masks[1:]]
    near_across = swap_over(near, "grp", 1)

    e_fwd, h_fwd, curls_fwd, total, edges, forced, drives, base, place = call(
        functools.partial(first_fwd_kernel, layout),
        [
            field_shape,
            field_shape,
            curls_shape,
            total_shape,
            edges_shape,
            on_chip(depth, width_x, width_y),
            on_chip(STEPS, width_y),
            plane,
            on_chip(nblock, nblock, width_y),
        ],
        [IN_VMEM] * 9,
        [fwd_fields, near, wave_idx, source_pos, block_ids, material_idx, material_eps],
        [IN_VMEM] * 2 + [IN_SMEM] + [IN_HBM] * 4,
        [
            pltpu.SMEM(source_pos.shape, jnp.int32),
            pltpu.SMEM(block_ids.shape, jnp.int32),
            pltpu.SMEM(material_idx.shape, jnp.int32),
            pltpu.SMEM(material_eps.shape, F32),
            pltpu.SemaphoreType.DMA((4,)),
        ],
        micros=1.5,
    )
    e_adj, h_adj, curls_adj = call(
        first_kernel,
        [field_shape, field_shape, curls_shape],
        [IN_VMEM] * 3,
        [adj_fields, near],
        [IN_VMEM, IN_VMEM],
        micros=1.2,
    )
    others = [tie(part, [e_fwd, e_adj]) for part in others]
    early = [near] + others + [near_across]
    last = [swap_over(part, "grp", 1) for part in others]
    first_slot = far * len(early)

    h_fwd, curls_fwd, h_adj, curls_adj, blocks = call(
        functools.partial(settle_kernel, layout[: len(early)]),
        [field_shape, curls_shape] * 2 + [on_chip(nblock, *piece)],
        [IN_VMEM] * 5,
        [h_fwd, curls_fwd, h_adj, curls_adj, e_fwd, e_adj, below, above] + early + [block_ids],
        [IN_VMEM] * (8 + len(early)) + [IN_HBM],
        [pltpu.SMEM(block_ids.shape, jnp.int32), pltpu.SemaphoreType.DMA],
        aliases={0: 0, 1: 1, 2: 2, 3: 3},
        micros=0.6,
    )
    placed = pltpu.VMEM((2, width_x + 2 * PAD, width_y), F32)
    coef = call(
        functools.partial(coef_edge_kernel, first_slot, len(last)),
        coef_shape,
        IN_VMEM,
        last + [place, base, blocks],
        [IN_VMEM] * (len(last) + 3),
        [placed],
    )

    arrived_fwd, arrived_adj = [curls_fwd], [curls_adj]
    for step in range(STEPS):
        more = npay if step < STEPS - 1 else 0

        def edge_fwd(e_fwd, h_fwd):
            return call(
                functools.partial(edge_kernel, step, 0),
                [field_shape] * 2 + [halo_shape] * more,
                [IN_VMEM] * (2 + more),
                [e_fwd, h_fwd, coef, drives, forced] + arrived_fwd,
                [IN_VMEM] * (5 + len(arrived_fwd)),
                aliases={0: 0, 1: 1},
            )

        if more:
            e_fwd, h_fwd, *pays = edge_fwd(e_fwd, h_fwd)
            arrived_fwd_next = trade(pays)
        if step > 0:
            e_adj, h_adj, e_fwd, total = call(
                functools.partial(inner_kernel, step, 1),
                [field_shape] * 3 + [total_shape],
                [IN_VMEM] * 4,
                [e_adj, h_adj, e_fwd, total, coef],
                [IN_VMEM] * 5,
                aliases={0: 0, 1: 1, 2: 2, 3: 3},
                micros=1.2,
            )
        if not more:
            e_fwd, h_fwd = edge_fwd(e_fwd, h_fwd)
            inner = by_owner(
                functools.partial(filter_inner_kernel, layout),
                depth - 2,
                [total, e_fwd, block_ids],
                [IN_VMEM, IN_VMEM, IN_HBM],
                [
                    pltpu.VMEM((nblock,) + piece, F32),
                    pltpu.VMEM((2, width_x, width_y), F32),
                    pltpu.SMEM(block_ids.shape, jnp.int32),
                    pltpu.SemaphoreType.DMA,
                ],
                0.8,
                middle,
            )
        if step == 0:
            coef = call(
                functools.partial(coef_inner_kernel, first_slot, len(last)),
                coef_shape,
                IN_VMEM,
                [coef] + last + [place, base, blocks],
                [IN_VMEM] * (len(last) + 4),
                [placed],
                aliases={0: 0},
                micros=0.6,
            )
            e_fwd, e_adj, total = call(
                begin_kernel,
                [field_shape, field_shape, total_shape],
                [IN_VMEM] * 3,
                [e_fwd, e_adj, total, coef, drives, forced, curls_fwd, curls_adj],
                [IN_VMEM] * 8,
                aliases={0: 0, 1: 1, 2: 2},
                micros=0.5,
            )
        e_adj, h_adj, e_fwd, edges, *pays = call(
            functools.partial(edge_kernel, step, 1),
            [field_shape] * 3 + [edges_shape] + [halo_shape] * more,
            [IN_VMEM] * (4 + more),
            [e_adj, h_adj, e_fwd, edges, coef] + arrived_adj,
            [IN_VMEM] * (5 + len(arrived_adj)),
            aliases={0: 0, 1: 1, 2: 2, 3: 3},
        )
        if not more:
            break
        arrived_fwd, arrived_adj = arrived_fwd_next, trade(pays)
        e_fwd, h_fwd = call(
            functools.partial(inner_kernel, step + 1, 0),
            [field_shape] * 2,
            [IN_VMEM] * 2,
            [e_fwd, h_fwd, coef, drives, forced],
            [IN_VMEM] * 5,
            aliases={0: 0, 1: 1},
            micros=1.1,
        )

    ends = by_owner(
        functools.partial(filter_edge_kernel, layout),
        2,
        [total, edges, place],
        [IN_VMEM] * 3,
        [
            pltpu.VMEM((2, width_x + 2 * PAD, width_y), F32),
            pltpu.VMEM((2, width_x, width_y), F32),
        ],
        0.3,
        1,
    )
    inner = add_middle(*inner, ends[0][:1])
    ends = add_middle(*ends, [])
    joined = call(
        functools.partial(join_kernel, middle, block_rows),
        on_chip(*group),
        IN_VMEM,
        inner + ends,
        [IN_VMEM] * (2 * middle),
    )
    lines = [[step * 2 * middle + line for step in range(far)] for line in range(2 * middle)]
    got = lax.all_to_all(joined, "grp", 0, 0, axis_index_groups=lines)
    scale = 3.0 / (STEPS * math.sqrt(ngrp))
    grad = call(
        functools.partial(last_kernel, scale),
        jax.ShapeDtypeStruct(piece, F32),
        IN_VMEM,
        [got],
        [IN_VMEM],
    )
    finals = call(
        out_kernel,
        jax.ShapeDtypeStruct(fwd_fields.shape, F32),
        IN_HBM,
        [e_fwd, h_fwd],
        [IN_VMEM] * 2,
        [
            pltpu.VMEM((3, depth, width_x, width_y), F32),
            pltpu.SemaphoreType.DMA((6,)),
        ],
        micros=1.7,
    )
    return finals, grad.reshape(density.shape)


def solution(mesh):
    placed = (
        P("grp", None, "slab", None, None),
        P("grp", None, "slab", None, None),
        P("slab", "grp", None),
        P(),
        P(),
        P(),
        P("grp", None),
        P("grp"),
    )
    return jax.shard_map(
        per_device,
        mesh=mesh,
        in_specs=placed,
        out_specs=(P("grp", None, "slab", None, None), P("slab", "grp", None)),
        check_vma=False,
    )
```

```python
import functools
import math

import jax
import jax.numpy as jnp
from jax import lax
from jax.experimental import pallas as pl
from jax.experimental.pallas import tpu as pltpu
from jax.sharding import PartitionSpec as P

STEPS = 4
AMPLITUDE = 4.0
PAD = 8
F32 = jnp.float32
HBM_PER_MICRO = 1.0e5

VMEM = pltpu.MemorySpace.VMEM
IN_VMEM = pl.BlockSpec(memory_space=pltpu.VMEM)
IN_SMEM = pl.BlockSpec(memory_space=pltpu.SMEM)
IN_HBM = pl.BlockSpec(memory_space=pltpu.MemorySpace.HBM)


def on_chip(*shape):
    return VMEM(shape, F32)


def held(array, spec):
    if spec is IN_SMEM:
        return array
    space = VMEM if spec is IN_VMEM else pltpu.MemorySpace.HBM
    return pltpu.with_memory_space_constraint(array, space)


def call(kernel, outs, out_specs, operands, specs, scratch=(), aliases=None, micros=0.3):
    operands = [held(a, s) for a, s in zip(operands, specs)]
    return pl.pallas_call(
        kernel,
        out_shape=outs,
        in_specs=specs,
        out_specs=out_specs,
        scratch_shapes=scratch,
        input_output_aliases=aliases or {},
        compiler_params=pltpu.CompilerParams(vmem_limit_bytes=8 << 20),
        cost_estimate=pl.CostEstimate(
            flops=0, bytes_accessed=int(micros * HBM_PER_MICRO), transcendentals=0
        ),
    )(*operands)


CHUNK = 16


def chunks(rows):
    size = CHUNK if rows % CHUNK == 0 else rows
    return [(first, size) for first in range(0, rows, size)]


def next_col(value):
    column = lax.broadcasted_iota(jnp.int32, value.shape, 1)
    moved = pltpu.roll(value, value.shape[1] - 1, 1)
    return jnp.where(column == value.shape[1] - 1, 0.0, moved)


def prev_col(value):
    column = lax.broadcasted_iota(jnp.int32, value.shape, 1)
    return jnp.where(column == 0, 0.0, pltpu.roll(value, 1, 1))


def neighbours():
    slab = lax.axis_index("slab")
    return slab < lax.axis_size("slab") - 1, slab > 0


class Window:
    def __init__(self, e, h, coef=None, force=None):
        self.e, self.h, self.coef, self.force = e, h, coef, force
        self.rows = e.shape[2] - 2 * PAD
        self.depth = e.shape[1] - 1
        self.top, self.under = self.depth - 1, self.depth

    def read(self, ref, layer, first, size):
        return [ref[c, layer, pl.ds(PAD + first, size), :] for c in range(3)]

    def write(self, ref, layer, first, size, values):
        for c, value in enumerate(values):
            ref[c, layer, pl.ds(PAD + first, size), :] = value

    def put_h(self, layer, given=None, alone=False):
        for first, size in chunks(self.rows):
            rows = pl.ds(PAD + first, size)
            after = pl.ds(PAD + first + 1, size)
            ex, ey, ez = self.read(self.e, layer, first, size)
            if given is None:
                hx, hy, hz = self.read(self.h, layer, first, size)
            else:
                hx, hy, hz = (value + value for value in given(layer, first, size))
            if alone:
                rise_x, rise_y = -ex, -ey
            else:
                rise_x = self.e[0, layer + 1, rows, :] - ex
                rise_y = self.e[1, layer + 1, rows, :] - ey
            ey_after = self.e[1, layer, after, :]
            ez_after = self.e[2, layer, after, :]
            hx = hx - ((next_col(ez) - ez) - rise_y)
            hy = hy - (rise_x - (ez_after - ez))
            hz = hz - ((ey_after - ey) - (next_col(ex) - ex))
            self.write(self.h, layer, first, size, (hx, hy, hz))

    def curl_h(self, layer, lower, first, size):
        rows = pl.ds(PAD + first, size)
        before = pl.ds(PAD + first - 1, size)
        hx, hy, hz = self.read(self.h, layer, first, size)
        step_x = hx - self.h[0, lower, rows, :]
        step_y = hy - self.h[1, lower, rows, :]
        hy_before = self.h[1, layer, before, :]
        hz_before = self.h[2, layer, before, :]
        return (
            (hz - prev_col(hz)) - step_y,
            step_x - (hz - hz_before),
            (hy - hy_before) - (hx - prev_col(hx)),
        )

    def put_curl(self, curls, layer, lower):
        for first, size in chunks(self.rows):
            for c, value in enumerate(self.curl_h(layer, lower, first, size)):
                curls[c, layer, pl.ds(first, size), :] = value

    def next_e(self, layer, lower, first, size, curls=None):
        here = pl.ds(first, size)
        cell = self.coef[layer, here, :]
        if curls is None:
            curl = self.curl_h(layer, lower, first, size)
        else:
            curl = [curls[c, layer, here, :] for c in range(3)]
        ex, ey, ez = [a + cell * b for a, b in zip(self.read(self.e, layer, first, size), curl)]
        if self.force is not None:
            ez = ez + self.force(layer, here)
        return ex, ey, ez

    def put_e(self, layer, lower, curls=None, other=None, total=None, slot=None):
        for first, size in chunks(self.rows):
            news = self.next_e(layer, lower, first, size, curls)
            self.write(self.e, layer, first, size, news)
            if total is not None:
                rows = pl.ds(PAD + first, size)
                part = [a * other[c, layer, rows, :] for c, a in enumerate(news)]
                total[layer if slot is None else slot, rows, :] += part[0] + part[1] + part[2]

    def take_above(self, above):
        for first, size in chunks(self.rows):
            here, rows = pl.ds(first, size), pl.ds(PAD + first, size)
            self.h[0, self.top, rows, :] += above[1, here, :]
            self.h[1, self.top, rows, :] -= above[0, here, :]

    def take_below(self, below):
        for first, size in chunks(self.rows):
            here, rows = pl.ds(first, size), pl.ds(PAD + first, size)
            self.h[0, self.under, rows, :] = below[0, here, :] + self.e[1, 0, rows, :]
            self.h[1, self.under, rows, :] = below[1, here, :] - self.e[0, 0, rows, :]


def forcing(step, drives, forced):
    if drives is None:
        return None
    return lambda layer, here: drives[pl.ds(step, 1), :] * forced[layer, here, :]


def opening_kernel(fwd, adj, density, own, *rest):
    pays, (planes, sems) = rest[:-2], rest[-2:]
    depth, rows, width_y = fwd.shape[2:]
    top = depth - 1
    has_up, has_low = neighbours()
    held_copy = pltpu.make_async_copy(density, own, sems.at[2, 0])
    held_copy.start()

    def up(pay):
        copies = []
        for evo, given in enumerate((fwd, adj)):
            for c in range(5):
                copies.append(
                    pltpu.make_async_copy(given.at[0, c, top], planes.at[evo, c], sems.at[evo, c])
                )
        for copy in copies:
            copy.start()
        for copy in copies:
            copy.wait()
        for evo in range(2):
            for first, size in chunks(rows):
                here = pl.ds(first, size)
                ex, ey, ez, hx, hy = (planes[evo, c, here, :] for c in range(5))
                if first + size < rows:
                    ez_after = planes[evo, 2, pl.ds(first + 1, size), :]
                else:
                    row = lax.broadcasted_iota(jnp.int32, ez.shape, 0)
                    ez_after = jnp.where(row == size - 1, 0.0, pltpu.roll(ez, size - 1, 0))
                pay[evo][0, here, :] = (hx + hx) - ((next_col(ez) - ez) + ey)
                pay[evo][1, here, :] = (hy + hy) + (ex + (ez_after - ez))

    def down(pay):
        copies = []
        for evo, given in enumerate((fwd, adj)):
            for c in range(2):
                copies.append(
                    pltpu.make_async_copy(given.at[0, c, 0], pay[evo].at[c], sems.at[evo, c])
                )
        for copy in copies:
            copy.start()
        for copy in copies:
            copy.wait()

    half = len(pays) // 2
    if half == 2:
        up(pays[0::2])
        down(pays[1::2])
    else:
        pl.when(has_up)(lambda: up(pays))
        pl.when(has_low)(lambda: down(pays))
    held_copy.wait()


def first_fwd_kernel(
    layout, given, other, near, wave_idx, source_far, ids_far, idx_far, eps_far,
    e, h, curls, total, edges, forced, drives, base, place,
    source, block_ids, material_idx, material_eps, sems,
):
    fetches = [
        pltpu.make_async_copy(far, here, sems.at[slot])
        for slot, (far, here) in enumerate(
            (
                (source_far, source),
                (ids_far, block_ids),
                (idx_far, material_idx),
                (eps_far, material_eps),
            )
        )
    ]
    for fetch in fetches:
        fetch.start()
    first_kernel(given, near, e, h, curls)
    depth, rows, width_y = forced.shape
    nblock = block_ids.shape[0]
    block_rows = rows // nblock
    empty = jnp.zeros(total.shape[1:], F32)
    edges[0] = empty
    edges[1] = empty
    for layer in range(depth):
        total[layer] = empty
    for fetch in fetches:
        fetch.wait()
    xcoord = lax.broadcasted_iota(jnp.int32, (rows, width_y), 0)
    ycoord = lax.broadcasted_iota(jnp.int32, (rows, width_y), 1)
    offset_x = (xcoord - source[0, 1]).astype(F32) / (rows / 4.0)
    offset_y = (ycoord - source[0, 2]).astype(F32) / (width_y / 4.0)
    profile = jnp.exp(-0.5 * (offset_x * offset_x + offset_y * offset_y))
    step = lax.broadcasted_iota(jnp.int32, drives.shape, 0).astype(F32) + 1.0
    wave = jnp.full(drives.shape, wave_idx[0], jnp.int32).astype(F32)
    drives[...] = AMPLITUDE * jnp.sin(2.0 * math.pi / (6.0 + 2.0 * wave) * step)
    level = source[0, 0] - lax.axis_index("slab") * depth
    for layer in range(depth):
        forced[layer] = jnp.where(level == layer, 1.0, 0.0) * profile
    for block in range(nblock):
        value = jnp.full((block_rows, width_y), material_eps[material_idx[block]], F32)
        base[pl.ds(block * block_rows, block_rows), :] = value
    me = lax.axis_index("grp")
    block = lax.broadcasted_iota(jnp.int32, (nblock, width_y), 0)
    for slot, mask in enumerate(mask for masks in layout for mask in masks):
        place[slot] = jnp.where(block == block_ids[me ^ mask], 1.0, 0.0)


def first_kernel(given, near, e, h, curls):
    win = Window(e, h)
    rows, width_y = win.rows, e.shape[3]
    margin = jnp.zeros((PAD, width_y), F32)
    empty = jnp.zeros((rows + 2 * PAD, width_y), F32)
    for comp in range(3):
        e[comp, win.depth] = empty
        h[comp, win.depth] = empty

    def copy(layer):
        for comp in range(3):
            for ref in (e, h):
                ref[comp, layer, pl.ds(0, PAD), :] = margin
                ref[comp, layer, pl.ds(PAD + rows, PAD), :] = margin
            for first, size in chunks(rows):
                here = pl.ds(first, size)
                e[comp, layer, pl.ds(PAD + first, size), :] = given[0, comp, layer, here, :]

    def from_given(layer, first, size):
        return [given[0, 3 + c, layer, pl.ds(first, size), :] for c in range(3)]

    copy(0)
    copy(1)
    win.put_h(0, from_given)
    copy(2)
    win.put_h(1, from_given)

    def body(layer, carry):
        pl.when(layer + 2 < win.depth)(lambda: copy(layer + 2))
        win.put_h(layer + 1, from_given)
        win.put_curl(curls, layer, layer - 1)
        return carry

    lax.fori_loop(1, win.top, body, 0)


def settle_kernel(h_in, curls_in, e, below, above, h, curls):
    win = Window(e, h)
    has_up, has_low = neighbours()
    pl.when(has_up)(lambda: win.take_above(above))
    pl.when(has_low)(lambda: win.take_below(below))
    win.put_curl(curls, win.top, win.top - 1)
    win.put_curl(curls, 0, win.under)


def settle_adj_kernel(
    masks, h_in, curls_in, e, below, above, near, near_across, ids_far,
    h, curls, blocks, block_ids, sem,
):
    fetch = pltpu.make_async_copy(ids_far, block_ids, sem)
    fetch.start()
    nothing = jnp.zeros(blocks.shape[1:], F32)
    for block in range(blocks.shape[0]):
        blocks[block] = nothing
    settle_kernel(h_in, curls_in, e, below, above, h, curls)
    fetch.wait()
    me = lax.axis_index("grp")
    for part, part_masks in zip((near, near_across), masks):
        for slot, mask in enumerate(part_masks):
            blocks[block_ids[me ^ mask]] = part[slot]


def edge_kernel(step, evo, *refs):
    refs = list(refs)
    e_in, h_in = refs.pop(0), refs.pop(0)
    if evo == 1:
        other_in, edges_in = refs.pop(0), refs.pop(0)
    coef = refs.pop(0)
    drives, forced = (refs.pop(0), refs.pop(0)) if evo == 0 else (None, None)
    curls = refs.pop(0) if step == 0 else None
    below, above = (refs.pop(0), refs.pop(0)) if step > 0 else (None, None)
    e, h = refs.pop(0), refs.pop(0)
    other, edges = (refs.pop(0), refs.pop(0)) if evo == 1 else (None, None)
    pays = refs
    win = Window(e, h, coef, forcing(step, drives, forced))
    top = win.top
    has_up, has_low = neighbours()

    @pl.when(has_up)
    def _():
        if step > 0:
            win.take_above(above)
        win.put_e(top, top - 1, curls, other, edges, 1)
        if pays:
            win.put_h(top, alone=True)
            for c in range(2):
                pays[0][c] = h[c, top, pl.ds(PAD, win.rows), :]

    @pl.when(has_low)
    def _():
        if step > 0:
            win.take_below(below)
        win.put_e(0, win.under, curls, other, edges, 0)
        if pays:
            for c in range(2):
                pays[-1][c] = e[c, 0, pl.ds(PAD, win.rows), :]


def inner_range(top):
    has_up, has_low = neighbours()
    return jnp.where(has_low, 1, 0), jnp.where(has_up, top - 1, top)


def begin_kernel(
    e_fwd_in, e_adj_in, total_in, coef, drives, forced, curls_fwd, curls_adj,
    e_fwd, e_adj, total,
):
    fwd = Window(e_fwd, None, coef, forcing(0, drives, forced))
    adj = Window(e_adj, None, coef)
    lowest, highest = inner_range(fwd.top)

    def body(layer, carry):
        fwd.put_e(layer, None, curls_fwd)
        adj.put_e(layer, None, curls_adj, e_fwd, total)
        return carry

    lax.fori_loop(lowest, highest + 1, body, 0)


def inner_kernel(step, evo, *refs):
    refs = list(refs)
    e_in, h_in = refs.pop(0), refs.pop(0)
    if evo == 1:
        other_in, total_in = refs.pop(0), refs.pop(0)
    coef = refs.pop(0)
    drives, forced = (refs.pop(0), refs.pop(0)) if evo == 0 else (None, None)
    e, h = refs.pop(0), refs.pop(0)
    other, total = (refs.pop(0), refs.pop(0)) if evo == 1 else (None, None)
    win = Window(e, h, coef, forcing(step, drives, forced))
    lowest, highest = inner_range(win.top)
    win.put_h(0)
    pl.when(lowest == 1)(lambda: win.put_h(1))

    def body(layer, carry):
        win.put_h(layer + 1)
        win.put_e(layer, jnp.where(layer == 0, win.under, layer - 1), None, other, total)
        return carry

    if lax.axis_size("slab") == 2:
        lax.fori_loop(0, win.depth - 2, lambda i, carry: body(lowest + i, carry), 0, unroll=2)
    else:
        lax.fori_loop(lowest, highest, body, 0)
    win.put_e(highest, highest - 1, None, other, total)


def coef_layer(layer, coef, placed, base):
    for first, size in chunks(base.shape[0]):
        here = pl.ds(first, size)
        coef[layer, here, :] = 0.25 / (base[here, :] + 3.0 * filtered(placed, first, size))


def clear_margins(placed):
    rows = placed.shape[0] - 2 * PAD
    margin = jnp.zeros((PAD, placed.shape[1]), F32)
    placed[pl.ds(0, PAD), :] = margin
    placed[pl.ds(PAD + rows, PAD), :] = margin


def place_layer(pieces, place, start, placed):
    nblock = place.shape[0]
    block_rows = (placed.shape[0] - 2 * PAD) // nblock
    clear_margins(placed)
    for block in range(nblock):
        value = start(block)
        for slot, piece in pieces:
            term = place[slot, pl.ds(block, 1), :] * piece
            value = term if value is None else value + term
        placed[pl.ds(PAD + block * block_rows, block_rows), :] = value


def coef_edge_kernel(count, *refs):
    parts, (place, base, coef, placed) = refs[:count], refs[count:]
    far = parts[0].shape[0]
    block_rows = base.shape[0] // place.shape[0]
    edge_layers = (0, coef.shape[0] - 1)
    for which, layer in enumerate(edge_layers):
        pieces = []
        for number, part in enumerate(parts):
            first = (layer if number % (count // 2) == 0 else which) * block_rows
            for slot in range(far):
                pieces.append((number * far + slot, part[slot, pl.ds(first, block_rows), :]))
        place_layer(pieces, place, lambda block: None, placed.at[which])
    for which, layer in enumerate(edge_layers):
        coef_layer(layer, coef, placed.at[which], base)


def coef_inner_kernel(numbers, coef_in, *refs):
    parts, (place, base, blocks, coef, placed) = refs[: len(numbers)], refs[len(numbers) :]
    block_rows = base.shape[0] // place.shape[0]

    def body(layer, carry):
        there = placed.at[lax.rem(layer, 2)]
        late = pl.ds(pl.multiple_of((layer - 1) * block_rows, block_rows), block_rows)
        source = pl.ds(pl.multiple_of(layer * block_rows, block_rows), block_rows)
        pieces = []
        for number, part in zip(numbers, parts):
            far = part.shape[0]
            for slot in range(far):
                pieces.append((number * far + slot, part[slot, late, :]))
        place_layer(pieces, place, lambda block: blocks[block, source, :], there)
        coef_layer(layer, coef, there, base)
        return carry

    lax.fori_loop(1, coef.shape[0] - 1, body, 0, unroll=2)


def filtered(padded, first, size):
    here = padded[pl.ds(PAD + first, size), :]
    before = padded[pl.ds(PAD + first - 1, size), :]
    after = padded[pl.ds(PAD + first + 1, size), :]
    along = before + 2.0 * here + after
    return (prev_col(along) + 2.0 * along + next_col(along)) * 0.0625


def tie_kernel(*refs):
    pass


def tie(array, others):
    return call(
        tie_kernel, on_chip(*array.shape), IN_VMEM, [array] + others,
        [IN_VMEM] * (1 + len(others)), aliases={0: 0},
    )


def pack_kernel(block_rows, *refs):
    pieces, (near, ends, rest) = refs[:-3], refs[-3:]
    rows = near.shape[1]
    for slot, piece in enumerate(pieces):
        near[slot] = piece[...]
        ends[slot, pl.ds(0, block_rows), :] = piece[pl.ds(0, block_rows), :]
        ends[slot, pl.ds(block_rows, block_rows), :] = piece[pl.ds(rows - block_rows, block_rows), :]
        rest[slot] = piece[pl.ds(block_rows, rows - 2 * block_rows), :]


def filter_inner_kernel(layout, total, after, block_ids_far, *rest):
    parts, (blocks, wide, block_ids, sem) = rest[:-4], rest[-4:]
    fetch = pltpu.make_async_copy(block_ids_far, block_ids, sem)
    fetch.start()
    depth = total.shape[0]
    nblock = blocks.shape[0]
    rows = wide.shape[1]
    block_rows = rows // nblock
    me = lax.axis_index("grp")

    def body(layer, carry):
        there = wide.at[lax.rem(layer, 2)]
        for first, size in chunks(rows):
            there[pl.ds(first, size), :] = filtered(total.at[layer], first, size)
        for block in range(nblock):
            target = pl.ds(pl.multiple_of((layer - 1) * block_rows, block_rows), block_rows)
            blocks[block, target, :] = there[pl.ds(block * block_rows, block_rows), :]
        return carry

    lax.fori_loop(1, depth - 1, body, 0, unroll=2)
    fetch.wait()
    inner = pl.ds(0, (depth - 2) * block_rows)
    for slot, mask in enumerate(mask for masks in layout for mask in masks):
        part = parts[slot // parts[0].shape[0]]
        part[slot % part.shape[0]] = blocks[block_ids[me ^ mask], inner, :]


def filter_edge_kernel(layout, total, edges, place, *rest):
    parts, (sums, wide) = rest[:-2], rest[-2:]
    depth = total.shape[0]
    nblock = place.shape[0]
    rows = wide.shape[1]
    block_rows = rows // nblock
    for which, layer in enumerate((0, depth - 1)):
        sums[which] = total[layer] + edges[which]
        for first, size in chunks(rows):
            wide[which, pl.ds(first, size), :] = filtered(sums.at[which], first, size)
    for which in range(2):
        blocks = [
            wide[which, pl.ds(block * block_rows, block_rows), :] for block in range(nblock)
        ]
        target = pl.ds(which * block_rows, block_rows)
        for slot in range(nblock):
            value = None
            for block, piece in enumerate(blocks):
                term = place[slot, pl.ds(block, 1), :] * piece
                value = term if value is None else value + term
            parts[slot // parts[0].shape[0]][slot % parts[0].shape[0], target, :] = value


def add_kernel(pairs, count, *refs):
    outs = refs[-count:]
    size, per = refs[0].shape[0], outs[0].shape[0]
    for pair in range(pairs):
        kept, got = refs[pair], refs[pairs + pair]
        for first in range(0, size, per):
            part = pl.ds(first, per)
            outs[(pair * size + first) // per][...] = kept[part] + got[part]


def join_kernel(count, block_rows, *refs):
    inner, edge, outs = refs[:count], refs[count : 2 * count], refs[2 * count :]
    rows = outs[0].shape[0]
    for slot, out in enumerate(outs):
        middle, ends = inner[0][slot], edge[0][slot]
        for a, b in zip(inner[1:], edge[1:]):
            middle, ends = middle + a[slot], ends + b[slot]
        out[pl.ds(0, block_rows), :] = ends[:block_rows]
        out[pl.ds(block_rows, rows - 2 * block_rows), :] = middle
        out[pl.ds(rows - block_rows, block_rows), :] = ends[block_rows:]


def last_kernel(scale, *refs):
    value = refs[0][...]
    for ref in refs[1:-1]:
        value = value + ref[...]
    refs[-1][...] = value * scale


def out_kernel(e, h, finals, halves, sems):
    depth = e.shape[1] - 1
    rows = e.shape[2] - 2 * PAD
    every = pl.ds(PAD, rows)
    copies = [
        pltpu.make_async_copy(e.at[c, pl.ds(0, depth), every, :], finals.at[0, c], sems.at[c])
        for c in range(3)
    ]
    for copy in copies:
        copy.start()
    for c in range(3):

        def body(layer, carry, c=c):
            halves[c, layer] = 0.5 * h[c, layer, every, :]
            return carry

        lax.fori_loop(0, depth, body, 0)
        copy = pltpu.make_async_copy(halves.at[c], finals.at[0, 3 + c], sems.at[3 + c])
        copy.start()
        copies.append(copy)
    for copy in copies:
        copy.wait()


def swap_over(array, axis, mask):
    return lax.ppermute(array, axis, [(i, i ^ mask) for i in range(lax.axis_size(axis))])


def shift_over(array, axis, distance):
    size = lax.axis_size(axis)
    route = [(i, i + distance) for i in range(size) if 0 <= i + distance < size]
    return lax.ppermute(array, axis, route)


def trade(pays):
    if len(pays) == 1:
        return [swap_over(pays[0], "slab", 1)] * 2
    return [shift_over(pays[0], "slab", 1), shift_over(pays[1], "slab", -1)]


def per_device(
    fwd_fields, adj_fields, density, block_ids, material_idx, material_eps, source_pos, wave_idx
):
    depth, width_x, width_y = fwd_fields.shape[2:]
    nblock = block_ids.shape[0]
    block_rows = width_x // nblock
    ngrp = lax.axis_size("grp")
    npay = 1 if lax.axis_size("slab") == 2 else 2

    far = 4
    middle = ngrp // (2 * far)
    far_masks = [2 * middle * j for j in range(far)]
    middle_masks = [2 * j for j in range(middle)]
    layout = [
        [core + mid + top for top in far_masks] for core in (0, 1) for mid in middle_masks
    ]
    piece = (depth * block_rows, width_y)
    group = (far,) + piece

    field_shape = on_chip(3, depth + 1, width_x + 2 * PAD, width_y)
    curls_shape = on_chip(3, depth, width_x, width_y)
    halo_shape = on_chip(2, width_x, width_y)
    total_shape = on_chip(depth, width_x + 2 * PAD, width_y)
    edges_shape = on_chip(2, width_x + 2 * PAD, width_y)
    coef_shape = on_chip(depth, width_x, width_y)
    plane = on_chip(width_x, width_y)

    def by_owner(kernel, layers, operands, specs, scratch, micros, messages):
        slots = middle * far // messages
        parts = call(
            kernel,
            [on_chip(slots, layers * block_rows, width_y)] * (2 * messages),
            [IN_VMEM] * (2 * messages),
            operands,
            specs,
            scratch,
            micros=micros,
        )
        return list(parts[:messages]), [swap_over(part, "grp", 1) for part in parts[messages:]]

    def add_middle(kept, got, after):
        sums = call(
            functools.partial(add_kernel, len(kept), middle),
            [on_chip(far, *kept[0].shape[1:])] * middle,
            [IN_VMEM] * middle,
            kept + got + after,
            [IN_VMEM] * (len(kept + got + after)),
        )
        return [sums[0]] + [
            swap_over(part, "grp", mask) for part, mask in zip(sums[1:], middle_masks[1:])
        ]

    design = density.reshape(piece)
    got = [swap_over(design, "grp", mask) for mask in far_masks[1:]]
    own, *pays = call(
        opening_kernel,
        [on_chip(*piece)] + [halo_shape] * (2 * npay),
        [IN_VMEM] * (1 + 2 * npay),
        [fwd_fields, adj_fields, design],
        [IN_HBM] * 3,
        [pltpu.VMEM((2, 5, width_x, width_y), F32), pltpu.SemaphoreType.DMA((3, 5))],
    )
    first_fwd, first_adj = trade(pays[:npay]), trade(pays[npay:])

    near, near_ends, near_rest = call(
        functools.partial(pack_kernel, block_rows),
        [
            on_chip(*group),
            on_chip(far, 2 * block_rows, width_y),
            on_chip(far, (depth - 2) * block_rows, width_y),
        ],
        [IN_VMEM] * 3,
        [own] + got,
        [IN_VMEM] * far,
    )
    ends = [swap_over(near_ends, "grp", mask) for mask in middle_masks[1:]]
    rest = [swap_over(near_rest, "grp", mask) for mask in middle_masks[1:]]
    near_across = swap_over(near, "grp", 1)

    e_fwd, h_fwd, curls_fwd, total, edges, forced, drives, base, place = call(
        functools.partial(first_fwd_kernel, layout),
        [
            field_shape,
            field_shape,
            curls_shape,
            total_shape,
            edges_shape,
            on_chip(depth, width_x, width_y),
            on_chip(STEPS, width_y),
            plane,
            on_chip(nblock, nblock, width_y),
        ],
        [IN_VMEM] * 9,
        [fwd_fields, adj_fields, near, wave_idx, source_pos, block_ids, material_idx, material_eps],
        [IN_VMEM] * 3 + [IN_SMEM] + [IN_HBM] * 4,
        [
            pltpu.SMEM(source_pos.shape, jnp.int32),
            pltpu.SMEM(block_ids.shape, jnp.int32),
            pltpu.SMEM(material_idx.shape, jnp.int32),
            pltpu.SMEM(material_eps.shape, F32),
            pltpu.SemaphoreType.DMA((4,)),
        ],
        micros=1.5,
    )
    ends = [tie(part, [e_fwd]) for part in ends]
    ends = [near] + ends + [near_across] + [swap_over(part, "grp", 1) for part in ends]
    h_fwd, curls_fwd = call(
        settle_kernel,
        [field_shape, curls_shape],
        [IN_VMEM] * 2,
        [h_fwd, curls_fwd, e_fwd] + first_fwd,
        [IN_VMEM] * 5,
        aliases={0: 0, 1: 1},
    )
    placed = pltpu.VMEM((2, width_x + 2 * PAD, width_y), F32)
    coef = call(
        functools.partial(coef_edge_kernel, len(ends)),
        coef_shape,
        IN_VMEM,
        ends + [place, base],
        [IN_VMEM] * (len(ends) + 2),
        [placed],
    )

    arrived_fwd, arrived_adj = [curls_fwd], []
    for step in range(STEPS):
        more = npay if step < STEPS - 1 else 0

        def edge_fwd(e_fwd, h_fwd):
            return call(
                functools.partial(edge_kernel, step, 0),
                [field_shape] * 2 + [halo_shape] * more,
                [IN_VMEM] * (2 + more),
                [e_fwd, h_fwd, coef, drives, forced] + arrived_fwd,
                [IN_VMEM] * (5 + len(arrived_fwd)),
                aliases={0: 0, 1: 1},
            )

        if more:
            e_fwd, h_fwd, *pays = edge_fwd(e_fwd, h_fwd)
            arrived_fwd_next = trade(pays)
        if step == 0:
            e_adj, h_adj, curls_adj = call(
                first_kernel,
                [field_shape, field_shape, curls_shape],
                [IN_VMEM] * 3,
                [adj_fields, pays[0]],
                [IN_VMEM, IN_VMEM],
                micros=1.2,
            )
            rest = [tie(part, [e_adj]) for part in rest]
            rest = rest + [swap_over(part, "grp", 1) for part in rest]
            late_numbers = [*range(1, middle), *range(middle + 1, 2 * middle)]
            h_adj, curls_adj, blocks = call(
                functools.partial(settle_adj_kernel, [layout[0], layout[middle]]),
                [field_shape, curls_shape, on_chip(nblock, *piece)],
                [IN_VMEM] * 3,
                [h_adj, curls_adj, e_adj] + first_adj + [near, near_across, block_ids],
                [IN_VMEM] * 7 + [IN_HBM],
                [pltpu.SMEM(block_ids.shape, jnp.int32), pltpu.SemaphoreType.DMA],
                aliases={0: 0, 1: 1},
                micros=0.6,
            )
            arrived_adj = [curls_adj]
        if step > 0:
            e_adj, h_adj, e_fwd, total = call(
                functools.partial(inner_kernel, step, 1),
                [field_shape] * 3 + [total_shape],
                [IN_VMEM] * 4,
                [e_adj, h_adj, e_fwd, total, coef],
                [IN_VMEM] * 5,
                aliases={0: 0, 1: 1, 2: 2, 3: 3},
                micros=1.2,
            )
        if not more:
            e_fwd, h_fwd = edge_fwd(e_fwd, h_fwd)
            inner = by_owner(
                functools.partial(filter_inner_kernel, layout),
                depth - 2,
                [total, e_fwd, block_ids],
                [IN_VMEM, IN_VMEM, IN_HBM],
                [
                    pltpu.VMEM((nblock,) + piece, F32),
                    pltpu.VMEM((2, width_x, width_y), F32),
                    pltpu.SMEM(block_ids.shape, jnp.int32),
                    pltpu.SemaphoreType.DMA,
                ],
                0.8,
                middle,
            )
        e_adj, h_adj, e_fwd, edges, *pays = call(
            functools.partial(edge_kernel, step, 1),
            [field_shape] * 3 + [edges_shape] + [halo_shape] * more,
            [IN_VMEM] * (4 + more),
            [e_adj, h_adj, e_fwd, edges, coef] + arrived_adj,
            [IN_VMEM] * (5 + len(arrived_adj)),
            aliases={0: 0, 1: 1, 2: 2, 3: 3},
        )
        if not more:
            break
        arrived_fwd, arrived_adj = arrived_fwd_next, trade(pays)
        if step == 0:
            coef = call(
                functools.partial(coef_inner_kernel, late_numbers),
                coef_shape,
                IN_VMEM,
                [coef] + rest + [place, base, blocks],
                [IN_VMEM] * (len(rest) + 4),
                [placed],
                aliases={0: 0},
                micros=0.6,
            )
            e_fwd, e_adj, total = call(
                begin_kernel,
                [field_shape, field_shape, total_shape],
                [IN_VMEM] * 3,
                [e_fwd, e_adj, total, coef, drives, forced, curls_fwd, curls_adj],
                [IN_VMEM] * 8,
                aliases={0: 0, 1: 1, 2: 2},
                micros=0.5,
            )
        e_fwd, h_fwd = call(
            functools.partial(inner_kernel, step + 1, 0),
            [field_shape] * 2,
            [IN_VMEM] * 2,
            [e_fwd, h_fwd, coef, drives, forced],
            [IN_VMEM] * 5,
            aliases={0: 0, 1: 1},
            micros=1.1,
        )

    ends = by_owner(
        functools.partial(filter_edge_kernel, layout),
        2,
        [total, edges, place],
        [IN_VMEM] * 3,
        [
            pltpu.VMEM((2, width_x + 2 * PAD, width_y), F32),
            pltpu.VMEM((2, width_x, width_y), F32),
        ],
        0.3,
        1,
    )
    inner = add_middle(*inner, ends[0][:1])
    ends = add_middle(*ends, [])
    pieces = call(
        functools.partial(join_kernel, middle, block_rows),
        [on_chip(*piece)] * far,
        [IN_VMEM] * far,
        inner + ends,
        [IN_VMEM] * (2 * middle),
    )
    got = [swap_over(part, "grp", mask) for part, mask in zip(pieces[:0:-1], far_masks[:0:-1])]
    scale = 3.0 / (STEPS * math.sqrt(ngrp))
    grad = call(
        functools.partial(last_kernel, scale),
        jax.ShapeDtypeStruct(piece, F32),
        IN_VMEM,
        [pieces[0]] + got,
        [IN_VMEM] * far,
    )
    finals = call(
        out_kernel,
        jax.ShapeDtypeStruct(fwd_fields.shape, F32),
        IN_HBM,
        [e_fwd, h_fwd],
        [IN_VMEM] * 2,
        [
            pltpu.VMEM((3, depth, width_x, width_y), F32),
            pltpu.SemaphoreType.DMA((6,)),
        ],
        micros=1.7,
    )
    return finals, grad.reshape(density.shape)


def solution(mesh):
    placed = (
        P("grp", None, "slab", None, None),
        P("grp", None, "slab", None, None),
        P("slab", "grp", None),
        P(),
        P(),
        P(),
        P("grp", None),
        P("grp"),
    )
    return jax.shard_map(
        per_device,
        mesh=mesh,
        in_specs=placed,
        out_specs=(P("grp", None, "slab", None, None), P("slab", "grp", None)),
        check_vma=False,
    )
```

```python
import functools
import math

import jax
import jax.numpy as jnp
from jax import lax
from jax.experimental import pallas as pl
from jax.experimental.pallas import tpu as pltpu
from jax.sharding import PartitionSpec as P

STEPS = 4
AMPLITUDE = 4.0
PAD = 8
F32 = jnp.float32
HBM_PER_MICRO = 1.0e5

VMEM = pltpu.MemorySpace.VMEM
IN_VMEM = pl.BlockSpec(memory_space=pltpu.VMEM)
IN_SMEM = pl.BlockSpec(memory_space=pltpu.SMEM)
IN_HBM = pl.BlockSpec(memory_space=pltpu.MemorySpace.HBM)


def on_chip(*shape):
    return VMEM(shape, F32)


def held(array, spec):
    if spec is IN_SMEM:
        return array
    space = VMEM if spec is IN_VMEM else pltpu.MemorySpace.HBM
    return pltpu.with_memory_space_constraint(array, space)


def call(kernel, outs, out_specs, operands, specs, scratch=(), aliases=None, micros=0.3):
    operands = [held(a, s) for a, s in zip(operands, specs)]
    return pl.pallas_call(
        kernel,
        out_shape=outs,
        in_specs=specs,
        out_specs=out_specs,
        scratch_shapes=scratch,
        input_output_aliases=aliases or {},
        compiler_params=pltpu.CompilerParams(vmem_limit_bytes=8 << 20),
        cost_estimate=pl.CostEstimate(
            flops=0, bytes_accessed=int(micros * HBM_PER_MICRO), transcendentals=0
        ),
    )(*operands)


CHUNK = 16


def chunks(rows):
    size = CHUNK if rows % CHUNK == 0 else rows
    return [(first, size) for first in range(0, rows, size)]


def next_col(value):
    column = lax.broadcasted_iota(jnp.int32, value.shape, 1)
    moved = pltpu.roll(value, value.shape[1] - 1, 1)
    return jnp.where(column == value.shape[1] - 1, 0.0, moved)


def prev_col(value):
    column = lax.broadcasted_iota(jnp.int32, value.shape, 1)
    return jnp.where(column == 0, 0.0, pltpu.roll(value, 1, 1))


def neighbours():
    slab = lax.axis_index("slab")
    return slab < lax.axis_size("slab") - 1, slab > 0


class Window:
    def __init__(self, e, h, coef=None, force=None):
        self.e, self.h, self.coef, self.force = e, h, coef, force
        self.rows = e.shape[2] - 2 * PAD
        self.depth = e.shape[1] - 1
        self.top, self.under = self.depth - 1, self.depth

    def read(self, ref, layer, first, size):
        return [ref[c, layer, pl.ds(PAD + first, size), :] for c in range(3)]

    def write(self, ref, layer, first, size, values):
        for c, value in enumerate(values):
            ref[c, layer, pl.ds(PAD + first, size), :] = value

    def put_h(self, layer, given=None, alone=False):
        for first, size in chunks(self.rows):
            rows = pl.ds(PAD + first, size)
            after = pl.ds(PAD + first + 1, size)
            ex, ey, ez = self.read(self.e, layer, first, size)
            if given is None:
                hx, hy, hz = self.read(self.h, layer, first, size)
            else:
                hx, hy, hz = (value + value for value in given(layer, first, size))
            if alone:
                rise_x, rise_y = -ex, -ey
            else:
                rise_x = self.e[0, layer + 1, rows, :] - ex
                rise_y = self.e[1, layer + 1, rows, :] - ey
            ey_after = self.e[1, layer, after, :]
            ez_after = self.e[2, layer, after, :]
            hx = hx - ((next_col(ez) - ez) - rise_y)
            hy = hy - (rise_x - (ez_after - ez))
            hz = hz - ((ey_after - ey) - (next_col(ex) - ex))
            self.write(self.h, layer, first, size, (hx, hy, hz))

    def curl_h(self, layer, lower, first, size):
        rows = pl.ds(PAD + first, size)
        before = pl.ds(PAD + first - 1, size)
        hx, hy, hz = self.read(self.h, layer, first, size)
        step_x = hx - self.h[0, lower, rows, :]
        step_y = hy - self.h[1, lower, rows, :]
        hy_before = self.h[1, layer, before, :]
        hz_before = self.h[2, layer, before, :]
        return (
            (hz - prev_col(hz)) - step_y,
            step_x - (hz - hz_before),
            (hy - hy_before) - (hx - prev_col(hx)),
        )

    def put_curl(self, curls, layer, lower):
        for first, size in chunks(self.rows):
            for c, value in enumerate(self.curl_h(layer, lower, first, size)):
                curls[c, layer, pl.ds(first, size), :] = value

    def next_e(self, layer, lower, first, size, curls=None):
        here = pl.ds(first, size)
        cell = self.coef[layer, here, :]
        if curls is None:
            curl = self.curl_h(layer, lower, first, size)
        else:
            curl = [curls[c, layer, here, :] for c in range(3)]
        ex, ey, ez = [a + cell * b for a, b in zip(self.read(self.e, layer, first, size), curl)]
        if self.force is not None:
            ez = ez + self.force(layer, here)
        return ex, ey, ez

    def put_e(self, layer, lower, curls=None, other=None, total=None, slot=None):
        for first, size in chunks(self.rows):
            news = self.next_e(layer, lower, first, size, curls)
            self.write(self.e, layer, first, size, news)
            if total is not None:
                rows = pl.ds(PAD + first, size)
                part = [a * other[c, layer, rows, :] for c, a in enumerate(news)]
                total[layer if slot is None else slot, rows, :] += part[0] + part[1] + part[2]

    def take_above(self, above):
        for first, size in chunks(self.rows):
            here, rows = pl.ds(first, size), pl.ds(PAD + first, size)
            self.h[0, self.top, rows, :] += above[1, here, :]
            self.h[1, self.top, rows, :] -= above[0, here, :]

    def take_below(self, below):
        for first, size in chunks(self.rows):
            here, rows = pl.ds(first, size), pl.ds(PAD + first, size)
            self.h[0, self.under, rows, :] = below[0, here, :] + self.e[1, 0, rows, :]
            self.h[1, self.under, rows, :] = below[1, here, :] - self.e[0, 0, rows, :]


def forcing(step, drives, forced):
    if drives is None:
        return None
    return lambda layer, here: drives[pl.ds(step, 1), :] * forced[layer, here, :]


def opening_kernel(fwd, adj, density, own, *rest):
    pays, (planes, sems) = rest[:-2], rest[-2:]
    depth, rows, width_y = fwd.shape[2:]
    top = depth - 1
    has_up, has_low = neighbours()
    held_copy = pltpu.make_async_copy(density, own, sems.at[2, 0])
    held_copy.start()

    def up(pay):
        copies = []
        for evo, given in enumerate((fwd, adj)):
            for c in range(5):
                copies.append(
                    pltpu.make_async_copy(given.at[0, c, top], planes.at[evo, c], sems.at[evo, c])
                )
        for copy in copies:
            copy.start()
        for copy in copies:
            copy.wait()
        for evo in range(2):
            for first, size in chunks(rows):
                here = pl.ds(first, size)
                ex, ey, ez, hx, hy = (planes[evo, c, here, :] for c in range(5))
                if first + size < rows:
                    ez_after = planes[evo, 2, pl.ds(first + 1, size), :]
                else:
                    row = lax.broadcasted_iota(jnp.int32, ez.shape, 0)
                    ez_after = jnp.where(row == size - 1, 0.0, pltpu.roll(ez, size - 1, 0))
                pay[evo, 0, here, :] = (hx + hx) - ((next_col(ez) - ez) + ey)
                pay[evo, 1, here, :] = (hy + hy) + (ex + (ez_after - ez))

    def down(pay):
        copies = []
        for evo, given in enumerate((fwd, adj)):
            for c in range(2):
                copies.append(
                    pltpu.make_async_copy(given.at[0, c, 0], pay.at[evo, c], sems.at[evo, c])
                )
        for copy in copies:
            copy.start()
        for copy in copies:
            copy.wait()

    if len(pays) == 2:
        up(pays[0])
        down(pays[1])
    else:
        pl.when(has_up)(lambda: up(pays[0]))
        pl.when(has_low)(lambda: down(pays[0]))
    held_copy.wait()


def first_fwd_kernel(
    layout, given, near, wave_idx, source_far, ids_far, idx_far, eps_far,
    e, h, curls, total, edges, forced, drives, base, place,
    source, block_ids, material_idx, material_eps, sems,
):
    fetches = [
        pltpu.make_async_copy(far, here, sems.at[slot])
        for slot, (far, here) in enumerate(
            (
                (source_far, source),
                (ids_far, block_ids),
                (idx_far, material_idx),
                (eps_far, material_eps),
            )
        )
    ]
    for fetch in fetches:
        fetch.start()
    first_kernel(given, near, e, h, curls)
    depth, rows, width_y = forced.shape
    nblock = block_ids.shape[0]
    block_rows = rows // nblock
    empty = jnp.zeros(total.shape[1:], F32)
    edges[0] = empty
    edges[1] = empty
    for layer in range(depth):
        total[layer] = empty
    for fetch in fetches:
        fetch.wait()
    xcoord = lax.broadcasted_iota(jnp.int32, (rows, width_y), 0)
    ycoord = lax.broadcasted_iota(jnp.int32, (rows, width_y), 1)
    offset_x = (xcoord - source[0, 1]).astype(F32) / (rows / 4.0)
    offset_y = (ycoord - source[0, 2]).astype(F32) / (width_y / 4.0)
    profile = jnp.exp(-0.5 * (offset_x * offset_x + offset_y * offset_y))
    step = lax.broadcasted_iota(jnp.int32, drives.shape, 0).astype(F32) + 1.0
    wave = jnp.full(drives.shape, wave_idx[0], jnp.int32).astype(F32)
    drives[...] = AMPLITUDE * jnp.sin(2.0 * math.pi / (6.0 + 2.0 * wave) * step)
    level = source[0, 0] - lax.axis_index("slab") * depth
    for layer in range(depth):
        forced[layer] = jnp.where(level == layer, 1.0, 0.0) * profile
    for block in range(nblock):
        value = jnp.full((block_rows, width_y), material_eps[material_idx[block]], F32)
        base[pl.ds(block * block_rows, block_rows), :] = value
    me = lax.axis_index("grp")
    block = lax.broadcasted_iota(jnp.int32, (nblock, width_y), 0)
    for slot, mask in enumerate(mask for masks in layout for mask in masks):
        place[slot] = jnp.where(block == block_ids[me ^ mask], 1.0, 0.0)


def first_kernel(given, near, e, h, curls):
    win = Window(e, h)
    rows, width_y = win.rows, e.shape[3]
    margin = jnp.zeros((PAD, width_y), F32)
    empty = jnp.zeros((rows + 2 * PAD, width_y), F32)
    for comp in range(3):
        e[comp, win.depth] = empty
        h[comp, win.depth] = empty

    def copy(layer):
        for comp in range(3):
            for ref in (e, h):
                ref[comp, layer, pl.ds(0, PAD), :] = margin
                ref[comp, layer, pl.ds(PAD + rows, PAD), :] = margin
            for first, size in chunks(rows):
                here = pl.ds(first, size)
                e[comp, layer, pl.ds(PAD + first, size), :] = given[0, comp, layer, here, :]

    def from_given(layer, first, size):
        return [given[0, 3 + c, layer, pl.ds(first, size), :] for c in range(3)]

    copy(0)
    copy(1)
    win.put_h(0, from_given)
    copy(2)
    win.put_h(1, from_given)

    def body(layer, carry):
        pl.when(layer + 2 < win.depth)(lambda: copy(layer + 2))
        win.put_h(layer + 1, from_given)
        win.put_curl(curls, layer, layer - 1)
        return carry

    lax.fori_loop(1, win.top, body, 0)


def settle_kernel(layout, *refs):
    refs = list(refs)
    del refs[:4]
    e_fwd, e_adj, below, above = (refs.pop(0) for _ in range(4))
    parts = [refs.pop(0) for _ in layout]
    ids_far, h_fwd, curls_fwd, h_adj, curls_adj, blocks, block_ids, sem = refs
    fetch = pltpu.make_async_copy(ids_far, block_ids, sem)
    fetch.start()
    nothing = jnp.zeros(blocks.shape[1:], F32)
    for block in range(blocks.shape[0]):
        blocks[block] = nothing
    has_up, has_low = neighbours()
    for evo, (e, h, curls) in enumerate(((e_fwd, h_fwd, curls_fwd), (e_adj, h_adj, curls_adj))):
        win = Window(e, h)
        pl.when(has_up)(lambda: win.take_above(above.at[evo]))
        pl.when(has_low)(lambda: win.take_below(below.at[evo]))
        win.put_curl(curls, win.top, win.top - 1)
        win.put_curl(curls, 0, win.under)
    fetch.wait()
    me = lax.axis_index("grp")
    for part, masks in zip(parts, layout):
        for slot, mask in enumerate(masks):
            blocks[block_ids[me ^ mask]] = part[slot]


def edge_kernel(step, evo, *refs):
    refs = list(refs)
    e_in, h_in = refs.pop(0), refs.pop(0)
    if evo == 1:
        other_in, edges_in = refs.pop(0), refs.pop(0)
    coef = refs.pop(0)
    drives, forced = (refs.pop(0), refs.pop(0)) if evo == 0 else (None, None)
    curls = refs.pop(0) if step == 0 else None
    below, above = (refs.pop(0), refs.pop(0)) if step > 0 else (None, None)
    e, h = refs.pop(0), refs.pop(0)
    other, edges = (refs.pop(0), refs.pop(0)) if evo == 1 else (None, None)
    pays = refs
    win = Window(e, h, coef, forcing(step, drives, forced))
    top = win.top
    has_up, has_low = neighbours()

    @pl.when(has_up)
    def _():
        if step > 0:
            win.take_above(above)
        win.put_e(top, top - 1, curls, other, edges, 1)
        if pays:
            win.put_h(top, alone=True)
            for c in range(2):
                pays[0][c] = h[c, top, pl.ds(PAD, win.rows), :]

    @pl.when(has_low)
    def _():
        if step > 0:
            win.take_below(below)
        win.put_e(0, win.under, curls, other, edges, 0)
        if pays:
            for c in range(2):
                pays[-1][c] = e[c, 0, pl.ds(PAD, win.rows), :]


def inner_range(top):
    has_up, has_low = neighbours()
    return jnp.where(has_low, 1, 0), jnp.where(has_up, top - 1, top)


def begin_kernel(
    e_fwd_in, e_adj_in, total_in, coef, drives, forced, curls_fwd, curls_adj,
    e_fwd, e_adj, total,
):
    fwd = Window(e_fwd, None, coef, forcing(0, drives, forced))
    adj = Window(e_adj, None, coef)
    lowest, highest = inner_range(fwd.top)

    def body(layer, carry):
        fwd.put_e(layer, None, curls_fwd)
        adj.put_e(layer, None, curls_adj, e_fwd, total)
        return carry

    lax.fori_loop(lowest, highest + 1, body, 0)


def inner_kernel(step, evo, *refs):
    refs = list(refs)
    e_in, h_in = refs.pop(0), refs.pop(0)
    if evo == 1:
        other_in, total_in = refs.pop(0), refs.pop(0)
    coef = refs.pop(0)
    drives, forced = (refs.pop(0), refs.pop(0)) if evo == 0 else (None, None)
    e, h = refs.pop(0), refs.pop(0)
    other, total = (refs.pop(0), refs.pop(0)) if evo == 1 else (None, None)
    win = Window(e, h, coef, forcing(step, drives, forced))
    lowest, highest = inner_range(win.top)
    win.put_h(0)
    pl.when(lowest == 1)(lambda: win.put_h(1))

    def body(layer, carry):
        win.put_h(layer + 1)
        win.put_e(layer, jnp.where(layer == 0, win.under, layer - 1), None, other, total)
        return carry

    if lax.axis_size("slab") == 2:
        lax.fori_loop(0, win.depth - 2, lambda i, carry: body(lowest + i, carry), 0, unroll=2)
    else:
        lax.fori_loop(lowest, highest, body, 0)
    win.put_e(highest, highest - 1, None, other, total)


def coef_layer(layer, coef, placed, base):
    for first, size in chunks(base.shape[0]):
        here = pl.ds(first, size)
        coef[layer, here, :] = 0.25 / (base[here, :] + 3.0 * filtered(placed, first, size))


def clear_margins(placed):
    rows = placed.shape[0] - 2 * PAD
    margin = jnp.zeros((PAD, placed.shape[1]), F32)
    placed[pl.ds(0, PAD), :] = margin
    placed[pl.ds(PAD + rows, PAD), :] = margin


def place_layer(layer, first_slot, parts, place, blocks, placed):
    nblock = blocks.shape[0]
    block_rows = (placed.shape[0] - 2 * PAD) // nblock
    clear_margins(placed)
    start = layer * block_rows
    source = pl.ds(start if isinstance(layer, int) else pl.multiple_of(start, block_rows), block_rows)
    pieces = [part[slot, source, :] for part in parts for slot in range(part.shape[0])]
    for block in range(nblock):
        value = blocks[block, source, :]
        for slot, piece in enumerate(pieces):
            value = value + place[first_slot + slot, pl.ds(block, 1), :] * piece
        placed[pl.ds(PAD + block * block_rows, block_rows), :] = value


def coef_edge_kernel(first_slot, count, *refs):
    parts, (place, base, blocks, coef, placed) = refs[:count], refs[count:]
    edge_layers = (0, coef.shape[0] - 1)
    for which, layer in enumerate(edge_layers):
        place_layer(layer, first_slot, parts, place, blocks, placed.at[which])
    for which, layer in enumerate(edge_layers):
        coef_layer(layer, coef, placed.at[which], base)


def coef_inner_kernel(first_slot, count, coef_in, *refs):
    parts, (place, base, blocks, coef, placed) = refs[:count], refs[count:]

    def body(layer, carry):
        there = placed.at[lax.rem(layer, 2)]
        place_layer(layer, first_slot, parts, place, blocks, there)
        coef_layer(layer, coef, there, base)
        return carry

    lax.fori_loop(1, coef.shape[0] - 1, body, 0, unroll=2)


def filtered(padded, first, size):
    here = padded[pl.ds(PAD + first, size), :]
    before = padded[pl.ds(PAD + first - 1, size), :]
    after = padded[pl.ds(PAD + first + 1, size), :]
    along = before + 2.0 * here + after
    return (prev_col(along) + 2.0 * along + next_col(along)) * 0.0625


def tie_kernel(*refs):
    pass


def tie(array, others):
    return call(
        tie_kernel, on_chip(*array.shape), IN_VMEM, [array] + others,
        [IN_VMEM] * (1 + len(others)), aliases={0: 0},
    )


def pack_kernel(*refs):
    out = refs[-1]
    for slot, ref in enumerate(refs[:-1]):
        out[slot] = ref[...]


def filter_inner_kernel(layout, total, after, block_ids_far, *rest):
    parts, (blocks, wide, block_ids, sem) = rest[:-4], rest[-4:]
    fetch = pltpu.make_async_copy(block_ids_far, block_ids, sem)
    fetch.start()
    depth = total.shape[0]
    nblock = blocks.shape[0]
    rows = wide.shape[1]
    block_rows = rows // nblock
    me = lax.axis_index("grp")

    def body(layer, carry):
        there = wide.at[lax.rem(layer, 2)]
        for first, size in chunks(rows):
            there[pl.ds(first, size), :] = filtered(total.at[layer], first, size)
        for block in range(nblock):
            target = pl.ds(pl.multiple_of((layer - 1) * block_rows, block_rows), block_rows)
            blocks[block, target, :] = there[pl.ds(block * block_rows, block_rows), :]
        return carry

    lax.fori_loop(1, depth - 1, body, 0, unroll=2)
    fetch.wait()
    inner = pl.ds(0, (depth - 2) * block_rows)
    for slot, mask in enumerate(mask for masks in layout for mask in masks):
        part = parts[slot // parts[0].shape[0]]
        part[slot % part.shape[0]] = blocks[block_ids[me ^ mask], inner, :]


def filter_edge_kernel(layout, total, edges, place, *rest):
    parts, (sums, wide) = rest[:-2], rest[-2:]
    depth = total.shape[0]
    nblock = place.shape[0]
    rows = wide.shape[1]
    block_rows = rows // nblock
    for which, layer in enumerate((0, depth - 1)):
        sums[which] = total[layer] + edges[which]
        for first, size in chunks(rows):
            wide[which, pl.ds(first, size), :] = filtered(sums.at[which], first, size)
    for which in range(2):
        blocks = [
            wide[which, pl.ds(block * block_rows, block_rows), :] for block in range(nblock)
        ]
        target = pl.ds(which * block_rows, block_rows)
        for slot in range(nblock):
            value = None
            for block, piece in enumerate(blocks):
                term = place[slot, pl.ds(block, 1), :] * piece
                value = term if value is None else value + term
            parts[slot // parts[0].shape[0]][slot % parts[0].shape[0], target, :] = value


def add_kernel(pairs, count, *refs):
    outs = refs[-count:]
    size, per = refs[0].shape[0], outs[0].shape[0]
    for pair in range(pairs):
        kept, got = refs[pair], refs[pairs + pair]
        for first in range(0, size, per):
            part = pl.ds(first, per)
            outs[(pair * size + first) // per][...] = kept[part] + got[part]


def join_kernel(count, block_rows, *refs):
    inner, edge, outs = refs[:count], refs[count : 2 * count], refs[2 * count :]
    rows = outs[0].shape[0]
    for slot, out in enumerate(outs):
        middle, ends = inner[0][slot], edge[0][slot]
        for a, b in zip(inner[1:], edge[1:]):
            middle, ends = middle + a[slot], ends + b[slot]
        out[pl.ds(0, block_rows), :] = ends[:block_rows]
        out[pl.ds(block_rows, rows - 2 * block_rows), :] = middle
        out[pl.ds(rows - block_rows, block_rows), :] = ends[block_rows:]


def last_kernel(scale, *refs):
    value = refs[0][...]
    for ref in refs[1:-1]:
        value = value + ref[...]
    refs[-1][...] = value * scale


def out_kernel(e, h, finals, halves, sems):
    depth = e.shape[1] - 1
    rows = e.shape[2] - 2 * PAD
    every = pl.ds(PAD, rows)
    copies = [
        pltpu.make_async_copy(e.at[c, pl.ds(0, depth), every, :], finals.at[0, c], sems.at[c])
        for c in range(3)
    ]
    for copy in copies:
        copy.start()
    for c in range(3):

        def body(layer, carry, c=c):
            halves[c, layer] = 0.5 * h[c, layer, every, :]
            return carry

        lax.fori_loop(0, depth, body, 0)
        copy = pltpu.make_async_copy(halves.at[c], finals.at[0, 3 + c], sems.at[3 + c])
        copy.start()
        copies.append(copy)
    for copy in copies:
        copy.wait()


def swap_over(array, axis, mask):
    return lax.ppermute(array, axis, [(i, i ^ mask) for i in range(lax.axis_size(axis))])


def shift_over(array, axis, distance):
    size = lax.axis_size(axis)
    route = [(i, i + distance) for i in range(size) if 0 <= i + distance < size]
    return lax.ppermute(array, axis, route)


def trade(pays):
    if len(pays) == 1:
        return [swap_over(pays[0], "slab", 1)] * 2
    return [shift_over(pays[0], "slab", 1), shift_over(pays[1], "slab", -1)]


def per_device(
    fwd_fields, adj_fields, density, block_ids, material_idx, material_eps, source_pos, wave_idx
):
    depth, width_x, width_y = fwd_fields.shape[2:]
    nblock = block_ids.shape[0]
    block_rows = width_x // nblock
    ngrp = lax.axis_size("grp")
    npay = 1 if lax.axis_size("slab") == 2 else 2

    far = 4
    middle = ngrp // (2 * far)
    far_masks = [2 * middle * j for j in range(far)]
    middle_masks = [2 * j for j in range(middle)]
    layout = [
        [core + mid + top for top in far_masks] for core in (0, 1) for mid in middle_masks
    ]
    piece = (depth * block_rows, width_y)
    group = (far,) + piece

    field_shape = on_chip(3, depth + 1, width_x + 2 * PAD, width_y)
    curls_shape = on_chip(3, depth, width_x, width_y)
    halo_shape = on_chip(2, width_x, width_y)
    total_shape = on_chip(depth, width_x + 2 * PAD, width_y)
    edges_shape = on_chip(2, width_x + 2 * PAD, width_y)
    coef_shape = on_chip(depth, width_x, width_y)
    plane = on_chip(width_x, width_y)

    def by_owner(kernel, layers, operands, specs, scratch, micros, messages):
        slots = middle * far // messages
        parts = call(
            kernel,
            [on_chip(slots, layers * block_rows, width_y)] * (2 * messages),
            [IN_VMEM] * (2 * messages),
            operands,
            specs,
            scratch,
            micros=micros,
        )
        return list(parts[:messages]), [swap_over(part, "grp", 1) for part in parts[messages:]]

    def add_middle(kept, got, after):
        sums = call(
            functools.partial(add_kernel, len(kept), middle),
            [on_chip(far, *kept[0].shape[1:])] * middle,
            [IN_VMEM] * middle,
            kept + got + after,
            [IN_VMEM] * (len(kept + got + after)),
        )
        return [sums[0]] + [
            swap_over(part, "grp", mask) for part, mask in zip(sums[1:], middle_masks[1:])
        ]

    design = density.reshape(piece)
    got = [swap_over(design, "grp", mask) for mask in far_masks[1:]]
    own, *pays = call(
        opening_kernel,
        [on_chip(*piece)] + [on_chip(2, 2, width_x, width_y)] * npay,
        [IN_VMEM] * (1 + npay),
        [fwd_fields, adj_fields, design],
        [IN_HBM] * 3,
        [pltpu.VMEM((2, 5, width_x, width_y), F32), pltpu.SemaphoreType.DMA((3, 5))],
    )
    below, above = trade(pays)

    near = call(pack_kernel, on_chip(*group), IN_VMEM, [own] + got, [IN_VMEM] * far)
    others = [swap_over(near, "grp", mask) for mask in middle_masks[1:]]
    near_across = swap_over(near, "grp", 1)

    e_fwd, h_fwd, curls_fwd, total, edges, forced, drives, base, place = call(
        functools.partial(first_fwd_kernel, layout),
        [
            field_shape,
            field_shape,
            curls_shape,
            total_shape,
            edges_shape,
            on_chip(depth, width_x, width_y),
            on_chip(STEPS, width_y),
            plane,
            on_chip(nblock, nblock, width_y),
        ],
        [IN_VMEM] * 9,
        [fwd_fields, near, wave_idx, source_pos, block_ids, material_idx, material_eps],
        [IN_VMEM] * 2 + [IN_SMEM] + [IN_HBM] * 4,
        [
            pltpu.SMEM(source_pos.shape, jnp.int32),
            pltpu.SMEM(block_ids.shape, jnp.int32),
            pltpu.SMEM(material_idx.shape, jnp.int32),
            pltpu.SMEM(material_eps.shape, F32),
            pltpu.SemaphoreType.DMA((4,)),
        ],
        micros=1.5,
    )
    e_adj, h_adj, curls_adj = call(
        first_kernel,
        [field_shape, field_shape, curls_shape],
        [IN_VMEM] * 3,
        [adj_fields, near],
        [IN_VMEM, IN_VMEM],
        micros=1.2,
    )
    others = [tie(part, [e_fwd, e_adj]) for part in others]
    early = [near] + others + [near_across]
    last = [swap_over(part, "grp", 1) for part in others]
    first_slot = far * len(early)

    h_fwd, curls_fwd, h_adj, curls_adj, blocks = call(
        functools.partial(settle_kernel, layout[: len(early)]),
        [field_shape, curls_shape] * 2 + [on_chip(nblock, *piece)],
        [IN_VMEM] * 5,
        [h_fwd, curls_fwd, h_adj, curls_adj, e_fwd, e_adj, below, above] + early + [block_ids],
        [IN_VMEM] * (8 + len(early)) + [IN_HBM],
        [pltpu.SMEM(block_ids.shape, jnp.int32), pltpu.SemaphoreType.DMA],
        aliases={0: 0, 1: 1, 2: 2, 3: 3},
        micros=0.6,
    )
    placed = pltpu.VMEM((2, width_x + 2 * PAD, width_y), F32)
    coef = call(
        functools.partial(coef_edge_kernel, first_slot, len(last)),
        coef_shape,
        IN_VMEM,
        last + [place, base, blocks],
        [IN_VMEM] * (len(last) + 3),
        [placed],
    )

    arrived_fwd, arrived_adj = [curls_fwd], [curls_adj]
    for step in range(STEPS):
        more = npay if step < STEPS - 1 else 0

        def edge_fwd(e_fwd, h_fwd):
            return call(
                functools.partial(edge_kernel, step, 0),
                [field_shape] * 2 + [halo_shape] * more,
                [IN_VMEM] * (2 + more),
                [e_fwd, h_fwd, coef, drives, forced] + arrived_fwd,
                [IN_VMEM] * (5 + len(arrived_fwd)),
                aliases={0: 0, 1: 1},
            )

        if more:
            e_fwd, h_fwd, *pays = edge_fwd(e_fwd, h_fwd)
            arrived_fwd_next = trade(pays)
        if step > 0:
            e_adj, h_adj, e_fwd, total = call(
                functools.partial(inner_kernel, step, 1),
                [field_shape] * 3 + [total_shape],
                [IN_VMEM] * 4,
                [e_adj, h_adj, e_fwd, total, coef],
                [IN_VMEM] * 5,
                aliases={0: 0, 1: 1, 2: 2, 3: 3},
                micros=1.2,
            )
        if not more:
            e_fwd, h_fwd = edge_fwd(e_fwd, h_fwd)
            inner = by_owner(
                functools.partial(filter_inner_kernel, layout),
                depth - 2,
                [total, e_fwd, block_ids],
                [IN_VMEM, IN_VMEM, IN_HBM],
                [
                    pltpu.VMEM((nblock,) + piece, F32),
                    pltpu.VMEM((2, width_x, width_y), F32),
                    pltpu.SMEM(block_ids.shape, jnp.int32),
                    pltpu.SemaphoreType.DMA,
                ],
                0.8,
                middle,
            )
        e_adj, h_adj, e_fwd, edges, *pays = call(
            functools.partial(edge_kernel, step, 1),
            [field_shape] * 3 + [edges_shape] + [halo_shape] * more,
            [IN_VMEM] * (4 + more),
            [e_adj, h_adj, e_fwd, edges, coef] + arrived_adj,
            [IN_VMEM] * (5 + len(arrived_adj)),
            aliases={0: 0, 1: 1, 2: 2, 3: 3},
        )
        if not more:
            break
        arrived_fwd, arrived_adj = arrived_fwd_next, trade(pays)
        if step == 0:
            coef = call(
                functools.partial(coef_inner_kernel, first_slot, len(last)),
                coef_shape,
                IN_VMEM,
                [coef] + last + [place, base, blocks],
                [IN_VMEM] * (len(last) + 4),
                [placed],
                aliases={0: 0},
                micros=0.6,
            )
            e_fwd, e_adj, total = call(
                begin_kernel,
                [field_shape, field_shape, total_shape],
                [IN_VMEM] * 3,
                [e_fwd, e_adj, total, coef, drives, forced, curls_fwd, curls_adj],
                [IN_VMEM] * 8,
                aliases={0: 0, 1: 1, 2: 2},
                micros=0.5,
            )
        e_fwd, h_fwd = call(
            functools.partial(inner_kernel, step + 1, 0),
            [field_shape] * 2,
            [IN_VMEM] * 2,
            [e_fwd, h_fwd, coef, drives, forced],
            [IN_VMEM] * 5,
            aliases={0: 0, 1: 1},
            micros=1.1,
        )

    ends = by_owner(
        functools.partial(filter_edge_kernel, layout),
        2,
        [total, edges, place],
        [IN_VMEM] * 3,
        [
            pltpu.VMEM((2, width_x + 2 * PAD, width_y), F32),
            pltpu.VMEM((2, width_x, width_y), F32),
        ],
        0.3,
        1,
    )
    inner = add_middle(*inner, ends[0][:1])
    ends = add_middle(*ends, [])
    pieces = call(
        functools.partial(join_kernel, middle, block_rows),
        [on_chip(*piece)] * far,
        [IN_VMEM] * far,
        inner + ends,
        [IN_VMEM] * (2 * middle),
    )
    got = [swap_over(part, "grp", mask) for part, mask in zip(pieces[:0:-1], far_masks[:0:-1])]
    scale = 3.0 / (STEPS * math.sqrt(ngrp))
    grad = call(
        functools.partial(last_kernel, scale),
        jax.ShapeDtypeStruct(piece, F32),
        IN_VMEM,
        [pieces[0]] + got,
        [IN_VMEM] * far,
    )
    finals = call(
        out_kernel,
        jax.ShapeDtypeStruct(fwd_fields.shape, F32),
        IN_HBM,
        [e_fwd, h_fwd],
        [IN_VMEM] * 2,
        [
            pltpu.VMEM((3, depth, width_x, width_y), F32),
            pltpu.SemaphoreType.DMA((6,)),
        ],
        micros=1.7,
    )
    return finals, grad.reshape(density.shape)


def solution(mesh):
    placed = (
        P("grp", None, "slab", None, None),
        P("grp", None, "slab", None, None),
        P("slab", "grp", None),
        P(),
        P(),
        P(),
        P("grp", None),
        P("grp"),
    )
    return jax.shard_map(
        per_device,
        mesh=mesh,
        in_specs=placed,
        out_specs=(P("grp", None, "slab", None, None), P("slab", "grp", None)),
        check_vma=False,
    )
```

```python
import functools
import math

import jax
import jax.numpy as jnp
from jax import lax
from jax.experimental import pallas as pl
from jax.experimental.pallas import tpu as pltpu
from jax.sharding import PartitionSpec as P

STEPS = 4
AMPLITUDE = 4.0
PAD = 8
F32 = jnp.float32
HBM_PER_MICRO = 1.0e5

VMEM = pltpu.MemorySpace.VMEM
IN_VMEM = pl.BlockSpec(memory_space=pltpu.VMEM)
IN_SMEM = pl.BlockSpec(memory_space=pltpu.SMEM)
IN_HBM = pl.BlockSpec(memory_space=pltpu.MemorySpace.HBM)


def on_chip(*shape):
    return VMEM(shape, F32)


def held(array, spec):
    if spec is IN_SMEM:
        return array
    space = VMEM if spec is IN_VMEM else pltpu.MemorySpace.HBM
    return pltpu.with_memory_space_constraint(array, space)


def call(kernel, outs, out_specs, operands, specs, scratch=(), aliases=None, micros=0.3):
    operands = [held(a, s) for a, s in zip(operands, specs)]
    return pl.pallas_call(
        kernel,
        out_shape=outs,
        in_specs=specs,
        out_specs=out_specs,
        scratch_shapes=scratch,
        input_output_aliases=aliases or {},
        compiler_params=pltpu.CompilerParams(vmem_limit_bytes=8 << 20),
        cost_estimate=pl.CostEstimate(
            flops=0, bytes_accessed=int(micros * HBM_PER_MICRO), transcendentals=0
        ),
    )(*operands)


CHUNK = 16


def chunks(rows):
    size = CHUNK if rows % CHUNK == 0 else rows
    return [(first, size) for first in range(0, rows, size)]


def next_col(value):
    column = lax.broadcasted_iota(jnp.int32, value.shape, 1)
    moved = pltpu.roll(value, value.shape[1] - 1, 1)
    return jnp.where(column == value.shape[1] - 1, 0.0, moved)


def prev_col(value):
    column = lax.broadcasted_iota(jnp.int32, value.shape, 1)
    return jnp.where(column == 0, 0.0, pltpu.roll(value, 1, 1))


def neighbours():
    slab = lax.axis_index("slab")
    return slab < lax.axis_size("slab") - 1, slab > 0


class Window:
    def __init__(self, e, h, coef=None, force=None):
        self.e, self.h, self.coef, self.force = e, h, coef, force
        self.rows = e.shape[2] - 2 * PAD
        self.depth = e.shape[1] - 1
        self.top, self.under = self.depth - 1, self.depth

    def read(self, ref, layer, first, size):
        return [ref[c, layer, pl.ds(PAD + first, size), :] for c in range(3)]

    def write(self, ref, layer, first, size, values):
        for c, value in enumerate(values):
            ref[c, layer, pl.ds(PAD + first, size), :] = value

    def put_h(self, layer, given=None, alone=False):
        for first, size in chunks(self.rows):
            rows = pl.ds(PAD + first, size)
            after = pl.ds(PAD + first + 1, size)
            ex, ey, ez = self.read(self.e, layer, first, size)
            if given is None:
                hx, hy, hz = self.read(self.h, layer, first, size)
            else:
                hx, hy, hz = (value + value for value in given(layer, first, size))
            if alone:
                rise_x, rise_y = -ex, -ey
            else:
                rise_x = self.e[0, layer + 1, rows, :] - ex
                rise_y = self.e[1, layer + 1, rows, :] - ey
            ey_after = self.e[1, layer, after, :]
            ez_after = self.e[2, layer, after, :]
            hx = hx - ((next_col(ez) - ez) - rise_y)
            hy = hy - (rise_x - (ez_after - ez))
            hz = hz - ((ey_after - ey) - (next_col(ex) - ex))
            self.write(self.h, layer, first, size, (hx, hy, hz))

    def curl_h(self, layer, lower, first, size):
        rows = pl.ds(PAD + first, size)
        before = pl.ds(PAD + first - 1, size)
        hx, hy, hz = self.read(self.h, layer, first, size)
        step_x = hx - self.h[0, lower, rows, :]
        step_y = hy - self.h[1, lower, rows, :]
        hy_before = self.h[1, layer, before, :]
        hz_before = self.h[2, layer, before, :]
        return (
            (hz - prev_col(hz)) - step_y,
            step_x - (hz - hz_before),
            (hy - hy_before) - (hx - prev_col(hx)),
        )

    def put_curl(self, curls, layer, lower):
        for first, size in chunks(self.rows):
            for c, value in enumerate(self.curl_h(layer, lower, first, size)):
                curls[c, layer, pl.ds(first, size), :] = value

    def next_e(self, layer, lower, first, size, curls=None):
        here = pl.ds(first, size)
        cell = self.coef[layer, here, :]
        if curls is None:
            curl = self.curl_h(layer, lower, first, size)
        else:
            curl = [curls[c, layer, here, :] for c in range(3)]
        ex, ey, ez = [a + cell * b for a, b in zip(self.read(self.e, layer, first, size), curl)]
        if self.force is not None:
            ez = ez + self.force(layer, here)
        return ex, ey, ez

    def put_e(self, layer, lower, curls=None, other=None, total=None, slot=None):
        for first, size in chunks(self.rows):
            news = self.next_e(layer, lower, first, size, curls)
            self.write(self.e, layer, first, size, news)
            if total is not None:
                rows = pl.ds(PAD + first, size)
                part = [a * other[c, layer, rows, :] for c, a in enumerate(news)]
                total[layer if slot is None else slot, rows, :] += part[0] + part[1] + part[2]

    def take_above(self, above):
        for first, size in chunks(self.rows):
            here, rows = pl.ds(first, size), pl.ds(PAD + first, size)
            self.h[0, self.top, rows, :] += above[1, here, :]
            self.h[1, self.top, rows, :] -= above[0, here, :]

    def take_below(self, below):
        for first, size in chunks(self.rows):
            here, rows = pl.ds(first, size), pl.ds(PAD + first, size)
            self.h[0, self.under, rows, :] = below[0, here, :] + self.e[1, 0, rows, :]
            self.h[1, self.under, rows, :] = below[1, here, :] - self.e[0, 0, rows, :]


def forcing(step, drives, forced):
    if drives is None:
        return None
    return lambda layer, here: drives[pl.ds(step, 1), :] * forced[layer, here, :]


def opening_kernel(fwd, adj, density, own, *rest):
    pays, (planes, sems) = rest[:-2], rest[-2:]
    depth, rows, width_y = fwd.shape[2:]
    top = depth - 1
    has_up, has_low = neighbours()
    held_copy = pltpu.make_async_copy(density, own, sems.at[2, 0])
    held_copy.start()

    def up(pay):
        copies = []
        for evo, given in enumerate((fwd, adj)):
            for c in range(5):
                copies.append(
                    pltpu.make_async_copy(given.at[0, c, top], planes.at[evo, c], sems.at[evo, c])
                )
        for copy in copies:
            copy.start()
        for copy in copies:
            copy.wait()
        for evo in range(2):
            for first, size in chunks(rows):
                here = pl.ds(first, size)
                ex, ey, ez, hx, hy = (planes[evo, c, here, :] for c in range(5))
                if first + size < rows:
                    ez_after = planes[evo, 2, pl.ds(first + 1, size), :]
                else:
                    row = lax.broadcasted_iota(jnp.int32, ez.shape, 0)
                    ez_after = jnp.where(row == size - 1, 0.0, pltpu.roll(ez, size - 1, 0))
                pay[evo, 0, here, :] = (hx + hx) - ((next_col(ez) - ez) + ey)
                pay[evo, 1, here, :] = (hy + hy) + (ex + (ez_after - ez))

    def down(pay):
        copies = []
        for evo, given in enumerate((fwd, adj)):
            for c in range(2):
                copies.append(
                    pltpu.make_async_copy(given.at[0, c, 0], pay.at[evo, c], sems.at[evo, c])
                )
        for copy in copies:
            copy.start()
        for copy in copies:
            copy.wait()

    if len(pays) == 2:
        up(pays[0])
        down(pays[1])
    else:
        pl.when(has_up)(lambda: up(pays[0]))
        pl.when(has_low)(lambda: down(pays[0]))
    held_copy.wait()


def first_fwd_kernel(
    layout, given, near, wave_idx, source_far, ids_far, idx_far, eps_far,
    e, h, curls, total, edges, forced, drives, base, place,
    source, block_ids, material_idx, material_eps, sems,
):
    fetches = [
        pltpu.make_async_copy(far, here, sems.at[slot])
        for slot, (far, here) in enumerate(
            (
                (source_far, source),
                (ids_far, block_ids),
                (idx_far, material_idx),
                (eps_far, material_eps),
            )
        )
    ]
    for fetch in fetches:
        fetch.start()
    first_kernel(given, near, e, h, curls)
    depth, rows, width_y = forced.shape
    nblock = block_ids.shape[0]
    block_rows = rows // nblock
    empty = jnp.zeros(total.shape[1:], F32)
    edges[0] = empty
    edges[1] = empty
    for layer in range(depth):
        total[layer] = empty
    for fetch in fetches:
        fetch.wait()
    xcoord = lax.broadcasted_iota(jnp.int32, (rows, width_y), 0)
    ycoord = lax.broadcasted_iota(jnp.int32, (rows, width_y), 1)
    offset_x = (xcoord - source[0, 1]).astype(F32) / (rows / 4.0)
    offset_y = (ycoord - source[0, 2]).astype(F32) / (width_y / 4.0)
    profile = jnp.exp(-0.5 * (offset_x * offset_x + offset_y * offset_y))
    step = lax.broadcasted_iota(jnp.int32, drives.shape, 0).astype(F32) + 1.0
    wave = jnp.full(drives.shape, wave_idx[0], jnp.int32).astype(F32)
    drives[...] = AMPLITUDE * jnp.sin(2.0 * math.pi / (6.0 + 2.0 * wave) * step)
    level = source[0, 0] - lax.axis_index("slab") * depth
    for layer in range(depth):
        forced[layer] = jnp.where(level == layer, 1.0, 0.0) * profile
    for block in range(nblock):
        value = jnp.full((block_rows, width_y), material_eps[material_idx[block]], F32)
        base[pl.ds(block * block_rows, block_rows), :] = value
    me = lax.axis_index("grp")
    block = lax.broadcasted_iota(jnp.int32, (nblock, width_y), 0)
    for slot, mask in enumerate(mask for masks in layout for mask in masks):
        place[slot] = jnp.where(block == block_ids[me ^ mask], 1.0, 0.0)


def first_kernel(given, near, e, h, curls):
    win = Window(e, h)
    rows, width_y = win.rows, e.shape[3]
    margin = jnp.zeros((PAD, width_y), F32)
    empty = jnp.zeros((rows + 2 * PAD, width_y), F32)
    for comp in range(3):
        e[comp, win.depth] = empty
        h[comp, win.depth] = empty

    def copy(layer):
        for comp in range(3):
            for ref in (e, h):
                ref[comp, layer, pl.ds(0, PAD), :] = margin
                ref[comp, layer, pl.ds(PAD + rows, PAD), :] = margin
            for first, size in chunks(rows):
                here = pl.ds(first, size)
                e[comp, layer, pl.ds(PAD + first, size), :] = given[0, comp, layer, here, :]

    def from_given(layer, first, size):
        return [given[0, 3 + c, layer, pl.ds(first, size), :] for c in range(3)]

    copy(0)
    copy(1)
    win.put_h(0, from_given)
    copy(2)
    win.put_h(1, from_given)

    def body(layer, carry):
        pl.when(layer + 2 < win.depth)(lambda: copy(layer + 2))
        win.put_h(layer + 1, from_given)
        win.put_curl(curls, layer, layer - 1)
        return carry

    lax.fori_loop(1, win.top, body, 0)


def settle_kernel(layout, *refs):
    refs = list(refs)
    del refs[:4]
    e_fwd, e_adj, below, above = (refs.pop(0) for _ in range(4))
    parts = [refs.pop(0) for _ in layout]
    ids_far, h_fwd, curls_fwd, h_adj, curls_adj, blocks, block_ids, sem = refs
    fetch = pltpu.make_async_copy(ids_far, block_ids, sem)
    fetch.start()
    nothing = jnp.zeros(blocks.shape[1:], F32)
    for block in range(blocks.shape[0]):
        blocks[block] = nothing
    has_up, has_low = neighbours()
    for evo, (e, h, curls) in enumerate(((e_fwd, h_fwd, curls_fwd), (e_adj, h_adj, curls_adj))):
        win = Window(e, h)
        pl.when(has_up)(lambda: win.take_above(above.at[evo]))
        pl.when(has_low)(lambda: win.take_below(below.at[evo]))
        win.put_curl(curls, win.top, win.top - 1)
        win.put_curl(curls, 0, win.under)
    fetch.wait()
    me = lax.axis_index("grp")
    for part, masks in zip(parts, layout):
        for slot, mask in enumerate(masks):
            blocks[block_ids[me ^ mask]] = part[slot]


def edge_kernel(step, evo, *refs):
    refs = list(refs)
    e_in, h_in = refs.pop(0), refs.pop(0)
    if evo == 1:
        other_in, edges_in = refs.pop(0), refs.pop(0)
    coef = refs.pop(0)
    drives, forced = (refs.pop(0), refs.pop(0)) if evo == 0 else (None, None)
    curls = refs.pop(0) if step == 0 else None
    below, above = (refs.pop(0), refs.pop(0)) if step > 0 else (None, None)
    e, h = refs.pop(0), refs.pop(0)
    other, edges = (refs.pop(0), refs.pop(0)) if evo == 1 else (None, None)
    pays = refs
    win = Window(e, h, coef, forcing(step, drives, forced))
    top = win.top
    has_up, has_low = neighbours()

    @pl.when(has_up)
    def _():
        if step > 0:
            win.take_above(above)
        win.put_e(top, top - 1, curls, other, edges, 1)
        if pays:
            win.put_h(top, alone=True)
            for c in range(2):
                pays[0][c] = h[c, top, pl.ds(PAD, win.rows), :]

    @pl.when(has_low)
    def _():
        if step > 0:
            win.take_below(below)
        win.put_e(0, win.under, curls, other, edges, 0)
        if pays:
            for c in range(2):
                pays[-1][c] = e[c, 0, pl.ds(PAD, win.rows), :]


def inner_range(top):
    has_up, has_low = neighbours()
    return jnp.where(has_low, 1, 0), jnp.where(has_up, top - 1, top)


def begin_kernel(
    e_fwd_in, e_adj_in, total_in, coef, drives, forced, curls_fwd, curls_adj,
    e_fwd, e_adj, total,
):
    fwd = Window(e_fwd, None, coef, forcing(0, drives, forced))
    adj = Window(e_adj, None, coef)
    lowest, highest = inner_range(fwd.top)

    def body(layer, carry):
        fwd.put_e(layer, None, curls_fwd)
        adj.put_e(layer, None, curls_adj, e_fwd, total)
        return carry

    lax.fori_loop(lowest, highest + 1, body, 0)


def inner_kernel(step, evo, *refs):
    refs = list(refs)
    e_in, h_in = refs.pop(0), refs.pop(0)
    if evo == 1:
        other_in, total_in = refs.pop(0), refs.pop(0)
    coef = refs.pop(0)
    drives, forced = (refs.pop(0), refs.pop(0)) if evo == 0 else (None, None)
    e, h = refs.pop(0), refs.pop(0)
    other, total = (refs.pop(0), refs.pop(0)) if evo == 1 else (None, None)
    win = Window(e, h, coef, forcing(step, drives, forced))
    lowest, highest = inner_range(win.top)
    win.put_h(0)
    pl.when(lowest == 1)(lambda: win.put_h(1))

    def body(layer, carry):
        win.put_h(layer + 1)
        win.put_e(layer, jnp.where(layer == 0, win.under, layer - 1), None, other, total)
        return carry

    if lax.axis_size("slab") == 2:
        lax.fori_loop(0, win.depth - 2, lambda i, carry: body(lowest + i, carry), 0, unroll=2)
    else:
        lax.fori_loop(lowest, highest, body, 0)
    win.put_e(highest, highest - 1, None, other, total)


def coef_layer(layer, coef, placed, base):
    for first, size in chunks(base.shape[0]):
        here = pl.ds(first, size)
        smooth = along_columns(along_rows(placed, first, size)) * 0.0625
        coef[layer, here, :] = 0.25 / (base[here, :] + 3.0 * smooth)


def clear_margins(placed):
    rows = placed.shape[0] - 2 * PAD
    margin = jnp.zeros((PAD, placed.shape[1]), F32)
    placed[pl.ds(0, PAD), :] = margin
    placed[pl.ds(PAD + rows, PAD), :] = margin


def place_layer(layer, first_slot, parts, place, blocks, placed):
    nblock = blocks.shape[0]
    block_rows = (placed.shape[0] - 2 * PAD) // nblock
    clear_margins(placed)
    start = layer * block_rows
    source = pl.ds(start if isinstance(layer, int) else pl.multiple_of(start, block_rows), block_rows)
    pieces = [part[slot, source, :] for part in parts for slot in range(part.shape[0])]
    for block in range(nblock):
        value = blocks[block, source, :]
        for slot, piece in enumerate(pieces):
            value = value + place[first_slot + slot, pl.ds(block, 1), :] * piece
        placed[pl.ds(PAD + block * block_rows, block_rows), :] = value


def coef_edge_kernel(first_slot, count, *refs):
    parts, (place, base, blocks, coef, placed) = refs[:count], refs[count:]
    edge_layers = (0, coef.shape[0] - 1)
    for which, layer in enumerate(edge_layers):
        place_layer(layer, first_slot, parts, place, blocks, placed.at[which])
    for which, layer in enumerate(edge_layers):
        coef_layer(layer, coef, placed.at[which], base)


def coef_inner_kernel(first_slot, count, coef_in, *refs):
    parts, (place, base, blocks, coef, placed) = refs[:count], refs[count:]

    def body(layer, carry):
        there = placed.at[lax.rem(layer, 2)]
        place_layer(layer, first_slot, parts, place, blocks, there)
        coef_layer(layer, coef, there, base)
        return carry

    lax.fori_loop(1, coef.shape[0] - 1, body, 0, unroll=2)


def along_rows(padded, first, size):
    here = padded[pl.ds(PAD + first, size), :]
    before = padded[pl.ds(PAD + first - 1, size), :]
    after = padded[pl.ds(PAD + first + 1, size), :]
    return before + 2.0 * here + after


def along_columns(value):
    return prev_col(value) + 2.0 * value + next_col(value)


def tie_kernel(*refs):
    pass


def tie(array, others):
    return call(
        tie_kernel, on_chip(*array.shape), IN_VMEM, [array] + others,
        [IN_VMEM] * (1 + len(others)), aliases={0: 0},
    )


def pack_kernel(*refs):
    out = refs[-1]
    for slot, ref in enumerate(refs[:-1]):
        out[slot] = ref[...]


def filter_inner_kernel(layout, total, after, block_ids_far, *rest):
    parts, (blocks, wide, block_ids, sem) = rest[:-4], rest[-4:]
    fetch = pltpu.make_async_copy(block_ids_far, block_ids, sem)
    fetch.start()
    depth = total.shape[0]
    nblock = blocks.shape[0]
    rows = wide.shape[1]
    block_rows = rows // nblock
    me = lax.axis_index("grp")

    def body(layer, carry):
        there = wide.at[lax.rem(layer, 2)]
        for first, size in chunks(rows):
            there[pl.ds(first, size), :] = along_rows(total.at[layer], first, size)
        for block in range(nblock):
            target = pl.ds(pl.multiple_of((layer - 1) * block_rows, block_rows), block_rows)
            blocks[block, target, :] = there[pl.ds(block * block_rows, block_rows), :]
        return carry

    lax.fori_loop(1, depth - 1, body, 0, unroll=2)
    fetch.wait()
    inner = pl.ds(0, (depth - 2) * block_rows)
    for slot, mask in enumerate(mask for masks in layout for mask in masks):
        part = parts[slot // parts[0].shape[0]]
        part[slot % part.shape[0]] = blocks[block_ids[me ^ mask], inner, :]


def filter_edge_kernel(layout, total, edges, place, *rest):
    parts, (sums, wide) = rest[:-2], rest[-2:]
    depth = total.shape[0]
    nblock = place.shape[0]
    rows = wide.shape[1]
    block_rows = rows // nblock
    for which, layer in enumerate((0, depth - 1)):
        sums[which] = total[layer] + edges[which]
        for first, size in chunks(rows):
            wide[which, pl.ds(first, size), :] = along_rows(sums.at[which], first, size)
    for which in range(2):
        blocks = [
            wide[which, pl.ds(block * block_rows, block_rows), :] for block in range(nblock)
        ]
        target = pl.ds(which * block_rows, block_rows)
        for slot in range(nblock):
            value = None
            for block, piece in enumerate(blocks):
                term = place[slot, pl.ds(block, 1), :] * piece
                value = term if value is None else value + term
            parts[slot // parts[0].shape[0]][slot % parts[0].shape[0], target, :] = value


def add_kernel(pairs, count, *refs):
    outs = refs[-count:]
    size, per = refs[0].shape[0], outs[0].shape[0]
    for pair in range(pairs):
        kept, got = refs[pair], refs[pairs + pair]
        for first in range(0, size, per):
            part = pl.ds(first, per)
            outs[(pair * size + first) // per][...] = kept[part] + got[part]


def join_kernel(count, block_rows, *refs):
    inner, edge, outs = refs[:count], refs[count : 2 * count], refs[2 * count :]
    rows = outs[0].shape[0]
    for slot, out in enumerate(outs):
        middle, ends = inner[0][slot], edge[0][slot]
        for a, b in zip(inner[1:], edge[1:]):
            middle, ends = middle + a[slot], ends + b[slot]
        out[pl.ds(0, block_rows), :] = ends[:block_rows]
        out[pl.ds(block_rows, rows - 2 * block_rows), :] = middle
        out[pl.ds(rows - block_rows, block_rows), :] = ends[block_rows:]


def last_kernel(scale, *refs):
    value = refs[0][...]
    for ref in refs[1:-1]:
        value = value + ref[...]
    refs[-1][...] = along_columns(value) * (scale * 0.0625)


def out_kernel(e, h, finals, halves, sems):
    depth = e.shape[1] - 1
    rows = e.shape[2] - 2 * PAD
    every = pl.ds(PAD, rows)
    copies = [
        pltpu.make_async_copy(e.at[c, pl.ds(0, depth), every, :], finals.at[0, c], sems.at[c])
        for c in range(3)
    ]
    for copy in copies:
        copy.start()
    for c in range(3):

        def body(layer, carry, c=c):
            halves[c, layer] = 0.5 * h[c, layer, every, :]
            return carry

        lax.fori_loop(0, depth, body, 0)
        copy = pltpu.make_async_copy(halves.at[c], finals.at[0, 3 + c], sems.at[3 + c])
        copy.start()
        copies.append(copy)
    for copy in copies:
        copy.wait()


def swap_over(array, axis, mask):
    return lax.ppermute(array, axis, [(i, i ^ mask) for i in range(lax.axis_size(axis))])


def shift_over(array, axis, distance):
    size = lax.axis_size(axis)
    route = [(i, i + distance) for i in range(size) if 0 <= i + distance < size]
    return lax.ppermute(array, axis, route)


def trade(pays):
    if len(pays) == 1:
        return [swap_over(pays[0], "slab", 1)] * 2
    return [shift_over(pays[0], "slab", 1), shift_over(pays[1], "slab", -1)]


def per_device(
    fwd_fields, adj_fields, density, block_ids, material_idx, material_eps, source_pos, wave_idx
):
    depth, width_x, width_y = fwd_fields.shape[2:]
    nblock = block_ids.shape[0]
    block_rows = width_x // nblock
    ngrp = lax.axis_size("grp")
    npay = 1 if lax.axis_size("slab") == 2 else 2

    far = 4
    middle = ngrp // (2 * far)
    far_masks = [2 * middle * j for j in range(far)]
    middle_masks = [2 * j for j in range(middle)]
    layout = [
        [core + mid + top for top in far_masks] for core in (0, 1) for mid in middle_masks
    ]
    piece = (depth * block_rows, width_y)
    group = (far,) + piece

    field_shape = on_chip(3, depth + 1, width_x + 2 * PAD, width_y)
    curls_shape = on_chip(3, depth, width_x, width_y)
    halo_shape = on_chip(2, width_x, width_y)
    total_shape = on_chip(depth, width_x + 2 * PAD, width_y)
    edges_shape = on_chip(2, width_x + 2 * PAD, width_y)
    coef_shape = on_chip(depth, width_x, width_y)
    plane = on_chip(width_x, width_y)

    def by_owner(kernel, layers, operands, specs, scratch, micros, messages):
        slots = middle * far // messages
        parts = call(
            kernel,
            [on_chip(slots, layers * block_rows, width_y)] * (2 * messages),
            [IN_VMEM] * (2 * messages),
            operands,
            specs,
            scratch,
            micros=micros,
        )
        return list(parts[:messages]), [swap_over(part, "grp", 1) for part in parts[messages:]]

    def add_middle(kept, got, after):
        sums = call(
            functools.partial(add_kernel, len(kept), middle),
            [on_chip(far, *kept[0].shape[1:])] * middle,
            [IN_VMEM] * middle,
            kept + got + after,
            [IN_VMEM] * (len(kept + got + after)),
        )
        return [sums[0]] + [
            swap_over(part, "grp", mask) for part, mask in zip(sums[1:], middle_masks[1:])
        ]

    design = density.reshape(piece)
    got = [swap_over(design, "grp", mask) for mask in far_masks[1:]]
    own, *pays = call(
        opening_kernel,
        [on_chip(*piece)] + [on_chip(2, 2, width_x, width_y)] * npay,
        [IN_VMEM] * (1 + npay),
        [fwd_fields, adj_fields, design],
        [IN_HBM] * 3,
        [pltpu.VMEM((2, 5, width_x, width_y), F32), pltpu.SemaphoreType.DMA((3, 5))],
    )
    below, above = trade(pays)

    near = call(pack_kernel, on_chip(*group), IN_VMEM, [own] + got, [IN_VMEM] * far)
    others = [swap_over(near, "grp", mask) for mask in middle_masks[1:]]
    near_across = swap_over(near, "grp", 1)

    e_fwd, h_fwd, curls_fwd, total, edges, forced, drives, base, place = call(
        functools.partial(first_fwd_kernel, layout),
        [
            field_shape,
            field_shape,
            curls_shape,
            total_shape,
            edges_shape,
            on_chip(depth, width_x, width_y),
            on_chip(STEPS, width_y),
            plane,
            on_chip(nblock, nblock, width_y),
        ],
        [IN_VMEM] * 9,
        [fwd_fields, near, wave_idx, source_pos, block_ids, material_idx, material_eps],
        [IN_VMEM] * 2 + [IN_SMEM] + [IN_HBM] * 4,
        [
            pltpu.SMEM(source_pos.shape, jnp.int32),
            pltpu.SMEM(block_ids.shape, jnp.int32),
            pltpu.SMEM(material_idx.shape, jnp.int32),
            pltpu.SMEM(material_eps.shape, F32),
            pltpu.SemaphoreType.DMA((4,)),
        ],
        micros=1.5,
    )
    e_adj, h_adj, curls_adj = call(
        first_kernel,
        [field_shape, field_shape, curls_shape],
        [IN_VMEM] * 3,
        [adj_fields, near],
        [IN_VMEM, IN_VMEM],
        micros=1.2,
    )
    others = [tie(part, [e_fwd, e_adj]) for part in others]
    early = [near] + others + [near_across]
    last = [swap_over(part, "grp", 1) for part in others]
    first_slot = far * len(early)

    h_fwd, curls_fwd, h_adj, curls_adj, blocks = call(
        functools.partial(settle_kernel, layout[: len(early)]),
        [field_shape, curls_shape] * 2 + [on_chip(nblock, *piece)],
        [IN_VMEM] * 5,
        [h_fwd, curls_fwd, h_adj, curls_adj, e_fwd, e_adj, below, above] + early + [block_ids],
        [IN_VMEM] * (8 + len(early)) + [IN_HBM],
        [pltpu.SMEM(block_ids.shape, jnp.int32), pltpu.SemaphoreType.DMA],
        aliases={0: 0, 1: 1, 2: 2, 3: 3},
        micros=0.6,
    )
    placed = pltpu.VMEM((2, width_x + 2 * PAD, width_y), F32)
    coef = call(
        functools.partial(coef_edge_kernel, first_slot, len(last)),
        coef_shape,
        IN_VMEM,
        last + [place, base, blocks],
        [IN_VMEM] * (len(last) + 3),
        [placed],
    )

    arrived_fwd, arrived_adj = [curls_fwd], [curls_adj]
    for step in range(STEPS):
        more = npay if step < STEPS - 1 else 0

        def edge_fwd(e_fwd, h_fwd):
            return call(
                functools.partial(edge_kernel, step, 0),
                [field_shape] * 2 + [halo_shape] * more,
                [IN_VMEM] * (2 + more),
                [e_fwd, h_fwd, coef, drives, forced] + arrived_fwd,
                [IN_VMEM] * (5 + len(arrived_fwd)),
                aliases={0: 0, 1: 1},
            )

        if more:
            e_fwd, h_fwd, *pays = edge_fwd(e_fwd, h_fwd)
            arrived_fwd_next = trade(pays)
        if step > 0:
            e_adj, h_adj, e_fwd, total = call(
                functools.partial(inner_kernel, step, 1),
                [field_shape] * 3 + [total_shape],
                [IN_VMEM] * 4,
                [e_adj, h_adj, e_fwd, total, coef],
                [IN_VMEM] * 5,
                aliases={0: 0, 1: 1, 2: 2, 3: 3},
                micros=1.2,
            )
        if not more:
            e_fwd, h_fwd = edge_fwd(e_fwd, h_fwd)
            inner = by_owner(
                functools.partial(filter_inner_kernel, layout),
                depth - 2,
                [total, e_fwd, block_ids],
                [IN_VMEM, IN_VMEM, IN_HBM],
                [
                    pltpu.VMEM((nblock,) + piece, F32),
                    pltpu.VMEM((2, width_x, width_y), F32),
                    pltpu.SMEM(block_ids.shape, jnp.int32),
                    pltpu.SemaphoreType.DMA,
                ],
                0.8,
                middle,
            )
        e_adj, h_adj, e_fwd, edges, *pays = call(
            functools.partial(edge_kernel, step, 1),
            [field_shape] * 3 + [edges_shape] + [halo_shape] * more,
            [IN_VMEM] * (4 + more),
            [e_adj, h_adj, e_fwd, edges, coef] + arrived_adj,
            [IN_VMEM] * (5 + len(arrived_adj)),
            aliases={0: 0, 1: 1, 2: 2, 3: 3},
        )
        if not more:
            break
        arrived_fwd, arrived_adj = arrived_fwd_next, trade(pays)
        if step == 0:
            coef = call(
                functools.partial(coef_inner_kernel, first_slot, len(last)),
                coef_shape,
                IN_VMEM,
                [coef] + last + [place, base, blocks],
                [IN_VMEM] * (len(last) + 4),
                [placed],
                aliases={0: 0},
                micros=0.6,
            )
            e_fwd, e_adj, total = call(
                begin_kernel,
                [field_shape, field_shape, total_shape],
                [IN_VMEM] * 3,
                [e_fwd, e_adj, total, coef, drives, forced, curls_fwd, curls_adj],
                [IN_VMEM] * 8,
                aliases={0: 0, 1: 1, 2: 2},
                micros=0.5,
            )
        e_fwd, h_fwd = call(
            functools.partial(inner_kernel, step + 1, 0),
            [field_shape] * 2,
            [IN_VMEM] * 2,
            [e_fwd, h_fwd, coef, drives, forced],
            [IN_VMEM] * 5,
            aliases={0: 0, 1: 1},
            micros=1.1,
        )

    ends = by_owner(
        functools.partial(filter_edge_kernel, layout),
        2,
        [total, edges, place],
        [IN_VMEM] * 3,
        [
            pltpu.VMEM((2, width_x + 2 * PAD, width_y), F32),
            pltpu.VMEM((2, width_x, width_y), F32),
        ],
        0.3,
        1,
    )
    inner = add_middle(*inner, ends[0][:1])
    ends = add_middle(*ends, [])
    pieces = call(
        functools.partial(join_kernel, middle, block_rows),
        [on_chip(*piece)] * far,
        [IN_VMEM] * far,
        inner + ends,
        [IN_VMEM] * (2 * middle),
    )
    got = [swap_over(part, "grp", mask) for part, mask in zip(pieces[:0:-1], far_masks[:0:-1])]
    scale = 3.0 / (STEPS * math.sqrt(ngrp))
    grad = call(
        functools.partial(last_kernel, scale),
        jax.ShapeDtypeStruct(piece, F32),
        IN_VMEM,
        [pieces[0]] + got,
        [IN_VMEM] * far,
    )
    finals = call(
        out_kernel,
        jax.ShapeDtypeStruct(fwd_fields.shape, F32),
        IN_HBM,
        [e_fwd, h_fwd],
        [IN_VMEM] * 2,
        [
            pltpu.VMEM((3, depth, width_x, width_y), F32),
            pltpu.SemaphoreType.DMA((6,)),
        ],
        micros=1.7,
    )
    return finals, grad.reshape(density.shape)


def solution(mesh):
    placed = (
        P("grp", None, "slab", None, None),
        P("grp", None, "slab", None, None),
        P("slab", "grp", None),
        P(),
        P(),
        P(),
        P("grp", None),
        P("grp"),
    )
    return jax.shard_map(
        per_device,
        mesh=mesh,
        in_specs=placed,
        out_specs=(P("grp", None, "slab", None, None), P("slab", "grp", None)),
        check_vma=False,
    )
```

```python
import functools
import math

import jax
import jax.numpy as jnp
from jax import lax
from jax.experimental import pallas as pl
from jax.experimental.pallas import tpu as pltpu
from jax.sharding import PartitionSpec as P

STEPS = 4
AMPLITUDE = 4.0
PAD = 8
F32 = jnp.float32
HBM_PER_MICRO = 1.0e5

VMEM = pltpu.MemorySpace.VMEM
IN_VMEM = pl.BlockSpec(memory_space=pltpu.VMEM)
IN_SMEM = pl.BlockSpec(memory_space=pltpu.SMEM)
IN_HBM = pl.BlockSpec(memory_space=pltpu.MemorySpace.HBM)


def on_chip(*shape):
    return VMEM(shape, F32)


def held(array, spec):
    if spec is IN_SMEM:
        return array
    space = VMEM if spec is IN_VMEM else pltpu.MemorySpace.HBM
    return pltpu.with_memory_space_constraint(array, space)


def call(kernel, outs, out_specs, operands, specs, scratch=(), aliases=None, micros=0.3):
    operands = [held(a, s) for a, s in zip(operands, specs)]
    return pl.pallas_call(
        kernel,
        out_shape=outs,
        in_specs=specs,
        out_specs=out_specs,
        scratch_shapes=scratch,
        input_output_aliases=aliases or {},
        compiler_params=pltpu.CompilerParams(vmem_limit_bytes=8 << 20),
        cost_estimate=pl.CostEstimate(
            flops=0, bytes_accessed=int(micros * HBM_PER_MICRO), transcendentals=0
        ),
    )(*operands)


CHUNK = 16


def chunks(rows):
    size = CHUNK if rows % CHUNK == 0 else rows
    return [(first, size) for first in range(0, rows, size)]


def next_col(value):
    column = lax.broadcasted_iota(jnp.int32, value.shape, 1)
    moved = pltpu.roll(value, value.shape[1] - 1, 1)
    return jnp.where(column == value.shape[1] - 1, 0.0, moved)


def prev_col(value):
    column = lax.broadcasted_iota(jnp.int32, value.shape, 1)
    return jnp.where(column == 0, 0.0, pltpu.roll(value, 1, 1))


def neighbours():
    slab = lax.axis_index("slab")
    return slab < lax.axis_size("slab") - 1, slab > 0


class Window:
    def __init__(self, e, h, coef=None, force=None):
        self.e, self.h, self.coef, self.force = e, h, coef, force
        self.rows = e.shape[2] - 2 * PAD
        self.depth = e.shape[1] - 1
        self.top, self.under = self.depth - 1, self.depth

    def read(self, ref, layer, first, size):
        return [ref[c, layer, pl.ds(PAD + first, size), :] for c in range(3)]

    def write(self, ref, layer, first, size, values):
        for c, value in enumerate(values):
            ref[c, layer, pl.ds(PAD + first, size), :] = value

    def put_h(self, layer, given=None, alone=False):
        for first, size in chunks(self.rows):
            rows = pl.ds(PAD + first, size)
            after = pl.ds(PAD + first + 1, size)
            ex, ey, ez = self.read(self.e, layer, first, size)
            if given is None:
                hx, hy, hz = self.read(self.h, layer, first, size)
            else:
                hx, hy, hz = (value + value for value in given(layer, first, size))
            if alone:
                rise_x, rise_y = -ex, -ey
            else:
                rise_x = self.e[0, layer + 1, rows, :] - ex
                rise_y = self.e[1, layer + 1, rows, :] - ey
            ey_after = self.e[1, layer, after, :]
            ez_after = self.e[2, layer, after, :]
            hx = hx - ((next_col(ez) - ez) - rise_y)
            hy = hy - (rise_x - (ez_after - ez))
            hz = hz - ((ey_after - ey) - (next_col(ex) - ex))
            self.write(self.h, layer, first, size, (hx, hy, hz))

    def curl_h(self, layer, lower, first, size):
        rows = pl.ds(PAD + first, size)
        before = pl.ds(PAD + first - 1, size)
        hx, hy, hz = self.read(self.h, layer, first, size)
        step_x = hx - self.h[0, lower, rows, :]
        step_y = hy - self.h[1, lower, rows, :]
        hy_before = self.h[1, layer, before, :]
        hz_before = self.h[2, layer, before, :]
        return (
            (hz - prev_col(hz)) - step_y,
            step_x - (hz - hz_before),
            (hy - hy_before) - (hx - prev_col(hx)),
        )

    def put_curl(self, curls, layer, lower):
        for first, size in chunks(self.rows):
            for c, value in enumerate(self.curl_h(layer, lower, first, size)):
                curls[c, layer, pl.ds(first, size), :] = value

    def next_e(self, layer, lower, first, size, curls=None):
        here = pl.ds(first, size)
        cell = self.coef[layer, here, :]
        if curls is None:
            curl = self.curl_h(layer, lower, first, size)
        else:
            curl = [curls[c, layer, here, :] for c in range(3)]
        ex, ey, ez = [a + cell * b for a, b in zip(self.read(self.e, layer, first, size), curl)]
        if self.force is not None:
            ez = ez + self.force(layer, here)
        return ex, ey, ez

    def put_e(self, layer, lower, curls=None, other=None, total=None, slot=None):
        for first, size in chunks(self.rows):
            news = self.next_e(layer, lower, first, size, curls)
            self.write(self.e, layer, first, size, news)
            if total is not None:
                rows = pl.ds(PAD + first, size)
                part = [a * other[c, layer, rows, :] for c, a in enumerate(news)]
                total[layer if slot is None else slot, rows, :] += part[0] + part[1] + part[2]

    def take_above(self, above):
        for first, size in chunks(self.rows):
            here, rows = pl.ds(first, size), pl.ds(PAD + first, size)
            self.h[0, self.top, rows, :] += above[1, here, :]
            self.h[1, self.top, rows, :] -= above[0, here, :]

    def take_below(self, below):
        for first, size in chunks(self.rows):
            here, rows = pl.ds(first, size), pl.ds(PAD + first, size)
            self.h[0, self.under, rows, :] = below[0, here, :] + self.e[1, 0, rows, :]
            self.h[1, self.under, rows, :] = below[1, here, :] - self.e[0, 0, rows, :]


def forcing(step, drives, forced):
    if drives is None:
        return None
    return lambda layer, here: drives[pl.ds(step, 1), :] * forced[layer, here, :]


def opening_kernel(fwd, adj, density, own, *rest):
    pays, (planes, sems) = rest[:-2], rest[-2:]
    depth, rows, width_y = fwd.shape[2:]
    top = depth - 1
    has_up, has_low = neighbours()
    held_copy = pltpu.make_async_copy(density, own, sems.at[2, 0])
    held_copy.start()

    def up(pay):
        copies = []
        for evo, given in enumerate((fwd, adj)):
            for c in range(5):
                copies.append(
                    pltpu.make_async_copy(given.at[0, c, top], planes.at[evo, c], sems.at[evo, c])
                )
        for copy in copies:
            copy.start()
        for copy in copies:
            copy.wait()
        for evo in range(2):
            for first, size in chunks(rows):
                here = pl.ds(first, size)
                ex, ey, ez, hx, hy = (planes[evo, c, here, :] for c in range(5))
                if first + size < rows:
                    ez_after = planes[evo, 2, pl.ds(first + 1, size), :]
                else:
                    row = lax.broadcasted_iota(jnp.int32, ez.shape, 0)
                    ez_after = jnp.where(row == size - 1, 0.0, pltpu.roll(ez, size - 1, 0))
                pay[evo, 0, here, :] = (hx + hx) - ((next_col(ez) - ez) + ey)
                pay[evo, 1, here, :] = (hy + hy) + (ex + (ez_after - ez))

    def down(pay):
        copies = []
        for evo, given in enumerate((fwd, adj)):
            for c in range(2):
                copies.append(
                    pltpu.make_async_copy(given.at[0, c, 0], pay.at[evo, c], sems.at[evo, c])
                )
        for copy in copies:
            copy.start()
        for copy in copies:
            copy.wait()

    if len(pays) == 2:
        up(pays[0])
        down(pays[1])
    else:
        pl.when(has_up)(lambda: up(pays[0]))
        pl.when(has_low)(lambda: down(pays[0]))
    held_copy.wait()


def first_fwd_kernel(
    layout, given, near, wave_idx, source_far, ids_far, idx_far, eps_far,
    e, h, curls, total, edges, forced, drives, base, place,
    source, block_ids, material_idx, material_eps, sems,
):
    fetches = [
        pltpu.make_async_copy(far, here, sems.at[slot])
        for slot, (far, here) in enumerate(
            (
                (source_far, source),
                (ids_far, block_ids),
                (idx_far, material_idx),
                (eps_far, material_eps),
            )
        )
    ]
    for fetch in fetches:
        fetch.start()
    first_kernel(given, near, e, h, curls)
    depth, rows, width_y = forced.shape
    nblock = block_ids.shape[0]
    block_rows = rows // nblock
    empty = jnp.zeros(total.shape[1:], F32)
    edges[0] = empty
    edges[1] = empty
    for layer in range(depth):
        total[layer] = empty
    for fetch in fetches:
        fetch.wait()
    xcoord = lax.broadcasted_iota(jnp.int32, (rows, width_y), 0)
    ycoord = lax.broadcasted_iota(jnp.int32, (rows, width_y), 1)
    offset_x = (xcoord - source[0, 1]).astype(F32) / (rows / 4.0)
    offset_y = (ycoord - source[0, 2]).astype(F32) / (width_y / 4.0)
    profile = jnp.exp(-0.5 * (offset_x * offset_x + offset_y * offset_y))
    step = lax.broadcasted_iota(jnp.int32, drives.shape, 0).astype(F32) + 1.0
    wave = jnp.full(drives.shape, wave_idx[0], jnp.int32).astype(F32)
    drives[...] = AMPLITUDE * jnp.sin(2.0 * math.pi / (6.0 + 2.0 * wave) * step)
    level = source[0, 0] - lax.axis_index("slab") * depth
    for layer in range(depth):
        forced[layer] = jnp.where(level == layer, 1.0, 0.0) * profile
    for block in range(nblock):
        value = jnp.full((block_rows, width_y), material_eps[material_idx[block]], F32)
        base[pl.ds(block * block_rows, block_rows), :] = value
    me = lax.axis_index("grp")
    block = lax.broadcasted_iota(jnp.int32, (nblock, width_y), 0)
    for slot, mask in enumerate(mask for masks in layout for mask in masks):
        place[slot] = jnp.where(block == block_ids[me ^ mask], 1.0, 0.0)


def first_kernel(given, near, e, h, curls):
    win = Window(e, h)
    rows, width_y = win.rows, e.shape[3]
    margin = jnp.zeros((PAD, width_y), F32)
    empty = jnp.zeros((rows + 2 * PAD, width_y), F32)
    for comp in range(3):
        e[comp, win.depth] = empty
        h[comp, win.depth] = empty

    def copy(layer):
        for comp in range(3):
            for ref in (e, h):
                ref[comp, layer, pl.ds(0, PAD), :] = margin
                ref[comp, layer, pl.ds(PAD + rows, PAD), :] = margin
            for first, size in chunks(rows):
                here = pl.ds(first, size)
                e[comp, layer, pl.ds(PAD + first, size), :] = given[0, comp, layer, here, :]

    def from_given(layer, first, size):
        return [given[0, 3 + c, layer, pl.ds(first, size), :] for c in range(3)]

    copy(0)
    copy(1)
    win.put_h(0, from_given)
    copy(2)
    win.put_h(1, from_given)

    def body(layer, carry):
        pl.when(layer + 2 < win.depth)(lambda: copy(layer + 2))
        win.put_h(layer + 1, from_given)
        win.put_curl(curls, layer, layer - 1)
        return carry

    lax.fori_loop(1, win.top, body, 0)


def settle_kernel(layout, *refs):
    refs = list(refs)
    del refs[:4]
    e_fwd, e_adj, below, above = (refs.pop(0) for _ in range(4))
    parts = [refs.pop(0) for _ in layout]
    ids_far, h_fwd, curls_fwd, h_adj, curls_adj, blocks, block_ids, sem = refs
    fetch = pltpu.make_async_copy(ids_far, block_ids, sem)
    fetch.start()
    nothing = jnp.zeros(blocks.shape[1:], F32)
    for block in range(blocks.shape[0]):
        blocks[block] = nothing
    has_up, has_low = neighbours()
    for evo, (e, h, curls) in enumerate(((e_fwd, h_fwd, curls_fwd), (e_adj, h_adj, curls_adj))):
        win = Window(e, h)
        pl.when(has_up)(lambda: win.take_above(above.at[evo]))
        pl.when(has_low)(lambda: win.take_below(below.at[evo]))
        win.put_curl(curls, win.top, win.top - 1)
        win.put_curl(curls, 0, win.under)
    fetch.wait()
    me = lax.axis_index("grp")
    for part, masks in zip(parts, layout):
        for slot, mask in enumerate(masks):
            blocks[block_ids[me ^ mask]] = part[slot]


def edge_kernel(step, evo, *refs):
    refs = list(refs)
    e_in, h_in = refs.pop(0), refs.pop(0)
    if evo == 1:
        other_in, edges_in = refs.pop(0), refs.pop(0)
    coef = refs.pop(0)
    drives, forced = (refs.pop(0), refs.pop(0)) if evo == 0 else (None, None)
    curls = refs.pop(0) if step == 0 else None
    below, above = (refs.pop(0), refs.pop(0)) if step > 0 else (None, None)
    e, h = refs.pop(0), refs.pop(0)
    other, edges = (refs.pop(0), refs.pop(0)) if evo == 1 else (None, None)
    pays = refs
    win = Window(e, h, coef, forcing(step, drives, forced))
    top = win.top
    has_up, has_low = neighbours()

    @pl.when(has_up)
    def _():
        if step > 0:
            win.take_above(above)
        win.put_e(top, top - 1, curls, other, edges, 1)
        if pays:
            win.put_h(top, alone=True)
            for c in range(2):
                pays[0][c] = h[c, top, pl.ds(PAD, win.rows), :]

    @pl.when(has_low)
    def _():
        if step > 0:
            win.take_below(below)
        win.put_e(0, win.under, curls, other, edges, 0)
        if pays:
            for c in range(2):
                pays[-1][c] = e[c, 0, pl.ds(PAD, win.rows), :]


def inner_range(top):
    has_up, has_low = neighbours()
    return jnp.where(has_low, 1, 0), jnp.where(has_up, top - 1, top)


def begin_kernel(
    e_fwd_in, e_adj_in, total_in, coef, drives, forced, curls_fwd, curls_adj,
    e_fwd, e_adj, total,
):
    fwd = Window(e_fwd, None, coef, forcing(0, drives, forced))
    adj = Window(e_adj, None, coef)
    lowest, highest = inner_range(fwd.top)

    def body(layer, carry):
        fwd.put_e(layer, None, curls_fwd)
        adj.put_e(layer, None, curls_adj, e_fwd, total)
        return carry

    lax.fori_loop(lowest, highest + 1, body, 0)


def inner_kernel(step, evo, *refs):
    refs = list(refs)
    e_in, h_in = refs.pop(0), refs.pop(0)
    if evo == 1:
        other_in, total_in = refs.pop(0), refs.pop(0)
    coef = refs.pop(0)
    drives, forced = (refs.pop(0), refs.pop(0)) if evo == 0 else (None, None)
    e, h = refs.pop(0), refs.pop(0)
    other, total = (refs.pop(0), refs.pop(0)) if evo == 1 else (None, None)
    win = Window(e, h, coef, forcing(step, drives, forced))
    lowest, highest = inner_range(win.top)
    win.put_h(0)
    pl.when(lowest == 1)(lambda: win.put_h(1))

    def body(layer, carry):
        win.put_h(layer + 1)
        win.put_e(layer, jnp.where(layer == 0, win.under, layer - 1), None, other, total)
        return carry

    if lax.axis_size("slab") == 2:
        lax.fori_loop(0, win.depth - 2, lambda i, carry: body(lowest + i, carry), 0, unroll=2)
    else:
        lax.fori_loop(lowest, highest, body, 0)
    win.put_e(highest, highest - 1, None, other, total)


def coef_layer(layer, coef, placed, base):
    for first, size in chunks(base.shape[0]):
        here = pl.ds(first, size)
        smooth = along_columns(along_rows(placed, first, size)) * 0.0625
        coef[layer, here, :] = 0.25 / (base[here, :] + 3.0 * smooth)


def clear_margins(placed):
    rows = placed.shape[0] - 2 * PAD
    margin = jnp.zeros((PAD, placed.shape[1]), F32)
    placed[pl.ds(0, PAD), :] = margin
    placed[pl.ds(PAD + rows, PAD), :] = margin


def place_layer(layer, first_slot, parts, place, blocks, placed):
    nblock = blocks.shape[0]
    block_rows = (placed.shape[0] - 2 * PAD) // nblock
    clear_margins(placed)
    start = layer * block_rows
    source = pl.ds(start if isinstance(layer, int) else pl.multiple_of(start, block_rows), block_rows)
    pieces = [part[slot, source, :] for part in parts for slot in range(part.shape[0])]
    for block in range(nblock):
        value = blocks[block, source, :]
        for slot, piece in enumerate(pieces):
            value = value + place[first_slot + slot, pl.ds(block, 1), :] * piece
        placed[pl.ds(PAD + block * block_rows, block_rows), :] = value


def coef_edge_kernel(first_slot, count, *refs):
    parts, (place, base, blocks, coef, placed) = refs[:count], refs[count:]
    edge_layers = (0, coef.shape[0] - 1)
    for which, layer in enumerate(edge_layers):
        place_layer(layer, first_slot, parts, place, blocks, placed.at[which])
    for which, layer in enumerate(edge_layers):
        coef_layer(layer, coef, placed.at[which], base)


def coef_inner_kernel(first_slot, count, coef_in, *refs):
    parts, (place, base, blocks, coef, placed) = refs[:count], refs[count:]

    def body(layer, carry):
        there = placed.at[lax.rem(layer, 2)]
        place_layer(layer, first_slot, parts, place, blocks, there)
        coef_layer(layer, coef, there, base)
        return carry

    lax.fori_loop(1, coef.shape[0] - 1, body, 0, unroll=2)


def along_rows(padded, first, size):
    here = padded[pl.ds(PAD + first, size), :]
    before = padded[pl.ds(PAD + first - 1, size), :]
    after = padded[pl.ds(PAD + first + 1, size), :]
    return before + 2.0 * here + after


def along_columns(value):
    return prev_col(value) + 2.0 * value + next_col(value)


def tie_kernel(*refs):
    pass


def tie(array, others):
    return call(
        tie_kernel, on_chip(*array.shape), IN_VMEM, [array] + others,
        [IN_VMEM] * (1 + len(others)), aliases={0: 0},
    )


def pack_kernel(*refs):
    out = refs[-1]
    for slot, ref in enumerate(refs[:-1]):
        out[slot] = ref[...]


def filter_inner_kernel(total, after, place, *rest):
    parts, wide = rest[:-1], rest[-1]
    nblock = place.shape[0]
    rows = wide.shape[1]
    block_rows = rows // nblock
    per = parts[0].shape[0]

    def body(layer, carry):
        there = wide.at[lax.rem(layer, 2)]
        for first, size in chunks(rows):
            there[pl.ds(first, size), :] = along_rows(total.at[layer], first, size)
        blocks = [there[pl.ds(block * block_rows, block_rows), :] for block in range(nblock)]
        target = pl.ds(pl.multiple_of((layer - 1) * block_rows, block_rows), block_rows)
        for slot in range(nblock):
            value = None
            for block, piece in enumerate(blocks):
                term = place[slot, pl.ds(block, 1), :] * piece
                value = term if value is None else value + term
            parts[slot // per][slot % per, target, :] = value
        return carry

    lax.fori_loop(1, total.shape[0] - 1, body, 0, unroll=2)


def filter_edge_kernel(layout, total, edges, place, *rest):
    parts, (sums, wide) = rest[:-2], rest[-2:]
    depth = total.shape[0]
    nblock = place.shape[0]
    rows = wide.shape[1]
    block_rows = rows // nblock
    for which, layer in enumerate((0, depth - 1)):
        sums[which] = total[layer] + edges[which]
        for first, size in chunks(rows):
            wide[which, pl.ds(first, size), :] = along_rows(sums.at[which], first, size)
    for which in range(2):
        blocks = [
            wide[which, pl.ds(block * block_rows, block_rows), :] for block in range(nblock)
        ]
        target = pl.ds(which * block_rows, block_rows)
        for slot in range(nblock):
            value = None
            for block, piece in enumerate(blocks):
                term = place[slot, pl.ds(block, 1), :] * piece
                value = term if value is None else value + term
            parts[slot // parts[0].shape[0]][slot % parts[0].shape[0], target, :] = value


def add_kernel(pairs, count, *refs):
    outs = refs[-count:]
    size, per = refs[0].shape[0], outs[0].shape[0]
    for pair in range(pairs):
        kept, got = refs[pair], refs[pairs + pair]
        for first in range(0, size, per):
            part = pl.ds(first, per)
            outs[(pair * size + first) // per][...] = kept[part] + got[part]


def join_kernel(count, block_rows, *refs):
    inner, edge, outs = refs[:count], refs[count : 2 * count], refs[2 * count :]
    rows = outs[0].shape[0]
    for slot, out in enumerate(outs):
        middle, ends = inner[0][slot], edge[0][slot]
        for a, b in zip(inner[1:], edge[1:]):
            middle, ends = middle + a[slot], ends + b[slot]
        out[pl.ds(0, block_rows), :] = ends[:block_rows]
        out[pl.ds(block_rows, rows - 2 * block_rows), :] = middle
        out[pl.ds(rows - block_rows, block_rows), :] = ends[block_rows:]


def last_kernel(scale, *refs):
    value = refs[0][...]
    for ref in refs[1:-1]:
        value = value + ref[...]
    refs[-1][...] = along_columns(value) * (scale * 0.0625)


def out_kernel(e, h, finals, halves, sems):
    depth = e.shape[1] - 1
    rows = e.shape[2] - 2 * PAD
    every = pl.ds(PAD, rows)
    copies = [
        pltpu.make_async_copy(e.at[c, pl.ds(0, depth), every, :], finals.at[0, c], sems.at[c])
        for c in range(3)
    ]
    for copy in copies:
        copy.start()
    for c in range(3):

        def body(layer, carry, c=c):
            halves[c, layer] = 0.5 * h[c, layer, every, :]
            return carry

        lax.fori_loop(0, depth, body, 0)
        copy = pltpu.make_async_copy(halves.at[c], finals.at[0, 3 + c], sems.at[3 + c])
        copy.start()
        copies.append(copy)
    for copy in copies:
        copy.wait()


def swap_over(array, axis, mask):
    return lax.ppermute(array, axis, [(i, i ^ mask) for i in range(lax.axis_size(axis))])


def shift_over(array, axis, distance):
    size = lax.axis_size(axis)
    route = [(i, i + distance) for i in range(size) if 0 <= i + distance < size]
    return lax.ppermute(array, axis, route)


def trade(pays):
    if len(pays) == 1:
        return [swap_over(pays[0], "slab", 1)] * 2
    return [shift_over(pays[0], "slab", 1), shift_over(pays[1], "slab", -1)]


def per_device(
    fwd_fields, adj_fields, density, block_ids, material_idx, material_eps, source_pos, wave_idx
):
    depth, width_x, width_y = fwd_fields.shape[2:]
    nblock = block_ids.shape[0]
    block_rows = width_x // nblock
    ngrp = lax.axis_size("grp")
    npay = 1 if lax.axis_size("slab") == 2 else 2

    far = 4
    middle = ngrp // (2 * far)
    far_masks = [2 * middle * j for j in range(far)]
    middle_masks = [2 * j for j in range(middle)]
    layout = [
        [core + mid + top for top in far_masks] for core in (0, 1) for mid in middle_masks
    ]
    piece = (depth * block_rows, width_y)
    group = (far,) + piece

    field_shape = on_chip(3, depth + 1, width_x + 2 * PAD, width_y)
    curls_shape = on_chip(3, depth, width_x, width_y)
    halo_shape = on_chip(2, width_x, width_y)
    total_shape = on_chip(depth, width_x + 2 * PAD, width_y)
    edges_shape = on_chip(2, width_x + 2 * PAD, width_y)
    coef_shape = on_chip(depth, width_x, width_y)
    plane = on_chip(width_x, width_y)

    def by_owner(kernel, layers, operands, specs, scratch, micros, messages):
        slots = middle * far // messages
        parts = call(
            kernel,
            [on_chip(slots, layers * block_rows, width_y)] * (2 * messages),
            [IN_VMEM] * (2 * messages),
            operands,
            specs,
            scratch,
            micros=micros,
        )
        return list(parts[:messages]), [swap_over(part, "grp", 1) for part in parts[messages:]]

    def add_middle(kept, got, after):
        sums = call(
            functools.partial(add_kernel, len(kept), middle),
            [on_chip(far, *kept[0].shape[1:])] * middle,
            [IN_VMEM] * middle,
            kept + got + after,
            [IN_VMEM] * (len(kept + got + after)),
        )
        return [sums[0]] + [
            swap_over(part, "grp", mask) for part, mask in zip(sums[1:], middle_masks[1:])
        ]

    design = density.reshape(piece)
    got = [swap_over(design, "grp", mask) for mask in far_masks[1:]]
    own, *pays = call(
        opening_kernel,
        [on_chip(*piece)] + [on_chip(2, 2, width_x, width_y)] * npay,
        [IN_VMEM] * (1 + npay),
        [fwd_fields, adj_fields, design],
        [IN_HBM] * 3,
        [pltpu.VMEM((2, 5, width_x, width_y), F32), pltpu.SemaphoreType.DMA((3, 5))],
    )
    below, above = trade(pays)

    near = call(pack_kernel, on_chip(*group), IN_VMEM, [own] + got, [IN_VMEM] * far)
    others = [swap_over(near, "grp", mask) for mask in middle_masks[1:]]
    near_across = swap_over(near, "grp", 1)

    e_fwd, h_fwd, curls_fwd, total, edges, forced, drives, base, place = call(
        functools.partial(first_fwd_kernel, layout),
        [
            field_shape,
            field_shape,
            curls_shape,
            total_shape,
            edges_shape,
            on_chip(depth, width_x, width_y),
            on_chip(STEPS, width_y),
            plane,
            on_chip(nblock, nblock, width_y),
        ],
        [IN_VMEM] * 9,
        [fwd_fields, near, wave_idx, source_pos, block_ids, material_idx, material_eps],
        [IN_VMEM] * 2 + [IN_SMEM] + [IN_HBM] * 4,
        [
            pltpu.SMEM(source_pos.shape, jnp.int32),
            pltpu.SMEM(block_ids.shape, jnp.int32),
            pltpu.SMEM(material_idx.shape, jnp.int32),
            pltpu.SMEM(material_eps.shape, F32),
            pltpu.SemaphoreType.DMA((4,)),
        ],
        micros=1.5,
    )
    e_adj, h_adj, curls_adj = call(
        first_kernel,
        [field_shape, field_shape, curls_shape],
        [IN_VMEM] * 3,
        [adj_fields, near],
        [IN_VMEM, IN_VMEM],
        micros=1.2,
    )
    others = [tie(part, [e_fwd, e_adj]) for part in others]
    early = [near] + others + [near_across]
    last = [swap_over(part, "grp", 1) for part in others]
    first_slot = far * len(early)

    h_fwd, curls_fwd, h_adj, curls_adj, blocks = call(
        functools.partial(settle_kernel, layout[: len(early)]),
        [field_shape, curls_shape] * 2 + [on_chip(nblock, *piece)],
        [IN_VMEM] * 5,
        [h_fwd, curls_fwd, h_adj, curls_adj, e_fwd, e_adj, below, above] + early + [block_ids],
        [IN_VMEM] * (8 + len(early)) + [IN_HBM],
        [pltpu.SMEM(block_ids.shape, jnp.int32), pltpu.SemaphoreType.DMA],
        aliases={0: 0, 1: 1, 2: 2, 3: 3},
        micros=0.6,
    )
    placed = pltpu.VMEM((2, width_x + 2 * PAD, width_y), F32)
    coef = call(
        functools.partial(coef_edge_kernel, first_slot, len(last)),
        coef_shape,
        IN_VMEM,
        last + [place, base, blocks],
        [IN_VMEM] * (len(last) + 3),
        [placed],
    )

    arrived_fwd, arrived_adj = [curls_fwd], [curls_adj]
    for step in range(STEPS):
        more = npay if step < STEPS - 1 else 0

        def edge_fwd(e_fwd, h_fwd):
            return call(
                functools.partial(edge_kernel, step, 0),
                [field_shape] * 2 + [halo_shape] * more,
                [IN_VMEM] * (2 + more),
                [e_fwd, h_fwd, coef, drives, forced] + arrived_fwd,
                [IN_VMEM] * (5 + len(arrived_fwd)),
                aliases={0: 0, 1: 1},
            )

        if more:
            e_fwd, h_fwd, *pays = edge_fwd(e_fwd, h_fwd)
            arrived_fwd_next = trade(pays)
        if step > 0:
            e_adj, h_adj, e_fwd, total = call(
                functools.partial(inner_kernel, step, 1),
                [field_shape] * 3 + [total_shape],
                [IN_VMEM] * 4,
                [e_adj, h_adj, e_fwd, total, coef],
                [IN_VMEM] * 5,
                aliases={0: 0, 1: 1, 2: 2, 3: 3},
                micros=1.2,
            )
        if not more:
            e_fwd, h_fwd = edge_fwd(e_fwd, h_fwd)
            inner = by_owner(
                filter_inner_kernel,
                depth - 2,
                [total, e_fwd, place],
                [IN_VMEM] * 3,
                [pltpu.VMEM((2, width_x, width_y), F32)],
                0.8,
                middle,
            )
        e_adj, h_adj, e_fwd, edges, *pays = call(
            functools.partial(edge_kernel, step, 1),
            [field_shape] * 3 + [edges_shape] + [halo_shape] * more,
            [IN_VMEM] * (4 + more),
            [e_adj, h_adj, e_fwd, edges, coef] + arrived_adj,
            [IN_VMEM] * (5 + len(arrived_adj)),
            aliases={0: 0, 1: 1, 2: 2, 3: 3},
        )
        if not more:
            break
        arrived_fwd, arrived_adj = arrived_fwd_next, trade(pays)
        if step == 0:
            coef = call(
                functools.partial(coef_inner_kernel, first_slot, len(last)),
                coef_shape,
                IN_VMEM,
                [coef] + last + [place, base, blocks],
                [IN_VMEM] * (len(last) + 4),
                [placed],
                aliases={0: 0},
                micros=0.6,
            )
            e_fwd, e_adj, total = call(
                begin_kernel,
                [field_shape, field_shape, total_shape],
                [IN_VMEM] * 3,
                [e_fwd, e_adj, total, coef, drives, forced, curls_fwd, curls_adj],
                [IN_VMEM] * 8,
                aliases={0: 0, 1: 1, 2: 2},
                micros=0.5,
            )
        e_fwd, h_fwd = call(
            functools.partial(inner_kernel, step + 1, 0),
            [field_shape] * 2,
            [IN_VMEM] * 2,
            [e_fwd, h_fwd, coef, drives, forced],
            [IN_VMEM] * 5,
            aliases={0: 0, 1: 1},
            micros=1.1,
        )

    ends = by_owner(
        functools.partial(filter_edge_kernel, layout),
        2,
        [total, edges, place],
        [IN_VMEM] * 3,
        [
            pltpu.VMEM((2, width_x + 2 * PAD, width_y), F32),
            pltpu.VMEM((2, width_x, width_y), F32),
        ],
        0.3,
        1,
    )
    inner = add_middle(*inner, ends[0][:1])
    ends = add_middle(*ends, [])
    pieces = call(
        functools.partial(join_kernel, middle, block_rows),
        [on_chip(*piece)] * far,
        [IN_VMEM] * far,
        inner + ends,
        [IN_VMEM] * (2 * middle),
    )
    got = [swap_over(part, "grp", mask) for part, mask in zip(pieces[:0:-1], far_masks[:0:-1])]
    scale = 3.0 / (STEPS * math.sqrt(ngrp))
    grad = call(
        functools.partial(last_kernel, scale),
        jax.ShapeDtypeStruct(piece, F32),
        IN_VMEM,
        [pieces[0]] + got,
        [IN_VMEM] * far,
    )
    finals = call(
        out_kernel,
        jax.ShapeDtypeStruct(fwd_fields.shape, F32),
        IN_HBM,
        [e_fwd, h_fwd],
        [IN_VMEM] * 2,
        [
            pltpu.VMEM((3, depth, width_x, width_y), F32),
            pltpu.SemaphoreType.DMA((6,)),
        ],
        micros=1.7,
    )
    return finals, grad.reshape(density.shape)


def solution(mesh):
    placed = (
        P("grp", None, "slab", None, None),
        P("grp", None, "slab", None, None),
        P("slab", "grp", None),
        P(),
        P(),
        P(),
        P("grp", None),
        P("grp"),
    )
    return jax.shard_map(
        per_device,
        mesh=mesh,
        in_specs=placed,
        out_specs=(P("grp", None, "slab", None, None), P("slab", "grp", None)),
        check_vma=False,
    )
```

```python
import functools
import math

import jax
import jax.numpy as jnp
from jax import lax
from jax.experimental import pallas as pl
from jax.experimental.pallas import tpu as pltpu
from jax.sharding import PartitionSpec as P

STEPS = 4
AMPLITUDE = 4.0
PAD = 8
F32 = jnp.float32
HBM_PER_MICRO = 1.0e5

VMEM = pltpu.MemorySpace.VMEM
IN_VMEM = pl.BlockSpec(memory_space=pltpu.VMEM)
IN_SMEM = pl.BlockSpec(memory_space=pltpu.SMEM)
IN_HBM = pl.BlockSpec(memory_space=pltpu.MemorySpace.HBM)


def on_chip(*shape):
    return VMEM(shape, F32)


def held(array, spec):
    if spec is IN_SMEM:
        return array
    space = VMEM if spec is IN_VMEM else pltpu.MemorySpace.HBM
    return pltpu.with_memory_space_constraint(array, space)


def call(kernel, outs, out_specs, operands, specs, scratch=(), aliases=None, micros=0.3):
    operands = [held(a, s) for a, s in zip(operands, specs)]
    return pl.pallas_call(
        kernel,
        out_shape=outs,
        in_specs=specs,
        out_specs=out_specs,
        scratch_shapes=scratch,
        input_output_aliases=aliases or {},
        compiler_params=pltpu.CompilerParams(vmem_limit_bytes=8 << 20),
        cost_estimate=pl.CostEstimate(
            flops=0, bytes_accessed=int(micros * HBM_PER_MICRO), transcendentals=0
        ),
    )(*operands)


CHUNK = 16


def chunks(rows):
    size = CHUNK if rows % CHUNK == 0 else rows
    return [(first, size) for first in range(0, rows, size)]


def next_col(value):
    column = lax.broadcasted_iota(jnp.int32, value.shape, 1)
    moved = pltpu.roll(value, value.shape[1] - 1, 1)
    return jnp.where(column == value.shape[1] - 1, 0.0, moved)


def prev_col(value):
    column = lax.broadcasted_iota(jnp.int32, value.shape, 1)
    return jnp.where(column == 0, 0.0, pltpu.roll(value, 1, 1))


def neighbours():
    slab = lax.axis_index("slab")
    return slab < lax.axis_size("slab") - 1, slab > 0


class Window:
    def __init__(self, e, h, coef=None, force=None):
        self.e, self.h, self.coef, self.force = e, h, coef, force
        self.rows = e.shape[2] - 2 * PAD
        self.depth = e.shape[1] - 1
        self.top, self.under = self.depth - 1, self.depth

    def read(self, ref, layer, first, size):
        return [ref[c, layer, pl.ds(PAD + first, size), :] for c in range(3)]

    def write(self, ref, layer, first, size, values):
        for c, value in enumerate(values):
            ref[c, layer, pl.ds(PAD + first, size), :] = value

    def put_h(self, layer, given=None, alone=False):
        for first, size in chunks(self.rows):
            rows = pl.ds(PAD + first, size)
            after = pl.ds(PAD + first + 1, size)
            ex, ey, ez = self.read(self.e, layer, first, size)
            if given is None:
                hx, hy, hz = self.read(self.h, layer, first, size)
            else:
                hx, hy, hz = (value + value for value in given(layer, first, size))
            if alone:
                rise_x, rise_y = -ex, -ey
            else:
                rise_x = self.e[0, layer + 1, rows, :] - ex
                rise_y = self.e[1, layer + 1, rows, :] - ey
            ey_after = self.e[1, layer, after, :]
            ez_after = self.e[2, layer, after, :]
            hx = hx - ((next_col(ez) - ez) - rise_y)
            hy = hy - (rise_x - (ez_after - ez))
            hz = hz - ((ey_after - ey) - (next_col(ex) - ex))
            self.write(self.h, layer, first, size, (hx, hy, hz))

    def curl_h(self, layer, lower, first, size):
        rows = pl.ds(PAD + first, size)
        before = pl.ds(PAD + first - 1, size)
        hx, hy, hz = self.read(self.h, layer, first, size)
        step_x = hx - self.h[0, lower, rows, :]
        step_y = hy - self.h[1, lower, rows, :]
        hy_before = self.h[1, layer, before, :]
        hz_before = self.h[2, layer, before, :]
        return (
            (hz - prev_col(hz)) - step_y,
            step_x - (hz - hz_before),
            (hy - hy_before) - (hx - prev_col(hx)),
        )

    def put_curl(self, curls, layer, lower):
        for first, size in chunks(self.rows):
            for c, value in enumerate(self.curl_h(layer, lower, first, size)):
                curls[c, layer, pl.ds(first, size), :] = value

    def next_e(self, layer, lower, first, size, curls=None):
        here = pl.ds(first, size)
        cell = self.coef[layer, here, :]
        if curls is None:
            curl = self.curl_h(layer, lower, first, size)
        else:
            curl = [curls[c, layer, here, :] for c in range(3)]
        ex, ey, ez = [a + cell * b for a, b in zip(self.read(self.e, layer, first, size), curl)]
        if self.force is not None:
            ez = ez + self.force(layer, here)
        return ex, ey, ez

    def put_e(self, layer, lower, curls=None, other=None, total=None, slot=None):
        for first, size in chunks(self.rows):
            news = self.next_e(layer, lower, first, size, curls)
            self.write(self.e, layer, first, size, news)
            if total is not None:
                rows = pl.ds(PAD + first, size)
                part = [a * other[c, layer, rows, :] for c, a in enumerate(news)]
                total[layer if slot is None else slot, rows, :] += part[0] + part[1] + part[2]

    def take_above(self, above):
        for first, size in chunks(self.rows):
            here, rows = pl.ds(first, size), pl.ds(PAD + first, size)
            self.h[0, self.top, rows, :] += above[1, here, :]
            self.h[1, self.top, rows, :] -= above[0, here, :]

    def take_below(self, below):
        for first, size in chunks(self.rows):
            here, rows = pl.ds(first, size), pl.ds(PAD + first, size)
            self.h[0, self.under, rows, :] = below[0, here, :] + self.e[1, 0, rows, :]
            self.h[1, self.under, rows, :] = below[1, here, :] - self.e[0, 0, rows, :]


def forcing(step, drives, forced):
    if drives is None:
        return None
    return lambda layer, here: drives[pl.ds(step, 1), :] * forced[layer, here, :]


def opening_kernel(fwd, adj, density, own, *rest):
    pays, (planes, sems) = rest[:-2], rest[-2:]
    depth, rows, width_y = fwd.shape[2:]
    top = depth - 1
    has_up, has_low = neighbours()
    held_copy = pltpu.make_async_copy(density, own, sems.at[2, 0])
    held_copy.start()

    def up(pay):
        copies = []
        for evo, given in enumerate((fwd, adj)):
            for c in range(5):
                copies.append(
                    pltpu.make_async_copy(given.at[0, c, top], planes.at[evo, c], sems.at[evo, c])
                )
        for copy in copies:
            copy.start()
        for copy in copies:
            copy.wait()
        for evo in range(2):
            for first, size in chunks(rows):
                here = pl.ds(first, size)
                ex, ey, ez, hx, hy = (planes[evo, c, here, :] for c in range(5))
                if first + size < rows:
                    ez_after = planes[evo, 2, pl.ds(first + 1, size), :]
                else:
                    row = lax.broadcasted_iota(jnp.int32, ez.shape, 0)
                    ez_after = jnp.where(row == size - 1, 0.0, pltpu.roll(ez, size - 1, 0))
                pay[evo, 0, here, :] = (hx + hx) - ((next_col(ez) - ez) + ey)
                pay[evo, 1, here, :] = (hy + hy) + (ex + (ez_after - ez))

    def down(pay):
        copies = []
        for evo, given in enumerate((fwd, adj)):
            for c in range(2):
                copies.append(
                    pltpu.make_async_copy(given.at[0, c, 0], pay.at[evo, c], sems.at[evo, c])
                )
        for copy in copies:
            copy.start()
        for copy in copies:
            copy.wait()

    if len(pays) == 2:
        up(pays[0])
        down(pays[1])
    else:
        pl.when(has_up)(lambda: up(pays[0]))
        pl.when(has_low)(lambda: down(pays[0]))
    held_copy.wait()


def first_fwd_kernel(
    layout, given, near, wave_idx, source_far, ids_far, idx_far, eps_far,
    e, h, curls, total, edges, forced, drives, base, place,
    source, block_ids, material_idx, material_eps, sems,
):
    fetches = [
        pltpu.make_async_copy(far, here, sems.at[slot])
        for slot, (far, here) in enumerate(
            (
                (source_far, source),
                (ids_far, block_ids),
                (idx_far, material_idx),
                (eps_far, material_eps),
            )
        )
    ]
    for fetch in fetches:
        fetch.start()
    first_kernel(given, near, e, h, curls)
    depth, rows, width_y = forced.shape
    nblock = block_ids.shape[0]
    block_rows = rows // nblock
    empty = jnp.zeros(total.shape[1:], F32)
    edges[0] = empty
    edges[1] = empty
    for layer in range(depth):
        total[layer] = empty
    for fetch in fetches:
        fetch.wait()
    xcoord = lax.broadcasted_iota(jnp.int32, (rows, width_y), 0)
    ycoord = lax.broadcasted_iota(jnp.int32, (rows, width_y), 1)
    offset_x = (xcoord - source[0, 1]).astype(F32) / (rows / 4.0)
    offset_y = (ycoord - source[0, 2]).astype(F32) / (width_y / 4.0)
    profile = jnp.exp(-0.5 * (offset_x * offset_x + offset_y * offset_y))
    step = lax.broadcasted_iota(jnp.int32, drives.shape, 0).astype(F32) + 1.0
    wave = jnp.full(drives.shape, wave_idx[0], jnp.int32).astype(F32)
    drives[...] = AMPLITUDE * jnp.sin(2.0 * math.pi / (6.0 + 2.0 * wave) * step)
    level = source[0, 0] - lax.axis_index("slab") * depth
    for layer in range(depth):
        forced[layer] = jnp.where(level == layer, 1.0, 0.0) * profile
    for block in range(nblock):
        value = jnp.full((block_rows, width_y), material_eps[material_idx[block]], F32)
        base[pl.ds(block * block_rows, block_rows), :] = value
    me = lax.axis_index("grp")
    block = lax.broadcasted_iota(jnp.int32, (nblock, width_y), 0)
    for slot, mask in enumerate(mask for masks in layout for mask in masks):
        place[slot] = jnp.where(block == block_ids[me ^ mask], 1.0, 0.0)


def first_kernel(given, near, e, h, curls):
    win = Window(e, h)
    rows, width_y = win.rows, e.shape[3]
    margin = jnp.zeros((PAD, width_y), F32)
    empty = jnp.zeros((rows + 2 * PAD, width_y), F32)
    for comp in range(3):
        e[comp, win.depth] = empty
        h[comp, win.depth] = empty

    def copy(layer):
        for comp in range(3):
            for ref in (e, h):
                ref[comp, layer, pl.ds(0, PAD), :] = margin
                ref[comp, layer, pl.ds(PAD + rows, PAD), :] = margin
            for first, size in chunks(rows):
                here = pl.ds(first, size)
                e[comp, layer, pl.ds(PAD + first, size), :] = given[0, comp, layer, here, :]

    def from_given(layer, first, size):
        return [given[0, 3 + c, layer, pl.ds(first, size), :] for c in range(3)]

    copy(0)
    copy(1)
    win.put_h(0, from_given)
    copy(2)
    win.put_h(1, from_given)

    def body(layer, carry):
        pl.when(layer + 2 < win.depth)(lambda: copy(layer + 2))
        win.put_h(layer + 1, from_given)
        win.put_curl(curls, layer, layer - 1)
        return carry

    lax.fori_loop(1, win.top, body, 0)


def settle_kernel(layout, *refs):
    refs = list(refs)
    del refs[:4]
    e_fwd, e_adj, below, above = (refs.pop(0) for _ in range(4))
    parts = [refs.pop(0) for _ in layout]
    ids_far, h_fwd, curls_fwd, h_adj, curls_adj, blocks, block_ids, sem = refs
    fetch = pltpu.make_async_copy(ids_far, block_ids, sem)
    fetch.start()
    nothing = jnp.zeros(blocks.shape[1:], F32)
    for block in range(blocks.shape[0]):
        blocks[block] = nothing
    has_up, has_low = neighbours()
    for evo, (e, h, curls) in enumerate(((e_fwd, h_fwd, curls_fwd), (e_adj, h_adj, curls_adj))):
        win = Window(e, h)
        pl.when(has_up)(lambda: win.take_above(above.at[evo]))
        pl.when(has_low)(lambda: win.take_below(below.at[evo]))
        win.put_curl(curls, win.top, win.top - 1)
        win.put_curl(curls, 0, win.under)
    fetch.wait()
    me = lax.axis_index("grp")
    for part, masks in zip(parts, layout):
        for slot, mask in enumerate(masks):
            blocks[block_ids[me ^ mask]] = part[slot]


def edge_kernel(step, evo, *refs):
    refs = list(refs)
    e_in, h_in = refs.pop(0), refs.pop(0)
    if evo == 1:
        other_in, edges_in = refs.pop(0), refs.pop(0)
    coef = refs.pop(0)
    drives, forced = (refs.pop(0), refs.pop(0)) if evo == 0 else (None, None)
    curls = refs.pop(0) if step == 0 else None
    below, above = (refs.pop(0), refs.pop(0)) if step > 0 else (None, None)
    e, h = refs.pop(0), refs.pop(0)
    other, edges = (refs.pop(0), refs.pop(0)) if evo == 1 else (None, None)
    pays = refs
    win = Window(e, h, coef, forcing(step, drives, forced))
    top = win.top
    has_up, has_low = neighbours()

    @pl.when(has_up)
    def _():
        if step > 0:
            win.take_above(above)
        win.put_e(top, top - 1, curls, other, edges, 1)
        if pays:
            win.put_h(top, alone=True)
            for c in range(2):
                pays[0][c] = h[c, top, pl.ds(PAD, win.rows), :]

    @pl.when(has_low)
    def _():
        if step > 0:
            win.take_below(below)
        win.put_e(0, win.under, curls, other, edges, 0)
        if pays:
            for c in range(2):
                pays[-1][c] = e[c, 0, pl.ds(PAD, win.rows), :]


def inner_range(top):
    has_up, has_low = neighbours()
    return jnp.where(has_low, 1, 0), jnp.where(has_up, top - 1, top)


def begin_kernel(
    e_fwd_in, e_adj_in, total_in, coef, drives, forced, curls_fwd, curls_adj,
    e_fwd, e_adj, total,
):
    fwd = Window(e_fwd, None, coef, forcing(0, drives, forced))
    adj = Window(e_adj, None, coef)
    lowest, highest = inner_range(fwd.top)

    def body(layer, carry):
        fwd.put_e(layer, None, curls_fwd)
        adj.put_e(layer, None, curls_adj, e_fwd, total)
        return carry

    lax.fori_loop(lowest, highest + 1, body, 0)


def inner_kernel(step, evo, *refs):
    refs = list(refs)
    e_in, h_in = refs.pop(0), refs.pop(0)
    if evo == 1:
        other_in, total_in = refs.pop(0), refs.pop(0)
    coef = refs.pop(0)
    drives, forced = (refs.pop(0), refs.pop(0)) if evo == 0 else (None, None)
    e, h = refs.pop(0), refs.pop(0)
    other, total = (refs.pop(0), refs.pop(0)) if evo == 1 else (None, None)
    win = Window(e, h, coef, forcing(step, drives, forced))
    lowest, highest = inner_range(win.top)
    win.put_h(0)
    pl.when(lowest == 1)(lambda: win.put_h(1))

    def body(layer, carry):
        win.put_h(layer + 1)
        win.put_e(layer, jnp.where(layer == 0, win.under, layer - 1), None, other, total)
        return carry

    if lax.axis_size("slab") == 2:
        lax.fori_loop(0, win.depth - 2, lambda i, carry: body(lowest + i, carry), 0, unroll=2)
    else:
        lax.fori_loop(lowest, highest, body, 0)
    win.put_e(highest, highest - 1, None, other, total)


def coef_layer(layer, coef, placed, base):
    for first, size in chunks(base.shape[0]):
        here = pl.ds(first, size)
        coef[layer, here, :] = 0.25 / (base[here, :] + 3.0 * filtered(placed, first, size))


def clear_margins(placed):
    rows = placed.shape[0] - 2 * PAD
    margin = jnp.zeros((PAD, placed.shape[1]), F32)
    placed[pl.ds(0, PAD), :] = margin
    placed[pl.ds(PAD + rows, PAD), :] = margin


def place_layer(layer, first_slot, parts, place, blocks, placed):
    nblock = blocks.shape[0]
    block_rows = (placed.shape[0] - 2 * PAD) // nblock
    clear_margins(placed)
    start = layer * block_rows
    source = pl.ds(start if isinstance(layer, int) else pl.multiple_of(start, block_rows), block_rows)
    pieces = [part[slot, source, :] for part in parts for slot in range(part.shape[0])]
    for block in range(nblock):
        value = blocks[block, source, :]
        for slot, piece in enumerate(pieces):
            value = value + place[first_slot + slot, pl.ds(block, 1), :] * piece
        placed[pl.ds(PAD + block * block_rows, block_rows), :] = value


def coef_edge_kernel(first_slot, count, *refs):
    parts, (place, base, blocks, coef, placed) = refs[:count], refs[count:]
    edge_layers = (0, coef.shape[0] - 1)
    for which, layer in enumerate(edge_layers):
        place_layer(layer, first_slot, parts, place, blocks, placed.at[which])
    for which, layer in enumerate(edge_layers):
        coef_layer(layer, coef, placed.at[which], base)


def coef_inner_kernel(first_slot, count, coef_in, *refs):
    parts, (place, base, blocks, coef, placed) = refs[:count], refs[count:]

    def body(layer, carry):
        there = placed.at[lax.rem(layer, 2)]
        place_layer(layer, first_slot, parts, place, blocks, there)
        coef_layer(layer, coef, there, base)
        return carry

    lax.fori_loop(1, coef.shape[0] - 1, body, 0, unroll=2)


def filtered(padded, first, size):
    here = padded[pl.ds(PAD + first, size), :]
    before = padded[pl.ds(PAD + first - 1, size), :]
    after = padded[pl.ds(PAD + first + 1, size), :]
    along = before + 2.0 * here + after
    return (prev_col(along) + 2.0 * along + next_col(along)) * 0.0625


def tie_kernel(*refs):
    pass


def tie(array, others):
    return call(
        tie_kernel, on_chip(*array.shape), IN_VMEM, [array] + others,
        [IN_VMEM] * (1 + len(others)), aliases={0: 0},
    )


def pack_kernel(*refs):
    out = refs[-1]
    for slot, ref in enumerate(refs[:-1]):
        out[slot] = ref[...]


def filter_inner_kernel(layout, total, after, block_ids_far, *rest):
    parts, (blocks, wide, block_ids, sem) = rest[:-4], rest[-4:]
    fetch = pltpu.make_async_copy(block_ids_far, block_ids, sem)
    fetch.start()
    depth = total.shape[0]
    nblock = blocks.shape[0]
    rows = wide.shape[1]
    block_rows = rows // nblock
    me = lax.axis_index("grp")

    def body(layer, carry):
        there = wide.at[lax.rem(layer, 2)]
        for first, size in chunks(rows):
            there[pl.ds(first, size), :] = filtered(total.at[layer], first, size)
        for block in range(nblock):
            target = pl.ds(pl.multiple_of((layer - 1) * block_rows, block_rows), block_rows)
            blocks[block, target, :] = there[pl.ds(block * block_rows, block_rows), :]
        return carry

    lax.fori_loop(1, depth - 1, body, 0, unroll=2)
    fetch.wait()
    inner = pl.ds(0, (depth - 2) * block_rows)
    for slot, mask in enumerate(mask for masks in layout for mask in masks):
        part = parts[slot // parts[0].shape[0]]
        part[slot % part.shape[0]] = blocks[block_ids[me ^ mask], inner, :]


def filter_edge_kernel(layout, total, edges, place, *rest):
    parts, (sums, wide) = rest[:-2], rest[-2:]
    depth = total.shape[0]
    nblock = place.shape[0]
    rows = wide.shape[1]
    block_rows = rows // nblock
    for which, layer in enumerate((0, depth - 1)):
        sums[which] = total[layer] + edges[which]
        for first, size in chunks(rows):
            wide[which, pl.ds(first, size), :] = filtered(sums.at[which], first, size)
    for which in range(2):
        blocks = [
            wide[which, pl.ds(block * block_rows, block_rows), :] for block in range(nblock)
        ]
        target = pl.ds(which * block_rows, block_rows)
        for slot in range(nblock):
            value = None
            for block, piece in enumerate(blocks):
                term = place[slot, pl.ds(block, 1), :] * piece
                value = term if value is None else value + term
            parts[slot // parts[0].shape[0]][slot % parts[0].shape[0], target, :] = value


def add_kernel(pairs, count, *refs):
    outs = refs[-count:]
    size, per = refs[0].shape[0], outs[0].shape[0]
    for pair in range(pairs):
        kept, got = refs[pair], refs[pairs + pair]
        for first in range(0, size, per):
            part = pl.ds(first, per)
            outs[(pair * size + first) // per][...] = kept[part] + got[part]


def join_kernel(count, block_rows, *refs):
    inner, edge, outs = refs[:count], refs[count : 2 * count], refs[2 * count :]
    rows = outs[0].shape[0]
    for slot, out in enumerate(outs):
        middle, ends = inner[0][slot], edge[0][slot]
        for a, b in zip(inner[1:], edge[1:]):
            middle, ends = middle + a[slot], ends + b[slot]
        out[pl.ds(0, block_rows), :] = ends[:block_rows]
        out[pl.ds(block_rows, rows - 2 * block_rows), :] = middle
        out[pl.ds(rows - block_rows, block_rows), :] = ends[block_rows:]


def last_kernel(scale, *refs):
    value = refs[0][...]
    for ref in refs[1:-1]:
        value = value + ref[...]
    refs[-1][...] = value * scale


def out_kernel(e, h, finals, halves, sems):
    depth = e.shape[1] - 1
    rows = e.shape[2] - 2 * PAD
    every = pl.ds(PAD, rows)
    copies = [
        pltpu.make_async_copy(e.at[c, pl.ds(0, depth), every, :], finals.at[0, c], sems.at[c])
        for c in range(3)
    ]
    for copy in copies:
        copy.start()
    for c in range(3):

        def body(layer, carry, c=c):
            halves[c, layer] = 0.5 * h[c, layer, every, :]
            return carry

        lax.fori_loop(0, depth, body, 0)
        copy = pltpu.make_async_copy(halves.at[c], finals.at[0, 3 + c], sems.at[3 + c])
        copy.start()
        copies.append(copy)
    for copy in copies:
        copy.wait()


def swap_over(array, axis, mask):
    return lax.ppermute(array, axis, [(i, i ^ mask) for i in range(lax.axis_size(axis))])


def shift_over(array, axis, distance):
    size = lax.axis_size(axis)
    route = [(i, i + distance) for i in range(size) if 0 <= i + distance < size]
    return lax.ppermute(array, axis, route)


def trade(pays):
    if len(pays) == 1:
        return [swap_over(pays[0], "slab", 1)] * 2
    return [shift_over(pays[0], "slab", 1), shift_over(pays[1], "slab", -1)]


def per_device(
    fwd_fields, adj_fields, density, block_ids, material_idx, material_eps, source_pos, wave_idx
):
    depth, width_x, width_y = fwd_fields.shape[2:]
    nblock = block_ids.shape[0]
    block_rows = width_x // nblock
    ngrp = lax.axis_size("grp")
    npay = 1 if lax.axis_size("slab") == 2 else 2

    far = 4
    middle = ngrp // (2 * far)
    far_masks = [2 * middle * j for j in range(far)]
    middle_masks = [2 * j for j in range(middle)]
    layout = [
        [core + mid + top for top in far_masks] for core in (0, 1) for mid in middle_masks
    ]
    piece = (depth * block_rows, width_y)
    group = (far,) + piece

    field_shape = on_chip(3, depth + 1, width_x + 2 * PAD, width_y)
    curls_shape = on_chip(3, depth, width_x, width_y)
    halo_shape = on_chip(2, width_x, width_y)
    total_shape = on_chip(depth, width_x + 2 * PAD, width_y)
    edges_shape = on_chip(2, width_x + 2 * PAD, width_y)
    coef_shape = on_chip(depth, width_x, width_y)
    plane = on_chip(width_x, width_y)

    def by_owner(kernel, layers, operands, specs, scratch, micros, messages):
        slots = middle * far // messages
        parts = call(
            kernel,
            [on_chip(slots, layers * block_rows, width_y)] * (2 * messages),
            [IN_VMEM] * (2 * messages),
            operands,
            specs,
            scratch,
            micros=micros,
        )
        return list(parts[:messages]), [swap_over(part, "grp", 1) for part in parts[messages:]]

    def add_middle(kept, got, after):
        sums = call(
            functools.partial(add_kernel, len(kept), middle),
            [on_chip(far, *kept[0].shape[1:])] * middle,
            [IN_VMEM] * middle,
            kept + got + after,
            [IN_VMEM] * (len(kept + got + after)),
        )
        return [sums[0]] + [
            swap_over(part, "grp", mask) for part, mask in zip(sums[1:], middle_masks[1:])
        ]

    design = density.reshape(piece)
    order = [2, 3, 1] if far == 4 else list(range(1, far))
    trips = {slot: swap_over(design, "grp", far_masks[slot]) for slot in reversed(order)}
    got = [trips[slot] for slot in range(1, far)]
    own, *pays = call(
        opening_kernel,
        [on_chip(*piece)] + [on_chip(2, 2, width_x, width_y)] * npay,
        [IN_VMEM] * (1 + npay),
        [fwd_fields, adj_fields, design],
        [IN_HBM] * 3,
        [pltpu.VMEM((2, 5, width_x, width_y), F32), pltpu.SemaphoreType.DMA((3, 5))],
    )
    below, above = trade(pays)

    near = call(pack_kernel, on_chip(*group), IN_VMEM, [own] + got, [IN_VMEM] * far)
    others = [swap_over(near, "grp", mask) for mask in middle_masks[1:]]
    near_across = swap_over(near, "grp", 1)

    e_fwd, h_fwd, curls_fwd, total, edges, forced, drives, base, place = call(
        functools.partial(first_fwd_kernel, layout),
        [
            field_shape,
            field_shape,
            curls_shape,
            total_shape,
            edges_shape,
            on_chip(depth, width_x, width_y),
            on_chip(STEPS, width_y),
            plane,
            on_chip(nblock, nblock, width_y),
        ],
        [IN_VMEM] * 9,
        [fwd_fields, near, wave_idx, source_pos, block_ids, material_idx, material_eps],
        [IN_VMEM] * 2 + [IN_SMEM] + [IN_HBM] * 4,
        [
            pltpu.SMEM(source_pos.shape, jnp.int32),
            pltpu.SMEM(block_ids.shape, jnp.int32),
            pltpu.SMEM(material_idx.shape, jnp.int32),
            pltpu.SMEM(material_eps.shape, F32),
            pltpu.SemaphoreType.DMA((4,)),
        ],
        micros=1.5,
    )
    e_adj, h_adj, curls_adj = call(
        first_kernel,
        [field_shape, field_shape, curls_shape],
        [IN_VMEM] * 3,
        [adj_fields, near],
        [IN_VMEM, IN_VMEM],
        micros=1.2,
    )
    others = [tie(part, [e_fwd, e_adj]) for part in others]
    early = [near] + others + [near_across]
    last = [swap_over(part, "grp", 1) for part in others]
    first_slot = far * len(early)

    h_fwd, curls_fwd, h_adj, curls_adj, blocks = call(
        functools.partial(settle_kernel, layout[: len(early)]),
        [field_shape, curls_shape] * 2 + [on_chip(nblock, *piece)],
        [IN_VMEM] * 5,
        [h_fwd, curls_fwd, h_adj, curls_adj, e_fwd, e_adj, below, above] + early + [block_ids],
        [IN_VMEM] * (8 + len(early)) + [IN_HBM],
        [pltpu.SMEM(block_ids.shape, jnp.int32), pltpu.SemaphoreType.DMA],
        aliases={0: 0, 1: 1, 2: 2, 3: 3},
        micros=0.6,
    )
    placed = pltpu.VMEM((2, width_x + 2 * PAD, width_y), F32)
    coef = call(
        functools.partial(coef_edge_kernel, first_slot, len(last)),
        coef_shape,
        IN_VMEM,
        last + [place, base, blocks],
        [IN_VMEM] * (len(last) + 3),
        [placed],
    )

    arrived_fwd, arrived_adj = [curls_fwd], [curls_adj]
    for step in range(STEPS):
        more = npay if step < STEPS - 1 else 0

        def edge_fwd(e_fwd, h_fwd):
            return call(
                functools.partial(edge_kernel, step, 0),
                [field_shape] * 2 + [halo_shape] * more,
                [IN_VMEM] * (2 + more),
                [e_fwd, h_fwd, coef, drives, forced] + arrived_fwd,
                [IN_VMEM] * (5 + len(arrived_fwd)),
                aliases={0: 0, 1: 1},
            )

        if more:
            e_fwd, h_fwd, *pays = edge_fwd(e_fwd, h_fwd)
            arrived_fwd_next = trade(pays)
        if step > 0:
            e_adj, h_adj, e_fwd, total = call(
                functools.partial(inner_kernel, step, 1),
                [field_shape] * 3 + [total_shape],
                [IN_VMEM] * 4,
                [e_adj, h_adj, e_fwd, total, coef],
                [IN_VMEM] * 5,
                aliases={0: 0, 1: 1, 2: 2, 3: 3},
                micros=1.2,
            )
        if not more:
            e_fwd, h_fwd = edge_fwd(e_fwd, h_fwd)
            inner = by_owner(
                functools.partial(filter_inner_kernel, layout),
                depth - 2,
                [total, e_fwd, block_ids],
                [IN_VMEM, IN_VMEM, IN_HBM],
                [
                    pltpu.VMEM((nblock,) + piece, F32),
                    pltpu.VMEM((2, width_x, width_y), F32),
                    pltpu.SMEM(block_ids.shape, jnp.int32),
                    pltpu.SemaphoreType.DMA,
                ],
                0.8,
                middle,
            )
        e_adj, h_adj, e_fwd, edges, *pays = call(
            functools.partial(edge_kernel, step, 1),
            [field_shape] * 3 + [edges_shape] + [halo_shape] * more,
            [IN_VMEM] * (4 + more),
            [e_adj, h_adj, e_fwd, edges, coef] + arrived_adj,
            [IN_VMEM] * (5 + len(arrived_adj)),
            aliases={0: 0, 1: 1, 2: 2, 3: 3},
        )
        if not more:
            break
        arrived_fwd, arrived_adj = arrived_fwd_next, trade(pays)
        if step == 0:
            coef = call(
                functools.partial(coef_inner_kernel, first_slot, len(last)),
                coef_shape,
                IN_VMEM,
                [coef] + last + [place, base, blocks],
                [IN_VMEM] * (len(last) + 4),
                [placed],
                aliases={0: 0},
                micros=0.6,
            )
            e_fwd, e_adj, total = call(
                begin_kernel,
                [field_shape, field_shape, total_shape],
                [IN_VMEM] * 3,
                [e_fwd, e_adj, total, coef, drives, forced, curls_fwd, curls_adj],
                [IN_VMEM] * 8,
                aliases={0: 0, 1: 1, 2: 2},
                micros=0.5,
            )
        e_fwd, h_fwd = call(
            functools.partial(inner_kernel, step + 1, 0),
            [field_shape] * 2,
            [IN_VMEM] * 2,
            [e_fwd, h_fwd, coef, drives, forced],
            [IN_VMEM] * 5,
            aliases={0: 0, 1: 1},
            micros=1.1,
        )

    ends = by_owner(
        functools.partial(filter_edge_kernel, layout),
        2,
        [total, edges, place],
        [IN_VMEM] * 3,
        [
            pltpu.VMEM((2, width_x + 2 * PAD, width_y), F32),
            pltpu.VMEM((2, width_x, width_y), F32),
        ],
        0.3,
        1,
    )
    inner = add_middle(*inner, ends[0][:1])
    ends = add_middle(*ends, [])
    pieces = call(
        functools.partial(join_kernel, middle, block_rows),
        [on_chip(*piece)] * far,
        [IN_VMEM] * far,
        inner + ends,
        [IN_VMEM] * (2 * middle),
    )
    got = [swap_over(pieces[slot], "grp", far_masks[slot]) for slot in order]
    scale = 3.0 / (STEPS * math.sqrt(ngrp))
    grad = call(
        functools.partial(last_kernel, scale),
        jax.ShapeDtypeStruct(piece, F32),
        IN_VMEM,
        [pieces[0]] + got,
        [IN_VMEM] * far,
    )
    finals = call(
        out_kernel,
        jax.ShapeDtypeStruct(fwd_fields.shape, F32),
        IN_HBM,
        [e_fwd, h_fwd],
        [IN_VMEM] * 2,
        [
            pltpu.VMEM((3, depth, width_x, width_y), F32),
            pltpu.SemaphoreType.DMA((6,)),
        ],
        micros=1.7,
    )
    return finals, grad.reshape(density.shape)


def solution(mesh):
    placed = (
        P("grp", None, "slab", None, None),
        P("grp", None, "slab", None, None),
        P("slab", "grp", None),
        P(),
        P(),
        P(),
        P("grp", None),
        P("grp"),
    )
    return jax.shard_map(
        per_device,
        mesh=mesh,
        in_specs=placed,
        out_specs=(P("grp", None, "slab", None, None), P("slab", "grp", None)),
        check_vma=False,
    )
```

```python
import functools
import math

import jax
import jax.numpy as jnp
from jax import lax
from jax.experimental import pallas as pl
from jax.experimental.pallas import tpu as pltpu
from jax.sharding import PartitionSpec as P

STEPS = 4
AMPLITUDE = 4.0
PAD = 8
F32 = jnp.float32
HBM_PER_MICRO = 1.0e5

VMEM = pltpu.MemorySpace.VMEM
IN_VMEM = pl.BlockSpec(memory_space=pltpu.VMEM)
IN_SMEM = pl.BlockSpec(memory_space=pltpu.SMEM)
IN_HBM = pl.BlockSpec(memory_space=pltpu.MemorySpace.HBM)


def on_chip(*shape):
    return VMEM(shape, F32)


def held(array, spec):
    if spec is IN_SMEM:
        return array
    space = VMEM if spec is IN_VMEM else pltpu.MemorySpace.HBM
    return pltpu.with_memory_space_constraint(array, space)


def call(kernel, outs, out_specs, operands, specs, scratch=(), aliases=None, micros=0.3):
    operands = [held(a, s) for a, s in zip(operands, specs)]
    return pl.pallas_call(
        kernel,
        out_shape=outs,
        in_specs=specs,
        out_specs=out_specs,
        scratch_shapes=scratch,
        input_output_aliases=aliases or {},
        compiler_params=pltpu.CompilerParams(vmem_limit_bytes=8 << 20),
        cost_estimate=pl.CostEstimate(
            flops=0, bytes_accessed=int(micros * HBM_PER_MICRO), transcendentals=0
        ),
    )(*operands)


CHUNK = 16


def chunks(rows):
    size = CHUNK if rows % CHUNK == 0 else rows
    return [(first, size) for first in range(0, rows, size)]


def next_col(value):
    column = lax.broadcasted_iota(jnp.int32, value.shape, 1)
    moved = pltpu.roll(value, value.shape[1] - 1, 1)
    return jnp.where(column == value.shape[1] - 1, 0.0, moved)


def prev_col(value):
    column = lax.broadcasted_iota(jnp.int32, value.shape, 1)
    return jnp.where(column == 0, 0.0, pltpu.roll(value, 1, 1))


def neighbours():
    slab = lax.axis_index("slab")
    return slab < lax.axis_size("slab") - 1, slab > 0


class Window:
    def __init__(self, e, h, coef=None, force=None):
        self.e, self.h, self.coef, self.force = e, h, coef, force
        self.rows = e.shape[2] - 2 * PAD
        self.depth = e.shape[1] - 1
        self.top, self.under = self.depth - 1, self.depth

    def read(self, ref, layer, first, size):
        return [ref[c, layer, pl.ds(PAD + first, size), :] for c in range(3)]

    def write(self, ref, layer, first, size, values):
        for c, value in enumerate(values):
            ref[c, layer, pl.ds(PAD + first, size), :] = value

    def put_h(self, layer, given=None, alone=False, pay=None):
        for first, size in chunks(self.rows):
            rows = pl.ds(PAD + first, size)
            after = pl.ds(PAD + first + 1, size)
            ex, ey, ez = self.read(self.e, layer, first, size)
            if given is None:
                hx, hy, hz = self.read(self.h, layer, first, size)
            else:
                hx, hy, hz = (value + value for value in given(layer, first, size))
            if alone:
                rise_x, rise_y = -ex, -ey
            else:
                rise_x = self.e[0, layer + 1, rows, :] - ex
                rise_y = self.e[1, layer + 1, rows, :] - ey
            ey_after = self.e[1, layer, after, :]
            ez_after = self.e[2, layer, after, :]
            hx = hx - ((next_col(ez) - ez) - rise_y)
            hy = hy - (rise_x - (ez_after - ez))
            hz = hz - ((ey_after - ey) - (next_col(ex) - ex))
            self.write(self.h, layer, first, size, (hx, hy, hz))
            if pay is not None:
                pay[0, pl.ds(first, size), :] = hx
                pay[1, pl.ds(first, size), :] = hy

    def curl_h(self, layer, lower, first, size):
        rows = pl.ds(PAD + first, size)
        before = pl.ds(PAD + first - 1, size)
        hx, hy, hz = self.read(self.h, layer, first, size)
        step_x = hx - self.h[0, lower, rows, :]
        step_y = hy - self.h[1, lower, rows, :]
        hy_before = self.h[1, layer, before, :]
        hz_before = self.h[2, layer, before, :]
        return (
            (hz - prev_col(hz)) - step_y,
            step_x - (hz - hz_before),
            (hy - hy_before) - (hx - prev_col(hx)),
        )

    def put_curl(self, curls, layer, lower):
        for first, size in chunks(self.rows):
            for c, value in enumerate(self.curl_h(layer, lower, first, size)):
                curls[c, layer, pl.ds(first, size), :] = value

    def next_e(self, layer, lower, first, size, curls=None):
        here = pl.ds(first, size)
        cell = self.coef[layer, here, :]
        if curls is None:
            curl = self.curl_h(layer, lower, first, size)
        else:
            curl = [curls[c, layer, here, :] for c in range(3)]
        ex, ey, ez = [a + cell * b for a, b in zip(self.read(self.e, layer, first, size), curl)]
        if self.force is not None:
            ez = ez + self.force(layer, here)
        return ex, ey, ez

    def put_e(self, layer, lower, curls=None, other=None, total=None, slot=None):
        for first, size in chunks(self.rows):
            news = self.next_e(layer, lower, first, size, curls)
            self.write(self.e, layer, first, size, news)
            if total is not None:
                rows = pl.ds(PAD + first, size)
                part = [a * other[c, layer, rows, :] for c, a in enumerate(news)]
                total[layer if slot is None else slot, rows, :] += part[0] + part[1] + part[2]

    def take_above(self, above):
        for first, size in chunks(self.rows):
            here, rows = pl.ds(first, size), pl.ds(PAD + first, size)
            self.h[0, self.top, rows, :] += above[1, here, :]
            self.h[1, self.top, rows, :] -= above[0, here, :]

    def take_below(self, below):
        for first, size in chunks(self.rows):
            here, rows = pl.ds(first, size), pl.ds(PAD + first, size)
            self.h[0, self.under, rows, :] = below[0, here, :] + self.e[1, 0, rows, :]
            self.h[1, self.under, rows, :] = below[1, here, :] - self.e[0, 0, rows, :]


def forcing(step, drives, forced):
    if drives is None:
        return None
    return lambda layer, here: drives[pl.ds(step, 1), :] * forced[layer, here, :]


def opening_kernel(fwd, adj, density, own, *rest):
    pays, (planes, sems) = rest[:-2], rest[-2:]
    depth, rows, width_y = fwd.shape[2:]
    top = depth - 1
    has_up, has_low = neighbours()
    held_copy = pltpu.make_async_copy(density, own, sems.at[2, 0])
    held_copy.start()

    def up(pay):
        copies = []
        for evo, given in enumerate((fwd, adj)):
            for c in range(5):
                copies.append(
                    pltpu.make_async_copy(given.at[0, c, top], planes.at[evo, c], sems.at[evo, c])
                )
        for copy in copies:
            copy.start()
        for copy in copies:
            copy.wait()
        for evo in range(2):
            for first, size in chunks(rows):
                here = pl.ds(first, size)
                ex, ey, ez, hx, hy = (planes[evo, c, here, :] for c in range(5))
                if first + size < rows:
                    ez_after = planes[evo, 2, pl.ds(first + 1, size), :]
                else:
                    row = lax.broadcasted_iota(jnp.int32, ez.shape, 0)
                    ez_after = jnp.where(row == size - 1, 0.0, pltpu.roll(ez, size - 1, 0))
                pay[evo, 0, here, :] = (hx + hx) - ((next_col(ez) - ez) + ey)
                pay[evo, 1, here, :] = (hy + hy) + (ex + (ez_after - ez))

    def down(pay):
        copies = []
        for evo, given in enumerate((fwd, adj)):
            for c in range(2):
                copies.append(
                    pltpu.make_async_copy(given.at[0, c, 0], pay.at[evo, c], sems.at[evo, c])
                )
        for copy in copies:
            copy.start()
        for copy in copies:
            copy.wait()

    if len(pays) == 2:
        up(pays[0])
        down(pays[1])
    else:
        pl.when(has_up)(lambda: up(pays[0]))
        pl.when(has_low)(lambda: down(pays[0]))
    held_copy.wait()


def first_fwd_kernel(
    layout, given, near, wave_idx, source_far, ids_far, idx_far, eps_far,
    e, h, curls, total, edges, forced, drives, base, place,
    source, block_ids, material_idx, material_eps, sems,
):
    fetches = [
        pltpu.make_async_copy(far, here, sems.at[slot])
        for slot, (far, here) in enumerate(
            (
                (source_far, source),
                (ids_far, block_ids),
                (idx_far, material_idx),
                (eps_far, material_eps),
            )
        )
    ]
    for fetch in fetches:
        fetch.start()
    first_kernel(given, near, e, h, curls)
    depth, rows, width_y = forced.shape
    nblock = block_ids.shape[0]
    block_rows = rows // nblock
    empty = jnp.zeros(total.shape[1:], F32)
    edges[0] = empty
    edges[1] = empty
    for layer in range(depth):
        total[layer] = empty
    for fetch in fetches:
        fetch.wait()
    xcoord = lax.broadcasted_iota(jnp.int32, (rows, width_y), 0)
    ycoord = lax.broadcasted_iota(jnp.int32, (rows, width_y), 1)
    offset_x = (xcoord - source[0, 1]).astype(F32) / (rows / 4.0)
    offset_y = (ycoord - source[0, 2]).astype(F32) / (width_y / 4.0)
    profile = jnp.exp(-0.5 * (offset_x * offset_x + offset_y * offset_y))
    step = lax.broadcasted_iota(jnp.int32, drives.shape, 0).astype(F32) + 1.0
    wave = jnp.full(drives.shape, wave_idx[0], jnp.int32).astype(F32)
    drives[...] = AMPLITUDE * jnp.sin(2.0 * math.pi / (6.0 + 2.0 * wave) * step)
    level = source[0, 0] - lax.axis_index("slab") * depth
    for layer in range(depth):
        forced[layer] = jnp.where(level == layer, 1.0, 0.0) * profile
    for block in range(nblock):
        value = jnp.full((block_rows, width_y), material_eps[material_idx[block]], F32)
        base[pl.ds(block * block_rows, block_rows), :] = value
    me = lax.axis_index("grp")
    block = lax.broadcasted_iota(jnp.int32, (nblock, width_y), 0)
    for slot, mask in enumerate(mask for masks in layout for mask in masks):
        place[slot] = jnp.where(block == block_ids[me ^ mask], 1.0, 0.0)


def first_kernel(given, near, e, h, curls):
    win = Window(e, h)
    rows, width_y = win.rows, e.shape[3]
    margin = jnp.zeros((PAD, width_y), F32)
    empty = jnp.zeros((rows + 2 * PAD, width_y), F32)
    for comp in range(3):
        e[comp, win.depth] = empty
        h[comp, win.depth] = empty

    def copy(layer):
        for comp in range(3):
            for ref in (e, h):
                ref[comp, layer, pl.ds(0, PAD), :] = margin
                ref[comp, layer, pl.ds(PAD + rows, PAD), :] = margin
            for first, size in chunks(rows):
                here = pl.ds(first, size)
                e[comp, layer, pl.ds(PAD + first, size), :] = given[0, comp, layer, here, :]

    def from_given(layer, first, size):
        return [given[0, 3 + c, layer, pl.ds(first, size), :] for c in range(3)]

    copy(0)
    copy(1)
    win.put_h(0, from_given)
    copy(2)
    win.put_h(1, from_given)

    def body(layer, carry):
        pl.when(layer + 2 < win.depth)(lambda: copy(layer + 2))
        win.put_h(layer + 1, from_given)
        win.put_curl(curls, layer, layer - 1)
        return carry

    lax.fori_loop(1, win.top, body, 0)


def settle_kernel(layout, *refs):
    refs = list(refs)
    del refs[:4]
    e_fwd, e_adj, below, above = (refs.pop(0) for _ in range(4))
    parts = [refs.pop(0) for _ in layout]
    ids_far, h_fwd, curls_fwd, h_adj, curls_adj, blocks, block_ids, sem = refs
    fetch = pltpu.make_async_copy(ids_far, block_ids, sem)
    fetch.start()
    nothing = jnp.zeros(blocks.shape[1:], F32)
    for block in range(blocks.shape[0]):
        blocks[block] = nothing
    has_up, has_low = neighbours()
    for evo, (e, h, curls) in enumerate(((e_fwd, h_fwd, curls_fwd), (e_adj, h_adj, curls_adj))):
        win = Window(e, h)
        pl.when(has_up)(lambda: win.take_above(above.at[evo]))
        pl.when(has_low)(lambda: win.take_below(below.at[evo]))
        win.put_curl(curls, win.top, win.top - 1)
        win.put_curl(curls, 0, win.under)
    fetch.wait()
    me = lax.axis_index("grp")
    for part, masks in zip(parts, layout):
        for slot, mask in enumerate(masks):
            blocks[block_ids[me ^ mask]] = part[slot]


def edge_kernel(step, evo, *refs):
    refs = list(refs)
    e_in, h_in = refs.pop(0), refs.pop(0)
    if evo == 1:
        other_in, edges_in = refs.pop(0), refs.pop(0)
    coef = refs.pop(0)
    drives, forced = (refs.pop(0), refs.pop(0)) if evo == 0 else (None, None)
    curls = refs.pop(0) if step == 0 else None
    below, above = (refs.pop(0), refs.pop(0)) if step > 0 else (None, None)
    e, h = refs.pop(0), refs.pop(0)
    other, edges = (refs.pop(0), refs.pop(0)) if evo == 1 else (None, None)
    pays = refs
    win = Window(e, h, coef, forcing(step, drives, forced))
    top = win.top
    has_up, has_low = neighbours()

    @pl.when(has_up)
    def _():
        if step > 0:
            win.take_above(above)
        win.put_e(top, top - 1, curls, other, edges, 1)
        if pays:
            win.put_h(top, alone=True, pay=pays[0])

    @pl.when(has_low)
    def _():
        if step > 0:
            win.take_below(below)
        win.put_e(0, win.under, curls, other, edges, 0)
        if pays:
            for c in range(2):
                pays[-1][c] = e[c, 0, pl.ds(PAD, win.rows), :]


def inner_range(top):
    has_up, has_low = neighbours()
    return jnp.where(has_low, 1, 0), jnp.where(has_up, top - 1, top)


def begin_kernel(
    e_fwd_in, e_adj_in, total_in, coef, drives, forced, curls_fwd, curls_adj,
    e_fwd, e_adj, total,
):
    fwd = Window(e_fwd, None, coef, forcing(0, drives, forced))
    adj = Window(e_adj, None, coef)
    lowest, highest = inner_range(fwd.top)

    def body(layer, carry):
        fwd.put_e(layer, None, curls_fwd)
        adj.put_e(layer, None, curls_adj, e_fwd, total)
        return carry

    lax.fori_loop(lowest, highest + 1, body, 0)


def inner_kernel(step, evo, *refs):
    refs = list(refs)
    e_in, h_in = refs.pop(0), refs.pop(0)
    if evo == 1:
        other_in, total_in = refs.pop(0), refs.pop(0)
    coef = refs.pop(0)
    drives, forced = (refs.pop(0), refs.pop(0)) if evo == 0 else (None, None)
    e, h = refs.pop(0), refs.pop(0)
    other, total = (refs.pop(0), refs.pop(0)) if evo == 1 else (None, None)
    win = Window(e, h, coef, forcing(step, drives, forced))
    lowest, highest = inner_range(win.top)
    win.put_h(0)
    pl.when(lowest == 1)(lambda: win.put_h(1))

    def body(layer, carry):
        win.put_h(layer + 1)
        win.put_e(layer, jnp.where(layer == 0, win.under, layer - 1), None, other, total)
        return carry

    if lax.axis_size("slab") == 2:
        lax.fori_loop(0, win.depth - 2, lambda i, carry: body(lowest + i, carry), 0, unroll=2)
    else:
        lax.fori_loop(lowest, highest, body, 0)
    win.put_e(highest, highest - 1, None, other, total)


def coef_layer(layer, coef, placed, base):
    for first, size in chunks(base.shape[0]):
        here = pl.ds(first, size)
        coef[layer, here, :] = 0.25 / (base[here, :] + 3.0 * filtered(placed, first, size))


def clear_margins(placed):
    rows = placed.shape[0] - 2 * PAD
    margin = jnp.zeros((PAD, placed.shape[1]), F32)
    placed[pl.ds(0, PAD), :] = margin
    placed[pl.ds(PAD + rows, PAD), :] = margin


def place_layer(layer, first_slot, parts, place, blocks, placed):
    nblock = blocks.shape[0]
    block_rows = (placed.shape[0] - 2 * PAD) // nblock
    clear_margins(placed)
    start = layer * block_rows
    source = pl.ds(start if isinstance(layer, int) else pl.multiple_of(start, block_rows), block_rows)
    pieces = [part[slot, source, :] for part in parts for slot in range(part.shape[0])]
    for block in range(nblock):
        value = blocks[block, source, :]
        for slot, piece in enumerate(pieces):
            value = value + place[first_slot + slot, pl.ds(block, 1), :] * piece
        placed[pl.ds(PAD + block * block_rows, block_rows), :] = value


def coef_edge_kernel(first_slot, count, *refs):
    parts, (place, base, blocks, coef, placed) = refs[:count], refs[count:]
    edge_layers = (0, coef.shape[0] - 1)
    for which, layer in enumerate(edge_layers):
        place_layer(layer, first_slot, parts, place, blocks, placed.at[which])
    for which, layer in enumerate(edge_layers):
        coef_layer(layer, coef, placed.at[which], base)


def coef_inner_kernel(first_slot, count, coef_in, *refs):
    parts, (place, base, blocks, coef, placed) = refs[:count], refs[count:]

    def body(layer, carry):
        there = placed.at[lax.rem(layer, 2)]
        place_layer(layer, first_slot, parts, place, blocks, there)
        coef_layer(layer, coef, there, base)
        return carry

    lax.fori_loop(1, coef.shape[0] - 1, body, 0, unroll=2)


def filtered(padded, first, size):
    here = padded[pl.ds(PAD + first, size), :]
    before = padded[pl.ds(PAD + first - 1, size), :]
    after = padded[pl.ds(PAD + first + 1, size), :]
    along = before + 2.0 * here + after
    return (prev_col(along) + 2.0 * along + next_col(along)) * 0.0625


def tie_kernel(*refs):
    pass


def tie(array, others):
    return call(
        tie_kernel, on_chip(*array.shape), IN_VMEM, [array] + others,
        [IN_VMEM] * (1 + len(others)), aliases={0: 0},
    )


def pack_kernel(*refs):
    out = refs[-1]
    for slot, ref in enumerate(refs[:-1]):
        out[slot] = ref[...]


def filter_inner_kernel(layout, total, after, block_ids_far, *rest):
    parts, (blocks, wide, block_ids, sem) = rest[:-4], rest[-4:]
    fetch = pltpu.make_async_copy(block_ids_far, block_ids, sem)
    fetch.start()
    depth = total.shape[0]
    nblock = blocks.shape[0]
    rows = wide.shape[1]
    block_rows = rows // nblock
    me = lax.axis_index("grp")

    def body(layer, carry):
        there = wide.at[lax.rem(layer, 2)]
        for first, size in chunks(rows):
            there[pl.ds(first, size), :] = filtered(total.at[layer], first, size)
        for block in range(nblock):
            target = pl.ds(pl.multiple_of((layer - 1) * block_rows, block_rows), block_rows)
            blocks[block, target, :] = there[pl.ds(block * block_rows, block_rows), :]
        return carry

    lax.fori_loop(1, depth - 1, body, 0, unroll=2)
    fetch.wait()
    inner = pl.ds(0, (depth - 2) * block_rows)
    for slot, mask in enumerate(mask for masks in layout for mask in masks):
        part = parts[slot // parts[0].shape[0]]
        part[slot % part.shape[0]] = blocks[block_ids[me ^ mask], inner, :]


def filter_edge_kernel(layout, total, edges, place, *rest):
    parts, (sums, wide) = rest[:-2], rest[-2:]
    depth = total.shape[0]
    nblock = place.shape[0]
    rows = wide.shape[1]
    block_rows = rows // nblock
    for which, layer in enumerate((0, depth - 1)):
        sums[which] = total[layer] + edges[which]
        for first, size in chunks(rows):
            wide[which, pl.ds(first, size), :] = filtered(sums.at[which], first, size)
    for which in range(2):
        blocks = [
            wide[which, pl.ds(block * block_rows, block_rows), :] for block in range(nblock)
        ]
        target = pl.ds(which * block_rows, block_rows)
        for slot in range(nblock):
            value = None
            for block, piece in enumerate(blocks):
                term = place[slot, pl.ds(block, 1), :] * piece
                value = term if value is None else value + term
            parts[slot // parts[0].shape[0]][slot % parts[0].shape[0], target, :] = value


def add_kernel(pairs, count, *refs):
    outs = refs[-count:]
    size, per = refs[0].shape[0], outs[0].shape[0]
    for pair in range(pairs):
        kept, got = refs[pair], refs[pairs + pair]
        for first in range(0, size, per):
            part = pl.ds(first, per)
            outs[(pair * size + first) // per][...] = kept[part] + got[part]


def join_kernel(count, block_rows, *refs):
    inner, edge, outs = refs[:count], refs[count : 2 * count], refs[2 * count :]
    rows = outs[0].shape[0]
    for slot, out in enumerate(outs):
        middle, ends = inner[0][slot], edge[0][slot]
        for a, b in zip(inner[1:], edge[1:]):
            middle, ends = middle + a[slot], ends + b[slot]
        out[pl.ds(0, block_rows), :] = ends[:block_rows]
        out[pl.ds(block_rows, rows - 2 * block_rows), :] = middle
        out[pl.ds(rows - block_rows, block_rows), :] = ends[block_rows:]


def last_kernel(scale, *refs):
    value = refs[0][...]
    for ref in refs[1:-1]:
        value = value + ref[...]
    refs[-1][...] = value * scale


def out_kernel(e, h, finals, halves, sems):
    depth = e.shape[1] - 1
    rows = e.shape[2] - 2 * PAD
    every = pl.ds(PAD, rows)
    copies = [
        pltpu.make_async_copy(e.at[c, pl.ds(0, depth), every, :], finals.at[0, c], sems.at[c])
        for c in range(3)
    ]
    for copy in copies:
        copy.start()
    for c in range(3):

        def body(layer, carry, c=c):
            halves[c, layer] = 0.5 * h[c, layer, every, :]
            return carry

        lax.fori_loop(0, depth, body, 0)
        copy = pltpu.make_async_copy(halves.at[c], finals.at[0, 3 + c], sems.at[3 + c])
        copy.start()
        copies.append(copy)
    for copy in copies:
        copy.wait()


def swap_over(array, axis, mask):
    return lax.ppermute(array, axis, [(i, i ^ mask) for i in range(lax.axis_size(axis))])


def shift_over(array, axis, distance):
    size = lax.axis_size(axis)
    route = [(i, i + distance) for i in range(size) if 0 <= i + distance < size]
    return lax.ppermute(array, axis, route)


def trade(pays):
    if len(pays) == 1:
        return [swap_over(pays[0], "slab", 1)] * 2
    return [shift_over(pays[0], "slab", 1), shift_over(pays[1], "slab", -1)]


def per_device(
    fwd_fields, adj_fields, density, block_ids, material_idx, material_eps, source_pos, wave_idx
):
    depth, width_x, width_y = fwd_fields.shape[2:]
    nblock = block_ids.shape[0]
    block_rows = width_x // nblock
    ngrp = lax.axis_size("grp")
    npay = 1 if lax.axis_size("slab") == 2 else 2

    far = 4
    middle = ngrp // (2 * far)
    far_masks = [2 * middle * j for j in range(far)]
    middle_masks = [2 * j for j in range(middle)]
    layout = [
        [core + mid + top for top in far_masks] for core in (0, 1) for mid in middle_masks
    ]
    piece = (depth * block_rows, width_y)
    group = (far,) + piece

    field_shape = on_chip(3, depth + 1, width_x + 2 * PAD, width_y)
    curls_shape = on_chip(3, depth, width_x, width_y)
    halo_shape = on_chip(2, width_x, width_y)
    total_shape = on_chip(depth, width_x + 2 * PAD, width_y)
    edges_shape = on_chip(2, width_x + 2 * PAD, width_y)
    coef_shape = on_chip(depth, width_x, width_y)
    plane = on_chip(width_x, width_y)

    def by_owner(kernel, layers, operands, specs, scratch, micros, messages):
        slots = middle * far // messages
        parts = call(
            kernel,
            [on_chip(slots, layers * block_rows, width_y)] * (2 * messages),
            [IN_VMEM] * (2 * messages),
            operands,
            specs,
            scratch,
            micros=micros,
        )
        return list(parts[:messages]), [swap_over(part, "grp", 1) for part in parts[messages:]]

    def add_middle(kept, got, after):
        sums = call(
            functools.partial(add_kernel, len(kept), middle),
            [on_chip(far, *kept[0].shape[1:])] * middle,
            [IN_VMEM] * middle,
            kept + got + after,
            [IN_VMEM] * (len(kept + got + after)),
        )
        return [sums[0]] + [
            swap_over(part, "grp", mask) for part, mask in zip(sums[1:], middle_masks[1:])
        ]

    design = density.reshape(piece)
    got = [swap_over(design, "grp", mask) for mask in far_masks[1:]]
    own, *pays = call(
        opening_kernel,
        [on_chip(*piece)] + [on_chip(2, 2, width_x, width_y)] * npay,
        [IN_VMEM] * (1 + npay),
        [fwd_fields, adj_fields, design],
        [IN_HBM] * 3,
        [pltpu.VMEM((2, 5, width_x, width_y), F32), pltpu.SemaphoreType.DMA((3, 5))],
    )
    below, above = trade(pays)

    near = call(pack_kernel, on_chip(*group), IN_VMEM, [own] + got, [IN_VMEM] * far)
    others = [swap_over(near, "grp", mask) for mask in middle_masks[1:]]
    near_across = swap_over(near, "grp", 1)

    e_fwd, h_fwd, curls_fwd, total, edges, forced, drives, base, place = call(
        functools.partial(first_fwd_kernel, layout),
        [
            field_shape,
            field_shape,
            curls_shape,
            total_shape,
            edges_shape,
            on_chip(depth, width_x, width_y),
            on_chip(STEPS, width_y),
            plane,
            on_chip(nblock, nblock, width_y),
        ],
        [IN_VMEM] * 9,
        [fwd_fields, near, wave_idx, source_pos, block_ids, material_idx, material_eps],
        [IN_VMEM] * 2 + [IN_SMEM] + [IN_HBM] * 4,
        [
            pltpu.SMEM(source_pos.shape, jnp.int32),
            pltpu.SMEM(block_ids.shape, jnp.int32),
            pltpu.SMEM(material_idx.shape, jnp.int32),
            pltpu.SMEM(material_eps.shape, F32),
            pltpu.SemaphoreType.DMA((4,)),
        ],
        micros=1.5,
    )
    e_adj, h_adj, curls_adj = call(
        first_kernel,
        [field_shape, field_shape, curls_shape],
        [IN_VMEM] * 3,
        [adj_fields, near],
        [IN_VMEM, IN_VMEM],
        micros=1.2,
    )
    others = [tie(part, [e_fwd, e_adj]) for part in others]
    early = [near] + others + [near_across]
    last = [swap_over(part, "grp", 1) for part in others]
    first_slot = far * len(early)

    h_fwd, curls_fwd, h_adj, curls_adj, blocks = call(
        functools.partial(settle_kernel, layout[: len(early)]),
        [field_shape, curls_shape] * 2 + [on_chip(nblock, *piece)],
        [IN_VMEM] * 5,
        [h_fwd, curls_fwd, h_adj, curls_adj, e_fwd, e_adj, below, above] + early + [block_ids],
        [IN_VMEM] * (8 + len(early)) + [IN_HBM],
        [pltpu.SMEM(block_ids.shape, jnp.int32), pltpu.SemaphoreType.DMA],
        aliases={0: 0, 1: 1, 2: 2, 3: 3},
        micros=0.6,
    )
    placed = pltpu.VMEM((2, width_x + 2 * PAD, width_y), F32)
    coef = call(
        functools.partial(coef_edge_kernel, first_slot, len(last)),
        coef_shape,
        IN_VMEM,
        last + [place, base, blocks],
        [IN_VMEM] * (len(last) + 3),
        [placed],
    )

    arrived_fwd, arrived_adj = [curls_fwd], [curls_adj]
    for step in range(STEPS):
        more = npay if step < STEPS - 1 else 0

        def edge_fwd(e_fwd, h_fwd):
            return call(
                functools.partial(edge_kernel, step, 0),
                [field_shape] * 2 + [halo_shape] * more,
                [IN_VMEM] * (2 + more),
                [e_fwd, h_fwd, coef, drives, forced] + arrived_fwd,
                [IN_VMEM] * (5 + len(arrived_fwd)),
                aliases={0: 0, 1: 1},
            )

        if more:
            e_fwd, h_fwd, *pays = edge_fwd(e_fwd, h_fwd)
            arrived_fwd_next = trade(pays)
        if step > 0:
            e_adj, h_adj, e_fwd, total = call(
                functools.partial(inner_kernel, step, 1),
                [field_shape] * 3 + [total_shape],
                [IN_VMEM] * 4,
                [e_adj, h_adj, e_fwd, total, coef],
                [IN_VMEM] * 5,
                aliases={0: 0, 1: 1, 2: 2, 3: 3},
                micros=1.2,
            )
        if not more:
            e_fwd, h_fwd = edge_fwd(e_fwd, h_fwd)
            inner = by_owner(
                functools.partial(filter_inner_kernel, layout),
                depth - 2,
                [total, e_fwd, block_ids],
                [IN_VMEM, IN_VMEM, IN_HBM],
                [
                    pltpu.VMEM((nblock,) + piece, F32),
                    pltpu.VMEM((2, width_x, width_y), F32),
                    pltpu.SMEM(block_ids.shape, jnp.int32),
                    pltpu.SemaphoreType.DMA,
                ],
                0.8,
                middle,
            )
        e_adj, h_adj, e_fwd, edges, *pays = call(
            functools.partial(edge_kernel, step, 1),
            [field_shape] * 3 + [edges_shape] + [halo_shape] * more,
            [IN_VMEM] * (4 + more),
            [e_adj, h_adj, e_fwd, edges, coef] + arrived_adj,
            [IN_VMEM] * (5 + len(arrived_adj)),
            aliases={0: 0, 1: 1, 2: 2, 3: 3},
        )
        if not more:
            break
        arrived_fwd, arrived_adj = arrived_fwd_next, trade(pays)
        if step == 0:
            coef = call(
                functools.partial(coef_inner_kernel, first_slot, len(last)),
                coef_shape,
                IN_VMEM,
                [coef] + last + [place, base, blocks],
                [IN_VMEM] * (len(last) + 4),
                [placed],
                aliases={0: 0},
                micros=0.6,
            )
            e_fwd, e_adj, total = call(
                begin_kernel,
                [field_shape, field_shape, total_shape],
                [IN_VMEM] * 3,
                [e_fwd, e_adj, total, coef, drives, forced, curls_fwd, curls_adj],
                [IN_VMEM] * 8,
                aliases={0: 0, 1: 1, 2: 2},
                micros=0.5,
            )
        e_fwd, h_fwd = call(
            functools.partial(inner_kernel, step + 1, 0),
            [field_shape] * 2,
            [IN_VMEM] * 2,
            [e_fwd, h_fwd, coef, drives, forced],
            [IN_VMEM] * 5,
            aliases={0: 0, 1: 1},
            micros=1.1,
        )

    ends = by_owner(
        functools.partial(filter_edge_kernel, layout),
        2,
        [total, edges, place],
        [IN_VMEM] * 3,
        [
            pltpu.VMEM((2, width_x + 2 * PAD, width_y), F32),
            pltpu.VMEM((2, width_x, width_y), F32),
        ],
        0.3,
        1,
    )
    inner = add_middle(*inner, ends[0][:1])
    ends = add_middle(*ends, [])
    pieces = call(
        functools.partial(join_kernel, middle, block_rows),
        [on_chip(*piece)] * far,
        [IN_VMEM] * far,
        inner + ends,
        [IN_VMEM] * (2 * middle),
    )
    got = [swap_over(part, "grp", mask) for part, mask in zip(pieces[:0:-1], far_masks[:0:-1])]
    scale = 3.0 / (STEPS * math.sqrt(ngrp))
    grad = call(
        functools.partial(last_kernel, scale),
        jax.ShapeDtypeStruct(piece, F32),
        IN_VMEM,
        [pieces[0]] + got,
        [IN_VMEM] * far,
    )
    finals = call(
        out_kernel,
        jax.ShapeDtypeStruct(fwd_fields.shape, F32),
        IN_HBM,
        [e_fwd, h_fwd],
        [IN_VMEM] * 2,
        [
            pltpu.VMEM((3, depth, width_x, width_y), F32),
            pltpu.SemaphoreType.DMA((6,)),
        ],
        micros=1.7,
    )
    return finals, grad.reshape(density.shape)


def solution(mesh):
    placed = (
        P("grp", None, "slab", None, None),
        P("grp", None, "slab", None, None),
        P("slab", "grp", None),
        P(),
        P(),
        P(),
        P("grp", None),
        P("grp"),
    )
    return jax.shard_map(
        per_device,
        mesh=mesh,
        in_specs=placed,
        out_specs=(P("grp", None, "slab", None, None), P("slab", "grp", None)),
        check_vma=False,
    )
```
